32 devices in a mesh: dp: 4 (over y, x), seq: 8 (over z, core).
Axes of the slice: x: 2, y: 2, z: 4, core: 2. Of those that a mesh axis runs over, the one named last changes fastest.
Arguments:
- resid_in: bfloat16 [12, 2048, 1536], P('dp', 'seq'), may hold values from -6 to 6
- out_grad: bfloat16 [12, 2048, 1536], P('dp', 'seq'), may hold values from -6 to 6
- lengths: int32 [12], P('dp'), may hold values from 512 to 2048, as said below
- norm_gain: float32 [1536], replicated, may hold values from 0.25 to 1.75
- in_proj: bfloat16 [1536, 6400], P(('dp', 'seq')), may hold values from -0.15625 to 0.15625
- dt_proj: bfloat16 [1536, 48], P(('dp', 'seq')), may hold values from -0.15625 to 0.15625
- conv_weight: float32 [4, 3328], replicated, may hold values from -3 to 3
- conv_bias: float32 [3328], replicated, may hold values from -3 to 3
- dt_bias: float32 [48], replicated, may hold values from -13 to -3.6
- a_log: float32 [48], replicated, may hold values from 0 to 2.7
- skip_scale: float32 [48], replicated, may hold values from 0.5 to 1.5
- gate_gain: float32 [3072], replicated, may hold values from 0.25 to 1.75
- out_proj: bfloat16 [3072, 1536], P(('dp', 'seq')), may hold values from -0.109375 to 0.109375
Outputs:
- output: bfloat16 [12, 2048, 1536], P('dp', 'seq')
- input_grad: bfloat16 [12, 2048, 1536], P('dp', 'seq')
- grad_in_proj: float32 [1536, 6400], P(('dp', 'seq'))
- grad_dt_proj: float32 [1536, 48], P(('dp', 'seq'))
- grad_out_proj: float32 [3072, 1536], P(('dp', 'seq'))
- grad_norm_gain: float32 [1536], replicated
- grad_conv_weight: float32 [4, 3328], replicated
- grad_conv_bias: float32 [3328], replicated
- grad_dt_bias: float32 [48], replicated
- grad_a_log: float32 [48], replicated
- grad_skip: float32 [48], replicated
- grad_gate_gain: float32 [3072], replicated
The draws below stay inside these ranges and needn't reach their ends.
Inputs may be any that keep to these rules, and one draw needn't show every extreme that they name: `lengths`: each of the groups of 3 consecutive sequences starting at a multiple of 3 holds at least one of length 2048.
All inputs are finite; a program needn't handle non-finite values.
Results may differ from the reference program's by a relative error of at most 0.012.
The reference program's roundings to bfloat16 on the way count: a program that leaves them out, or rounds other values in their place, can miss the bound.
Values may be sent and summed in bfloat16 or wider, within the bound.
A program may use at most 576 MiB of HBM per device.

```python
from functools import partial
import jax
import jax.numpy as jnp
from jax import lax

D = 1536
DI = 3072
H = 48
P_SIZE = 64
N = 128
K = 4
SEG = 256
MICRO = 3
S_MB = 1
CH = 3328
PROJ = 6400
LEN = 2048
MINLEN = 512
SEQS = 12


def draw_lengths(key, part):
    key = jax.random.fold_in(key, 7)
    first_key, second_key = jax.random.split(key)
    drawn_rows = jax.random.randint(first_key, (SEQS,), MINLEN, LEN + 1)
    group_len = MICRO * S_MB
    groups = SEQS // group_len
    chosen = jax.random.randint(second_key, (groups, 1), 0, group_len)
    slot_ids = lax.iota(jnp.int32, group_len)[None, :]
    full_rows = jnp.where(slot_ids == chosen, LEN, drawn_rows.reshape(groups, group_len))
    return full_rows.reshape(SEQS).astype(jnp.int32)


def draw_dt_bias(key, part):
    key = jax.random.fold_in(key, 13)
    first_key, second_key = jax.random.split(key)
    slow_share = 0.5
    slow_heads = jax.random.uniform(first_key, (H,), jnp.float32) < slow_share
    position = jax.random.uniform(second_key, (H,), jnp.float32)
    slow_level = -4.0 + 3.0 * position
    fast_level = 1.0 + (jnp.log(LEN / 40.0) - 1.0) * position
    drawn = jnp.where(slow_heads, slow_level, fast_level) - jnp.log(LEN * 1.0)
    return jnp.clip(drawn, -13.0, -3.6).astype(jnp.float32)


def block_scale(rng, dims, shards, smallest, top_value):
    level = 1.0
    for dim, shards_of in shards:
        steps = jax.random.uniform(jax.random.fold_in(jax.random.fold_in(rng, 6), dim), (shards_of,), jnp.float32, smallest / len(shards), top_value / len(shards))
        level = level * jnp.repeat(jnp.exp(steps), dims[dim] // shards_of).reshape((-1,) + (1,) * (len(dims) - 1 - dim))
    return level


def noise(stream_key, extent, width, reach, pieces=(), dtype=jnp.bfloat16):
    entries = width * jax.random.normal(stream_key, extent, jnp.float32)
    if pieces:
        entries = entries * block_scale(stream_key, extent, pieces, -0.22, 0.18)
    return jnp.clip(entries, -reach, reach).astype(dtype)


def setup_inputs(seed: int = 0) -> dict:
    arg_keys = jax.random.split(jax.random.key(seed), 14)
    resid_in = noise(arg_keys[0], (SEQS, LEN, D), 1.0, 6.0, ((0, 4), (1, 8)))
    out_grad = noise(arg_keys[1], (SEQS, LEN, D), 1.0, 6.0, ((0, 4), (1, 8)))
    lengths = draw_lengths(jax.random.fold_in(arg_keys[13], 71), 0)
    norm_gain = jnp.clip(1.0 + 0.15 * jax.random.normal(arg_keys[3], (D,), jnp.float32), 0.25, 1.75)
    in_proj = noise(arg_keys[4], (D, PROJ), D ** -0.5, 0.15625, ((0, 32),))
    dt_proj = noise(arg_keys[5], (D, H), D ** -0.5, 0.15625, ((0, 32),))
    conv_weight = noise(arg_keys[6], (K, CH), K ** -0.5, 3.0, (), jnp.float32)
    conv_bias = noise(arg_keys[7], (CH,), 0.5, 3.0, (), jnp.float32)
    dt_bias = draw_dt_bias(jax.random.fold_in(arg_keys[13], 71), 0)
    a_log = jnp.clip(jax.random.uniform(arg_keys[9], (H,), jnp.float32, 0.0, 2.7), 0.0, 2.7)
    skip_scale = jnp.clip(jax.random.uniform(arg_keys[10], (H,), jnp.float32, 0.5, 1.5), 0.5, 1.5)
    gate_gain = jnp.clip(1.0 + 0.15 * jax.random.normal(arg_keys[11], (DI,), jnp.float32), 0.25, 1.75)
    out_proj = noise(arg_keys[12], (DI, D), DI ** -0.5, 0.109375, ((0, 32),))
    return dict(resid_in=resid_in, out_grad=out_grad, lengths=lengths, norm_gain=norm_gain, in_proj=in_proj, dt_proj=dt_proj, conv_weight=conv_weight, conv_bias=conv_bias, dt_bias=dt_bias, a_log=a_log, skip_scale=skip_scale, gate_gain=gate_gain, out_proj=out_proj)


epsilon = 1e-05
highest = lax.Precision.HIGHEST

@jax.custom_vjp
def low(v):
    return lax.optimization_barrier(v.astype(jnp.bfloat16)).astype(jnp.float32)

@jax.custom_vjp
def low_back(v):
    return v

def low_keep(v):
    return (low(v), None)

def low_pass(kept, grad):
    return (grad,)

def back_keep(v):
    return (v, None)

def back_low(kept, grad):
    return (low(grad),)
low.defvjp(low_keep, low_pass)
low_back.defvjp(back_keep, back_low)

def rms_input(resid_rows, norm_gain):
    inv_rms = lax.rsqrt(lax.optimization_barrier(jnp.mean(resid_rows * resid_rows, axis=-1, keepdims=True)) + epsilon)
    return resid_rows * inv_rms * norm_gain

def gated_norm(ssd_rows, gate_in, gate_gain):
    gated_rows = ssd_rows * jax.nn.silu(gate_in)
    inv_rms = lax.rsqrt(lax.optimization_barrier(jnp.mean(gated_rows * gated_rows, axis=-1, keepdims=True)) + epsilon)
    return gated_rows * inv_rms * gate_gain

def conv_silu(padded, conv_weight, conv_bias):
    tap_count = conv_weight.shape[0]
    span_len = padded.shape[1] - tap_count + 1
    summed = conv_bias + conv_weight[0] * padded[:, 0:span_len]
    for offset in range(1, tap_count):
        summed = summed + conv_weight[offset] * padded[:, offset:offset + span_len]
    return jax.nn.silu(summed)

def step_sizes(dt_raw, dt_bias, a_log):
    step_size = jax.nn.softplus(dt_raw + dt_bias)
    return (step_size, jnp.cumsum(step_size * -jnp.exp(a_log), axis=1))

def ssd_state(values, dt_raw, dt_bias, a_log, in_keys):
    step_size, log_decay = step_sizes(dt_raw, dt_bias, a_log)
    log_total = log_decay[:, -1]
    weighted = values * (jnp.exp(log_total[:, None, :] - log_decay) * step_size)[..., None]
    local_state = jnp.einsum('bshp,bsn->bhpn', weighted, in_keys, precision=highest)
    return (local_state, jnp.exp(log_total))

def ssd_out(values, dt_raw, dt_bias, a_log, in_keys, out_keys, skip_scale, carried):
    step_size, log_decay = step_sizes(dt_raw, dt_bias, a_log)
    span_len = values.shape[1]
    key_scores = jnp.einsum('btn,bsn->bts', out_keys, in_keys, precision=highest)
    decay_heads = jnp.swapaxes(log_decay, 1, 2)
    causal_mask = lax.iota(jnp.int32, span_len)[:, None] >= lax.iota(jnp.int32, span_len)[None, :]
    log_gaps = jnp.where(causal_mask, decay_heads[:, :, :, None] - decay_heads[:, :, None, :], -jnp.inf)
    weights = jnp.exp(log_gaps) * jnp.swapaxes(step_size, 1, 2)[:, :, None, :] * key_scores[:, None]
    inside = jnp.einsum('bhts,bshp->bthp', weights, values, precision=highest)
    carried_part = jnp.einsum('btn,bhpn->bthp', out_keys, carried, precision=highest) * jnp.exp(log_decay)[..., None]
    return inside + carried_part + skip_scale[:, None] * values

def layer(mask_rows, resid_rows, norm_gain, in_proj, dt_proj, conv_weight, conv_bias, dt_bias, a_log, skip_scale, gate_gain, out_proj):
    normed = low(rms_input(resid_rows, norm_gain))
    projected = low_back(jnp.dot(normed, in_proj, precision=highest))
    dt_rows = low_back(jnp.dot(normed, dt_proj, precision=highest))
    gate_in = projected[:, :DI]
    padded = jnp.concatenate([jnp.zeros((K - 1, CH), jnp.float32), projected[:, DI:]], axis=0)
    conv_rows = low(conv_silu(padded[None], conv_weight, conv_bias)[0])
    blocks = LEN // SEG
    values = conv_rows[:, :DI].reshape(blocks, SEG, H, P_SIZE)
    in_keys = conv_rows[:, DI:DI + N].reshape(blocks, SEG, N)
    out_keys = conv_rows[:, DI + N:].reshape(blocks, SEG, N)
    dt_raw = dt_rows.reshape(blocks, SEG, H)
    local_state, block_decay = ssd_state(values, dt_raw, dt_bias, a_log, in_keys)

    def carry_step(state_now, block_item):
        decay_item, local_item = block_item
        return (local_item + decay_item[:, None, None] * state_now, state_now)
    _, carried = lax.scan(carry_step, jnp.zeros((H, P_SIZE, N), jnp.float32), (block_decay, local_state))
    ssd_rows = ssd_out(values, dt_raw, dt_bias, a_log, in_keys, out_keys, skip_scale, carried).reshape(LEN, DI)
    normed_out = low(gated_norm(ssd_rows, gate_in, gate_gain))
    mixer_out = low_back(jnp.dot(normed_out, out_proj, precision=highest))
    return mask_rows[:, None] * (resid_rows + mixer_out)

def reference(resid_in, out_grad, lengths, norm_gain, in_proj, dt_proj, conv_weight, conv_bias, dt_bias, a_log, skip_scale, gate_gain, out_proj):
    params = (norm_gain.astype(jnp.float32), in_proj.astype(jnp.float32), dt_proj.astype(jnp.float32), conv_weight.astype(jnp.float32), conv_bias.astype(jnp.float32), dt_bias.astype(jnp.float32), a_log.astype(jnp.float32), skip_scale.astype(jnp.float32), gate_gain.astype(jnp.float32), out_proj.astype(jnp.float32))
    positions = lax.iota(jnp.int32, LEN)

    def one_sequence(totals, seq_item):
        resid_rows, grad_rows, length_one = seq_item
        mask_rows = (positions < length_one).astype(jnp.float32)
        output_rows, pullback = jax.vjp(partial(layer, mask_rows), resid_rows.astype(jnp.float32), *params)
        seq_grads = pullback(grad_rows.astype(jnp.float32))
        totals = tuple((total_one + grad_one for total_one, grad_one in zip(totals, seq_grads[1:])))
        return (totals, (output_rows.astype(jnp.bfloat16), seq_grads[0].astype(jnp.bfloat16)))
    start_totals = tuple((jnp.zeros_like(weight_one) for weight_one in params))
    totals, (outputs, input_grads) = lax.scan(one_sequence, start_totals, (resid_in, out_grad, lengths))
    return (outputs, input_grads, totals[1], totals[2], totals[9], totals[0], totals[3], totals[4], totals[5], totals[6], totals[7], totals[8])
```

```python
import functools

import jax
import jax.numpy as jnp
from jax import lax
from jax.experimental import pallas as pl
from jax.experimental.pallas import tpu as pltpu
from jax.sharding import PartitionSpec as P

epsilon = 1e-05
highest = lax.Precision.HIGHEST
HALO = 16
HEADS = 8
LOG2E = 1.4426950408889634
f32 = jnp.float32
bf16 = jnp.bfloat16
MESH = pl.DeviceIdType.MESH


def mm(a, b):
    return lax.dot_general(a, b, (((1,), (0,)), ((), ())), preferred_element_type=f32)


def mm_nt(a, b):
    return lax.dot_general(a, b, (((1,), (1,)), ((), ())), preferred_element_type=f32)


def mm_tn(a, b):
    return lax.dot_general(a, b, (((0,), (0,)), ((), ())), preferred_element_type=f32)


def shifted(block, axis, distance):
    devices = range(lax.axis_size(axis))
    route = [(i - distance, i) for i in devices if i - distance in devices]
    return lax.ppermute(block, axis, route)


def spread(cols, width):
    rows, heads = cols.shape
    low_half = lax.broadcasted_iota(jnp.int32, (rows, 2 * width), 1) < width
    pairs = [
        jnp.where(low_half, cols[:, i : i + 1], cols[:, i + 1 : i + 2]) for i in range(0, heads, 2)
    ]
    return jnp.concatenate(pairs, axis=1)


def gather_heads(x, width):
    rows, total = x.shape
    low_half = lax.broadcasted_iota(jnp.int32, (rows, 2 * width), 1) < width
    head_lane = lax.broadcasted_iota(jnp.int32, (rows, total // width), 1)
    out = jnp.zeros((rows, total // width), f32)
    for i in range(total // (2 * width)):
        pair = x[:, i * 2 * width : (i + 1) * 2 * width]
        one = jnp.sum(jnp.where(low_half, pair, 0.0), axis=1, keepdims=True)
        two = jnp.sum(jnp.where(low_half, 0.0, pair), axis=1, keepdims=True)
        out = jnp.where(head_lane == 2 * i, one, out)
        out = jnp.where(head_lane == 2 * i + 1, two, out)
    return out


def silu_parts(v):
    sg = 1.0 / (1.0 + jnp.exp(-v))
    return v * sg, sg


def conv_pre(a, cw, cb, span):
    first = HALO - (cw.shape[0] - 1)
    out = cb
    for k in range(cw.shape[0]):
        out = out + cw[k : k + 1] * a[first + k : first + k + span]
    return out


def params_of(limit_mb, dims=None):
    return pltpu.CompilerParams(vmem_limit_bytes=limit_mb * 1024 * 1024, dimension_semantics=dims)


def keys_kernel(span, x_ref, w_ref, cw_ref, cb_ref, rows_ref, cin_ref):
    batch = rows_ref.shape[0]
    ext = span + HALO
    acc = mm(x_ref[...], w_ref[...])
    for b in range(batch):
        a = acc[b * ext : (b + 1) * ext]
        row, _ = silu_parts(conv_pre(a, cw_ref[...], cb_ref[...], span))
        rows_ref[b] = row.astype(bf16)
        cin_ref[b] = a.astype(bf16)


def keys_forward(x2, w_conv, col_block, cw, cb, batch, span):
    width = 2 * (cw.shape[1] // 2)
    ext = span + HALO
    return pl.pallas_call(
        functools.partial(keys_kernel, span),
        grid=(1,),
        in_specs=[
            pl.BlockSpec(x2.shape, lambda i: (0, 0)),
            pl.BlockSpec((w_conv.shape[0], width), lambda i: (0, col_block)),
            pl.BlockSpec(cw.shape, lambda i: (0, 0)),
            pl.BlockSpec(cb.shape, lambda i: (0, 0)),
        ],
        out_specs=[
            pl.BlockSpec((batch, span, width), lambda i: (0, 0, 0)),
            pl.BlockSpec((batch, ext, width), lambda i: (0, 0, 0)),
        ],
        out_shape=[
            jax.ShapeDtypeStruct((batch, span, width), bf16),
            jax.ShapeDtypeStruct((batch, ext, width), bf16),
        ],
        compiler_params=params_of(40),
    )(x2, w_conv, cw, cb)


def values_kernel(span, hw, x_ref, w_ref, cw_ref, cb_ref, keys_ref, col_ref, rows_ref, cin_ref, st_ref):
    batch = rows_ref.shape[0]
    n = keys_ref.shape[2] // 2
    ext = span + HALO
    acc = mm(x_ref[...], w_ref[...])
    for b in range(batch):
        a = acc[b * ext : (b + 1) * ext]
        row, _ = silu_parts(conv_pre(a, cw_ref[...], cb_ref[...], span))
        row = row.astype(bf16)
        rows_ref[b] = row
        cin_ref[b] = a.astype(bf16)
        cols = col_ref[0, b]
        c, step = cols[:, :HEADS], cols[:, HEADS:]
        weight = jnp.exp2(c[span - 1 : span] - c) * step
        vw = (row.astype(f32) * spread(weight, hw)).astype(bf16)
        st_ref[b] = mm_tn(keys_ref[b, :, :n], vw)


def values_forward(x2, w_conv, first_block, cw, cb, keys, colpack, hw, span):
    batch = keys.shape[0]
    groups = colpack.shape[0]
    cb_w = HEADS * hw
    ext = span + HALO
    inner = groups * cb_w
    return pl.pallas_call(
        functools.partial(values_kernel, span, hw),
        grid=(groups,),
        in_specs=[
            pl.BlockSpec(x2.shape, lambda i: (0, 0)),
            pl.BlockSpec((w_conv.shape[0], cb_w), lambda i: (0, first_block + i)),
            pl.BlockSpec((cw.shape[0], cb_w), lambda i: (0, i)),
            pl.BlockSpec((1, cb_w), lambda i: (0, i)),
            pl.BlockSpec(keys.shape, lambda i: (0, 0, 0)),
            pl.BlockSpec((1,) + colpack.shape[1:], lambda i: (i, 0, 0, 0)),
        ],
        out_specs=[
            pl.BlockSpec((batch, span, cb_w), lambda i: (0, 0, i)),
            pl.BlockSpec((batch, ext, cb_w), lambda i: (0, 0, i)),
            pl.BlockSpec((batch, keys.shape[2] // 2, cb_w), lambda i: (0, 0, i)),
        ],
        out_shape=[
            jax.ShapeDtypeStruct((batch, span, inner), bf16),
            jax.ShapeDtypeStruct((batch, ext, inner), bf16),
            jax.ShapeDtypeStruct((batch, keys.shape[2] // 2, inner), f32),
        ],
        compiler_params=params_of(50),
    )(x2, w_conv, cw, cb, keys, colpack)


def chain_kernel(backward, size, local_ref, decay_ref, carried_ref, sent, landed, send_sem, recv_sem):
    me = lax.axis_index("seq")
    count = lax.axis_size("seq")
    turn = -1 if backward else 1
    has_prev = me != (count - 1 if backward else 0)
    has_next = me != (0 if backward else count - 1)
    nxt = jnp.clip(me + turn, 0, count - 1)
    prv = jnp.clip(me - turn, 0, count - 1)
    barrier = pltpu.get_barrier_semaphore()

    @pl.when(has_prev)
    def _():
        pl.semaphore_signal(barrier, inc=1, device_id={"seq": prv}, device_id_type=MESH)

    @pl.when(has_next)
    def _():
        pl.semaphore_wait(barrier, 1)

    batch, _, total = local_ref.shape
    per = total // size

    def copy_of(k):
        return pltpu.make_async_remote_copy(
            src_ref=sent.at[k],
            dst_ref=landed.at[k],
            send_sem=send_sem.at[k],
            recv_sem=recv_sem.at[k],
            device_id={"seq": nxt},
            device_id_type=MESH,
        )

    for k in range(batch * per):
        b, part = k % batch, k // batch
        cols = pl.ds(part * size, size)

        @pl.when(has_prev)
        def _():
            copy_of(k).wait_recv()
            carried_ref[b, :, cols] = landed[k].astype(f32)

        @pl.when(jnp.logical_not(has_prev))
        def _():
            carried_ref[b, :, cols] = jnp.zeros_like(carried_ref[b, :, cols])

        @pl.when(has_next)
        def _():
            out = decay_ref[b, :, cols] * carried_ref[b, :, cols] + local_ref[b, :, cols]
            sent[k] = out.astype(bf16)
            copy_of(k).start()

    @pl.when(has_next)
    def _():
        for k in range(batch * per):
            copy_of(k).wait_send()


def chain(local, decay, backward, collective_id):
    size = 512
    count = local.shape[0] * (local.shape[2] // size)
    return pl.pallas_call(
        functools.partial(chain_kernel, backward, size),
        in_specs=[pl.BlockSpec(memory_space=pltpu.VMEM)] * 2,
        out_specs=pl.BlockSpec(memory_space=pltpu.VMEM),
        out_shape=jax.ShapeDtypeStruct(local.shape, f32),
        scratch_shapes=[
            pltpu.VMEM((count, local.shape[1], size), bf16),
            pltpu.VMEM((count, local.shape[1], size), bf16),
            pltpu.SemaphoreType.DMA((count,)),
            pltpu.SemaphoreType.DMA((count,)),
        ],
        compiler_params=pltpu.CompilerParams(
            collective_id=collective_id, has_side_effects=True, vmem_limit_bytes=40 * 1024 * 1024
        ),
    )(local, decay)


def causal(span, transposed):
    one = lax.broadcasted_iota(jnp.int32, (span, span), 0)
    two = lax.broadcasted_iota(jnp.int32, (span, span), 1)
    return (one <= two) if transposed else (one >= two)


def out_kernel(
    span, hw, x_ref, w_ref, v_ref, keys_ref, col_ref, row_ref, h_ref, skip_ref, gain_ref,
    y_ref, gate_ref, no_ref, rg_ref, scores, gated, squares,
):
    g, b = pl.program_id(0), pl.program_id(1)
    groups, batch = pl.num_programs(0), pl.num_programs(1)
    n = keys_ref.shape[2] // 2
    cb_w = HEADS * hw
    k_in, k_out = keys_ref[0, :, :n], keys_ref[0, :, n:]

    @pl.when(g == 0)
    def _():
        scores[b] = jnp.where(causal(span, False), mm_nt(k_out, k_in), 0.0)
        squares[b] = jnp.zeros_like(squares[b])

    cols = col_ref[0, 0]
    c, step = cols[:, :HEADS], cols[:, HEADS:]
    v = v_ref[0].astype(f32)
    vs = (v * spread(step, hw)).astype(bf16)
    s = scores[b]
    low_half = lax.broadcasted_iota(jnp.int32, (span, 2 * hw), 1) < hw
    parts = []
    for i in range(HEADS // 2):
        pair = vs[:, i * 2 * hw : (i + 1) * 2 * hw]
        total = None
        for j in range(2):
            h = 2 * i + j
            gap = jnp.minimum(c[:, h : h + 1] - row_ref[0, 0, h : h + 1, :], 0.0)
            u = (jnp.exp2(gap) * s).astype(bf16)
            half = jnp.where(low_half if j == 0 else jnp.logical_not(low_half), pair, jnp.zeros_like(pair))
            term = mm(u, half)
            total = term if total is None else total + term
        parts.append(total)
    y = jnp.concatenate(parts, axis=1)
    y = y + mm(k_out, h_ref[0].astype(bf16)) * spread(jnp.exp2(c), hw) + skip_ref[...] * v
    y_ref[0] = y
    gate = mm(x_ref[0, HALO:], w_ref[...])
    gate_ref[0] = gate.astype(bf16)
    act, _ = silu_parts(gate)
    gr = y * act
    gated[b, g] = gr
    squares[b] += jnp.broadcast_to(jnp.sum(gr * gr, axis=1, keepdims=True), squares.shape[1:])

    @pl.when(g == groups - 1)
    def _():
        rg = lax.rsqrt(squares[b][:, :1] * (1.0 / (groups * cb_w)) + epsilon)
        rg_ref[b] = jnp.broadcast_to(rg, rg_ref.shape[1:])
        for i in range(no_ref.shape[2] // cb_w):
            part = slice(i * cb_w, (i + 1) * cb_w)
            no_ref[b, :, part] = (gated[b, i] * rg * gain_ref[:, part]).astype(bf16)


def rows_forward(x_ext, w_gate, v, keys, colpack, rowpack, carried, skip, gain, hw, span):
    batch, ext, width = x_ext.shape
    groups = colpack.shape[0]
    cb_w = HEADS * hw
    inner = groups * cb_w
    n = keys.shape[2] // 2
    return pl.pallas_call(
        functools.partial(out_kernel, span, hw),
        grid=(groups, batch),
        in_specs=[
            pl.BlockSpec((1, ext, width), lambda g, b: (b, 0, 0)),
            pl.BlockSpec((width, cb_w), lambda g, b: (0, g)),
            pl.BlockSpec((1, span, cb_w), lambda g, b: (b, 0, g)),
            pl.BlockSpec((1, span, 2 * n), lambda g, b: (b, 0, 0)),
            pl.BlockSpec((1, 1, span, 2 * HEADS), lambda g, b: (g, b, 0, 0)),
            pl.BlockSpec((1, 1, HEADS, span), lambda g, b: (g, b, 0, 0)),
            pl.BlockSpec((1, n, cb_w), lambda g, b: (b, 0, g)),
            pl.BlockSpec((1, cb_w), lambda g, b: (0, g)),
            pl.BlockSpec((1, inner), lambda g, b: (0, 0)),
        ],
        out_specs=[
            pl.BlockSpec((1, span, cb_w), lambda g, b: (b, 0, g)),
            pl.BlockSpec((1, span, cb_w), lambda g, b: (b, 0, g)),
            pl.BlockSpec((batch, span, inner), lambda g, b: (0, 0, 0)),
            pl.BlockSpec((batch, span, 8), lambda g, b: (0, 0, 0)),
        ],
        out_shape=[
            jax.ShapeDtypeStruct((batch, span, inner), f32),
            jax.ShapeDtypeStruct((batch, span, inner), bf16),
            jax.ShapeDtypeStruct((batch, span, inner), bf16),
            jax.ShapeDtypeStruct((batch, span, 8), f32),
        ],
        scratch_shapes=[
            pltpu.VMEM((batch, span, span), f32),
            pltpu.VMEM((batch, groups, span, cb_w), f32),
            pltpu.VMEM((batch, span, 128), f32),
        ],
        compiler_params=params_of(56),
    )(x_ext, w_gate, v, keys, colpack, rowpack, carried, skip, gain)


def gate_back_kernel(
    span, hw, mg_ref, w_ref, y_ref, gate_ref, norm_ref, gain_ref, v_ref, keys_ref, col_ref, row_ref,
    h_ref, skip_ref,
    dgate_ref, dv_ref, dh_ref, cols_ref, dq_ref, dk_ref, dgain_ref, dskip_ref, scores, dscores, dqacc,
):
    g, b = pl.program_id(0), pl.program_id(1)
    groups = pl.num_programs(0)
    n = keys_ref.shape[2] // 2
    k_in, k_out = keys_ref[0, :, :n], keys_ref[0, :, n:]

    @pl.when(g == 0)
    def _():
        scores[b] = jnp.where(causal(span, True), mm_nt(k_in, k_out), 0.0)
        dscores[b] = jnp.zeros_like(dscores[b])
        dqacc[b] = jnp.zeros_like(dqacc[b])

    no_grad = mm_nt(mg_ref[0], w_ref[...])
    gate = gate_ref[0].astype(f32)
    y = y_ref[0]
    rg = norm_ref[0][:, 0:1]
    mean = norm_ref[0][:, 1:2]
    act, sg = silu_parts(gate)
    gn = y * act * rg
    dgain = jnp.sum(no_grad * gn, axis=0, keepdims=True)
    dg = rg * (no_grad * gain_ref[...] - gn * mean)
    dgate_ref[0] = (dg * y * (sg * (1.0 + gate * (1.0 - sg)))).astype(bf16)
    gb = (dg * act).astype(bf16)
    gf = gb.astype(f32)

    cols = col_ref[0, 0]
    c, step = cols[:, :HEADS], cols[:, HEADS:]
    v = v_ref[0].astype(f32)
    step_wide = spread(step, hw)
    vs = (v * step_wide).astype(bf16)
    skip = skip_ref[...]
    dskip = jnp.sum(gf * v, axis=0, keepdims=True)

    @pl.when(b == 0)
    def _():
        dgain_ref[...] = dgain
        dskip_ref[...] = dskip

    @pl.when(b != 0)
    def _():
        dgain_ref[...] += dgain
        dskip_ref[...] += dskip

    s = scores[b]
    low_half = lax.broadcasted_iota(jnp.int32, (span, 2 * hw), 1) < hw
    parts = []
    ds = dscores[b]
    for i in range(HEADS // 2):
        lanes = slice(i * 2 * hw, (i + 1) * 2 * hw)
        total = None
        for j in range(2):
            h = 2 * i + j
            gap = jnp.minimum(row_ref[0, 0, h : h + 1, :] - c[:, h : h + 1], 0.0)
            decay = jnp.exp2(gap)
            u = (decay * s).astype(bf16)
            keep = low_half if j == 0 else jnp.logical_not(low_half)
            half = jnp.where(keep, gb[:, lanes], jnp.zeros_like(gb[:, lanes]))
            term = mm(u, half)
            total = term if total is None else total + term
            ds = ds + decay * mm_nt(vs[:, lanes], half)
        parts.append(total)
    dscores[b] = ds
    u_all = jnp.concatenate(parts, axis=1)
    dv_ref[0] = (u_all * step_wide + skip * gf).astype(bf16)
    rise = gather_heads(gf * (y - skip * v) - vs.astype(f32) * u_all, hw)
    direct = gather_heads(v * u_all, hw)
    cols_ref[0, 0] = jnp.concatenate([rise, direct], axis=1)
    ge = (gf * spread(jnp.exp2(c), hw)).astype(bf16)
    dh_ref[0] = mm_tn(k_out, ge)
    dqacc[b] += mm_nt(ge, h_ref[0].astype(bf16))

    @pl.when(g == groups - 1)
    def _():
        low = jnp.where(causal(span, True), dscores[b], 0.0).astype(bf16)
        dq_ref[b] = dqacc[b] + mm_tn(low, k_in)
        dk_ref[b] = mm(low, k_out)


def gate_backward(mg, w_out, y, gate, norms, gain, v, keys, colpack, rowpack, carried, skip, hw, span):
    batch, _, width = mg.shape
    groups = colpack.shape[0]
    cb_w = HEADS * hw
    inner = groups * cb_w
    n = keys.shape[2] // 2
    block = pl.BlockSpec((1, span, cb_w), lambda g, b: (b, 0, g))
    lanes = pl.BlockSpec((1, cb_w), lambda g, b: (0, g))
    return pl.pallas_call(
        functools.partial(gate_back_kernel, span, hw),
        grid=(groups, batch),
        in_specs=[
            pl.BlockSpec((1, span, width), lambda g, b: (b, 0, 0)),
            pl.BlockSpec((cb_w, width), lambda g, b: (g, 0)),
            block,
            block,
            pl.BlockSpec((1, span, 8), lambda g, b: (b, 0, 0)),
            lanes,
            block,
            pl.BlockSpec((1, span, 2 * n), lambda g, b: (b, 0, 0)),
            pl.BlockSpec((1, 1, span, 2 * HEADS), lambda g, b: (g, b, 0, 0)),
            pl.BlockSpec((1, 1, HEADS, span), lambda g, b: (g, b, 0, 0)),
            pl.BlockSpec((1, n, cb_w), lambda g, b: (b, 0, g)),
            lanes,
        ],
        out_specs=[
            block,
            block,
            pl.BlockSpec((1, n, cb_w), lambda g, b: (b, 0, g)),
            pl.BlockSpec((1, 1, span, 2 * HEADS), lambda g, b: (g, b, 0, 0)),
            pl.BlockSpec((batch, span, n), lambda g, b: (0, 0, 0)),
            pl.BlockSpec((batch, span, n), lambda g, b: (0, 0, 0)),
            lanes,
            lanes,
        ],
        out_shape=[
            jax.ShapeDtypeStruct((batch, span, inner), bf16),
            jax.ShapeDtypeStruct((batch, span, inner), bf16),
            jax.ShapeDtypeStruct((batch, n, inner), f32),
            jax.ShapeDtypeStruct((groups, batch, span, 2 * HEADS), f32),
            jax.ShapeDtypeStruct((batch, span, n), f32),
            jax.ShapeDtypeStruct((batch, span, n), f32),
            jax.ShapeDtypeStruct((1, inner), f32),
            jax.ShapeDtypeStruct((1, inner), f32),
        ],
        scratch_shapes=[
            pltpu.VMEM((batch, span, span), f32),
            pltpu.VMEM((batch, span, span), f32),
            pltpu.VMEM((batch, span, n), f32),
        ],
        compiler_params=params_of(50),
    )(mg, w_out, y, gate, norms, gain, v, keys, colpack, rowpack, carried, skip)


def conv_back(dv, a, cw, cb, span, padded, out_ref, b):
    taps = cw.shape[0]
    first = HALO - (taps - 1)
    pre = conv_pre(a, cw, cb, span)
    _, sg = silu_parts(pre)
    pg = dv * (sg * (1.0 + pre * (1.0 - sg)))
    padded[16 : 16 + span] = pg
    ext = span + HALO
    total = jnp.zeros((ext, cw.shape[1]), f32)
    for k in range(taps):
        total = total + cw[k : k + 1] * padded[taps - 1 - k : taps - 1 - k + ext]
    out_ref[b] = total.astype(bf16)
    dcw = jnp.concatenate(
        [jnp.sum(pg * a[first + k : first + k + span], axis=0, keepdims=True) for k in range(taps)], axis=0
    )
    return dcw, jnp.sum(pg, axis=0, keepdims=True)


def state_back_kernel(
    span, hw, later_ref, h_ref, keys_ref, v_ref, dv_ref, col_ref, cin_ref, cw_ref, cb_ref,
    cig_ref, cols_ref, dk_ref, dcw_ref, dcb_ref, dlast_ref, padded, dkacc,
):
    g, b = pl.program_id(0), pl.program_id(1)
    n = keys_ref.shape[2] // 2
    cols = col_ref[0, 0]
    c, step = cols[:, :HEADS], cols[:, HEADS:]
    later = later_ref[0]
    low = later.astype(bf16)
    left = spread(jnp.exp2(c[span - 1 : span] - c), hw)
    kdh = mm(keys_ref[0, :, :n], low) * left
    v = v_ref[0].astype(f32)
    step_wide = spread(step, hw)
    cols_ref[0, 0] = gather_heads(v * kdh, hw)
    dlast_ref[0] = jnp.broadcast_to(jnp.sum(later * h_ref[0], axis=0, keepdims=True), dlast_ref.shape[1:])
    vw = (v * step_wide * left).astype(bf16)
    part = mm_nt(vw, low)

    @pl.when(g == 0)
    def _():
        dkacc[b] = part

    @pl.when(g != 0)
    def _():
        dkacc[b] += part

    @pl.when(g == pl.num_programs(0) - 1)
    def _():
        dk_ref[b] = dkacc[b]

    padded[0:16] = jnp.zeros((16, padded.shape[1]), f32)
    padded[16 + span :] = jnp.zeros((padded.shape[0] - 16 - span, padded.shape[1]), f32)
    dv = dv_ref[0].astype(f32) + kdh * step_wide
    dcw, dcb = conv_back(dv, cin_ref[0].astype(f32), cw_ref[...], cb_ref[...], span, padded, cig_ref, 0)

    @pl.when(b == 0)
    def _():
        dcw_ref[...] = dcw
        dcb_ref[...] = dcb

    @pl.when(b != 0)
    def _():
        dcw_ref[...] += dcw
        dcb_ref[...] += dcb


def state_backward(later, carried, keys, v, dv, colpack, cin, cw, cb, hw, span):
    batch = v.shape[0]
    groups = colpack.shape[0]
    cb_w = HEADS * hw
    inner = groups * cb_w
    n = keys.shape[2] // 2
    ext = span + HALO
    taps = cw.shape[0]
    block = pl.BlockSpec((1, span, cb_w), lambda g, b: (b, 0, g))
    state = pl.BlockSpec((1, n, cb_w), lambda g, b: (b, 0, g))
    return pl.pallas_call(
        functools.partial(state_back_kernel, span, hw),
        grid=(groups, batch),
        in_specs=[
            state,
            state,
            pl.BlockSpec((1, span, 2 * n), lambda g, b: (b, 0, 0)),
            block,
            block,
            pl.BlockSpec((1, 1, span, 2 * HEADS), lambda g, b: (g, b, 0, 0)),
            pl.BlockSpec((1, ext, cb_w), lambda g, b: (b, 0, g)),
            pl.BlockSpec((taps, cb_w), lambda g, b: (0, g)),
            pl.BlockSpec((1, cb_w), lambda g, b: (0, g)),
        ],
        out_specs=[
            pl.BlockSpec((1, ext, cb_w), lambda g, b: (b, 0, g)),
            pl.BlockSpec((1, 1, span, HEADS), lambda g, b: (g, b, 0, 0)),
            pl.BlockSpec((batch, span, n), lambda g, b: (0, 0, 0)),
            pl.BlockSpec((taps, cb_w), lambda g, b: (0, g)),
            pl.BlockSpec((1, cb_w), lambda g, b: (0, g)),
            pl.BlockSpec((1, 8, cb_w), lambda g, b: (b, 0, g)),
        ],
        out_shape=[
            jax.ShapeDtypeStruct((batch, ext, inner), bf16),
            jax.ShapeDtypeStruct((groups, batch, span, HEADS), f32),
            jax.ShapeDtypeStruct((batch, span, n), f32),
            jax.ShapeDtypeStruct((taps, inner), f32),
            jax.ShapeDtypeStruct((1, inner), f32),
            jax.ShapeDtypeStruct((batch, 8, inner), f32),
        ],
        scratch_shapes=[
            pltpu.VMEM((span + 32, cb_w), f32),
            pltpu.VMEM((batch, span, n), f32),
        ],
        compiler_params=params_of(50),
    )(later, carried, keys, v, dv, colpack, cin, cw, cb)


def keys_back_kernel(span, dk_ref, dk2_ref, dq_ref, cin_ref, cw_ref, cb_ref, cig_ref, dcw_ref, dcb_ref, padded):
    batch = dk_ref.shape[0]
    padded[...] = jnp.zeros_like(padded)
    for b in range(batch):
        dv = jnp.concatenate([dk_ref[b] + dk2_ref[b], dq_ref[b]], axis=1)
        dcw, dcb = conv_back(dv, cin_ref[b].astype(f32), cw_ref[...], cb_ref[...], span, padded, cig_ref, b)
        if b == 0:
            dcw_ref[...] = dcw
            dcb_ref[...] = dcb
        else:
            dcw_ref[...] += dcw
            dcb_ref[...] += dcb


def keys_backward(dk, dk2, dq, cin, cw, cb, span):
    batch, ext, width = cin.shape
    return pl.pallas_call(
        functools.partial(keys_back_kernel, span),
        in_specs=[pl.BlockSpec(memory_space=pltpu.VMEM)] * 6,
        out_specs=[pl.BlockSpec(memory_space=pltpu.VMEM)] * 3,
        out_shape=[
            jax.ShapeDtypeStruct(cin.shape, bf16),
            jax.ShapeDtypeStruct(cw.shape, f32),
            jax.ShapeDtypeStruct(cb.shape, f32),
        ],
        scratch_shapes=[pltpu.VMEM((span + 32, width), f32)],
        compiler_params=params_of(40),
    )(dk, dk2, dq, cin, cw, cb)


def grouped(cols, groups):
    batch, span, heads = cols.shape
    return jnp.transpose(cols.reshape(batch, span, groups, heads // groups), (2, 0, 1, 3))


def ungrouped(cols):
    groups, batch, span, each = cols.shape
    return jnp.transpose(cols, (1, 2, 0, 3)).reshape(batch, span, groups * each)


def on_device(
    resid_in, out_grad, lengths, norm_gain, in_proj, dt_proj, conv_weight, conv_bias, dt_bias, a_log,
    skip_scale, gate_gain, out_proj,
):
    batch, span, width = resid_in.shape
    inner = gate_gain.shape[0]
    heads = a_log.shape[0]
    hw = inner // heads
    n = (in_proj.shape[1] - 2 * inner) // 2
    groups = heads // HEADS
    cb_w = HEADS * hw
    positions = lax.axis_index("seq") * span + lax.iota(jnp.int32, span)
    mask = (positions[None, :] < lengths[:, None]).astype(f32)[..., None]

    halo = shifted(resid_in[:, span - HALO :], "seq", 1)
    resid_ext = jnp.concatenate([halo, resid_in], axis=1).astype(f32)
    rs_ext = lax.rsqrt(jnp.mean(resid_ext * resid_ext, axis=-1, keepdims=True) + epsilon)
    x_ext = (resid_ext * rs_ext * norm_gain).astype(bf16)
    ext = span + HALO
    x2 = x_ext.reshape(batch * ext, width)
    resid_wide = resid_in.astype(f32)
    rs = rs_ext[:, HALO:]

    full_in = lax.all_gather(in_proj, ("dp", "seq"), axis=0, tiled=True)
    full_dt = lax.all_gather(dt_proj, ("dp", "seq"), axis=0, tiled=True)
    full_out = lax.all_gather(out_proj, ("dp", "seq"), axis=0, tiled=True)

    dt_raw = jnp.dot(x_ext[:, HALO:], full_dt, preferred_element_type=f32)
    step = jax.nn.softplus(dt_raw + dt_bias)
    rate = -jnp.exp(a_log)
    tri = causal(span, False).astype(f32)
    log_decay = jnp.einsum("ts,bsh->bth", tri, step * rate, precision=highest)
    scaled = log_decay * LOG2E
    colpack = jnp.concatenate([grouped(scaled, groups), grouped(step, groups)], axis=-1)
    rowpack = jnp.transpose(scaled, (0, 2, 1)).reshape(batch, groups, HEADS, span).transpose(1, 0, 2, 3)
    block_decay = jnp.exp(log_decay[:, span - 1])
    decay_wide = jnp.repeat(block_decay, hw, axis=1)[:, None, :]
    skip_wide = jnp.repeat(skip_scale, hw)[None]
    gain_wide = gate_gain[None]

    cw_keys, cb_keys = conv_weight[:, inner:], conv_bias[None, inner:]
    cw_vals, cb_vals = conv_weight[:, :inner], conv_bias[None, :inner]
    keys, cin_keys = keys_forward(x2, full_in, 2 * inner // (2 * n), cw_keys, cb_keys, batch, span)
    v, cin_vals, local = values_forward(
        x2, full_in, inner // cb_w, cw_vals, cb_vals, keys, colpack, hw, span
    )
    carried = chain(local, decay_wide, False, 1)
    y, gate, normed_out, rg = rows_forward(
        x_ext, full_in, v, keys, colpack, rowpack, carried, skip_wide, gain_wide, hw, span
    )
    mixer_out = jnp.dot(normed_out, full_out, preferred_element_type=f32)
    output = (mask * (resid_wide + mixer_out)).astype(bf16)

    mixer_grad = (mask * out_grad.astype(f32)).astype(bf16)
    mean = jnp.sum(mixer_grad.astype(f32) * mixer_out, axis=-1, keepdims=True) * (1.0 / inner)
    norms = jnp.concatenate([rg[..., :1], mean, jnp.zeros((batch, span, 6), f32)], axis=-1)
    grad_out = jnp.einsum("bsi,bsd->id", normed_out, mixer_grad, preferred_element_type=f32)
    dgate, dv, dh, cols_one, dq, dk, dgain, dskip = gate_backward(
        mixer_grad, full_out, y, gate, norms, gain_wide, v, keys, colpack, rowpack, carried, skip_wide, hw, span
    )
    later = chain(dh, decay_wide, True, 2)
    cig_vals, cols_two, dk2, dcw_vals, dcb_vals, dlast = state_backward(
        later, carried, keys, v, dv, colpack, cin_vals, cw_vals, cb_vals, hw, span
    )
    cig_keys, dcw_keys, dcb_keys = keys_backward(dk, dk2, dq, cin_keys, cw_keys, cb_keys, span)

    rise = ungrouped(cols_one[..., :HEADS])
    direct = ungrouped(cols_one[..., HEADS:])
    ahead = ungrouped(cols_two)
    moved = ahead * step
    last = jnp.sum(moved, axis=1) + dlast[:, 0].reshape(batch, heads, hw).sum(-1) * block_decay
    dlog = rise - moved
    dlog = jnp.einsum("ts,bth->bsh", tri, dlog, precision=highest) + last[:, None, :]
    grad_a = jnp.sum(dlog * step, axis=(0, 1)) * rate
    step_grad = direct + ahead + dlog * rate
    dt_grad = step_grad * jax.nn.sigmoid(dt_raw + dt_bias)
    grad_bias = jnp.sum(dt_grad, axis=(0, 1))
    step_low = dt_grad.astype(bf16)

    x_rows = x_ext[:, HALO:]
    grad_gate = jnp.einsum("bsd,bse->de", x_rows, dgate, preferred_element_type=f32)
    cig = jnp.concatenate([cig_vals, cig_keys], axis=-1)
    grad_conv = jnp.einsum("bsd,bse->de", x_ext, cig, preferred_element_type=f32)
    grad_dt = jnp.einsum("bsd,bsh->dh", x_rows, step_low, preferred_element_type=f32)
    normed_ext = jnp.einsum("bse,de->bsd", cig, full_in[:, inner:], preferred_element_type=f32)
    from_next = shifted(normed_ext[:, :HALO].astype(bf16), "seq", -1).astype(f32)
    normed_grad = normed_ext[:, HALO:]
    normed_grad = jnp.concatenate([normed_grad[:, : span - HALO], normed_grad[:, span - HALO :] + from_next], axis=1)
    normed_grad = normed_grad + jnp.einsum(
        "bse,de->bsd", dgate, full_in[:, :inner], preferred_element_type=f32
    )
    normed_grad = normed_grad + jnp.einsum("bsh,dh->bsd", step_low, full_dt, preferred_element_type=f32)
    nz = resid_wide * rs
    fg = normed_grad * norm_gain
    grad_norm = jnp.sum(normed_grad * nz, axis=(0, 1))
    input_grad = mixer_grad.astype(f32) + rs * (fg - nz * jnp.mean(fg * nz, axis=-1, keepdims=True))

    big = jnp.concatenate([grad_gate, grad_conv, grad_dt], axis=1).astype(bf16)
    sum_in = lax.psum_scatter(big, ("dp", "seq"), scatter_dimension=0, tiled=True).astype(f32)
    sum_out = lax.psum_scatter(grad_out.astype(bf16), ("dp", "seq"), scatter_dimension=0, tiled=True).astype(f32)
    small = lax.psum(
        (
            grad_norm,
            jnp.concatenate([dcw_vals, dcw_keys], axis=1),
            jnp.concatenate([dcb_vals, dcb_keys], axis=1)[0],
            grad_bias,
            grad_a,
            dskip[0].reshape(heads, hw).sum(-1),
            dgain[0],
        ),
        ("dp", "seq"),
    )
    proj = in_proj.shape[1]
    return (
        output,
        input_grad.astype(bf16),
        sum_in[:, :proj],
        sum_in[:, proj:],
        sum_out,
    ) + tuple(small)


def solution(mesh):
    rows = P("dp", "seq", None)
    shard = P(("dp", "seq"), None)
    return jax.shard_map(
        on_device,
        mesh=mesh,
        in_specs=(rows, rows, P("dp"), P(), shard, shard, P(), P(), P(), P(), P(), P(), shard),
        out_specs=(rows, rows, shard, shard, shard, P(), P(), P(), P(), P(), P(), P()),
        check_vma=False,
    )
```

```python
import functools

import jax
import jax.numpy as jnp
from jax import lax
from jax.experimental import pallas as pl
from jax.experimental.pallas import tpu as pltpu
from jax.sharding import PartitionSpec as P

epsilon = 1e-05
highest = lax.Precision.HIGHEST
HALO = 16
HEADS = 8
LOG2E = 1.4426950408889634
f32 = jnp.float32
bf16 = jnp.bfloat16
MESH = pl.DeviceIdType.MESH


def mm(a, b):
    return lax.dot_general(a, b, (((1,), (0,)), ((), ())), preferred_element_type=f32)


def mm_nt(a, b):
    return lax.dot_general(a, b, (((1,), (1,)), ((), ())), preferred_element_type=f32)


def mm_tn(a, b):
    return lax.dot_general(a, b, (((0,), (0,)), ((), ())), preferred_element_type=f32)


def shifted(block, axis, distance):
    devices = range(lax.axis_size(axis))
    route = [(i - distance, i) for i in devices if i - distance in devices]
    return lax.ppermute(block, axis, route)


def spread(cols, width):
    rows, heads = cols.shape
    low_half = lax.broadcasted_iota(jnp.int32, (rows, 2 * width), 1) < width
    pairs = [
        jnp.where(low_half, cols[:, i : i + 1], cols[:, i + 1 : i + 2]) for i in range(0, heads, 2)
    ]
    return jnp.concatenate(pairs, axis=1)


def gather_heads(x, width):
    rows, total = x.shape
    low_half = lax.broadcasted_iota(jnp.int32, (rows, 2 * width), 1) < width
    head_lane = lax.broadcasted_iota(jnp.int32, (rows, total // width), 1)
    out = jnp.zeros((rows, total // width), f32)
    for i in range(total // (2 * width)):
        pair = x[:, i * 2 * width : (i + 1) * 2 * width]
        one = jnp.sum(jnp.where(low_half, pair, 0.0), axis=1, keepdims=True)
        two = jnp.sum(jnp.where(low_half, 0.0, pair), axis=1, keepdims=True)
        out = jnp.where(head_lane == 2 * i, one, out)
        out = jnp.where(head_lane == 2 * i + 1, two, out)
    return out


def silu_parts(v):
    sg = 1.0 / (1.0 + jnp.exp(-v))
    return v * sg, sg


def conv_pre(a, cw, cb, span):
    first = HALO - (cw.shape[0] - 1)
    out = cb
    for k in range(cw.shape[0]):
        out = out + cw[k : k + 1] * a[first + k : first + k + span]
    return out


def params_of(limit_mb, dims=None):
    return pltpu.CompilerParams(vmem_limit_bytes=limit_mb * 1024 * 1024, dimension_semantics=dims)


def keys_kernel(span, x_ref, w_ref, cw_ref, cb_ref, rows_ref, cin_ref):
    batch = rows_ref.shape[0]
    ext = span + HALO
    acc = mm(x_ref[...], w_ref[...])
    for b in range(batch):
        a = acc[b * ext : (b + 1) * ext]
        row, _ = silu_parts(conv_pre(a, cw_ref[...], cb_ref[...], span))
        rows_ref[b] = row.astype(bf16)
        cin_ref[b] = a.astype(bf16)


def keys_forward(x2, w_conv, col_block, cw, cb, batch, span):
    width = 2 * (cw.shape[1] // 2)
    ext = span + HALO
    return pl.pallas_call(
        functools.partial(keys_kernel, span),
        grid=(1,),
        in_specs=[
            pl.BlockSpec(x2.shape, lambda i: (0, 0)),
            pl.BlockSpec((w_conv.shape[0], width), lambda i: (0, col_block)),
            pl.BlockSpec(cw.shape, lambda i: (0, 0)),
            pl.BlockSpec(cb.shape, lambda i: (0, 0)),
        ],
        out_specs=[
            pl.BlockSpec((batch, span, width), lambda i: (0, 0, 0)),
            pl.BlockSpec((batch, ext, width), lambda i: (0, 0, 0)),
        ],
        out_shape=[
            jax.ShapeDtypeStruct((batch, span, width), bf16),
            jax.ShapeDtypeStruct((batch, ext, width), bf16),
        ],
        compiler_params=params_of(40),
    )(x2, w_conv, cw, cb)


def values_kernel(span, hw, x_ref, w_ref, cw_ref, cb_ref, keys_ref, col_ref, rows_ref, cin_ref, st_ref):
    batch = rows_ref.shape[0]
    n = keys_ref.shape[2] // 2
    ext = span + HALO
    acc = mm(x_ref[...], w_ref[...])
    for b in range(batch):
        a = acc[b * ext : (b + 1) * ext]
        row, _ = silu_parts(conv_pre(a, cw_ref[...], cb_ref[...], span))
        row = row.astype(bf16)
        rows_ref[b] = row
        cin_ref[b] = a.astype(bf16)
        cols = col_ref[0, b]
        c, step = cols[:, :HEADS], cols[:, HEADS:]
        weight = jnp.exp2(c[span - 1 : span] - c) * step
        vw = (row.astype(f32) * spread(weight, hw)).astype(bf16)
        st_ref[b] = mm_tn(keys_ref[b, :, :n], vw)


def values_forward(x2, w_conv, first_block, cw, cb, keys, colpack, hw, span):
    batch = keys.shape[0]
    groups = colpack.shape[0]
    cb_w = HEADS * hw
    ext = span + HALO
    inner = groups * cb_w
    return pl.pallas_call(
        functools.partial(values_kernel, span, hw),
        grid=(groups,),
        in_specs=[
            pl.BlockSpec(x2.shape, lambda i: (0, 0)),
            pl.BlockSpec((w_conv.shape[0], cb_w), lambda i: (0, first_block + i)),
            pl.BlockSpec((cw.shape[0], cb_w), lambda i: (0, i)),
            pl.BlockSpec((1, cb_w), lambda i: (0, i)),
            pl.BlockSpec(keys.shape, lambda i: (0, 0, 0)),
            pl.BlockSpec((1,) + colpack.shape[1:], lambda i: (i, 0, 0, 0)),
        ],
        out_specs=[
            pl.BlockSpec((batch, span, cb_w), lambda i: (0, 0, i)),
            pl.BlockSpec((batch, ext, cb_w), lambda i: (0, 0, i)),
            pl.BlockSpec((batch, keys.shape[2] // 2, cb_w), lambda i: (0, 0, i)),
        ],
        out_shape=[
            jax.ShapeDtypeStruct((batch, span, inner), bf16),
            jax.ShapeDtypeStruct((batch, ext, inner), bf16),
            jax.ShapeDtypeStruct((batch, keys.shape[2] // 2, inner), f32),
        ],
        compiler_params=params_of(50),
    )(x2, w_conv, cw, cb, keys, colpack)


def chain_kernel(backward, size, local_ref, decay_ref, carried_ref, sent, landed, send_sem, recv_sem):
    me = lax.axis_index("seq")
    count = lax.axis_size("seq")
    turn = -1 if backward else 1
    has_prev = me != (count - 1 if backward else 0)
    has_next = me != (0 if backward else count - 1)
    nxt = jnp.clip(me + turn, 0, count - 1)
    prv = jnp.clip(me - turn, 0, count - 1)
    barrier = pltpu.get_barrier_semaphore()

    @pl.when(has_prev)
    def _():
        pl.semaphore_signal(barrier, inc=1, device_id={"seq": prv}, device_id_type=MESH)

    @pl.when(has_next)
    def _():
        pl.semaphore_wait(barrier, 1)

    batch, _, total = local_ref.shape
    per = total // size

    def copy_of(k):
        return pltpu.make_async_remote_copy(
            src_ref=sent.at[k],
            dst_ref=landed.at[k],
            send_sem=send_sem.at[k],
            recv_sem=recv_sem.at[k],
            device_id={"seq": nxt},
            device_id_type=MESH,
        )

    for k in range(batch * per):
        b, part = k % batch, k // batch
        cols = pl.ds(part * size, size)

        @pl.when(has_prev)
        def _():
            copy_of(k).wait_recv()
            carried_ref[b, :, cols] = landed[k].astype(f32)

        @pl.when(jnp.logical_not(has_prev))
        def _():
            carried_ref[b, :, cols] = jnp.zeros_like(carried_ref[b, :, cols])

        @pl.when(has_next)
        def _():
            out = decay_ref[b, :, cols] * carried_ref[b, :, cols] + local_ref[b, :, cols]
            sent[k] = out.astype(bf16)
            copy_of(k).start()

    @pl.when(has_next)
    def _():
        for k in range(batch * per):
            copy_of(k).wait_send()


def chain(local, decay, backward, collective_id):
    size = 512
    count = local.shape[0] * (local.shape[2] // size)
    return pl.pallas_call(
        functools.partial(chain_kernel, backward, size),
        in_specs=[pl.BlockSpec(memory_space=pltpu.VMEM)] * 2,
        out_specs=pl.BlockSpec(memory_space=pltpu.VMEM),
        out_shape=jax.ShapeDtypeStruct(local.shape, f32),
        scratch_shapes=[
            pltpu.VMEM((count, local.shape[1], size), bf16),
            pltpu.VMEM((count, local.shape[1], size), bf16),
            pltpu.SemaphoreType.DMA((count,)),
            pltpu.SemaphoreType.DMA((count,)),
        ],
        compiler_params=pltpu.CompilerParams(
            collective_id=collective_id, has_side_effects=True, vmem_limit_bytes=40 * 1024 * 1024
        ),
    )(local, decay)


def causal(span, transposed):
    one = lax.broadcasted_iota(jnp.int32, (span, span), 0)
    two = lax.broadcasted_iota(jnp.int32, (span, span), 1)
    return (one <= two) if transposed else (one >= two)


def out_kernel(
    span, hw, x_ref, w_ref, v_ref, keys_ref, col_ref, row_ref, h_ref, skip_ref, gain_ref,
    y_ref, gate_ref, no_ref, rg_ref, scores, gated, squares,
):
    g, b = pl.program_id(0), pl.program_id(1)
    groups, batch = pl.num_programs(0), pl.num_programs(1)
    n = keys_ref.shape[2] // 2
    cb_w = HEADS * hw
    k_in, k_out = keys_ref[0, :, :n], keys_ref[0, :, n:]

    @pl.when(g == 0)
    def _():
        scores[b] = jnp.where(causal(span, False), mm_nt(k_out, k_in), 0.0)
        squares[b] = jnp.zeros_like(squares[b])

    cols = col_ref[0, 0]
    c, step = cols[:, :HEADS], cols[:, HEADS:]
    v = v_ref[0].astype(f32)
    vs = (v * spread(step, hw)).astype(bf16)
    s = scores[b]
    low_half = lax.broadcasted_iota(jnp.int32, (span, 2 * hw), 1) < hw
    parts = []
    for i in range(HEADS // 2):
        pair = vs[:, i * 2 * hw : (i + 1) * 2 * hw]
        total = None
        for j in range(2):
            h = 2 * i + j
            gap = jnp.minimum(c[:, h : h + 1] - row_ref[0, 0, h : h + 1, :], 0.0)
            u = (jnp.exp2(gap) * s).astype(bf16)
            half = jnp.where(low_half if j == 0 else jnp.logical_not(low_half), pair, jnp.zeros_like(pair))
            term = mm(u, half)
            total = term if total is None else total + term
        parts.append(total)
    y = jnp.concatenate(parts, axis=1)
    y = y + mm(k_out, h_ref[0].astype(bf16)) * spread(jnp.exp2(c), hw) + skip_ref[...] * v
    y_ref[0] = y
    gate = mm(x_ref[0, HALO:], w_ref[...])
    gate_ref[0] = gate.astype(bf16)
    act, _ = silu_parts(gate)
    gr = y * act
    gated[b, g] = gr
    squares[b] += jnp.broadcast_to(jnp.sum(gr * gr, axis=1, keepdims=True), squares.shape[1:])

    @pl.when(g == groups - 1)
    def _():
        rg = lax.rsqrt(squares[b][:, :1] * (1.0 / (groups * cb_w)) + epsilon)
        rg_ref[b] = jnp.broadcast_to(rg, rg_ref.shape[1:])
        for i in range(no_ref.shape[2] // cb_w):
            part = slice(i * cb_w, (i + 1) * cb_w)
            no_ref[b, :, part] = (gated[b, i] * rg * gain_ref[:, part]).astype(bf16)


def rows_forward(x_ext, w_gate, v, keys, colpack, rowpack, carried, skip, gain, hw, span):
    batch, ext, width = x_ext.shape
    groups = colpack.shape[0]
    cb_w = HEADS * hw
    inner = groups * cb_w
    n = keys.shape[2] // 2
    return pl.pallas_call(
        functools.partial(out_kernel, span, hw),
        grid=(groups, batch),
        in_specs=[
            pl.BlockSpec((1, ext, width), lambda g, b: (b, 0, 0)),
            pl.BlockSpec((width, cb_w), lambda g, b: (0, g)),
            pl.BlockSpec((1, span, cb_w), lambda g, b: (b, 0, g)),
            pl.BlockSpec((1, span, 2 * n), lambda g, b: (b, 0, 0)),
            pl.BlockSpec((1, 1, span, 2 * HEADS), lambda g, b: (g, b, 0, 0)),
            pl.BlockSpec((1, 1, HEADS, span), lambda g, b: (g, b, 0, 0)),
            pl.BlockSpec((1, n, cb_w), lambda g, b: (b, 0, g)),
            pl.BlockSpec((1, cb_w), lambda g, b: (0, g)),
            pl.BlockSpec((1, inner), lambda g, b: (0, 0)),
        ],
        out_specs=[
            pl.BlockSpec((1, span, cb_w), lambda g, b: (b, 0, g)),
            pl.BlockSpec((1, span, cb_w), lambda g, b: (b, 0, g)),
            pl.BlockSpec((batch, span, inner), lambda g, b: (0, 0, 0)),
            pl.BlockSpec((batch, span, 8), lambda g, b: (0, 0, 0)),
        ],
        out_shape=[
            jax.ShapeDtypeStruct((batch, span, inner), f32),
            jax.ShapeDtypeStruct((batch, span, inner), bf16),
            jax.ShapeDtypeStruct((batch, span, inner), bf16),
            jax.ShapeDtypeStruct((batch, span, 8), f32),
        ],
        scratch_shapes=[
            pltpu.VMEM((batch, span, span), f32),
            pltpu.VMEM((batch, groups, span, cb_w), f32),
            pltpu.VMEM((batch, span, 128), f32),
        ],
        compiler_params=params_of(56),
    )(x_ext, w_gate, v, keys, colpack, rowpack, carried, skip, gain)


def gate_back_kernel(
    span, hw, mg_ref, w_ref, y_ref, gate_ref, norm_ref, gain_ref, v_ref, keys_ref, col_ref, row_ref,
    h_ref, skip_ref,
    dgate_ref, dv_ref, dh_ref, cols_ref, dq_ref, dk_ref, dgain_ref, dskip_ref, scores, dscores, dqacc,
):
    g, b = pl.program_id(0), pl.program_id(1)
    groups = pl.num_programs(0)
    n = keys_ref.shape[2] // 2
    k_in, k_out = keys_ref[0, :, :n], keys_ref[0, :, n:]

    @pl.when(g == 0)
    def _():
        scores[b] = jnp.where(causal(span, True), mm_nt(k_in, k_out), 0.0)
        dscores[b] = jnp.zeros_like(dscores[b])
        dqacc[b] = jnp.zeros_like(dqacc[b])

    no_grad = mm_nt(mg_ref[0], w_ref[...])
    gate = gate_ref[0].astype(f32)
    y = y_ref[0]
    rg = norm_ref[0][:, 0:1]
    mean = norm_ref[0][:, 1:2]
    act, sg = silu_parts(gate)
    gn = y * act * rg
    dgain = jnp.sum(no_grad * gn, axis=0, keepdims=True)
    dg = rg * (no_grad * gain_ref[...] - gn * mean)
    dgate_ref[0] = (dg * y * (sg * (1.0 + gate * (1.0 - sg)))).astype(bf16)
    gb = (dg * act).astype(bf16)
    gf = gb.astype(f32)

    cols = col_ref[0, 0]
    c, step = cols[:, :HEADS], cols[:, HEADS:]
    v = v_ref[0].astype(f32)
    step_wide = spread(step, hw)
    vs = (v * step_wide).astype(bf16)
    skip = skip_ref[...]
    dskip = jnp.sum(gf * v, axis=0, keepdims=True)

    @pl.when(b == 0)
    def _():
        dgain_ref[...] = dgain
        dskip_ref[...] = dskip

    @pl.when(b != 0)
    def _():
        dgain_ref[...] += dgain
        dskip_ref[...] += dskip

    s = scores[b]
    low_half = lax.broadcasted_iota(jnp.int32, (span, 2 * hw), 1) < hw
    parts = []
    ds = dscores[b]
    for i in range(HEADS // 2):
        lanes = slice(i * 2 * hw, (i + 1) * 2 * hw)
        total = None
        for j in range(2):
            h = 2 * i + j
            gap = jnp.minimum(row_ref[0, 0, h : h + 1, :] - c[:, h : h + 1], 0.0)
            decay = jnp.exp2(gap)
            u = (decay * s).astype(bf16)
            keep = low_half if j == 0 else jnp.logical_not(low_half)
            half = jnp.where(keep, gb[:, lanes], jnp.zeros_like(gb[:, lanes]))
            term = mm(u, half)
            total = term if total is None else total + term
            ds = ds + decay * mm_nt(vs[:, lanes], half)
        parts.append(total)
    dscores[b] = ds
    u_all = jnp.concatenate(parts, axis=1)
    dv_ref[0] = (u_all * step_wide + skip * gf).astype(bf16)
    rise = gather_heads(gf * (y - skip * v) - vs.astype(f32) * u_all, hw)
    direct = gather_heads(v * u_all, hw)
    cols_ref[0, 0] = jnp.concatenate([rise, direct], axis=1)
    ge = (gf * spread(jnp.exp2(c), hw)).astype(bf16)
    dh_ref[0] = mm_tn(k_out, ge)
    dqacc[b] += mm_nt(ge, h_ref[0].astype(bf16))

    @pl.when(g == groups - 1)
    def _():
        low = jnp.where(causal(span, True), dscores[b], 0.0).astype(bf16)
        dq_ref[b] = dqacc[b] + mm_tn(low, k_in)
        dk_ref[b] = mm(low, k_out)


def gate_backward(mg, w_out, y, gate, norms, gain, v, keys, colpack, rowpack, carried, skip, hw, span):
    batch, _, width = mg.shape
    groups = colpack.shape[0]
    cb_w = HEADS * hw
    inner = groups * cb_w
    n = keys.shape[2] // 2
    block = pl.BlockSpec((1, span, cb_w), lambda g, b: (b, 0, g))
    lanes = pl.BlockSpec((1, cb_w), lambda g, b: (0, g))
    return pl.pallas_call(
        functools.partial(gate_back_kernel, span, hw),
        grid=(groups, batch),
        in_specs=[
            pl.BlockSpec((1, span, width), lambda g, b: (b, 0, 0)),
            pl.BlockSpec((cb_w, width), lambda g, b: (g, 0)),
            block,
            block,
            pl.BlockSpec((1, span, 8), lambda g, b: (b, 0, 0)),
            lanes,
            block,
            pl.BlockSpec((1, span, 2 * n), lambda g, b: (b, 0, 0)),
            pl.BlockSpec((1, 1, span, 2 * HEADS), lambda g, b: (g, b, 0, 0)),
            pl.BlockSpec((1, 1, HEADS, span), lambda g, b: (g, b, 0, 0)),
            pl.BlockSpec((1, n, cb_w), lambda g, b: (b, 0, g)),
            lanes,
        ],
        out_specs=[
            block,
            block,
            pl.BlockSpec((1, n, cb_w), lambda g, b: (b, 0, g)),
            pl.BlockSpec((1, 1, span, 2 * HEADS), lambda g, b: (g, b, 0, 0)),
            pl.BlockSpec((batch, span, n), lambda g, b: (0, 0, 0)),
            pl.BlockSpec((batch, span, n), lambda g, b: (0, 0, 0)),
            lanes,
            lanes,
        ],
        out_shape=[
            jax.ShapeDtypeStruct((batch, span, inner), bf16),
            jax.ShapeDtypeStruct((batch, span, inner), bf16),
            jax.ShapeDtypeStruct((batch, n, inner), f32),
            jax.ShapeDtypeStruct((groups, batch, span, 2 * HEADS), f32),
            jax.ShapeDtypeStruct((batch, span, n), f32),
            jax.ShapeDtypeStruct((batch, span, n), f32),
            jax.ShapeDtypeStruct((1, inner), f32),
            jax.ShapeDtypeStruct((1, inner), f32),
        ],
        scratch_shapes=[
            pltpu.VMEM((batch, span, span), f32),
            pltpu.VMEM((batch, span, span), f32),
            pltpu.VMEM((batch, span, n), f32),
        ],
        compiler_params=params_of(50),
    )(mg, w_out, y, gate, norms, gain, v, keys, colpack, rowpack, carried, skip)


def conv_back(dv, a, cw, cb, span, padded, out_ref, b):
    taps = cw.shape[0]
    first = HALO - (taps - 1)
    pre = conv_pre(a, cw, cb, span)
    _, sg = silu_parts(pre)
    pg = dv * (sg * (1.0 + pre * (1.0 - sg)))
    padded[16 : 16 + span] = pg
    ext = span + HALO
    total = jnp.zeros((ext, cw.shape[1]), f32)
    for k in range(taps):
        total = total + cw[k : k + 1] * padded[taps - 1 - k : taps - 1 - k + ext]
    out_ref[b] = total.astype(bf16)
    dcw = jnp.concatenate(
        [jnp.sum(pg * a[first + k : first + k + span], axis=0, keepdims=True) for k in range(taps)], axis=0
    )
    return dcw, jnp.sum(pg, axis=0, keepdims=True)


def state_back_kernel(
    span, hw, later_ref, h_ref, keys_ref, v_ref, dv_ref, col_ref, cin_ref, cw_ref, cb_ref,
    cig_ref, cols_ref, dk_ref, dcw_ref, dcb_ref, dlast_ref, padded, dkacc,
):
    g, b = pl.program_id(0), pl.program_id(1)
    n = keys_ref.shape[2] // 2
    cols = col_ref[0, 0]
    c, step = cols[:, :HEADS], cols[:, HEADS:]
    later = later_ref[0]
    low = later.astype(bf16)
    left = spread(jnp.exp2(c[span - 1 : span] - c), hw)
    kdh = mm(keys_ref[0, :, :n], low) * left
    v = v_ref[0].astype(f32)
    step_wide = spread(step, hw)
    cols_ref[0, 0] = gather_heads(v * kdh, hw)
    dlast_ref[0] = jnp.broadcast_to(jnp.sum(later * h_ref[0], axis=0, keepdims=True), dlast_ref.shape[1:])
    vw = (v * step_wide * left).astype(bf16)
    part = mm_nt(vw, low)

    @pl.when(g == 0)
    def _():
        dkacc[b] = part

    @pl.when(g != 0)
    def _():
        dkacc[b] += part

    @pl.when(g == pl.num_programs(0) - 1)
    def _():
        dk_ref[b] = dkacc[b]

    padded[0:16] = jnp.zeros((16, padded.shape[1]), f32)
    padded[16 + span :] = jnp.zeros((padded.shape[0] - 16 - span, padded.shape[1]), f32)
    dv = dv_ref[0].astype(f32) + kdh * step_wide
    dcw, dcb = conv_back(dv, cin_ref[0].astype(f32), cw_ref[...], cb_ref[...], span, padded, cig_ref, 0)

    @pl.when(b == 0)
    def _():
        dcw_ref[...] = dcw
        dcb_ref[...] = dcb

    @pl.when(b != 0)
    def _():
        dcw_ref[...] += dcw
        dcb_ref[...] += dcb


def state_backward(later, carried, keys, v, dv, colpack, cin, cw, cb, hw, span):
    batch = v.shape[0]
    groups = colpack.shape[0]
    cb_w = HEADS * hw
    inner = groups * cb_w
    n = keys.shape[2] // 2
    ext = span + HALO
    taps = cw.shape[0]
    block = pl.BlockSpec((1, span, cb_w), lambda g, b: (b, 0, g))
    state = pl.BlockSpec((1, n, cb_w), lambda g, b: (b, 0, g))
    return pl.pallas_call(
        functools.partial(state_back_kernel, span, hw),
        grid=(groups, batch),
        in_specs=[
            state,
            state,
            pl.BlockSpec((1, span, 2 * n), lambda g, b: (b, 0, 0)),
            block,
            block,
            pl.BlockSpec((1, 1, span, 2 * HEADS), lambda g, b: (g, b, 0, 0)),
            pl.BlockSpec((1, ext, cb_w), lambda g, b: (b, 0, g)),
            pl.BlockSpec((taps, cb_w), lambda g, b: (0, g)),
            pl.BlockSpec((1, cb_w), lambda g, b: (0, g)),
        ],
        out_specs=[
            pl.BlockSpec((1, ext, cb_w), lambda g, b: (b, 0, g)),
            pl.BlockSpec((1, 1, span, HEADS), lambda g, b: (g, b, 0, 0)),
            pl.BlockSpec((batch, span, n), lambda g, b: (0, 0, 0)),
            pl.BlockSpec((taps, cb_w), lambda g, b: (0, g)),
            pl.BlockSpec((1, cb_w), lambda g, b: (0, g)),
            pl.BlockSpec((1, 8, cb_w), lambda g, b: (b, 0, g)),
        ],
        out_shape=[
            jax.ShapeDtypeStruct((batch, ext, inner), bf16),
            jax.ShapeDtypeStruct((groups, batch, span, HEADS), f32),
            jax.ShapeDtypeStruct((batch, span, n), f32),
            jax.ShapeDtypeStruct((taps, inner), f32),
            jax.ShapeDtypeStruct((1, inner), f32),
            jax.ShapeDtypeStruct((batch, 8, inner), f32),
        ],
        scratch_shapes=[
            pltpu.VMEM((span + 32, cb_w), f32),
            pltpu.VMEM((batch, span, n), f32),
        ],
        compiler_params=params_of(50),
    )(later, carried, keys, v, dv, colpack, cin, cw, cb)


def keys_back_kernel(span, dk_ref, dk2_ref, dq_ref, cin_ref, cw_ref, cb_ref, cig_ref, dcw_ref, dcb_ref, padded):
    batch = dk_ref.shape[0]
    padded[...] = jnp.zeros_like(padded)
    for b in range(batch):
        dv = jnp.concatenate([dk_ref[b] + dk2_ref[b], dq_ref[b]], axis=1)
        dcw, dcb = conv_back(dv, cin_ref[b].astype(f32), cw_ref[...], cb_ref[...], span, padded, cig_ref, b)
        if b == 0:
            dcw_ref[...] = dcw
            dcb_ref[...] = dcb
        else:
            dcw_ref[...] += dcw
            dcb_ref[...] += dcb


def keys_backward(dk, dk2, dq, cin, cw, cb, span):
    batch, ext, width = cin.shape
    return pl.pallas_call(
        functools.partial(keys_back_kernel, span),
        in_specs=[pl.BlockSpec(memory_space=pltpu.VMEM)] * 6,
        out_specs=[pl.BlockSpec(memory_space=pltpu.VMEM)] * 3,
        out_shape=[
            jax.ShapeDtypeStruct(cin.shape, bf16),
            jax.ShapeDtypeStruct(cw.shape, f32),
            jax.ShapeDtypeStruct(cb.shape, f32),
        ],
        scratch_shapes=[pltpu.VMEM((span + 32, width), f32)],
        compiler_params=params_of(40),
    )(dk, dk2, dq, cin, cw, cb)


class Place:
    def __init__(self):
        self.dp = lax.axis_index("dp")
        self.seq = lax.axis_index("seq")
        y, x = self.dp // 2, self.dp % 2
        self.z, self.core = self.seq // 2, self.seq % 2
        self.dx = 2 * y + (1 - x)
        self.dy = 2 * (1 - y) + x
        self.dxy = 2 * (1 - y) + (1 - x)
        self.to_x = (self.dx, self.seq)
        self.to_y = (self.dy, self.seq)
        self.to_core = (self.dp, 2 * self.z + 1 - self.core)
        self.to_up = (self.dp, 2 * jnp.minimum(self.z + 1, 3) + self.core)
        self.to_down = (self.dp, 2 * jnp.maximum(self.z - 1, 0) + self.core)
        self.to_across = (self.dp, 2 * jnp.where(self.z < 2, self.z + 2, self.z - 2) + self.core)
        self.has_up = self.z < 3
        self.has_down = self.z > 0

    def near(self, k):
        z = self.z
        return (z, z + 1 - 2 * (z % 2), jnp.where(z < 2, 2, 1), jnp.where(z < 2, 3, 0))[k]

    def greet(self, others=()):
        barrier = pltpu.get_barrier_semaphore()
        for device in (self.to_x, self.to_y, self.to_core) + tuple(others):
            pl.semaphore_signal(barrier, inc=1, device_id=device, device_id_type=MESH)

        @pl.when(self.has_up)
        def _():
            pl.semaphore_signal(barrier, inc=1, device_id=self.to_up, device_id_type=MESH)

        @pl.when(self.has_down)
        def _():
            pl.semaphore_signal(barrier, inc=1, device_id=self.to_down, device_id_type=MESH)

        ends = self.has_up.astype(jnp.int32) + self.has_down.astype(jnp.int32)
        pl.semaphore_wait(barrier, 3 + len(others) + ends)


GATHER_KINDS = 11


def gather_steps(place, shard, full, split, own_sem, send, recv):
    rows, width = shard.shape
    z, core = place.z, place.core
    every, left, right = pl.ds(0, width), pl.ds(0, split), pl.ds(split, width - split)

    def view(d, zz, cc, cols):
        start = pl.multiple_of((d * 8 + zz * 2 + cc) * rows, 16)
        return full.at[pl.ds(start, rows), cols]

    def copy(kind, slot, device, d, zz, cc, cols, src=None):
        dst = view(d, zz, cc, cols)
        return pltpu.make_async_remote_copy(
            src_ref=dst if src is None else src,
            dst_ref=dst,
            send_sem=send.at[kind, slot],
            recv_sem=recv.at[kind, slot],
            device_id=device,
            device_id_type=MESH,
        )

    def pieces(k):
        zk = place.near(k)
        src = shard if k == 0 else None
        dp = place.dp
        return dict(
            x=copy(2, k, place.to_x, dp, zk, core, every, src),
            y=copy(3, k, place.to_y, dp, zk, core, every, src),
            own=copy(6, k, place.to_core, dp, zk, core, every, src),
        )

    def along(k, up):
        zk = place.near(k)
        src = shard if k == 0 else None
        device = place.to_up if up else place.to_down
        dst = view(place.dp, zk, core, every)
        return pltpu.make_async_remote_copy(
            src_ref=dst if src is None else src,
            dst_ref=dst,
            send_sem=send.at[0 if up else 1, k],
            recv_sem=recv.at[0, zk],
            device_id=device,
            device_id_type=MESH,
        )

    def arrive(k):
        zk = place.near(k)
        if k > 0:
            along(k, True).wait_recv()

        @pl.when(jnp.logical_and(zk <= z, place.has_up))
        def _():
            along(k, True).start()

        @pl.when(jnp.logical_and(zk >= z, place.has_down))
        def _():
            along(k, False).start()

        made = pieces(k)
        made["x"].start()
        made["y"].start()
        made["own"].start()

    def cross(k):
        zk = place.near(k)
        return (
            copy(2, k, place.to_x, place.dx, zk, core, every),
            copy(3, k, place.to_y, place.dy, zk, core, every),
            copy(4, k, place.to_y, place.dx, zk, core, left),
            copy(5, k, place.to_x, place.dy, zk, core, right),
            copy(7, k, place.to_core, place.dx, zk, core, every),
            copy(8, k, place.to_core, place.dy, zk, core, every),
        )

    def forward(k):
        from_x, from_y, left_on, right_on, core_x, core_y = cross(k)
        from_x.wait_recv()
        left_on.start()
        core_x.start()
        from_y.wait_recv()
        right_on.start()
        core_y.start()

    def corner(k):
        zk = place.near(k)
        return (
            copy(4, k, place.to_y, place.dxy, zk, core, left),
            copy(5, k, place.to_x, place.dxy, zk, core, right),
            copy(9, k, place.to_core, place.dxy, zk, core, left),
            copy(10, k, place.to_core, place.dxy, zk, core, right),
        )

    def last(k):
        from_y, from_x, core_left, core_right = corner(k)
        from_y.wait_recv()
        core_left.start()
        from_x.wait_recv()
        core_right.start()

    def mine():
        return pltpu.make_async_copy(shard, view(place.dp, z, core, every), own_sem)

    def begin():
        mine().start()
        arrive(0)

    def finish():
        mine().wait()
        other = 1 - core
        for k in range(4):
            zk = place.near(k)
            for kind, d, cols in (
                (6, place.dp, every), (7, place.dx, every), (8, place.dy, every),
                (9, place.dxy, left), (10, place.dxy, right),
            ):
                copy(kind, k, place.to_core, d, zk, other, cols).wait_recv()
        for k in range(4):
            zk = place.near(k)

            @pl.when(jnp.logical_and(zk <= z, place.has_up))
            def _():
                along(k, True).wait_send()

            @pl.when(jnp.logical_and(zk >= z, place.has_down))
            def _():
                along(k, False).wait_send()

            made = pieces(k)
            made["x"].wait_send()
            made["y"].wait_send()
            made["own"].wait_send()
            for one in cross(k)[2:]:
                one.wait_send()
            for one in corner(k)[2:]:
                one.wait_send()

    return [
        begin,
        lambda: arrive(1),
        lambda: forward(0),
        lambda: arrive(2),
        lambda: forward(1),
        lambda: arrive(3),
        lambda: forward(2),
        lambda: last(0),
        lambda: forward(3),
        lambda: last(1),
        lambda: last(2),
        lambda: last(3),
        finish,
    ]


def gather_scratch():
    return [
        pltpu.SemaphoreType.DMA,
        pltpu.SemaphoreType.DMA((GATHER_KINDS, 4)),
        pltpu.SemaphoreType.DMA((GATHER_KINDS, 4)),
    ]


def gather_kernel(splits, *refs):
    count = len(splits)
    shards, fulls, sems = refs[:count], refs[count : 2 * count], refs[2 * count :]
    place = Place()
    place.greet()
    plans = [
        gather_steps(place, shards[i], fulls[i], splits[i], *sems[3 * i : 3 * i + 3]) for i in range(count)
    ]
    for step in zip(*plans):
        for one in step:
            one()


def gather(shards, splits, collective_id):
    count = len(shards)
    spec = pl.BlockSpec(memory_space=pl.ANY)
    return pl.pallas_call(
        functools.partial(gather_kernel, splits),
        in_specs=[spec] * count,
        out_specs=[spec] * count,
        out_shape=[jax.ShapeDtypeStruct((s.shape[0] * 32, s.shape[1]), s.dtype) for s in shards],
        scratch_shapes=gather_scratch() * count,
        compiler_params=pltpu.CompilerParams(collective_id=collective_id, has_side_effects=True),
    )(*shards)


class Scatter:
    def __init__(self, place, big, out, own, land_core, land_xy, land_z, local, send, recv, split):
        self.place, self.big, self.out = place, big, out
        self.own, self.land_core, self.land_xy, self.land_z = own, land_core, land_xy, land_z
        self.local, self.send, self.recv = local, send, recv
        self.rows, self.width = out.shape
        self.split = split
        self.left, self.right = slice(0, split), slice(split, self.width)

    def groups(self):
        p = self.place
        return (p.dxy, p.dx, p.dy, p.dp)

    def far(self, k):
        return self.place.near(3 - k)

    def source(self, d, zz, cc):
        start = pl.multiple_of((d * 8 + zz * 2 + cc) * self.rows, 16)
        return self.big.at[pl.ds(start, self.rows)]

    def remote(self, src, dst, kind, slot, device):
        return pltpu.make_async_remote_copy(
            src_ref=src, dst_ref=dst, send_sem=self.send.at[kind, slot], recv_sem=self.recv.at[kind, slot],
            device_id=device, device_id_type=MESH,
        )

    def to_other(self, i, k):
        p = self.place
        src = self.source(self.groups()[i], self.far(k), 1 - p.core)
        return self.remote(src, self.land_core.at[i, k], i, k, p.to_core)

    def load(self, i, k):
        p = self.place
        return pltpu.make_async_copy(
            self.source(self.groups()[i], self.far(k), p.core), self.own.at[i, k], self.local.at[i, k]
        )

    def start_group(self, i):
        for k in range(4):
            self.to_other(i, k).start()
            self.load(i, k).start()

    def join(self, i, k):
        self.load(i, k).wait()
        self.to_other(i, k).wait_recv()
        self.own[i, k] = self.own[i, k] + self.land_core[i, k]

    def side(self, kind, k):
        p = self.place
        left, right = pl.ds(0, self.split), pl.ds(self.split, self.width - self.split)
        group, cols, device = (
            (0, left, p.to_y),
            (0, right, p.to_x),
            (2, left, p.to_y),
            (1, right, p.to_x),
            (2, right, p.to_y),
            (1, left, p.to_x),
        )[kind]
        size = self.split if cols is left else self.width - self.split
        return self.remote(
            self.own.at[group, k, :, cols], self.land_xy.at[kind, k, :, pl.ds(0, size)], 4 + kind, k, device
        )

    def take(self, kind, group, cols, k):
        self.side(kind, k).wait_recv()
        size = cols.stop - cols.start
        self.own[group, k, :, cols] = self.own[group, k, :, cols] + self.land_xy[kind, k, :, 0:size]

    def corner(self, k):
        self.join(0, k)
        self.side(0, k).start()
        self.side(1, k).start()

    def sides(self, k):
        self.join(1, k)
        self.side(3, k).start()
        self.join(2, k)
        self.side(2, k).start()
        self.take(0, 1, self.left, k)
        self.side(5, k).start()
        self.take(1, 2, self.right, k)
        self.side(4, k).start()

    def along(self, k, up):
        p = self.place
        zk = self.far(k)
        return pltpu.make_async_remote_copy(
            src_ref=self.own.at[3, k],
            dst_ref=self.land_z.at[0 if up else 1, zk],
            send_sem=self.send.at[10, k],
            recv_sem=self.recv.at[10 if up else 11, zk],
            device_id=p.to_up if up else p.to_down,
            device_id_type=MESH,
        )

    def mine(self, k):
        p = self.place
        self.join(3, k)
        self.take(2, 3, self.left, k)
        self.take(3, 3, self.right, k)
        self.take(5, 3, self.left, k)
        self.take(4, 3, self.right, k)
        if k == 3:
            return
        zk = self.far(k)
        rising = zk > p.z
        behind = jnp.logical_or(
            jnp.logical_and(rising, p.has_down), jnp.logical_and(jnp.logical_not(rising), p.has_up)
        )

        @pl.when(jnp.logical_and(behind, rising))
        def _():
            self.along(k, True).wait_recv()
            self.own[3, k] = self.own[3, k] + self.land_z[0, zk]

        @pl.when(jnp.logical_and(behind, jnp.logical_not(rising)))
        def _():
            self.along(k, False).wait_recv()
            self.own[3, k] = self.own[3, k] + self.land_z[1, zk]

        @pl.when(rising)
        def _():
            self.along(k, True).start()

        @pl.when(jnp.logical_not(rising))
        def _():
            self.along(k, False).start()

    def result(self):
        p = self.place
        self.out[...] = self.own[3, 3].astype(f32)

        @pl.when(p.has_down)
        def _():
            self.along(3, True).wait_recv()
            self.out[...] += self.land_z[0, p.z].astype(f32)

        @pl.when(p.has_up)
        def _():
            self.along(3, False).wait_recv()
            self.out[...] += self.land_z[1, p.z].astype(f32)

    def drain(self):
        for k in range(4):
            for i in range(4):
                self.to_other(i, k).wait_send()
            for kind in range(6):
                self.side(kind, k).wait_send()
            if k < 3:
                self.along(k, True).wait_send()

    @staticmethod
    def scratch(rows, width, split):
        half = max(split, width - split)
        return [
            pltpu.VMEM((4, 4, rows, width), bf16),
            pltpu.VMEM((4, 4, rows, width), bf16),
            pltpu.VMEM((6, 4, rows, half), bf16),
            pltpu.VMEM((2, 4, rows, width), bf16),
            pltpu.SemaphoreType.DMA((4, 4)),
            pltpu.SemaphoreType.DMA((11, 4)),
            pltpu.SemaphoreType.DMA((12, 4)),
        ]


class Small:
    def __init__(self, place, value, out, sent, landed, send, recv):
        p = place
        self.value, self.out, self.sent, self.landed, self.send, self.recv = value, out, sent, landed, send, recv
        pair = 2 * (p.z + 1 - 2 * (p.z % 2)) + p.core
        self.devices = (p.to_core, p.to_x, p.to_y, (p.dp, pair), p.to_across)

    def copy(self, i):
        return pltpu.make_async_remote_copy(
            src_ref=self.sent.at[i], dst_ref=self.landed.at[i], send_sem=self.send.at[i],
            recv_sem=self.recv.at[i], device_id=self.devices[i], device_id_type=MESH,
        )

    def go(self, i):
        if i == 0:
            self.sent[0] = self.value[...]
            self.copy(0).start()
            return
        self.copy(i - 1).wait_recv()
        total = self.sent[i - 1] + self.landed[i - 1]
        if i < 5:
            self.sent[i] = total
            self.copy(i).start()
        else:
            self.out[...] = total
            for k in range(5):
                self.copy(k).wait_send()

    @staticmethod
    def scratch(shape):
        return [
            pltpu.VMEM((5,) + shape, f32),
            pltpu.VMEM((5,) + shape, f32),
            pltpu.SemaphoreType.DMA((5,)),
            pltpu.SemaphoreType.DMA((5,)),
        ]


def scatter_kernel(splits, with_small, *refs):
    count = len(splits)
    ins = count + (1 if with_small else 0)
    bigs, outs = refs[:count], refs[ins : ins + count]
    scratch = refs[2 * ins :]
    place = Place()
    place.greet((place.to_across,) if with_small else ())
    plans = [
        Scatter(place, bigs[i], outs[i], *scratch[7 * i : 7 * i + 7], splits[i]) for i in range(count)
    ]
    small = None
    if with_small:
        small = Small(place, refs[count], refs[ins + count], *scratch[7 * count :])
    for i in range(4):
        for plan in plans:
            plan.start_group(i)
    if small:
        small.go(0)
    for k in range(4):
        for plan in plans:
            plan.corner(k)
    if small:
        small.go(1)
    for k in range(4):
        for plan in plans:
            plan.sides(k)
        if small and k % 2 == 1:
            small.go(2 + k // 2)
    for k in range(4):
        for plan in plans:
            plan.mine(k)
    if small:
        small.go(4)
    for plan in plans:
        plan.result()
    if small:
        small.go(5)
    for plan in plans:
        plan.drain()


def scatter(bigs, splits, small, collective_id):
    count = len(bigs)
    spec = pl.BlockSpec(memory_space=pl.ANY)
    vmem = pl.BlockSpec(memory_space=pltpu.VMEM)
    shapes = [(b.shape[0] // 32, b.shape[1]) for b in bigs]
    extra = [] if small is None else [small]
    scratch = sum([Scatter.scratch(s[0], s[1], sp) for s, sp in zip(shapes, splits)], [])
    if small is not None:
        scratch = scratch + Small.scratch(small.shape)
    return pl.pallas_call(
        functools.partial(scatter_kernel, splits, small is not None),
        in_specs=[spec] * count + [vmem] * len(extra),
        out_specs=[vmem] * (count + len(extra)),
        out_shape=[jax.ShapeDtypeStruct(s, f32) for s in shapes]
        + [jax.ShapeDtypeStruct(e.shape, f32) for e in extra],
        scratch_shapes=scratch,
        compiler_params=pltpu.CompilerParams(
            collective_id=collective_id, has_side_effects=True, vmem_limit_bytes=60 * 1024 * 1024
        ),
    )(*bigs, *extra)


def own_kernels():
    return lax.axis_size("dp") == 4 and lax.axis_size("seq") == 8


def gather_rows(shards, splits, collective_id):
    if own_kernels():
        return gather(shards, splits, collective_id)
    return [lax.all_gather(s, ("dp", "seq"), axis=0, tiled=True) for s in shards]


def scatter_rows(bigs, splits, small, collective_id):
    if own_kernels():
        return scatter(bigs, splits, small, collective_id)
    outs = [lax.psum_scatter(b, ("dp", "seq"), scatter_dimension=0, tiled=True).astype(f32) for b in bigs]
    return outs + ([] if small is None else [lax.psum(small, ("dp", "seq"))])


def half_of(width):
    return (width // 2 + 127) // 128 * 128


def grouped(cols, groups):
    batch, span, heads = cols.shape
    return jnp.transpose(cols.reshape(batch, span, groups, heads // groups), (2, 0, 1, 3))


def ungrouped(cols):
    groups, batch, span, each = cols.shape
    return jnp.transpose(cols, (1, 2, 0, 3)).reshape(batch, span, groups * each)


def on_device(
    resid_in, out_grad, lengths, norm_gain, in_proj, dt_proj, conv_weight, conv_bias, dt_bias, a_log,
    skip_scale, gate_gain, out_proj,
):
    batch, span, width = resid_in.shape
    inner = gate_gain.shape[0]
    heads = a_log.shape[0]
    hw = inner // heads
    n = (in_proj.shape[1] - 2 * inner) // 2
    groups = heads // HEADS
    cb_w = HEADS * hw
    positions = lax.axis_index("seq") * span + lax.iota(jnp.int32, span)
    mask = (positions[None, :] < lengths[:, None]).astype(f32)[..., None]

    halo = shifted(resid_in[:, span - HALO :], "seq", 1)
    resid_ext = jnp.concatenate([halo, resid_in], axis=1).astype(f32)
    rs_ext = lax.rsqrt(jnp.mean(resid_ext * resid_ext, axis=-1, keepdims=True) + epsilon)
    x_ext = (resid_ext * rs_ext * norm_gain).astype(bf16)
    ext = span + HALO
    x2 = x_ext.reshape(batch * ext, width)
    resid_wide = resid_in.astype(f32)
    rs = rs_ext[:, HALO:]

    conv_cols = in_proj.shape[1] - inner
    dt_pad = (-(conv_cols + heads)) % 128
    conv_shard = jnp.concatenate(
        [in_proj[:, inner:], dt_proj, jnp.zeros((in_proj.shape[0], dt_pad), bf16)], axis=1
    )
    conv_all = conv_cols + heads + dt_pad
    (full_conv,) = gather_rows([conv_shard], [half_of(conv_all)], 3)
    full_gate, full_out = gather_rows(
        [in_proj[:, :inner], out_proj], [half_of(inner), half_of(width)], 4
    )
    full_dt = full_conv[:, conv_cols : conv_cols + heads]

    dt_raw = jnp.dot(x_ext[:, HALO:], full_dt, preferred_element_type=f32)
    step = jax.nn.softplus(dt_raw + dt_bias)
    rate = -jnp.exp(a_log)
    tri = causal(span, False).astype(f32)
    log_decay = jnp.einsum("ts,bsh->bth", tri, step * rate, precision=highest)
    scaled = log_decay * LOG2E
    colpack = jnp.concatenate([grouped(scaled, groups), grouped(step, groups)], axis=-1)
    rowpack = jnp.transpose(scaled, (0, 2, 1)).reshape(batch, groups, HEADS, span).transpose(1, 0, 2, 3)
    block_decay = jnp.exp(log_decay[:, span - 1])
    decay_wide = jnp.repeat(block_decay, hw, axis=1)[:, None, :]
    skip_wide = jnp.repeat(skip_scale, hw)[None]
    gain_wide = gate_gain[None]

    cw_keys, cb_keys = conv_weight[:, inner:], conv_bias[None, inner:]
    cw_vals, cb_vals = conv_weight[:, :inner], conv_bias[None, :inner]
    keys, cin_keys = keys_forward(x2, full_conv, inner // (2 * n), cw_keys, cb_keys, batch, span)
    v, cin_vals, local = values_forward(
        x2, full_conv, 0, cw_vals, cb_vals, keys, colpack, hw, span
    )
    carried = chain(local, decay_wide, False, 1)
    y, gate, normed_out, rg = rows_forward(
        x_ext, full_gate, v, keys, colpack, rowpack, carried, skip_wide, gain_wide, hw, span
    )
    mixer_out = jnp.dot(normed_out, full_out, preferred_element_type=f32)
    output = (mask * (resid_wide + mixer_out)).astype(bf16)

    mixer_grad = (mask * out_grad.astype(f32)).astype(bf16)
    mean = jnp.sum(mixer_grad.astype(f32) * mixer_out, axis=-1, keepdims=True) * (1.0 / inner)
    norms = jnp.concatenate([rg[..., :1], mean, jnp.zeros((batch, span, 6), f32)], axis=-1)
    grad_out = jnp.einsum("bsi,bsd->id", normed_out, mixer_grad, preferred_element_type=f32)
    dgate, dv, dh, cols_one, dq, dk, dgain, dskip = gate_backward(
        mixer_grad, full_out, y, gate, norms, gain_wide, v, keys, colpack, rowpack, carried, skip_wide, hw, span
    )
    later = chain(dh, decay_wide, True, 2)
    cig_vals, cols_two, dk2, dcw_vals, dcb_vals, dlast = state_backward(
        later, carried, keys, v, dv, colpack, cin_vals, cw_vals, cb_vals, hw, span
    )
    cig_keys, dcw_keys, dcb_keys = keys_backward(dk, dk2, dq, cin_keys, cw_keys, cb_keys, span)

    rise = ungrouped(cols_one[..., :HEADS])
    direct = ungrouped(cols_one[..., HEADS:])
    ahead = ungrouped(cols_two)
    moved = ahead * step
    last = jnp.sum(moved, axis=1) + dlast[:, 0].reshape(batch, heads, hw).sum(-1) * block_decay
    dlog = rise - moved
    dlog = jnp.einsum("ts,bth->bsh", tri, dlog, precision=highest) + last[:, None, :]
    grad_a = jnp.sum(dlog * step, axis=(0, 1)) * rate
    step_grad = direct + ahead + dlog * rate
    dt_grad = step_grad * jax.nn.sigmoid(dt_raw + dt_bias)
    grad_bias = jnp.sum(dt_grad, axis=(0, 1))
    step_low = dt_grad.astype(bf16)

    x_rows = x_ext[:, HALO:]
    grad_gate = jnp.einsum("bsd,bse->de", x_rows, dgate, preferred_element_type=f32)
    cig = jnp.concatenate([cig_vals, cig_keys], axis=-1)
    grad_conv = jnp.einsum("bsd,bse->de", x_ext, cig, preferred_element_type=f32)
    grad_dt = jnp.einsum("bsd,bsh->dh", x_rows, step_low, preferred_element_type=f32)
    normed_ext = jnp.einsum("bse,de->bsd", cig, full_conv[:, :conv_cols], preferred_element_type=f32)
    from_next = shifted(normed_ext[:, :HALO].astype(bf16), "seq", -1).astype(f32)
    normed_grad = normed_ext[:, HALO:]
    normed_grad = jnp.concatenate([normed_grad[:, : span - HALO], normed_grad[:, span - HALO :] + from_next], axis=1)
    normed_grad = normed_grad + jnp.einsum(
        "bse,de->bsd", dgate, full_gate, preferred_element_type=f32
    )
    normed_grad = normed_grad + jnp.einsum("bsh,dh->bsd", step_low, full_dt, preferred_element_type=f32)
    nz = resid_wide * rs
    fg = normed_grad * norm_gain
    grad_norm = jnp.sum(normed_grad * nz, axis=(0, 1))
    input_grad = mixer_grad.astype(f32) + rs * (fg - nz * jnp.mean(fg * nz, axis=-1, keepdims=True))

    grad_conv = jnp.concatenate([grad_conv, grad_dt, jnp.zeros((width, dt_pad), f32)], axis=1)
    pieces = (
        grad_norm,
        jnp.concatenate([dcw_vals, dcw_keys], axis=1),
        jnp.concatenate([dcb_vals, dcb_keys], axis=1)[0],
        dgain[0],
        grad_bias,
        grad_a,
        dskip[0].reshape(heads, hw).sum(-1),
    )
    flat = jnp.concatenate([p.reshape(-1) for p in pieces])
    small = jnp.pad(flat, (0, (-flat.size) % 1024)).reshape(-1, 128)
    sum_gate, sum_out = scatter_rows(
        [grad_gate.astype(bf16), grad_out.astype(bf16)], [half_of(inner), half_of(width)], None, 5
    )
    sum_conv, small = scatter_rows([grad_conv.astype(bf16)], [half_of(conv_all)], small, 6)
    flat, sums, at = small.reshape(-1), [], 0
    for p in pieces:
        sums.append(flat[at : at + p.size].reshape(p.shape))
        at += p.size
    sum_norm, sum_cw, sum_cb, sum_gain, sum_bias, sum_a, sum_skip = sums
    return (
        output,
        input_grad.astype(bf16),
        jnp.concatenate([sum_gate, sum_conv[:, :conv_cols]], axis=1),
        sum_conv[:, conv_cols : conv_cols + heads],
        sum_out,
        sum_norm,
        sum_cw,
        sum_cb,
        sum_bias,
        sum_a,
        sum_skip,
        sum_gain,
    )


def solution(mesh):
    rows = P("dp", "seq", None)
    shard = P(("dp", "seq"), None)
    return jax.shard_map(
        on_device,
        mesh=mesh,
        in_specs=(rows, rows, P("dp"), P(), shard, shard, P(), P(), P(), P(), P(), P(), shard),
        out_specs=(rows, rows, shard, shard, shard, P(), P(), P(), P(), P(), P(), P()),
        check_vma=False,
    )
```

```python
import functools

import jax
import jax.numpy as jnp
from jax import lax
from jax.experimental import pallas as pl
from jax.experimental.pallas import tpu as pltpu
from jax.sharding import PartitionSpec as P

epsilon = 1e-05
highest = lax.Precision.HIGHEST
HALO = 16
HEADS = 8
LOG2E = 1.4426950408889634
f32 = jnp.float32
bf16 = jnp.bfloat16
MESH = pl.DeviceIdType.MESH


def mm(a, b):
    return lax.dot_general(a, b, (((1,), (0,)), ((), ())), preferred_element_type=f32)


def mm_nt(a, b):
    return lax.dot_general(a, b, (((1,), (1,)), ((), ())), preferred_element_type=f32)


def mm_tn(a, b):
    return lax.dot_general(a, b, (((0,), (0,)), ((), ())), preferred_element_type=f32)


def shifted(block, axis, distance):
    devices = range(lax.axis_size(axis))
    route = [(i - distance, i) for i in devices if i - distance in devices]
    return lax.ppermute(block, axis, route)


def spread(cols, width):
    rows, heads = cols.shape
    low_half = lax.broadcasted_iota(jnp.int32, (rows, 2 * width), 1) < width
    pairs = [
        jnp.where(low_half, cols[:, i : i + 1], cols[:, i + 1 : i + 2]) for i in range(0, heads, 2)
    ]
    return jnp.concatenate(pairs, axis=1)


def gather_heads(x, width):
    rows, total = x.shape
    low_half = lax.broadcasted_iota(jnp.int32, (rows, 2 * width), 1) < width
    head_lane = lax.broadcasted_iota(jnp.int32, (rows, total // width), 1)
    out = jnp.zeros((rows, total // width), f32)
    for i in range(total // (2 * width)):
        pair = x[:, i * 2 * width : (i + 1) * 2 * width]
        one = jnp.sum(jnp.where(low_half, pair, 0.0), axis=1, keepdims=True)
        two = jnp.sum(jnp.where(low_half, 0.0, pair), axis=1, keepdims=True)
        out = jnp.where(head_lane == 2 * i, one, out)
        out = jnp.where(head_lane == 2 * i + 1, two, out)
    return out


def silu_parts(v):
    sg = 1.0 / (1.0 + jnp.exp(-v))
    return v * sg, sg


def conv_pre(a, cw, cb, span):
    first = HALO - (cw.shape[0] - 1)
    out = cb
    for k in range(cw.shape[0]):
        out = out + cw[k : k + 1] * a[first + k : first + k + span]
    return out


def params_of(limit_mb, dims=None):
    return pltpu.CompilerParams(vmem_limit_bytes=limit_mb * 1024 * 1024, dimension_semantics=dims)


def causal(span, transposed):
    one = lax.broadcasted_iota(jnp.int32, (span, span), 0)
    two = lax.broadcasted_iota(jnp.int32, (span, span), 1)
    return (one <= two) if transposed else (one >= two)


class Place:
    def __init__(self):
        self.dp = lax.axis_index("dp")
        self.seq = lax.axis_index("seq")
        y, x = self.dp // 2, self.dp % 2
        self.z, self.core = self.seq // 2, self.seq % 2
        self.dx = 2 * y + (1 - x)
        self.dy = 2 * (1 - y) + x
        self.dxy = 2 * (1 - y) + (1 - x)
        self.to_x = (self.dx, self.seq)
        self.to_y = (self.dy, self.seq)
        self.to_core = (self.dp, 2 * self.z + 1 - self.core)
        self.to_up = (self.dp, 2 * jnp.minimum(self.z + 1, 3) + self.core)
        self.to_down = (self.dp, 2 * jnp.maximum(self.z - 1, 0) + self.core)
        self.to_across = (self.dp, 2 * jnp.where(self.z < 2, self.z + 2, self.z - 2) + self.core)
        self.has_up = self.z < 3
        self.has_down = self.z > 0

    def near(self, k):
        z = self.z
        return (z, z + 1 - 2 * (z % 2), jnp.where(z < 2, 2, 1), jnp.where(z < 2, 3, 0))[k]

    def greet(self, others=()):
        barrier = pltpu.get_barrier_semaphore()
        for device in (self.to_x, self.to_y, self.to_core) + tuple(others):
            pl.semaphore_signal(barrier, inc=1, device_id=device, device_id_type=MESH)

        @pl.when(self.has_up)
        def _():
            pl.semaphore_signal(barrier, inc=1, device_id=self.to_up, device_id_type=MESH)

        @pl.when(self.has_down)
        def _():
            pl.semaphore_signal(barrier, inc=1, device_id=self.to_down, device_id_type=MESH)

        ends = self.has_up.astype(jnp.int32) + self.has_down.astype(jnp.int32)
        pl.semaphore_wait(barrier, 3 + len(others) + ends)


GATHER_KINDS = 11


def gather_steps(place, shard, full, split, own_sem, send, recv):
    rows, width = full.shape[0] // 32, full.shape[1]
    z, core = place.z, place.core
    every, left, right = pl.ds(0, width), pl.ds(0, split), pl.ds(split, width - split)
    two = split < width

    def view(d, zz, cc, cols):
        start = pl.multiple_of((d * 8 + zz * 2 + cc) * rows, 16)
        return full.at[pl.ds(start, rows), cols]

    def copy(kind, slot, device, d, zz, cc, cols, src=None):
        dst = view(d, zz, cc, cols)
        return pltpu.make_async_remote_copy(
            src_ref=dst if src is None else src,
            dst_ref=dst,
            send_sem=send.at[kind, slot],
            recv_sem=recv.at[kind, slot],
            device_id=device,
            device_id_type=MESH,
        )

    def pieces(k):
        zk = place.near(k)
        src = shard if k == 0 else None
        dp = place.dp
        return dict(
            x=copy(2, k, place.to_x, dp, zk, core, every, src),
            y=copy(3, k, place.to_y, dp, zk, core, every, src),
            own=copy(6, k, place.to_core, dp, zk, core, every, src),
        )

    def along(k, up):
        zk = place.near(k)
        src = shard if k == 0 else None
        device = place.to_up if up else place.to_down
        dst = view(place.dp, zk, core, every)
        return pltpu.make_async_remote_copy(
            src_ref=dst if src is None else src,
            dst_ref=dst,
            send_sem=send.at[0 if up else 1, k],
            recv_sem=recv.at[0, zk],
            device_id=device,
            device_id_type=MESH,
        )

    def arrive(k):
        zk = place.near(k)
        if k > 0:
            along(k, True).wait_recv()

        @pl.when(jnp.logical_and(zk <= z, place.has_up))
        def _():
            along(k, True).start()

        @pl.when(jnp.logical_and(zk >= z, place.has_down))
        def _():
            along(k, False).start()

        made = pieces(k)
        made["x"].start()
        made["y"].start()
        made["own"].start()

    def cross(k):
        zk = place.near(k)
        return (
            copy(2, k, place.to_x, place.dx, zk, core, every),
            copy(3, k, place.to_y, place.dy, zk, core, every),
            copy(4, k, place.to_y, place.dx, zk, core, left),
            copy(5, k, place.to_x, place.dy, zk, core, right) if two else None,
            copy(7, k, place.to_core, place.dx, zk, core, every),
            copy(8, k, place.to_core, place.dy, zk, core, every),
        )

    def forward(k):
        from_x, from_y, left_on, right_on, core_x, core_y = cross(k)
        from_x.wait_recv()
        left_on.start()
        core_x.start()
        from_y.wait_recv()
        if two:
            right_on.start()
        core_y.start()

    def corner(k):
        zk = place.near(k)
        return (
            copy(4, k, place.to_y, place.dxy, zk, core, left),
            copy(5, k, place.to_x, place.dxy, zk, core, right) if two else None,
            copy(9, k, place.to_core, place.dxy, zk, core, left),
            copy(10, k, place.to_core, place.dxy, zk, core, right) if two else None,
        )

    def last(k):
        from_y, from_x, core_left, core_right = corner(k)
        from_y.wait_recv()
        core_left.start()
        if two:
            from_x.wait_recv()
            core_right.start()

    def mine():
        return pltpu.make_async_copy(shard, view(place.dp, z, core, every), own_sem)

    def begin():
        mine().start()
        arrive(0)

    def finish():
        mine().wait()
        other = 1 - core
        for k in range(4):
            zk = place.near(k)
            for kind, d, cols in (
                (6, place.dp, every), (7, place.dx, every), (8, place.dy, every),
                (9, place.dxy, left), (10, place.dxy, right),
            ):
                if kind == 10 and not two:
                    continue
                copy(kind, k, place.to_core, d, zk, other, cols).wait_recv()
        for k in range(4):
            zk = place.near(k)

            @pl.when(jnp.logical_and(zk <= z, place.has_up))
            def _():
                along(k, True).wait_send()

            @pl.when(jnp.logical_and(zk >= z, place.has_down))
            def _():
                along(k, False).wait_send()

            made = pieces(k)
            made["x"].wait_send()
            made["y"].wait_send()
            made["own"].wait_send()
            for one in cross(k)[2:] + corner(k)[2:]:
                if one is not None:
                    one.wait_send()

    return [
        begin,
        lambda: arrive(1),
        lambda: forward(0),
        lambda: arrive(2),
        lambda: forward(1),
        lambda: arrive(3),
        lambda: forward(2),
        lambda: last(0),
        lambda: forward(3),
        lambda: last(1),
        lambda: last(2),
        lambda: last(3),
        finish,
    ]


def gather_scratch():
    return [
        pltpu.SemaphoreType.DMA,
        pltpu.SemaphoreType.DMA((GATHER_KINDS, 4)),
        pltpu.SemaphoreType.DMA((GATHER_KINDS, 4)),
    ]


def part_of(ref, part):
    return ref.at[:, pl.ds(part[0], part[1])]


def gather_kernel(splits, parts, *refs):
    count = len(splits)
    shards, fulls, sems = refs[:count], refs[count : 2 * count], refs[2 * count :]
    place = Place()
    place.greet()
    plans = [
        gather_steps(place, part_of(shards[i], parts[i]), fulls[i], splits[i], *sems[3 * i : 3 * i + 3])
        for i in range(count)
    ]
    for step in zip(*plans):
        for one in step:
            one()


def gather(shards, parts, splits, collective_id):
    count = len(shards)
    spec = pl.BlockSpec(memory_space=pl.ANY)
    return pl.pallas_call(
        functools.partial(gather_kernel, splits, parts),
        in_specs=[spec] * count,
        out_specs=[spec] * count,
        out_shape=[jax.ShapeDtypeStruct((s.shape[0] * 32, p[1]), s.dtype) for s, p in zip(shards, parts)],
        scratch_shapes=gather_scratch() * count,
        compiler_params=pltpu.CompilerParams(collective_id=collective_id, has_side_effects=True),
    )(*shards)


class Scatter:
    def __init__(self, place, big, out, own, land_core, land_xy, land_z, local, send, recv, split):
        self.place, self.big, self.out = place, big, out
        self.own, self.land_core, self.land_xy, self.land_z = own, land_core, land_xy, land_z
        self.local, self.send, self.recv = local, send, recv
        self.rows, self.width = out.shape
        self.split = split
        self.left, self.right = slice(0, split), slice(split, self.width)

    def groups(self):
        p = self.place
        return (p.dxy, p.dx, p.dy, p.dp)

    def far(self, k):
        return self.place.near(3 - k)

    def source(self, d, zz, cc):
        start = pl.multiple_of((d * 8 + zz * 2 + cc) * self.rows, 16)
        return self.big.at[pl.ds(start, self.rows)]

    def remote(self, src, dst, kind, slot, device):
        return pltpu.make_async_remote_copy(
            src_ref=src, dst_ref=dst, send_sem=self.send.at[kind, slot], recv_sem=self.recv.at[kind, slot],
            device_id=device, device_id_type=MESH,
        )

    def to_other(self, i, k):
        p = self.place
        src = self.source(self.groups()[i], self.far(k), 1 - p.core)
        return self.remote(src, self.land_core.at[i, k], i, k, p.to_core)

    def load(self, i, k):
        p = self.place
        return pltpu.make_async_copy(
            self.source(self.groups()[i], self.far(k), p.core), self.own.at[i, k], self.local.at[i, k]
        )

    def start(self, k):
        for i in range(4):
            self.to_other(i, k).start()
            self.load(i, k).start()

    def join(self, i, k):
        self.load(i, k).wait()
        self.to_other(i, k).wait_recv()
        self.own[i, k] = self.own[i, k] + self.land_core[i, k]

    def side(self, kind, k):
        p = self.place
        left, right = pl.ds(0, self.split), pl.ds(self.split, self.width - self.split)
        group, cols, device = (
            (0, left, p.to_y),
            (0, right, p.to_x),
            (2, left, p.to_y),
            (1, right, p.to_x),
            (2, right, p.to_y),
            (1, left, p.to_x),
        )[kind]
        size = self.split if cols is left else self.width - self.split
        return self.remote(
            self.own.at[group, k, :, cols], self.land_xy.at[kind, k, :, pl.ds(0, size)], 4 + kind, k, device
        )

    def take(self, kind, group, cols, k):
        self.side(kind, k).wait_recv()
        size = cols.stop - cols.start
        self.own[group, k, :, cols] = self.own[group, k, :, cols] + self.land_xy[kind, k, :, 0:size]

    def corner(self, k):
        self.join(0, k)
        self.side(0, k).start()
        self.side(1, k).start()

    def sides(self, k):
        self.join(1, k)
        self.side(3, k).start()
        self.join(2, k)
        self.side(2, k).start()

    def turns(self, k):
        self.take(0, 1, self.left, k)
        self.side(5, k).start()
        self.take(1, 2, self.right, k)
        self.side(4, k).start()

    def along(self, k, up):
        p = self.place
        zk = self.far(k)
        return pltpu.make_async_remote_copy(
            src_ref=self.own.at[3, k],
            dst_ref=self.land_z.at[0 if up else 1, zk],
            send_sem=self.send.at[10, k],
            recv_sem=self.recv.at[10 if up else 11, zk],
            device_id=p.to_up if up else p.to_down,
            device_id_type=MESH,
        )

    def rising(self, k):
        return self.far(k) > self.place.z

    def behind(self, k):
        p = self.place
        rising = self.rising(k)
        return jnp.logical_or(
            jnp.logical_and(rising, p.has_down), jnp.logical_and(jnp.logical_not(rising), p.has_up)
        )

    def send_along(self, k):
        @pl.when(self.rising(k))
        def _():
            self.along(k, True).start()

        @pl.when(jnp.logical_not(self.rising(k)))
        def _():
            self.along(k, False).start()

    def mine(self, k):
        self.join(3, k)
        self.take(2, 3, self.left, k)
        self.take(3, 3, self.right, k)
        self.take(5, 3, self.left, k)
        self.take(4, 3, self.right, k)
        if k < 3:

            @pl.when(jnp.logical_not(self.behind(k)))
            def _():
                self.send_along(k)

    def line(self, k):
        zk = self.far(k)

        @pl.when(jnp.logical_and(self.behind(k), self.rising(k)))
        def _():
            self.along(k, True).wait_recv()
            self.own[3, k] = self.own[3, k] + self.land_z[0, zk]

        @pl.when(jnp.logical_and(self.behind(k), jnp.logical_not(self.rising(k))))
        def _():
            self.along(k, False).wait_recv()
            self.own[3, k] = self.own[3, k] + self.land_z[1, zk]

        @pl.when(self.behind(k))
        def _():
            self.send_along(k)

    def result(self):
        p = self.place
        self.out[...] = self.own[3, 3].astype(f32)

        @pl.when(p.has_down)
        def _():
            self.along(3, True).wait_recv()
            self.out[...] += self.land_z[0, p.z].astype(f32)

        @pl.when(p.has_up)
        def _():
            self.along(3, False).wait_recv()
            self.out[...] += self.land_z[1, p.z].astype(f32)

    def drain(self):
        for k in range(4):
            for i in range(4):
                self.to_other(i, k).wait_send()
            for kind in range(6):
                self.side(kind, k).wait_send()
            if k < 3:
                self.along(k, True).wait_send()

    def steps(self):
        start, corner, sides, turns, mine, line = (
            self.start, self.corner, self.sides, self.turns, self.mine, self.line
        )
        return [
            (0, lambda: start(0)),
            (2, lambda: start(1)),
            (3, lambda: corner(0)),
            (4, lambda: sides(0)),
            (6, lambda: start(2)),
            (8, lambda: turns(0)),
            (9, lambda: corner(1)),
            (10, lambda: sides(1)),
            (12, lambda: start(3)),
            (14, lambda: mine(0)),
            (17, lambda: turns(1)),
            (18, lambda: corner(2)),
            (19, lambda: sides(2)),
            (22, lambda: line(0)),
            (23, lambda: mine(1)),
            (26, lambda: turns(2)),
            (27, lambda: corner(3)),
            (28, lambda: sides(3)),
            (31, lambda: line(1)),
            (32, lambda: mine(2)),
            (35, lambda: turns(3)),
            (40, lambda: line(2)),
            (42, lambda: mine(3)),
            (47, self.result),
            (50, self.drain),
        ]

    @staticmethod
    def scratch(rows, width, split):
        half = max(split, width - split)
        return [
            pltpu.VMEM((4, 4, rows, width), bf16),
            pltpu.VMEM((4, 4, rows, width), bf16),
            pltpu.VMEM((6, 4, rows, half), bf16),
            pltpu.VMEM((2, 4, rows, width), bf16),
            pltpu.SemaphoreType.DMA((4, 4)),
            pltpu.SemaphoreType.DMA((11, 4)),
            pltpu.SemaphoreType.DMA((12, 4)),
        ]


class Small:
    def __init__(self, place, value, out, sent, landed, send, recv):
        p = place
        self.value, self.out, self.sent, self.landed, self.send, self.recv = value, out, sent, landed, send, recv
        pair = 2 * (p.z + 1 - 2 * (p.z % 2)) + p.core
        self.devices = (p.to_core, p.to_x, p.to_y, (p.dp, pair), p.to_across)

    def copy(self, i):
        return pltpu.make_async_remote_copy(
            src_ref=self.sent.at[i], dst_ref=self.landed.at[i], send_sem=self.send.at[i],
            recv_sem=self.recv.at[i], device_id=self.devices[i], device_id_type=MESH,
        )

    def go(self, i):
        if i == 0:
            self.sent[0] = self.value[...]
            self.copy(0).start()
            return
        self.copy(i - 1).wait_recv()
        total = self.sent[i - 1] + self.landed[i - 1]
        if i < 5:
            self.sent[i] = total
            self.copy(i).start()
        else:
            self.out[...] = total
            for k in range(5):
                self.copy(k).wait_send()

    @staticmethod
    def scratch(shape):
        return [
            pltpu.VMEM((5,) + shape, f32),
            pltpu.VMEM((5,) + shape, f32),
            pltpu.SemaphoreType.DMA((5,)),
            pltpu.SemaphoreType.DMA((5,)),
        ]


def scatter_kernel(splits, with_small, *refs):
    count = len(splits)
    ins = count + (1 if with_small else 0)
    bigs, outs = refs[:count], refs[ins : ins + count]
    scratch = refs[2 * ins :]
    place = Place()
    place.greet((place.to_across,) if with_small else ())
    plans = [
        Scatter(place, bigs[i], outs[i], *scratch[7 * i : 7 * i + 7], splits[i]) for i in range(count)
    ]
    small = None
    if with_small:
        small = Small(place, refs[count], refs[ins + count], *scratch[7 * count :])
    small_at = {0: 0, 5: 1, 9: 2, 13: 3, 17: 4, 21: 5}
    for i, steps in enumerate(zip(*[plan.steps() for plan in plans])):
        for _, step in steps:
            step()
        if small and i in small_at:
            small.go(small_at[i])


def scatter(bigs, splits, small, collective_id):
    count = len(bigs)
    spec = pl.BlockSpec(memory_space=pl.ANY)
    vmem = pl.BlockSpec(memory_space=pltpu.VMEM)
    shapes = [(b.shape[0] // 32, b.shape[1]) for b in bigs]
    extra = [] if small is None else [small]
    scratch = sum([Scatter.scratch(s[0], s[1], sp) for s, sp in zip(shapes, splits)], [])
    if small is not None:
        scratch = scratch + Small.scratch(small.shape)
    return pl.pallas_call(
        functools.partial(scatter_kernel, splits, small is not None),
        in_specs=[spec] * count + [vmem] * len(extra),
        out_specs=[vmem] * (count + len(extra)),
        out_shape=[jax.ShapeDtypeStruct(s, f32) for s in shapes]
        + [jax.ShapeDtypeStruct(e.shape, f32) for e in extra],
        scratch_shapes=scratch,
        compiler_params=pltpu.CompilerParams(
            collective_id=collective_id, has_side_effects=True, vmem_limit_bytes=60 * 1024 * 1024
        ),
    )(*bigs, *extra)


def prep_kernel(span, heads, x_ref, wk_ref, wd_ref, cw_ref, cb_ref, bias_ref, rate_ref,
                rows_ref, cin_ref, col_ref, row_ref, raw_ref, step_ref):
    batch = rows_ref.shape[0]
    ext = span + HALO
    acc = mm(x_ref[...], wk_ref[...])
    raw_all = mm(x_ref[...], wd_ref[...])
    tri = causal(span, False).astype(f32)
    for b in range(batch):
        a = acc[b * ext : (b + 1) * ext]
        row, _ = silu_parts(conv_pre(a, cw_ref[...], cb_ref[...], span))
        rows_ref[b] = row.astype(bf16)
        cin_ref[b] = a.astype(bf16)
        raw = raw_all[b * ext + HALO : (b + 1) * ext] + bias_ref[...]
        step = jnp.maximum(raw, 0.0) + jnp.log1p(jnp.exp(-jnp.abs(raw)))
        scaled = lax.dot_general(
            tri, step * rate_ref[...], (((1,), (0,)), ((), ())), precision=highest, preferred_element_type=f32
        ) * LOG2E
        raw_ref[b] = raw
        step_ref[b] = step
        turned = jnp.transpose(scaled)
        for g in range(heads // HEADS):
            some = slice(g * HEADS, (g + 1) * HEADS)
            col_ref[g, b] = jnp.concatenate([scaled[:, some], step[:, some]], axis=1)
            row_ref[g, b] = turned[some]


def prepare(x2, w_conv, key_block, w_dt, cw, cb, bias, rate, batch, span, heads):
    width = cw.shape[1]
    ext = span + HALO
    groups = heads // HEADS
    lanes = bias.shape[1]
    whole = lambda shape: pl.BlockSpec(shape, lambda i: (0,) * len(shape))
    shapes = [
        ((batch, span, width), bf16),
        ((batch, ext, width), bf16),
        ((groups, batch, span, 2 * HEADS), f32),
        ((groups, batch, HEADS, span), f32),
        ((batch, span, lanes), f32),
        ((batch, span, lanes), f32),
    ]
    return pl.pallas_call(
        functools.partial(prep_kernel, span, heads),
        grid=(1,),
        in_specs=[
            whole(x2.shape),
            pl.BlockSpec((w_conv.shape[0], width), lambda i: (0, key_block)),
            whole(w_dt.shape),
            whole(cw.shape), whole(cb.shape), whole(bias.shape), whole(rate.shape),
        ],
        out_specs=[whole(s) for s, _ in shapes],
        out_shape=[jax.ShapeDtypeStruct(s, d) for s, d in shapes],
        compiler_params=params_of(50),
    )(x2, w_conv, w_dt, cw, cb, bias, rate)


class Chain:
    def __init__(self, backward, sent, landed, send, recv):
        self.sent, self.landed, self.send, self.recv = sent, landed, send, recv
        me, count = lax.axis_index("seq"), lax.axis_size("seq")
        turn = -1 if backward else 1
        self.place = count - 1 - me if backward else me
        self.has_prev = self.place > 0
        self.has_next = self.place < count - 1
        self.next = (lax.axis_index("dp"), jnp.clip(me + turn, 0, count - 1))
        self.prev = (lax.axis_index("dp"), jnp.clip(me - turn, 0, count - 1))

    def copy(self, k):
        return pltpu.make_async_remote_copy(
            src_ref=self.sent.at[k], dst_ref=self.landed.at[k], send_sem=self.send.at[k],
            recv_sem=self.recv.at[k], device_id=self.next, device_id_type=MESH,
        )

    def pass_on(self, k, decay, local):
        @pl.when(self.has_prev)
        def _():
            self.copy(k).wait_recv()

        @pl.when(jnp.logical_not(self.has_prev))
        def _():
            self.landed[k] = jnp.zeros_like(self.landed[k])

        @pl.when(self.has_next)
        def _():
            self.sent[k] = (decay() * self.landed[k].astype(f32) + local()).astype(bf16)
            self.copy(k).start()

    def drain(self):
        @pl.when(self.has_next)
        def _():
            for k in range(self.sent.shape[0]):
                self.copy(k).wait_send()

    @staticmethod
    def scratch(count, n, size):
        return [
            pltpu.VMEM((count, n, size), bf16),
            pltpu.VMEM((count, n, size), bf16),
            pltpu.SemaphoreType.DMA((count,)),
            pltpu.SemaphoreType.DMA((count,)),
        ]


def greet_all(place, chain):
    barrier = pltpu.get_barrier_semaphore()
    flags = [chain.has_prev, chain.has_next]
    devices = [chain.prev, chain.next]
    total = chain.has_prev.astype(jnp.int32) + chain.has_next.astype(jnp.int32)
    if place is not None:
        flags += [place.has_up, place.has_down]
        devices += [place.to_up, place.to_down]
        total = total + place.has_up.astype(jnp.int32) + place.has_down.astype(jnp.int32) + 3
        for device in (place.to_x, place.to_y, place.to_core):
            pl.semaphore_signal(barrier, inc=1, device_id=device, device_id_type=MESH)
    for flag, device in zip(flags, devices):

        @pl.when(flag)
        def _(device=device):
            pl.semaphore_signal(barrier, inc=1, device_id=device, device_id_type=MESH)

    pl.semaphore_wait(barrier, total)


def front_kernel(span, hw, groups, splits, parts, hooks, *refs):
    count = len(splits)
    (x_ref, w_ref, cw_ref, cb_ref, keys_ref, col_ref, row_ref, skip_ref) = refs[:8]
    shards = refs[8 : 8 + count]
    rows_ref, cin_ref, y_ref, carried_ref = refs[8 + count : 12 + count]
    fulls = refs[12 + count : 12 + 2 * count]
    rest = refs[12 + 2 * count :]
    values, local, scores = rest[:3]
    chain = Chain(False, *rest[3:7])
    batch = rows_ref.shape[0]
    n = keys_ref.shape[2] // 2
    ext = span + HALO
    i = pl.program_id(0)
    last_decay = rest[-1]
    place = Place() if count else None
    plans = [
        gather_steps(place, part_of(shards[j], parts[j]), fulls[j], splits[j], *rest[7 + 3 * j : 10 + 3 * j])
        for j in range(count)
    ]
    low_half = lax.broadcasted_iota(jnp.int32, (span, 2 * hw), 1) < hw

    @pl.when(i == 0)
    def _():
        greet_all(place, chain)

    def hook(b):
        for slot, plan in zip(hooks, zip(*plans)):
            if slot % batch == b:

                @pl.when(i == slot // batch)
                def _(plan=plan):
                    for one in plan:
                        one()

    def ready(j):
        for b in range(batch):
            k = j * batch + b
            chain.pass_on(k, lambda: last_decay[k], lambda: local[k])

    def values_part(b, acc):
        a = acc[b * ext : (b + 1) * ext]
        row, _ = silu_parts(conv_pre(a, cw_ref[...], cb_ref[...], span))
        row = row.astype(bf16)
        rows_ref[b] = row
        values[i * batch + b] = row
        cin_ref[b] = a.astype(bf16)
        cols = col_ref[0, b]
        c, step = cols[:, :HEADS], cols[:, HEADS:]
        weight = jnp.exp2(c[span - 1 : span] - c) * step
        vw = (row.astype(f32) * spread(weight, hw)).astype(bf16)
        local[i * batch + b] = mm_tn(keys_ref[b, :, :n], vw)
        last_decay[i * batch + b] = spread(jnp.exp2(c[span - 1 : span]), hw)

    def rows_part(b):
        g = i - groups
        at = g * batch + b
        k_in, k_out = keys_ref[b, :, :n], keys_ref[b, :, n:]

        @pl.when(g == 0)
        def _():
            scores[b] = jnp.where(causal(span, False), mm_nt(k_out, k_in), 0.0)

        cols = col_ref[0, b]
        c, step = cols[:, :HEADS], cols[:, HEADS:]
        v = values[at].astype(f32)
        vs = (v * spread(step, hw)).astype(bf16)
        s = scores[b]
        rows = row_ref[0, b]
        parts_y = []
        for p in range(HEADS // 2):
            pair = vs[:, p * 2 * hw : (p + 1) * 2 * hw]
            total = None
            for q in range(2):
                h = 2 * p + q
                gap = jnp.minimum(c[:, h : h + 1] - rows[h : h + 1, :], 0.0)
                u = (jnp.exp2(gap) * s).astype(bf16)
                keep = low_half if q == 0 else jnp.logical_not(low_half)
                term = mm(u, jnp.where(keep, pair, jnp.zeros_like(pair)))
                total = term if total is None else total + term
            parts_y.append(total)
        inside = jnp.concatenate(parts_y, axis=1)
        came = chain.landed[at]
        carried_ref[b] = came
        y_ref[b] = inside + mm(k_out, came) * spread(jnp.exp2(c), hw) + skip_ref[...] * v

    @pl.when(i < groups)
    def _():
        acc = mm(x_ref[...], w_ref[...])
        for b in range(batch):
            hook(b)
            values_part(b, acc)

    @pl.when(i >= groups)
    def _():
        for b in range(batch):
            hook(b)
            rows_part(b)

    early = i - chain.place

    @pl.when(jnp.logical_and(jnp.logical_and(early >= 0, early < groups), i <= groups - 1 + early))
    def _():
        ready(early)

    late = i - (groups - 1)

    @pl.when(jnp.logical_and(jnp.logical_and(late >= 0, late < groups), chain.place > groups - 1))
    def _():
        ready(late)

    @pl.when(i == 2 * groups - 1)
    def _():
        chain.drain()


def front(x2, w_conv, cw, cb, keys, colpack, rowpack, skip, shards, parts, splits, hooks, hw, span, collective_id):
    batch = keys.shape[0]
    groups = colpack.shape[0]
    cb_w = HEADS * hw
    ext = span + HALO
    inner = groups * cb_w
    n = keys.shape[2] // 2
    first = lambda i: jnp.minimum(i, groups - 1)
    then = lambda i: jnp.maximum(i - groups, 0)
    group = lambda i: i % groups
    hbm = pl.BlockSpec(memory_space=pl.ANY)
    count = len(shards)
    return pl.pallas_call(
        functools.partial(front_kernel, span, hw, groups, splits, parts, hooks),
        grid=(2 * groups,),
        in_specs=[
            pl.BlockSpec(x2.shape, lambda i: (0, 0)),
            pl.BlockSpec((w_conv.shape[0], cb_w), lambda i: (0, first(i))),
            pl.BlockSpec((cw.shape[0], cb_w), lambda i: (0, first(i))),
            pl.BlockSpec((1, cb_w), lambda i: (0, first(i))),
            pl.BlockSpec(keys.shape, lambda i: (0, 0, 0)),
            pl.BlockSpec((1,) + colpack.shape[1:], lambda i: (group(i), 0, 0, 0)),
            pl.BlockSpec((1,) + rowpack.shape[1:], lambda i: (group(i), 0, 0, 0)),
            pl.BlockSpec((1, cb_w), lambda i: (0, then(i))),
        ]
        + [hbm] * count,
        out_specs=[
            pl.BlockSpec((batch, span, cb_w), lambda i: (0, 0, first(i))),
            pl.BlockSpec((batch, ext, cb_w), lambda i: (0, 0, first(i))),
            pl.BlockSpec((batch, span, cb_w), lambda i: (0, 0, then(i))),
            pl.BlockSpec((batch, n, cb_w), lambda i: (0, 0, then(i))),
        ]
        + [hbm] * count,
        out_shape=[
            jax.ShapeDtypeStruct((batch, span, inner), bf16),
            jax.ShapeDtypeStruct((batch, ext, inner), bf16),
            jax.ShapeDtypeStruct((batch, span, inner), f32),
            jax.ShapeDtypeStruct((batch, n, inner), bf16),
        ]
        + [jax.ShapeDtypeStruct((s.shape[0] * 32, p[1]), s.dtype) for s, p in zip(shards, parts)],
        scratch_shapes=[
            pltpu.VMEM((groups * batch, span, cb_w), bf16),
            pltpu.VMEM((groups * batch, n, cb_w), f32),
            pltpu.VMEM((batch, span, span), f32),
        ]
        + Chain.scratch(groups * batch, n, cb_w)
        + gather_scratch() * count
        + [pltpu.VMEM((groups * batch, 1, cb_w), f32)],
        compiler_params=pltpu.CompilerParams(
            collective_id=collective_id, has_side_effects=True, vmem_limit_bytes=58 * 1024 * 1024
        ),
    )(x2, w_conv, cw, cb, keys, colpack, rowpack, skip, *shards)


def norm_kernel(span, x_ref, w_ref, y_ref, gain_ref, gate_ref, no_ref, rg_ref, gated, squares):
    g = pl.program_id(0)
    groups = pl.num_programs(0)
    batch = x_ref.shape[0]
    cb_w = w_ref.shape[1]

    @pl.when(g == 0)
    def _():
        squares[...] = jnp.zeros_like(squares)

    for b in range(batch):
        gate = mm(x_ref[b, HALO:], w_ref[...])
        gate_ref[b] = gate.astype(bf16)
        act, _ = silu_parts(gate)
        gr = y_ref[b] * act
        gated[g, b] = gr
        squares[b] += sum([gr[:, i * 128 : (i + 1) * 128] * gr[:, i * 128 : (i + 1) * 128] for i in range(cb_w // 128)])

    @pl.when(g == groups - 1)
    def _():
        for b in range(batch):
            total = jnp.sum(squares[b], axis=1, keepdims=True)
            rg = lax.rsqrt(total * (1.0 / (no_ref.shape[2])) + epsilon)
            rg_ref[b] = jnp.broadcast_to(rg, rg_ref.shape[1:])
            for i in range(no_ref.shape[2] // cb_w):
                part = slice(i * cb_w, (i + 1) * cb_w)
                no_ref[b, :, part] = (gated[i, b] * rg * gain_ref[:, part]).astype(bf16)


def gated_norm(x_ext, w_gate, y, gain, span, cb_w):
    batch, ext, width = x_ext.shape
    inner = y.shape[2]
    groups = inner // cb_w
    block = pl.BlockSpec((batch, span, cb_w), lambda g: (0, 0, g))
    return pl.pallas_call(
        functools.partial(norm_kernel, span),
        grid=(groups,),
        in_specs=[
            pl.BlockSpec((batch, ext, width), lambda g: (0, 0, 0)),
            pl.BlockSpec((width, cb_w), lambda g: (0, g)),
            block,
            pl.BlockSpec((1, inner), lambda g: (0, 0)),
        ],
        out_specs=[
            block,
            pl.BlockSpec((batch, span, inner), lambda g: (0, 0, 0)),
            pl.BlockSpec((batch, span, 8), lambda g: (0, 0, 0)),
        ],
        out_shape=[
            jax.ShapeDtypeStruct((batch, span, inner), bf16),
            jax.ShapeDtypeStruct((batch, span, inner), bf16),
            jax.ShapeDtypeStruct((batch, span, 8), f32),
        ],
        scratch_shapes=[
            pltpu.VMEM((groups, batch, span, cb_w), f32),
            pltpu.VMEM((batch, span, 128), f32),
        ],
        compiler_params=params_of(56),
    )(x_ext, w_gate, y, gain)


def scatter_beside(i, batch, slots, starts, splits, bigs, outs, scratch):
    if not splits:
        return lambda b: None
    place = Place()
    plans = [
        Scatter(place, bigs[j], outs[j], *scratch[7 * j : 7 * j + 7], splits[j]).steps()
        for j in range(len(splits))
    ]
    at = {}
    for steps in zip(*plans):
        for time, step in steps:
            slot = min([k for k in range(slots) if starts(k) >= time] + [slots - 1])
            at.setdefault(slot, []).append(step)

    def run(b):
        for slot, steps in at.items():
            if slot % batch == b:

                @pl.when(i == slot // batch)
                def _(steps=steps):
                    for step in steps:
                        step()

    return run


def gate_back_kernel(span, hw, groups, splits, *refs):
    count = len(splits)
    (mg_ref, w_ref, y_ref, gate_ref, norm_ref, gain_ref, v_ref, keys_ref, col_ref, row_ref) = refs[:10]
    h_ref, skip_ref = refs[10:12]
    bigs = refs[12 : 12 + count]
    (dgate_ref, dv_ref, later_ref, cols_ref, dq_ref, dk_ref, dgain_ref, dskip_ref) = refs[12 + count : 20 + count]
    outs = refs[20 + count : 20 + 2 * count]
    rest = refs[20 + 2 * count :]
    scores, dscores, dqacc, gbs, rises, local, decays = rest[:7]
    chain = Chain(True, *rest[7:11])
    batch = mg_ref.shape[0]
    blocks = groups * batch
    i = pl.program_id(0)
    g = i % groups
    n = keys_ref.shape[2] // 2
    skip = skip_ref[...]
    low_half = lax.broadcasted_iota(jnp.int32, (span, 2 * hw), 1) < hw

    @pl.when(i == 0)
    def _():
        greet_all(Place() if count else None, chain)

    hook = scatter_beside(i, batch, 2 * blocks, lambda k: gate_start(k, blocks), splits, bigs, outs, rest[11:])

    def gate_part(b):
        at = g * batch + b
        cols = col_ref[0, b]
        c = cols[:, :HEADS]
        no_grad = mm_nt(mg_ref[b], w_ref[...])
        gate = gate_ref[b].astype(f32)
        y = y_ref[b]
        rg = norm_ref[b][:, 0:1]
        mean = norm_ref[b][:, 1:2]
        act, sg = silu_parts(gate)
        gn = y * act * rg
        dgain = jnp.sum(no_grad * gn, axis=0, keepdims=True)
        dg = rg * (no_grad * gain_ref[...] - gn * mean)
        dgate_ref[b] = (dg * y * (sg * (1.0 + gate * (1.0 - sg)))).astype(bf16)
        gb = (dg * act).astype(bf16)
        gbs[at] = gb
        gf = gb.astype(f32)
        v = v_ref[b].astype(f32)
        dskip = jnp.sum(gf * v, axis=0, keepdims=True)
        rises[at] = gather_heads(gf * (y - skip * v), hw)
        ge = (gf * spread(jnp.exp2(c), hw)).astype(bf16)
        local[at] = mm_tn(keys_ref[b, :, n:], ge)
        decays[at] = spread(jnp.exp2(c[span - 1 : span]), hw)
        part = mm_nt(ge, h_ref[b])

        @pl.when(g == 0)
        def _():
            dqacc[b] = part

        @pl.when(g != 0)
        def _():
            dqacc[b] += part

        if b == 0:
            dgain_ref[...] = dgain
            dskip_ref[...] = dskip
        else:
            dgain_ref[...] += dgain
            dskip_ref[...] += dskip

    def block_part(b):
        at = g * batch + b
        cols = col_ref[0, b]
        c, step = cols[:, :HEADS], cols[:, HEADS:]
        k_in, k_out = keys_ref[b, :, :n], keys_ref[b, :, n:]

        @pl.when(g == 0)
        def _():
            scores[b] = jnp.where(causal(span, True), mm_nt(k_in, k_out), 0.0)
            dscores[b] = jnp.zeros_like(dscores[b])

        later_ref[b] = chain.landed[at]
        gb = gbs[at]
        gf = gb.astype(f32)
        v = v_ref[b].astype(f32)
        step_wide = spread(step, hw)
        vs = (v * step_wide).astype(bf16)
        rows = row_ref[0, b]
        s = scores[b]
        parts = []
        ds = dscores[b]
        for p in range(HEADS // 2):
            lanes = slice(p * 2 * hw, (p + 1) * 2 * hw)
            total = None
            for q in range(2):
                h = 2 * p + q
                gap = jnp.minimum(rows[h : h + 1, :] - c[:, h : h + 1], 0.0)
                decay = jnp.exp2(gap)
                u = (decay * s).astype(bf16)
                keep = low_half if q == 0 else jnp.logical_not(low_half)
                half = jnp.where(keep, gb[:, lanes], jnp.zeros_like(gb[:, lanes]))
                term = mm(u, half)
                total = term if total is None else total + term
                ds = ds + decay * mm_nt(vs[:, lanes], half)
            parts.append(total)
        dscores[b] = ds
        u_all = jnp.concatenate(parts, axis=1)
        dv_ref[b] = (u_all * step_wide + skip * gf).astype(bf16)
        fall = gather_heads(vs.astype(f32) * u_all, hw)
        direct = gather_heads(v * u_all, hw)
        cols_ref[0, b] = jnp.concatenate([rises[at] - fall, direct], axis=1)

        @pl.when(g == groups - 1)
        def _():
            low = jnp.where(causal(span, True), dscores[b], 0.0).astype(bf16)
            dq_ref[b] = dqacc[b] + mm_tn(low, k_in)
            dk_ref[b] = mm(low, k_out)

    lag = jnp.minimum(3 * chain.place, blocks - 1)
    for b in range(batch):
        hook(b)

        @pl.when(i < groups)
        def _():
            gate_part(b)

        @pl.when(i >= groups)
        def _():
            block_part(b)

        k = i * batch + b - lag

        @pl.when(jnp.logical_and(k >= 0, k < blocks))
        def _():
            chain.pass_on(k, lambda: decays[k], lambda: local[k])

    @pl.when(i == 2 * groups - 1)
    def _():
        chain.drain()


def gate_backward(
    mg, w_out, y, gate, norms, gain, v, keys, colpack, rowpack, carried, skip, bigs, splits, hw, span,
    collective_id,
):
    hbm = pl.BlockSpec(memory_space=pl.ANY)
    shapes = [(x.shape[0] // 32, x.shape[1]) for x in bigs]
    batch, _, width = mg.shape
    groups = colpack.shape[0]
    cb_w = HEADS * hw
    inner = groups * cb_w
    n = keys.shape[2] // 2
    blocks = groups * batch
    first = lambda i: jnp.minimum(i, groups - 1)
    then = lambda i: jnp.maximum(i - groups, 0)
    both = lambda i: i % groups
    block = lambda f, rows: pl.BlockSpec((batch, rows, cb_w), lambda i: (0, 0, f(i)))
    lanes = lambda f: pl.BlockSpec((1, cb_w), lambda i: (0, f(i)))
    whole = lambda shape: pl.BlockSpec(shape, lambda i: (0,) * len(shape))
    return pl.pallas_call(
        functools.partial(gate_back_kernel, span, hw, groups, splits),
        grid=(2 * groups,),
        in_specs=[
            whole(mg.shape),
            pl.BlockSpec((cb_w, width), lambda i: (first(i), 0)),
            block(first, span),
            block(first, span),
            whole(norms.shape),
            lanes(first),
            block(both, span),
            whole(keys.shape),
            pl.BlockSpec((1,) + colpack.shape[1:], lambda i: (both(i), 0, 0, 0)),
            pl.BlockSpec((1,) + rowpack.shape[1:], lambda i: (then(i), 0, 0, 0)),
            block(first, n),
            lanes(both),
        ]
        + [hbm] * len(bigs),
        out_specs=[
            block(first, span),
            block(then, span),
            block(then, n),
            pl.BlockSpec((1, batch, span, 2 * HEADS), lambda i: (then(i), 0, 0, 0)),
            whole((batch, span, n)),
            whole((batch, span, n)),
            lanes(first),
            lanes(first),
        ]
        + [whole(s) for s in shapes],
        out_shape=[
            jax.ShapeDtypeStruct((batch, span, inner), bf16),
            jax.ShapeDtypeStruct((batch, span, inner), bf16),
            jax.ShapeDtypeStruct((batch, n, inner), bf16),
            jax.ShapeDtypeStruct((groups, batch, span, 2 * HEADS), f32),
            jax.ShapeDtypeStruct((batch, span, n), f32),
            jax.ShapeDtypeStruct((batch, span, n), f32),
            jax.ShapeDtypeStruct((1, inner), f32),
            jax.ShapeDtypeStruct((1, inner), f32),
        ]
        + [jax.ShapeDtypeStruct(s, f32) for s in shapes],
        scratch_shapes=[
            pltpu.VMEM((batch, span, span), f32),
            pltpu.VMEM((batch, span, span), f32),
            pltpu.VMEM((batch, span, n), f32),
            pltpu.VMEM((blocks, span, cb_w), bf16),
            pltpu.VMEM((blocks, span, HEADS), f32),
            pltpu.VMEM((blocks, n, cb_w), f32),
            pltpu.VMEM((blocks, 1, cb_w), f32),
        ]
        + Chain.scratch(blocks, n, cb_w)
        + sum([Scatter.scratch(s[0], s[1], sp) for s, sp in zip(shapes, splits)], []),
        compiler_params=pltpu.CompilerParams(
            collective_id=collective_id, has_side_effects=True, vmem_limit_bytes=60 * 1024 * 1024
        ),
    )(mg, w_out, y, gate, norms, gain, v, keys, colpack, rowpack, carried, skip, *bigs)


def conv_back(dv, a, cw, cb, span, padded, out_ref, b):
    taps = cw.shape[0]
    first = HALO - (taps - 1)
    pre = conv_pre(a, cw, cb, span)
    _, sg = silu_parts(pre)
    pg = dv * (sg * (1.0 + pre * (1.0 - sg)))
    padded[16 : 16 + span] = pg
    ext = span + HALO
    total = jnp.zeros((ext, cw.shape[1]), f32)
    for k in range(taps):
        total = total + cw[k : k + 1] * padded[taps - 1 - k : taps - 1 - k + ext]
    out_ref[b] = total.astype(bf16)
    dcw = jnp.concatenate(
        [jnp.sum(pg * a[first + k : first + k + span], axis=0, keepdims=True) for k in range(taps)], axis=0
    )
    return dcw, jnp.sum(pg, axis=0, keepdims=True)


def back_kernel(span, hw, groups, splits, *refs):
    count = len(splits)
    (later_ref, h_ref, keys_ref, v_ref, dv_ref, col_ref, cin_ref, cw_ref, cb_ref) = refs[:9]
    bigs = refs[9 : 9 + count]
    cig_ref, cols_ref, dk_ref, dcw_ref, dcb_ref, dlast_ref = refs[9 + count : 15 + count]
    outs = refs[15 + count : 15 + 2 * count]
    rest = refs[15 + 2 * count :]
    padded, dkacc = rest[:2]
    i = pl.program_id(0)
    batch = dk_ref.shape[0]
    n = keys_ref.shape[2] // 2

    @pl.when(i == 0)
    def _():
        if count:
            Place().greet()
        padded[0:16] = jnp.zeros((16, padded.shape[1]), f32)
        padded[16 + span :] = jnp.zeros((padded.shape[0] - 16 - span, padded.shape[1]), f32)

    hook = scatter_beside(i, batch, groups * batch, back_start, splits, bigs, outs, rest[2:])
    for b in range(batch):
        hook(b)
        cols = col_ref[0, b]
        c, step = cols[:, :HEADS], cols[:, HEADS:]
        low = later_ref[b]
        left = spread(jnp.exp2(c[span - 1 : span] - c), hw)
        kdh = mm(keys_ref[b, :, :n], low) * left
        v = v_ref[b].astype(f32)
        step_wide = spread(step, hw)
        cols_ref[0, b] = gather_heads(v * kdh, hw)
        dlast_ref[b] = jnp.broadcast_to(
            jnp.sum(low.astype(f32) * h_ref[b].astype(f32), axis=0, keepdims=True), dlast_ref.shape[1:]
        )
        vw = (v * step_wide * left).astype(bf16)
        part = mm_nt(vw, low)

        @pl.when(i == 0)
        def _():
            dkacc[b] = part

        @pl.when(i != 0)
        def _():
            dkacc[b] += part

        @pl.when(i == groups - 1)
        def _():
            dk_ref[b] = dkacc[b]

        dv = dv_ref[b].astype(f32) + kdh * step_wide
        dcw, dcb = conv_back(dv, cin_ref[b].astype(f32), cw_ref[...], cb_ref[...], span, padded, cig_ref, b)
        if b == 0:
            dcw_ref[...] = dcw
            dcb_ref[...] = dcb
        else:
            dcw_ref[...] += dcw
            dcb_ref[...] += dcb


def back(later, carried, keys, v, dv, colpack, cin, cw, cb, bigs, splits, hw, span, collective_id):
    batch = v.shape[0]
    groups = colpack.shape[0]
    cb_w = HEADS * hw
    inner = groups * cb_w
    n = keys.shape[2] // 2
    ext = span + HALO
    taps = cw.shape[0]
    block = lambda rows: pl.BlockSpec((batch, rows, cb_w), lambda i: (0, 0, i))
    lanes = lambda rows: pl.BlockSpec((rows, cb_w), lambda i: (0, i))
    hbm = pl.BlockSpec(memory_space=pl.ANY)
    shapes = [(x.shape[0] // 32, x.shape[1]) for x in bigs]
    return pl.pallas_call(
        functools.partial(back_kernel, span, hw, groups, splits),
        grid=(groups,),
        in_specs=[
            block(n),
            block(n),
            pl.BlockSpec(keys.shape, lambda i: (0, 0, 0)),
            block(span),
            block(span),
            pl.BlockSpec((1,) + colpack.shape[1:], lambda i: (i, 0, 0, 0)),
            block(ext),
            lanes(taps),
            lanes(1),
        ]
        + [hbm] * len(bigs),
        out_specs=[
            block(ext),
            pl.BlockSpec((1, batch, span, HEADS), lambda i: (i, 0, 0, 0)),
            pl.BlockSpec((batch, span, n), lambda i: (0, 0, 0)),
            lanes(taps),
            lanes(1),
            block(8),
        ]
        + [pl.BlockSpec(s, lambda i: (0, 0)) for s in shapes],
        out_shape=[
            jax.ShapeDtypeStruct((batch, ext, inner), bf16),
            jax.ShapeDtypeStruct((groups, batch, span, HEADS), f32),
            jax.ShapeDtypeStruct((batch, span, n), f32),
            jax.ShapeDtypeStruct((taps, inner), f32),
            jax.ShapeDtypeStruct((1, inner), f32),
            jax.ShapeDtypeStruct((batch, 8, inner), f32),
        ]
        + [jax.ShapeDtypeStruct(s, f32) for s in shapes],
        scratch_shapes=[
            pltpu.VMEM((span + 32, cb_w), f32),
            pltpu.VMEM((batch, span, n), f32),
        ]
        + sum([Scatter.scratch(s[0], s[1], sp) for s, sp in zip(shapes, splits)], []),
        compiler_params=pltpu.CompilerParams(
            collective_id=collective_id if bigs else None,
            has_side_effects=bool(bigs),
            vmem_limit_bytes=58 * 1024 * 1024,
        ),
    )(later, carried, keys, v, dv, colpack, cin, cw, cb, *bigs)


def keys_back_kernel(span, dk_ref, dk2_ref, dq_ref, cin_ref, cw_ref, cb_ref, cig_ref, dcw_ref, dcb_ref, padded):
    batch = dk_ref.shape[0]
    padded[...] = jnp.zeros_like(padded)
    for b in range(batch):
        dv = jnp.concatenate([dk_ref[b] + dk2_ref[b], dq_ref[b]], axis=1)
        dcw, dcb = conv_back(dv, cin_ref[b].astype(f32), cw_ref[...], cb_ref[...], span, padded, cig_ref, b)
        if b == 0:
            dcw_ref[...] = dcw
            dcb_ref[...] = dcb
        else:
            dcw_ref[...] += dcw
            dcb_ref[...] += dcb


def keys_backward(dk, dk2, dq, cin, cw, cb, span):
    batch, ext, width = cin.shape
    return pl.pallas_call(
        functools.partial(keys_back_kernel, span),
        in_specs=[pl.BlockSpec(memory_space=pltpu.VMEM)] * 6,
        out_specs=[pl.BlockSpec(memory_space=pltpu.VMEM)] * 3,
        out_shape=[
            jax.ShapeDtypeStruct(cin.shape, bf16),
            jax.ShapeDtypeStruct(cw.shape, f32),
            jax.ShapeDtypeStruct(cb.shape, f32),
        ],
        scratch_shapes=[pltpu.VMEM((span + 32, width), f32)],
        compiler_params=params_of(40),
    )(dk, dk2, dq, cin, cw, cb)


def own_kernels():
    return lax.axis_size("dp") == 4 and lax.axis_size("seq") == 8


def gather_rows(shards, parts, splits, collective_id):
    if own_kernels():
        return gather(shards, parts, splits, collective_id)
    return [
        lax.all_gather(s[:, p[0] : p[0] + p[1]], ("dp", "seq"), axis=0, tiled=True)
        for s, p in zip(shards, parts)
    ]


def scatter_rows(bigs, splits, small, collective_id):
    if own_kernels():
        return scatter(bigs, splits, small, collective_id)
    outs = [lax.psum_scatter(b, ("dp", "seq"), scatter_dimension=0, tiled=True).astype(f32) for b in bigs]
    return outs + ([] if small is None else [lax.psum(small, ("dp", "seq"))])


def half_of(width):
    return (width // 2 + 127) // 128 * 128


def ungrouped(cols):
    groups, batch, span, each = cols.shape
    return jnp.transpose(cols, (1, 2, 0, 3)).reshape(batch, span, groups * each)


FRONT_HOOKS = (0, 6, 7, 13, 14, 20, 22, 24, 31, 33, 35, 35, 35)


def gate_start(k, blocks):
    return 1.0 * k if k < blocks else 1.0 * blocks + 1.6 * (k - blocks)


def back_start(k):
    return 2.9 * k


def on_device(
    resid_in, out_grad, lengths, norm_gain, in_proj, dt_proj, conv_weight, conv_bias, dt_bias, a_log,
    skip_scale, gate_gain, out_proj,
):
    batch, span, width = resid_in.shape
    inner = gate_gain.shape[0]
    heads = a_log.shape[0]
    hw = inner // heads
    n = (in_proj.shape[1] - 2 * inner) // 2
    cb_w = HEADS * hw
    positions = lax.axis_index("seq") * span + lax.iota(jnp.int32, span)
    mask = (positions[None, :] < lengths[:, None]).astype(f32)[..., None]

    conv_cols = in_proj.shape[1] - inner
    dt_pad = (-(conv_cols + heads)) % 128
    conv_all = conv_cols + heads + dt_pad
    dt_shard = jnp.pad(dt_proj, ((0, 0), (0, dt_pad)))
    later_shards, later_parts = [in_proj, out_proj], [(0, inner), (0, width)]
    later_splits = [half_of(inner), half_of(width)]
    full_conv, full_dt = gather_rows(
        [in_proj, dt_shard], [(inner, conv_cols), (0, heads + dt_pad)], [half_of(conv_cols), heads + dt_pad], 3
    )

    halo = shifted(resid_in[:, span - HALO :], "seq", 1)
    resid_ext = jnp.concatenate([halo, resid_in], axis=1).astype(f32)
    rs_ext = lax.rsqrt(jnp.mean(resid_ext * resid_ext, axis=-1, keepdims=True) + epsilon)
    x_ext = (resid_ext * rs_ext * norm_gain).astype(bf16)
    ext = span + HALO
    x2 = x_ext.reshape(batch * ext, width)
    resid_wide = resid_in.astype(f32)
    rs = rs_ext[:, HALO:]

    rate = -jnp.exp(a_log)
    lane_pad = (0, (-heads) % 128)
    skip_wide = jnp.repeat(skip_scale, hw)[None]
    gain_wide = gate_gain[None]
    cw_keys, cb_keys = conv_weight[:, inner:], conv_bias[None, inner:]
    cw_vals, cb_vals = conv_weight[:, :inner], conv_bias[None, :inner]
    keys, cin_keys, colpack, rowpack, raw, step = prepare(
        x2, full_conv, inner // (2 * n), full_dt, cw_keys, cb_keys,
        jnp.pad(dt_bias, lane_pad)[None], jnp.pad(rate, lane_pad)[None], batch, span, heads,
    )
    inside = own_kernels()
    made = front(
        x2, full_conv, cw_vals, cb_vals, keys, colpack, rowpack, skip_wide,
        later_shards if inside else [], later_parts, later_splits if inside else [], FRONT_HOOKS, hw, span, 1,
    )
    v, cin_vals, y, carried = made[:4]
    full_gate, full_out = made[4:] if inside else gather_rows(later_shards, later_parts, later_splits, 4)
    gate, normed_out, rg = gated_norm(x_ext, full_gate, y, gain_wide, span, cb_w)
    mixer_out = jnp.dot(normed_out, full_out, preferred_element_type=f32)
    output = (mask * (resid_wide + mixer_out)).astype(bf16)

    mixer_grad = (mask * out_grad.astype(f32)).astype(bf16)
    mean = jnp.sum(mixer_grad.astype(f32) * mixer_out, axis=-1, keepdims=True) * (1.0 / inner)
    norms = jnp.concatenate([rg[..., :1], mean, jnp.zeros((batch, span, 6), f32)], axis=-1)
    grad_out = jnp.einsum("bsi,bsd->id", normed_out, mixer_grad, preferred_element_type=f32).astype(bf16)
    made = gate_backward(
        mixer_grad, full_out, y, gate, norms, gain_wide, v, keys, colpack, rowpack, carried, skip_wide,
        [grad_out] if inside else [], later_splits[1:] if inside else [], hw, span, 7,
    )
    dgate, dv, later, cols_one, dq, dk, dgain, dskip = made[:8]
    (sum_out,) = made[8:] if inside else scatter_rows([grad_out], later_splits[1:], None, 5)
    x_rows = x_ext[:, HALO:]
    grad_gate = jnp.einsum("bsd,bse->de", x_rows, dgate, preferred_element_type=f32).astype(bf16)
    made = back(
        later, carried, keys, v, dv, colpack, cin_vals, cw_vals, cb_vals,
        [grad_gate] if inside else [], later_splits[:1] if inside else [], hw, span, 2,
    )
    cig_vals, cols_two, dk2, dcw_vals, dcb_vals, dlast = made[:6]
    (sum_gate,) = made[6:] if inside else scatter_rows([grad_gate], later_splits[:1], None, 5)
    cig_keys, dcw_keys, dcb_keys = keys_backward(dk, dk2, dq, cin_keys, cw_keys, cb_keys, span)

    raw, step = raw[..., :heads], step[..., :heads]
    rise = ungrouped(cols_one[..., :HEADS])
    direct = ungrouped(cols_one[..., HEADS:])
    ahead = ungrouped(cols_two)
    moved = ahead * step
    tri = causal(span, False).astype(f32)
    block_decay = jnp.exp2(colpack[:, :, span - 1, :HEADS]).transpose(1, 0, 2).reshape(batch, heads)
    last = jnp.sum(moved, axis=1) + dlast[:, 0].reshape(batch, heads, hw).sum(-1) * block_decay
    dlog = rise - moved
    dlog = jnp.einsum("ts,bth->bsh", tri, dlog, precision=highest) + last[:, None, :]
    grad_a = jnp.sum(dlog * step, axis=(0, 1)) * rate
    step_grad = direct + ahead + dlog * rate
    dt_grad = step_grad * jax.nn.sigmoid(raw)
    grad_bias = jnp.sum(dt_grad, axis=(0, 1))
    step_low = jnp.pad(dt_grad.astype(bf16), ((0, 0), (HALO, 0), (0, dt_pad)))

    cig = jnp.concatenate([cig_vals, cig_keys, step_low], axis=-1)
    grad_conv = jnp.einsum("bsd,bse->de", x_ext, cig, preferred_element_type=f32).astype(bf16)
    normed_ext = jnp.einsum("bse,de->bsd", cig[..., :conv_cols], full_conv, preferred_element_type=f32)
    normed_ext = normed_ext + jnp.einsum("bse,de->bsd", step_low, full_dt, preferred_element_type=f32)
    from_next = shifted(normed_ext[:, :HALO].astype(bf16), "seq", -1).astype(f32)
    normed_grad = normed_ext[:, HALO:]
    normed_grad = jnp.concatenate([normed_grad[:, : span - HALO], normed_grad[:, span - HALO :] + from_next], axis=1)
    normed_grad = normed_grad + jnp.einsum("bse,de->bsd", dgate, full_gate, preferred_element_type=f32)
    nz = resid_wide * rs
    fg = normed_grad * norm_gain
    grad_norm = jnp.sum(normed_grad * nz, axis=(0, 1))
    input_grad = mixer_grad.astype(f32) + rs * (fg - nz * jnp.mean(fg * nz, axis=-1, keepdims=True))

    pieces = (
        grad_norm,
        jnp.concatenate([dcw_vals, dcw_keys], axis=1),
        jnp.concatenate([dcb_vals, dcb_keys], axis=1)[0],
        dgain[0],
        grad_bias,
        grad_a,
        dskip[0].reshape(heads, hw).sum(-1),
    )
    flat = jnp.concatenate([p.reshape(-1) for p in pieces])
    small = jnp.pad(flat, (0, (-flat.size) % 1024)).reshape(-1, 128)
    sum_conv, small = scatter_rows([grad_conv], [half_of(conv_all)], small, 6)
    flat, sums, at = small.reshape(-1), [], 0
    for p in pieces:
        sums.append(flat[at : at + p.size].reshape(p.shape))
        at += p.size
    sum_norm, sum_cw, sum_cb, sum_gain, sum_bias, sum_a, sum_skip = sums
    return (
        output,
        input_grad.astype(bf16),
        jnp.concatenate([sum_gate, sum_conv[:, :conv_cols]], axis=1),
        sum_conv[:, conv_cols : conv_cols + heads],
        sum_out,
        sum_norm,
        sum_cw,
        sum_cb,
        sum_bias,
        sum_a,
        sum_skip,
        sum_gain,
    )


def solution(mesh):
    rows = P("dp", "seq", None)
    shard = P(("dp", "seq"), None)
    return jax.shard_map(
        on_device,
        mesh=mesh,
        in_specs=(rows, rows, P("dp"), P(), shard, shard, P(), P(), P(), P(), P(), P(), shard),
        out_specs=(rows, rows, shard, shard, shard, P(), P(), P(), P(), P(), P(), P()),
        check_vma=False,
    )
```

```python
import functools

import jax
import jax.numpy as jnp
from jax import lax
from jax.experimental import pallas as pl
from jax.experimental.pallas import tpu as pltpu
from jax.sharding import PartitionSpec as P

epsilon = 1e-05
highest = lax.Precision.HIGHEST
HALO = 16
HEADS = 8
LOG2E = 1.4426950408889634
f32 = jnp.float32
bf16 = jnp.bfloat16
MESH = pl.DeviceIdType.MESH


def mm(a, b):
    return lax.dot_general(a, b, (((1,), (0,)), ((), ())), preferred_element_type=f32)


def mm_nt(a, b):
    return lax.dot_general(a, b, (((1,), (1,)), ((), ())), preferred_element_type=f32)


def mm_tn(a, b):
    return lax.dot_general(a, b, (((0,), (0,)), ((), ())), preferred_element_type=f32)


def shifted(block, axis, distance):
    devices = range(lax.axis_size(axis))
    route = [(i - distance, i) for i in devices if i - distance in devices]
    return lax.ppermute(block, axis, route)


def spread(cols, width):
    rows, heads = cols.shape
    low_half = lax.broadcasted_iota(jnp.int32, (rows, 2 * width), 1) < width
    pairs = [
        jnp.where(low_half, cols[:, i : i + 1], cols[:, i + 1 : i + 2]) for i in range(0, heads, 2)
    ]
    return jnp.concatenate(pairs, axis=1)


def gather_heads(x, width):
    rows, total = x.shape
    low_half = lax.broadcasted_iota(jnp.int32, (rows, 2 * width), 1) < width
    head_lane = lax.broadcasted_iota(jnp.int32, (rows, total // width), 1)
    out = jnp.zeros((rows, total // width), f32)
    for i in range(total // (2 * width)):
        pair = x[:, i * 2 * width : (i + 1) * 2 * width]
        one = jnp.sum(jnp.where(low_half, pair, 0.0), axis=1, keepdims=True)
        two = jnp.sum(jnp.where(low_half, 0.0, pair), axis=1, keepdims=True)
        out = jnp.where(head_lane == 2 * i, one, out)
        out = jnp.where(head_lane == 2 * i + 1, two, out)
    return out


def silu_parts(v):
    sg = 1.0 / (1.0 + jnp.exp(-v))
    return v * sg, sg


def silu_slope(v):
    act, sg = silu_parts(v)
    return act, sg * (1.0 + v * (1.0 - sg))


def conv_pre(a, cw, cb, span):
    first = HALO - (cw.shape[0] - 1)
    out = cb
    for k in range(cw.shape[0]):
        out = out + cw[k : k + 1] * a[first + k : first + k + span]
    return out


def params_of(limit_mb, dims=None):
    return pltpu.CompilerParams(vmem_limit_bytes=limit_mb * 1024 * 1024, dimension_semantics=dims)


def causal(span, transposed):
    one = lax.broadcasted_iota(jnp.int32, (span, span), 0)
    two = lax.broadcasted_iota(jnp.int32, (span, span), 1)
    return (one <= two) if transposed else (one >= two)


class Place:
    def __init__(self):
        self.dp = lax.axis_index("dp")
        self.seq = lax.axis_index("seq")
        y, x = self.dp // 2, self.dp % 2
        self.z, self.core = self.seq // 2, self.seq % 2
        self.dx = 2 * y + (1 - x)
        self.dy = 2 * (1 - y) + x
        self.dxy = 2 * (1 - y) + (1 - x)
        self.to_x = (self.dx, self.seq)
        self.to_y = (self.dy, self.seq)
        self.to_core = (self.dp, 2 * self.z + 1 - self.core)
        self.to_up = (self.dp, 2 * jnp.minimum(self.z + 1, 3) + self.core)
        self.to_down = (self.dp, 2 * jnp.maximum(self.z - 1, 0) + self.core)
        self.to_across = (self.dp, 2 * jnp.where(self.z < 2, self.z + 2, self.z - 2) + self.core)
        self.has_up = self.z < 3
        self.has_down = self.z > 0

    def near(self, k):
        z = self.z
        return (z, z + 1 - 2 * (z % 2), jnp.where(z < 2, 2, 1), jnp.where(z < 2, 3, 0))[k]

    def greet(self, others=()):
        barrier = pltpu.get_barrier_semaphore()
        for device in (self.to_x, self.to_y, self.to_core) + tuple(others):
            pl.semaphore_signal(barrier, inc=1, device_id=device, device_id_type=MESH)

        @pl.when(self.has_up)
        def _():
            pl.semaphore_signal(barrier, inc=1, device_id=self.to_up, device_id_type=MESH)

        @pl.when(self.has_down)
        def _():
            pl.semaphore_signal(barrier, inc=1, device_id=self.to_down, device_id_type=MESH)

        ends = self.has_up.astype(jnp.int32) + self.has_down.astype(jnp.int32)
        pl.semaphore_wait(barrier, 3 + len(others) + ends)


GATHER_KINDS = 11


def gather_steps(place, shard, full, split, own_sem, send, recv):
    rows, width = full.shape[0] // 32, full.shape[1]
    z, core = place.z, place.core
    every, left, right = pl.ds(0, width), pl.ds(0, split), pl.ds(split, width - split)
    two = split < width

    def view(d, zz, cc, cols):
        start = pl.multiple_of((d * 8 + zz * 2 + cc) * rows, 16)
        return full.at[pl.ds(start, rows), cols]

    def copy(kind, slot, device, d, zz, cc, cols, src=None):
        dst = view(d, zz, cc, cols)
        return pltpu.make_async_remote_copy(
            src_ref=dst if src is None else src,
            dst_ref=dst,
            send_sem=send.at[kind, slot],
            recv_sem=recv.at[kind, slot],
            device_id=device,
            device_id_type=MESH,
        )

    def pieces(k):
        zk = place.near(k)
        src = shard if k == 0 else None
        dp = place.dp
        return dict(
            x=copy(2, k, place.to_x, dp, zk, core, every, src),
            y=copy(3, k, place.to_y, dp, zk, core, every, src),
            own=copy(6, k, place.to_core, dp, zk, core, every, src),
        )

    def along(k, up):
        zk = place.near(k)
        src = shard if k == 0 else None
        device = place.to_up if up else place.to_down
        dst = view(place.dp, zk, core, every)
        return pltpu.make_async_remote_copy(
            src_ref=dst if src is None else src,
            dst_ref=dst,
            send_sem=send.at[0 if up else 1, k],
            recv_sem=recv.at[0, zk],
            device_id=device,
            device_id_type=MESH,
        )

    def arrive(k):
        zk = place.near(k)
        if k > 0:
            along(k, True).wait_recv()

        @pl.when(jnp.logical_and(zk <= z, place.has_up))
        def _():
            along(k, True).start()

        @pl.when(jnp.logical_and(zk >= z, place.has_down))
        def _():
            along(k, False).start()

        made = pieces(k)
        made["x"].start()
        made["y"].start()
        made["own"].start()

    def cross(k):
        zk = place.near(k)
        return (
            copy(2, k, place.to_x, place.dx, zk, core, every),
            copy(3, k, place.to_y, place.dy, zk, core, every),
            copy(4, k, place.to_y, place.dx, zk, core, left),
            copy(5, k, place.to_x, place.dy, zk, core, right) if two else None,
            copy(7, k, place.to_core, place.dx, zk, core, every),
            copy(8, k, place.to_core, place.dy, zk, core, every),
        )

    def forward(k):
        from_x, from_y, left_on, right_on, core_x, core_y = cross(k)
        from_x.wait_recv()
        left_on.start()
        core_x.start()
        from_y.wait_recv()
        if two:
            right_on.start()
        core_y.start()

    def corner(k):
        zk = place.near(k)
        return (
            copy(4, k, place.to_y, place.dxy, zk, core, left),
            copy(5, k, place.to_x, place.dxy, zk, core, right) if two else None,
            copy(9, k, place.to_core, place.dxy, zk, core, left),
            copy(10, k, place.to_core, place.dxy, zk, core, right) if two else None,
        )

    def last(k):
        from_y, from_x, core_left, core_right = corner(k)
        from_y.wait_recv()
        core_left.start()
        if two:
            from_x.wait_recv()
            core_right.start()

    def mine():
        return pltpu.make_async_copy(shard, view(place.dp, z, core, every), own_sem)

    def begin():
        mine().start()
        arrive(0)

    def finish():
        mine().wait()
        other = 1 - core
        for k in range(4):
            zk = place.near(k)
            for kind, d, cols in (
                (6, place.dp, every), (7, place.dx, every), (8, place.dy, every),
                (9, place.dxy, left), (10, place.dxy, right),
            ):
                if kind == 10 and not two:
                    continue
                copy(kind, k, place.to_core, d, zk, other, cols).wait_recv()
        for k in range(4):
            zk = place.near(k)

            @pl.when(jnp.logical_and(zk <= z, place.has_up))
            def _():
                along(k, True).wait_send()

            @pl.when(jnp.logical_and(zk >= z, place.has_down))
            def _():
                along(k, False).wait_send()

            made = pieces(k)
            made["x"].wait_send()
            made["y"].wait_send()
            made["own"].wait_send()
            for one in cross(k)[2:] + corner(k)[2:]:
                if one is not None:
                    one.wait_send()

    return [
        begin,
        lambda: arrive(1),
        lambda: forward(0),
        lambda: arrive(2),
        lambda: forward(1),
        lambda: arrive(3),
        lambda: forward(2),
        lambda: last(0),
        lambda: forward(3),
        lambda: last(1),
        lambda: last(2),
        lambda: last(3),
        finish,
    ]


def gather_scratch():
    return [
        pltpu.SemaphoreType.DMA,
        pltpu.SemaphoreType.DMA((GATHER_KINDS, 4)),
        pltpu.SemaphoreType.DMA((GATHER_KINDS, 4)),
    ]


def part_of(ref, part):
    return ref.at[:, pl.ds(part[0], part[1])]


class Scatter:
    def __init__(self, place, big, out, own, land_core, land_xy, land_z, local, send, recv, split):
        self.place, self.big, self.out = place, big, out
        self.own, self.land_core, self.land_xy, self.land_z = own, land_core, land_xy, land_z
        self.local, self.send, self.recv = local, send, recv
        self.rows, self.width = out.shape
        self.split = split
        self.left, self.right = slice(0, split), slice(split, self.width)

    def groups(self):
        p = self.place
        return (p.dxy, p.dx, p.dy, p.dp)

    def far(self, k):
        return self.place.near(3 - k)

    def source(self, d, zz, cc):
        start = pl.multiple_of((d * 8 + zz * 2 + cc) * self.rows, 16)
        return self.big.at[pl.ds(start, self.rows)]

    def remote(self, src, dst, kind, slot, device):
        return pltpu.make_async_remote_copy(
            src_ref=src, dst_ref=dst, send_sem=self.send.at[kind, slot], recv_sem=self.recv.at[kind, slot],
            device_id=device, device_id_type=MESH,
        )

    def to_other(self, i, k):
        p = self.place
        src = self.source(self.groups()[i], self.far(k), 1 - p.core)
        return self.remote(src, self.land_core.at[i, k], i, k, p.to_core)

    def load(self, i, k):
        p = self.place
        return pltpu.make_async_copy(
            self.source(self.groups()[i], self.far(k), p.core), self.own.at[i, k], self.local.at[i, k]
        )

    def start(self, k):
        for i in range(4):
            self.to_other(i, k).start()
            self.load(i, k).start()

    def join(self, i, k):
        self.load(i, k).wait()
        self.to_other(i, k).wait_recv()
        self.own[i, k] = self.own[i, k] + self.land_core[i, k]

    def side(self, kind, k):
        p = self.place
        left, right = pl.ds(0, self.split), pl.ds(self.split, self.width - self.split)
        group, cols, device = (
            (0, left, p.to_y),
            (0, right, p.to_x),
            (2, left, p.to_y),
            (1, right, p.to_x),
            (2, right, p.to_y),
            (1, left, p.to_x),
        )[kind]
        size = self.split if cols is left else self.width - self.split
        return self.remote(
            self.own.at[group, k, :, cols], self.land_xy.at[kind, k, :, pl.ds(0, size)], 4 + kind, k, device
        )

    def take(self, kind, group, cols, k):
        self.side(kind, k).wait_recv()
        size = cols.stop - cols.start
        self.own[group, k, :, cols] = self.own[group, k, :, cols] + self.land_xy[kind, k, :, 0:size]

    def corner(self, k):
        self.join(0, k)
        self.side(0, k).start()
        self.side(1, k).start()

    def sides(self, k):
        self.join(1, k)
        self.side(3, k).start()
        self.join(2, k)
        self.side(2, k).start()

    def turns(self, k):
        self.take(0, 1, self.left, k)
        self.side(5, k).start()
        self.take(1, 2, self.right, k)
        self.side(4, k).start()

    def along(self, k, up):
        p = self.place
        zk = self.far(k)
        return pltpu.make_async_remote_copy(
            src_ref=self.own.at[3, k],
            dst_ref=self.land_z.at[0 if up else 1, zk],
            send_sem=self.send.at[10, k],
            recv_sem=self.recv.at[10 if up else 11, zk],
            device_id=p.to_up if up else p.to_down,
            device_id_type=MESH,
        )

    def rising(self, k):
        return self.far(k) > self.place.z

    def behind(self, k):
        p = self.place
        rising = self.rising(k)
        return jnp.logical_or(
            jnp.logical_and(rising, p.has_down), jnp.logical_and(jnp.logical_not(rising), p.has_up)
        )

    def send_along(self, k):
        @pl.when(self.rising(k))
        def _():
            self.along(k, True).start()

        @pl.when(jnp.logical_not(self.rising(k)))
        def _():
            self.along(k, False).start()

    def mine(self, k):
        self.join(3, k)
        self.take(2, 3, self.left, k)
        self.take(3, 3, self.right, k)
        self.take(5, 3, self.left, k)
        self.take(4, 3, self.right, k)
        if k < 3:

            @pl.when(jnp.logical_not(self.behind(k)))
            def _():
                self.send_along(k)

    def line(self, k):
        zk = self.far(k)

        @pl.when(jnp.logical_and(self.behind(k), self.rising(k)))
        def _():
            self.along(k, True).wait_recv()
            self.own[3, k] = self.own[3, k] + self.land_z[0, zk]

        @pl.when(jnp.logical_and(self.behind(k), jnp.logical_not(self.rising(k))))
        def _():
            self.along(k, False).wait_recv()
            self.own[3, k] = self.own[3, k] + self.land_z[1, zk]

        @pl.when(self.behind(k))
        def _():
            self.send_along(k)

    def result(self):
        p = self.place
        self.out[...] = self.own[3, 3].astype(f32)

        @pl.when(p.has_down)
        def _():
            self.along(3, True).wait_recv()
            self.out[...] += self.land_z[0, p.z].astype(f32)

        @pl.when(p.has_up)
        def _():
            self.along(3, False).wait_recv()
            self.out[...] += self.land_z[1, p.z].astype(f32)

    def drain(self):
        for k in range(4):
            for i in range(4):
                self.to_other(i, k).wait_send()
            for kind in range(6):
                self.side(kind, k).wait_send()
            if k < 3:
                self.along(k, True).wait_send()

    def steps(self):
        start, corner, sides, turns, mine, line = (
            self.start, self.corner, self.sides, self.turns, self.mine, self.line
        )
        return [
            (0, lambda: start(0)),
            (2, lambda: start(1)),
            (3, lambda: corner(0)),
            (4, lambda: sides(0)),
            (6, lambda: start(2)),
            (8, lambda: turns(0)),
            (9, lambda: corner(1)),
            (10, lambda: sides(1)),
            (12, lambda: start(3)),
            (14, lambda: mine(0)),
            (17, lambda: turns(1)),
            (18, lambda: corner(2)),
            (19, lambda: sides(2)),
            (22, lambda: line(0)),
            (23, lambda: mine(1)),
            (26, lambda: turns(2)),
            (27, lambda: corner(3)),
            (28, lambda: sides(3)),
            (31, lambda: line(1)),
            (32, lambda: mine(2)),
            (35, lambda: turns(3)),
            (40, lambda: line(2)),
            (42, lambda: mine(3)),
            (47, self.result),
            (50, self.drain),
        ]

    @staticmethod
    def scratch(rows, width, split):
        half = max(split, width - split)
        return [
            pltpu.VMEM((4, 4, rows, width), bf16),
            pltpu.VMEM((4, 4, rows, width), bf16),
            pltpu.VMEM((6, 4, rows, half), bf16),
            pltpu.VMEM((2, 4, rows, width), bf16),
            pltpu.SemaphoreType.DMA((4, 4)),
            pltpu.SemaphoreType.DMA((11, 4)),
            pltpu.SemaphoreType.DMA((12, 4)),
        ]


class Small:
    def __init__(self, place, value, out, sent, landed, send, recv):
        p = place
        self.value, self.out, self.sent, self.landed, self.send, self.recv = value, out, sent, landed, send, recv
        pair = 2 * (p.z + 1 - 2 * (p.z % 2)) + p.core
        self.devices = (p.to_core, p.to_x, p.to_y, (p.dp, pair), p.to_across)

    def copy(self, i):
        return pltpu.make_async_remote_copy(
            src_ref=self.sent.at[i], dst_ref=self.landed.at[i], send_sem=self.send.at[i],
            recv_sem=self.recv.at[i], device_id=self.devices[i], device_id_type=MESH,
        )

    def go(self, i):
        if i == 0:
            self.sent[0] = self.value[...]
            self.copy(0).start()
            return
        self.copy(i - 1).wait_recv()
        total = self.sent[i - 1] + self.landed[i - 1]
        if i < 5:
            self.sent[i] = total
            self.copy(i).start()
        else:
            self.out[...] = total
            for k in range(5):
                self.copy(k).wait_send()

    @staticmethod
    def scratch(shape):
        return [
            pltpu.VMEM((5,) + shape, f32),
            pltpu.VMEM((5,) + shape, f32),
            pltpu.SemaphoreType.DMA((5,)),
            pltpu.SemaphoreType.DMA((5,)),
        ]


def scatter_kernel(splits, with_small, *refs):
    count = len(splits)
    ins = count + (1 if with_small else 0)
    bigs, outs = refs[:count], refs[ins : ins + count]
    scratch = refs[2 * ins :]
    place = Place()
    place.greet((place.to_across,) if with_small else ())
    plans = [
        Scatter(place, bigs[i], outs[i], *scratch[7 * i : 7 * i + 7], splits[i]) for i in range(count)
    ]
    small = None
    if with_small:
        small = Small(place, refs[count], refs[ins + count], *scratch[7 * count :])
    small_at = {0: 0, 5: 1, 9: 2, 13: 3, 17: 4, 21: 5}
    for i, steps in enumerate(zip(*[plan.steps() for plan in plans])):
        for _, step in steps:
            step()
        if small and i in small_at:
            small.go(small_at[i])


def scatter(bigs, splits, small, collective_id):
    count = len(bigs)
    spec = pl.BlockSpec(memory_space=pl.ANY)
    vmem = pl.BlockSpec(memory_space=pltpu.VMEM)
    shapes = [(b.shape[0] // 32, b.shape[1]) for b in bigs]
    extra = [] if small is None else [small]
    scratch = sum([Scatter.scratch(s[0], s[1], sp) for s, sp in zip(shapes, splits)], [])
    if small is not None:
        scratch = scratch + Small.scratch(small.shape)
    return pl.pallas_call(
        functools.partial(scatter_kernel, splits, small is not None),
        in_specs=[spec] * count + [vmem] * len(extra),
        out_specs=[vmem] * (count + len(extra)),
        out_shape=[jax.ShapeDtypeStruct(s, f32) for s in shapes]
        + [jax.ShapeDtypeStruct(e.shape, f32) for e in extra],
        scratch_shapes=scratch,
        compiler_params=pltpu.CompilerParams(
            collective_id=collective_id, has_side_effects=True, vmem_limit_bytes=60 * 1024 * 1024
        ),
    )(*bigs, *extra)


class Chain:
    def __init__(self, backward, sent, landed, send, recv):
        self.sent, self.landed, self.send, self.recv = sent, landed, send, recv
        me, count = lax.axis_index("seq"), lax.axis_size("seq")
        turn = -1 if backward else 1
        self.place = count - 1 - me if backward else me
        self.has_prev = self.place > 0
        self.has_next = self.place < count - 1
        self.next = (lax.axis_index("dp"), jnp.clip(me + turn, 0, count - 1))
        self.prev = (lax.axis_index("dp"), jnp.clip(me - turn, 0, count - 1))

    def copy(self, k):
        return pltpu.make_async_remote_copy(
            src_ref=self.sent.at[k], dst_ref=self.landed.at[k], send_sem=self.send.at[k],
            recv_sem=self.recv.at[k], device_id=self.next, device_id_type=MESH,
        )

    def pass_on(self, k, decay, local):
        @pl.when(self.has_prev)
        def _():
            self.copy(k).wait_recv()

        @pl.when(jnp.logical_not(self.has_prev))
        def _():
            self.landed[k] = jnp.zeros_like(self.landed[k])

        @pl.when(self.has_next)
        def _():
            self.sent[k] = (decay() * self.landed[k].astype(f32) + local()).astype(bf16)
            self.copy(k).start()

    def drain(self):
        @pl.when(self.has_next)
        def _():
            for k in range(self.sent.shape[0]):
                self.copy(k).wait_send()

    @staticmethod
    def scratch(count, n, size):
        return [
            pltpu.VMEM((count, n, size), bf16),
            pltpu.VMEM((count, n, size), bf16),
            pltpu.SemaphoreType.DMA((count,)),
            pltpu.SemaphoreType.DMA((count,)),
        ]


def greet_all(place, chain, others=()):
    barrier = pltpu.get_barrier_semaphore()
    flags = [chain.has_prev, chain.has_next]
    devices = [chain.prev, chain.next]
    total = chain.has_prev.astype(jnp.int32) + chain.has_next.astype(jnp.int32)
    if place is not None:
        flags += [place.has_up, place.has_down]
        devices += [place.to_up, place.to_down]
        total = total + place.has_up.astype(jnp.int32) + place.has_down.astype(jnp.int32) + 3 + len(others)
        for device in (place.to_x, place.to_y, place.to_core) + tuple(others):
            pl.semaphore_signal(barrier, inc=1, device_id=device, device_id_type=MESH)
    for flag, device in zip(flags, devices):

        @pl.when(flag)
        def _(device=device):
            pl.semaphore_signal(barrier, inc=1, device_id=device, device_id_type=MESH)

    pl.semaphore_wait(barrier, total)


def front_time(slot):
    if slot < 18:
        return 60 + 1.4 * slot
    if slot < 36:
        return 85 + 1.4 * (slot - 18)
    return 110 + 0.95 * (slot - 36)


GATHER_TIMES = (0, 7, 13, 20, 24, 32, 38, 40, 50, 54, 64, 70, 76)
GATHER_BEGIN = 45


def front_kernel(span, hw, heads, splits, parts, *refs):
    count = len(splits)
    (resid_ref, halo_ref, ngain_ref, cw_ref, cb_ref, bias_ref, rate_ref, skip_ref, gain_ref) = refs[:9]
    given = refs[9:13]
    x_ref, keys_ref, kslope_ref, kcin_ref, col_ref, row_ref, raw_ref, step_ref = refs[13:21]
    rows_ref, slope_ref, cin_ref, y_ref, carried_ref, gate_ref, no_ref, rg_ref = refs[21:29]
    fulls = refs[29 : 29 + count] if count else given
    rest = refs[29 + count :]
    values, local, scores, decays, gated, squares, wbuf, wkeys, wdt, wsem, ksem = rest[:11]
    chain = Chain(False, *rest[11:15])
    batch, _, width = resid_ref.shape
    ext = span + HALO
    groups = heads // HEADS
    cb_w = HEADS * hw
    inner = groups * cb_w
    n = keys_ref.shape[2] // 2
    i = pl.program_id(0)
    place = Place() if count else None
    plans = [
        gather_steps(place, part_of(given[j], parts[j]), fulls[j], splits[j], *rest[15 + 3 * j : 18 + 3 * j])
        for j in range(count)
    ]
    low_half = lax.broadcasted_iota(jnp.int32, (span, 2 * hw), 1) < hw

    def weights(j, full):
        cols = pl.ds(pl.multiple_of(j * cb_w, cb_w), cb_w)
        return pltpu.make_async_copy(full.at[:, cols], wbuf.at[j % 2], wsem.at[j % 2])

    def key_weights():
        return (
            pltpu.make_async_copy(fulls[0].at[:, pl.ds(inner, 2 * n)], wkeys, ksem.at[0]),
            pltpu.make_async_copy(fulls[1], wdt, ksem.at[1]),
        )

    at = {}
    if count:
        for j, (time, steps) in enumerate(zip(GATHER_TIMES, zip(*plans[2:]))):
            if j >= 2:
                slot = min([k for k in range(54) if front_time(k) >= GATHER_BEGIN + time] + [53])
                slot = min(slot, 35)
                at.setdefault(slot, []).extend(steps)

    def hook(b):
        for slot in sorted(at):
            if slot % batch == b:

                @pl.when(i == 1 + slot // batch)
                def _(slot=slot):
                    for step in at[slot]:
                        step()

    def input_norm():
        for b in range(batch):
            for src, lo, size in ((halo_ref, 0, HALO), (resid_ref, HALO, span)):
                x = src[b].astype(f32)
                rs = lax.rsqrt(jnp.mean(x * x, axis=-1, keepdims=True) + epsilon)
                x_ref[b * ext + lo : b * ext + lo + size] = (x * rs * ngain_ref[...]).astype(bf16)

    def key_part():
        cw, cb = cw_ref[:, inner:], cb_ref[:, inner:]
        acc = mm(x_ref[...], wkeys[...])
        raw_all = mm(x_ref[...], wdt[...])
        tri = causal(span, False).astype(f32)
        for b in range(batch):
            a = acc[b * ext : (b + 1) * ext]
            row, slope = silu_slope(conv_pre(a, cw, cb, span))
            keys_ref[b] = row.astype(bf16)
            kslope_ref[b] = slope.astype(bf16)
            kcin_ref[b] = a.astype(bf16)
            raw = raw_all[b * ext + HALO : (b + 1) * ext] + bias_ref[...]
            step = jnp.maximum(raw, 0.0) + jnp.log1p(jnp.exp(-jnp.abs(raw)))
            scaled = lax.dot_general(
                tri, step * rate_ref[...], (((1,), (0,)), ((), ())), precision=highest,
                preferred_element_type=f32,
            ) * LOG2E
            raw_ref[b] = raw
            step_ref[b] = step
            turned = jnp.transpose(scaled)
            for g in range(groups):
                some = slice(g * HEADS, (g + 1) * HEADS)
                col_ref[g, b] = jnp.concatenate([scaled[:, some], step[:, some]], axis=1)
                row_ref[g, b] = turned[some]

    @pl.when(i == 0)
    def _():
        greet_all(place, chain)
        first = list(zip(*plans[:2])) if count else []
        for j, steps in enumerate(first):
            for step in steps:
                step()
            if j == 0:
                input_norm()
            if j == 8:
                for plan in plans[2:]:
                    plan[0]()
        for plan in plans[2:]:
            plan[1]()
        if not count:
            input_norm()
        for copy in key_weights():
            copy.start()
        weights(0, fulls[0]).start()
        for copy in key_weights():
            copy.wait()
        key_part()

    def values_part(g, b, acc):
        a = acc[b * ext : (b + 1) * ext]
        some = pl.ds(pl.multiple_of(g * cb_w, cb_w), cb_w)
        row, slope = silu_slope(conv_pre(a, cw_ref[:, some], cb_ref[:, some], span))
        row = row.astype(bf16)
        rows_ref[b] = row
        slope_ref[b] = slope.astype(bf16)
        values[g * batch + b] = row
        cin_ref[b] = a.astype(bf16)
        cols = col_ref[g, b]
        c, step = cols[:, :HEADS], cols[:, HEADS:]
        weight = jnp.exp2(c[span - 1 : span] - c) * step
        vw = (row.astype(f32) * spread(weight, hw)).astype(bf16)
        local[g * batch + b] = mm_tn(keys_ref[b, :, :n], vw)
        decays[g * batch + b] = spread(jnp.exp2(c[span - 1 : span]), hw)

    def rows_part(g, b):
        k_in, k_out = keys_ref[b, :, :n], keys_ref[b, :, n:]

        @pl.when(g == 0)
        def _():
            scores[b] = jnp.where(causal(span, False), mm_nt(k_out, k_in), 0.0)

        cols = col_ref[g, b]
        c, step = cols[:, :HEADS], cols[:, HEADS:]
        v = values[g * batch + b].astype(f32)
        vs = (v * spread(step, hw)).astype(bf16)
        s = scores[b]
        rows = row_ref[g, b]
        sums = []
        for p in range(HEADS // 2):
            pair = vs[:, p * 2 * hw : (p + 1) * 2 * hw]
            total = None
            for q in range(2):
                h = 2 * p + q
                gap = jnp.minimum(c[:, h : h + 1] - rows[h : h + 1, :], 0.0)
                u = (jnp.exp2(gap) * s).astype(bf16)
                keep = low_half if q == 0 else jnp.logical_not(low_half)
                term = mm(u, jnp.where(keep, pair, jnp.zeros_like(pair)))
                total = term if total is None else total + term
            sums.append(total)
        inside = jnp.concatenate(sums, axis=1)
        came = chain.landed[g * batch + b]
        carried_ref[b] = came
        skip = skip_ref[:, pl.ds(pl.multiple_of(g * cb_w, cb_w), cb_w)]
        y = inside + mm(k_out, came) * spread(jnp.exp2(c), hw) + skip * v
        y_ref[b] = y
        gated[g * batch + b] = y

    def gate_part(g, b, w):
        gate = mm(x_ref[b * ext + HALO : (b + 1) * ext], w)
        gate_ref[b] = gate.astype(bf16)
        act, _ = silu_parts(gate)
        gr = gated[g * batch + b] * act
        gated[g * batch + b] = gr
        total = sum([gr[:, j * 128 : (j + 1) * 128] * gr[:, j * 128 : (j + 1) * 128] for j in range(cb_w // 128)])
        squares[b] = jnp.where(g == 0, 0.0, squares[b]) + total

    @pl.when(jnp.logical_and(i > 0, i <= groups))
    def _():
        g = i - 1
        weights(g, fulls[0]).wait()

        @pl.when(g < groups - 1)
        def _():
            weights(g + 1, fulls[0]).start()

        acc = mm(x_ref[...], wbuf[g % 2])
        for b in range(batch):
            hook(b)
            values_part(g, b, acc)

    @pl.when(jnp.logical_and(i > groups, i <= 2 * groups))
    def _():
        for b in range(batch):
            hook(b)
            rows_part(i - 1 - groups, b)

    @pl.when(i > 2 * groups)
    def _():
        g = i - 1 - 2 * groups

        @pl.when(g == 0)
        def _():
            weights(0, fulls[2]).start()

        weights(g, fulls[2]).wait()

        @pl.when(g < groups - 1)
        def _():
            weights(g + 1, fulls[2]).start()

        for b in range(batch):
            hook(b)
            gate_part(g, b, wbuf[g % 2])

    def ready(j):
        for b in range(batch):
            k = j * batch + b
            chain.pass_on(k, lambda: decays[k], lambda: local[k])

    early = i - 1 - chain.place

    @pl.when(jnp.logical_and(jnp.logical_and(early >= 0, early < groups), i - 1 <= groups - 1 + early))
    def _():
        ready(early)

    late = i - groups

    @pl.when(jnp.logical_and(jnp.logical_and(late >= 0, late < groups), chain.place > groups - 1))
    def _():
        ready(late)

    @pl.when(i == 3 * groups)
    def _():
        for b in range(batch):
            total = jnp.sum(squares[b], axis=1, keepdims=True)
            rg = lax.rsqrt(total * (1.0 / inner) + epsilon)
            rg_ref[b] = jnp.broadcast_to(rg, rg_ref.shape[1:])
            for g in range(groups):
                part = slice(g * cb_w, (g + 1) * cb_w)
                no_ref[b, :, part] = (gated[g * batch + b] * rg * gain_ref[:, part]).astype(bf16)
        chain.drain()


def front(resid, halo, norm_gain, cw, cb, bias, rate, skip, gain, shards, parts, splits, hw, heads, n, collective_id):
    batch, span, width = resid.shape
    ext = span + HALO
    groups = heads // HEADS
    cb_w = HEADS * hw
    inner = groups * cb_w
    blocks = groups * batch
    lanes = bias.shape[1]
    hbm = pl.BlockSpec(memory_space=pl.ANY)
    count = len(splits)
    clip = lambda k: jnp.clip(k, 0, groups - 1)
    first = lambda i: clip(i - 1)
    then = lambda i: clip(i - 1 - groups)
    last = lambda i: clip(i - 1 - 2 * groups)
    once = lambda shape: pl.BlockSpec(shape, lambda i: (0,) * len(shape), pipeline_mode=pl.Buffered(1))
    block = lambda f, rows: pl.BlockSpec((batch, rows, cb_w), lambda i: (0, 0, f(i)))
    shaped = lambda shape, dtype: (once(shape), jax.ShapeDtypeStruct(shape, dtype))
    columns = lambda f, rows, dtype: (block(f, rows), jax.ShapeDtypeStruct((batch, rows, inner), dtype))
    outs = [
        shaped((batch * ext, width), bf16),
        shaped((batch, span, 2 * n), bf16),
        shaped((batch, span, 2 * n), bf16),
        shaped((batch, ext, 2 * n), bf16),
        shaped((groups, batch, span, 2 * HEADS), f32),
        shaped((groups, batch, HEADS, span), f32),
        shaped((batch, span, lanes), f32),
        shaped((batch, span, lanes), f32),
        columns(first, span, bf16),
        columns(first, span, bf16),
        columns(first, ext, bf16),
        columns(then, span, f32),
        columns(then, n, bf16),
        columns(last, span, bf16),
        shaped((batch, span, inner), bf16),
        shaped((batch, span, 8), f32),
    ]
    if count:
        outs += [
            (hbm, jax.ShapeDtypeStruct((s.shape[0] * 32, p[1]), s.dtype)) for s, p in zip(shards, parts)
        ]
    small_ins = [resid, halo, norm_gain, cw, cb, bias, rate, skip, gain]
    return pl.pallas_call(
        functools.partial(front_kernel, span, hw, heads, splits, parts),
        grid=(1 + 3 * groups,),
        in_specs=[once(x.shape) for x in small_ins] + [hbm] * 4,
        out_specs=[o[0] for o in outs],
        out_shape=[o[1] for o in outs],
        scratch_shapes=[
            pltpu.VMEM((blocks, span, cb_w), bf16),
            pltpu.VMEM((blocks, n, cb_w), f32),
            pltpu.VMEM((batch, span, span), f32),
            pltpu.VMEM((blocks, 1, cb_w), f32),
            pltpu.VMEM((blocks, span, cb_w), f32),
            pltpu.VMEM((batch, span, 128), f32),
            pltpu.VMEM((2, width, cb_w), bf16),
            pltpu.VMEM((width, 2 * n), bf16),
            pltpu.VMEM((width, lanes), bf16),
            pltpu.SemaphoreType.DMA((2,)),
            pltpu.SemaphoreType.DMA((2,)),
        ]
        + Chain.scratch(blocks, n, cb_w)
        + gather_scratch() * count,
        compiler_params=pltpu.CompilerParams(
            collective_id=collective_id, has_side_effects=True, vmem_limit_bytes=62 * 1024 * 1024
        ),
    )(*small_ins, *shards)


def scatter_beside(i, batch, slots, starts, splits, bigs, outs, scratch):
    if not splits:
        return lambda b: None
    place = Place()
    plans = [
        Scatter(place, bigs[j], outs[j], *scratch[7 * j : 7 * j + 7], splits[j]).steps()
        for j in range(len(splits))
    ]
    at = {}
    for steps in zip(*plans):
        for time, step in steps:
            slot = min([k for k in range(slots) if starts(k) >= time] + [slots - 1])
            at.setdefault(slot, []).append(step)

    def run(b):
        for slot, steps in at.items():
            if slot % batch == b:

                @pl.when(i == slot // batch)
                def _(steps=steps):
                    for step in steps:
                        step()

    return run


def gate_back_kernel(span, hw, groups, splits, *refs):
    count = len(splits)
    (mg_ref, w_ref, y_ref, gate_ref, norm_ref, gain_ref, v_ref, keys_ref, col_ref, row_ref) = refs[:10]
    h_ref, skip_ref = refs[10:12]
    bigs = refs[12 : 12 + count]
    (dgate_ref, dv_ref, later_ref, cols_ref, dq_ref, dk_ref, dgain_ref, dskip_ref) = refs[12 + count : 20 + count]
    outs = refs[20 + count : 20 + 2 * count]
    rest = refs[20 + 2 * count :]
    scores, dscores, dqacc, gbs, rises, local, decays = rest[:7]
    chain = Chain(True, *rest[7:11])
    batch = mg_ref.shape[0]
    blocks = groups * batch
    i = pl.program_id(0)
    g = i % groups
    n = keys_ref.shape[2] // 2
    skip = skip_ref[...]
    low_half = lax.broadcasted_iota(jnp.int32, (span, 2 * hw), 1) < hw

    @pl.when(i == 0)
    def _():
        greet_all(Place() if count else None, chain)

    hook = scatter_beside(i, batch, 2 * blocks, lambda k: gate_start(k, blocks), splits, bigs, outs, rest[11:])

    def gate_part(b):
        at = g * batch + b
        cols = col_ref[0, b]
        c = cols[:, :HEADS]
        no_grad = mm_nt(mg_ref[b], w_ref[...])
        gate = gate_ref[b].astype(f32)
        y = y_ref[b]
        rg = norm_ref[b][:, 0:1]
        mean = norm_ref[b][:, 1:2]
        act, sg = silu_parts(gate)
        gn = y * act * rg
        dgain = jnp.sum(no_grad * gn, axis=0, keepdims=True)
        dg = rg * (no_grad * gain_ref[...] - gn * mean)
        dgate_ref[b] = (dg * y * (sg * (1.0 + gate * (1.0 - sg)))).astype(bf16)
        gb = (dg * act).astype(bf16)
        gbs[at] = gb
        gf = gb.astype(f32)
        v = v_ref[b].astype(f32)
        dskip = jnp.sum(gf * v, axis=0, keepdims=True)
        rises[at] = gather_heads(gf * (y - skip * v), hw)
        ge = (gf * spread(jnp.exp2(c), hw)).astype(bf16)
        local[at] = mm_tn(keys_ref[b, :, n:], ge)
        decays[at] = spread(jnp.exp2(c[span - 1 : span]), hw)
        part = mm_nt(ge, h_ref[b])

        @pl.when(g == 0)
        def _():
            dqacc[b] = part

        @pl.when(g != 0)
        def _():
            dqacc[b] += part

        if b == 0:
            dgain_ref[...] = dgain
            dskip_ref[...] = dskip
        else:
            dgain_ref[...] += dgain
            dskip_ref[...] += dskip

    def block_part(b):
        at = g * batch + b
        cols = col_ref[0, b]
        c, step = cols[:, :HEADS], cols[:, HEADS:]
        k_in, k_out = keys_ref[b, :, :n], keys_ref[b, :, n:]

        @pl.when(g == 0)
        def _():
            scores[b] = jnp.where(causal(span, True), mm_nt(k_in, k_out), 0.0)
            dscores[b] = jnp.zeros_like(dscores[b])

        later_ref[b] = chain.landed[at]
        gb = gbs[at]
        gf = gb.astype(f32)
        v = v_ref[b].astype(f32)
        step_wide = spread(step, hw)
        vs = (v * step_wide).astype(bf16)
        rows = row_ref[0, b]
        s = scores[b]
        parts = []
        ds = dscores[b]
        for p in range(HEADS // 2):
            lanes = slice(p * 2 * hw, (p + 1) * 2 * hw)
            total = None
            for q in range(2):
                h = 2 * p + q
                gap = jnp.minimum(rows[h : h + 1, :] - c[:, h : h + 1], 0.0)
                decay = jnp.exp2(gap)
                u = (decay * s).astype(bf16)
                keep = low_half if q == 0 else jnp.logical_not(low_half)
                half = jnp.where(keep, gb[:, lanes], jnp.zeros_like(gb[:, lanes]))
                term = mm(u, half)
                total = term if total is None else total + term
                ds = ds + decay * mm_nt(vs[:, lanes], half)
            parts.append(total)
        dscores[b] = ds
        u_all = jnp.concatenate(parts, axis=1)
        dv_ref[b] = (u_all * step_wide + skip * gf).astype(bf16)
        fall = gather_heads(vs.astype(f32) * u_all, hw)
        direct = gather_heads(v * u_all, hw)
        cols_ref[0, b] = jnp.concatenate([rises[at] - fall, direct], axis=1)

        @pl.when(g == groups - 1)
        def _():
            low = jnp.where(causal(span, True), dscores[b], 0.0).astype(bf16)
            dq_ref[b] = dqacc[b] + mm_tn(low, k_in)
            dk_ref[b] = mm(low, k_out)

    lag = jnp.minimum(3 * chain.place, blocks - 1)
    for b in range(batch):
        hook(b)

        @pl.when(i < groups)
        def _():
            gate_part(b)

        @pl.when(i >= groups)
        def _():
            block_part(b)

        k = i * batch + b - lag

        @pl.when(jnp.logical_and(k >= 0, k < blocks))
        def _():
            chain.pass_on(k, lambda: decays[k], lambda: local[k])

    @pl.when(i == 2 * groups - 1)
    def _():
        chain.drain()


def gate_backward(
    mg, w_out, y, gate, norms, gain, v, keys, colpack, rowpack, carried, skip, bigs, splits, hw, span,
    collective_id,
):
    hbm = pl.BlockSpec(memory_space=pl.ANY)
    shapes = [(x.shape[0] // 32, x.shape[1]) for x in bigs]
    batch, _, width = mg.shape
    groups = colpack.shape[0]
    cb_w = HEADS * hw
    inner = groups * cb_w
    n = keys.shape[2] // 2
    blocks = groups * batch
    first = lambda i: jnp.minimum(i, groups - 1)
    then = lambda i: jnp.maximum(i - groups, 0)
    both = lambda i: i % groups
    block = lambda f, rows: pl.BlockSpec((batch, rows, cb_w), lambda i: (0, 0, f(i)))
    lanes = lambda f: pl.BlockSpec((1, cb_w), lambda i: (0, f(i)))
    whole = lambda shape: pl.BlockSpec(shape, lambda i: (0,) * len(shape))
    return pl.pallas_call(
        functools.partial(gate_back_kernel, span, hw, groups, splits),
        grid=(2 * groups,),
        in_specs=[
            whole(mg.shape),
            pl.BlockSpec((cb_w, width), lambda i: (first(i), 0)),
            block(first, span),
            block(first, span),
            whole(norms.shape),
            lanes(first),
            block(both, span),
            whole(keys.shape),
            pl.BlockSpec((1,) + colpack.shape[1:], lambda i: (both(i), 0, 0, 0)),
            pl.BlockSpec((1,) + rowpack.shape[1:], lambda i: (then(i), 0, 0, 0)),
            block(first, n),
            lanes(both),
        ]
        + [hbm] * len(bigs),
        out_specs=[
            block(first, span),
            block(then, span),
            block(then, n),
            pl.BlockSpec((1, batch, span, 2 * HEADS), lambda i: (then(i), 0, 0, 0)),
            whole((batch, span, n)),
            whole((batch, span, n)),
            lanes(first),
            lanes(first),
        ]
        + [whole(s) for s in shapes],
        out_shape=[
            jax.ShapeDtypeStruct((batch, span, inner), bf16),
            jax.ShapeDtypeStruct((batch, span, inner), bf16),
            jax.ShapeDtypeStruct((batch, n, inner), bf16),
            jax.ShapeDtypeStruct((groups, batch, span, 2 * HEADS), f32),
            jax.ShapeDtypeStruct((batch, span, n), f32),
            jax.ShapeDtypeStruct((batch, span, n), f32),
            jax.ShapeDtypeStruct((1, inner), f32),
            jax.ShapeDtypeStruct((1, inner), f32),
        ]
        + [jax.ShapeDtypeStruct(s, f32) for s in shapes],
        scratch_shapes=[
            pltpu.VMEM((batch, span, span), f32),
            pltpu.VMEM((batch, span, span), f32),
            pltpu.VMEM((batch, span, n), f32),
            pltpu.VMEM((blocks, span, cb_w), bf16),
            pltpu.VMEM((blocks, span, HEADS), f32),
            pltpu.VMEM((blocks, n, cb_w), f32),
            pltpu.VMEM((blocks, 1, cb_w), f32),
        ]
        + Chain.scratch(blocks, n, cb_w)
        + sum([Scatter.scratch(s[0], s[1], sp) for s, sp in zip(shapes, splits)], []),
        compiler_params=pltpu.CompilerParams(
            collective_id=collective_id, has_side_effects=True, vmem_limit_bytes=60 * 1024 * 1024
        ),
    )(mg, w_out, y, gate, norms, gain, v, keys, colpack, rowpack, carried, skip, *bigs)


def conv_back(dv, slope, a, cw, span, padded, out_ref, b):
    taps = cw.shape[0]
    ext = span + HALO
    pg = dv * slope
    padded[HALO : HALO + span] = pg
    total, dcw = None, []
    for k in range(taps):
        moved = padded[taps - 1 - k : taps - 1 - k + ext]
        term = cw[k : k + 1] * moved
        total = term if total is None else total + term
        dcw.append(jnp.sum(moved * a, axis=0, keepdims=True))
    out_ref[b] = total.astype(bf16)
    return jnp.concatenate(dcw, axis=0), jnp.sum(pg, axis=0, keepdims=True)


def back_kernel(span, hw, groups, splits, *refs):
    count = len(splits)
    (later_ref, h_ref, keys_ref, v_ref, dv_ref, col_ref, cin_ref, cw_ref, slope_ref) = refs[:9]
    bigs = refs[9 : 9 + count]
    cig_ref, cols_ref, dk_ref, dcw_ref, dcb_ref, dlast_ref = refs[9 + count : 15 + count]
    outs = refs[15 + count : 15 + 2 * count]
    rest = refs[15 + 2 * count :]
    padded, dkacc = rest[:2]
    i = pl.program_id(0)
    batch = dk_ref.shape[0]
    n = keys_ref.shape[2] // 2

    @pl.when(i == 0)
    def _():
        if count:
            Place().greet()
        padded[0:16] = jnp.zeros((16, padded.shape[1]), f32)
        padded[16 + span :] = jnp.zeros((padded.shape[0] - 16 - span, padded.shape[1]), f32)

    hook = scatter_beside(i, batch, groups * batch, back_start, splits, bigs, outs, rest[2:])
    for b in range(batch):
        hook(b)
        cols = col_ref[0, b]
        c, step = cols[:, :HEADS], cols[:, HEADS:]
        low = later_ref[b]
        left = spread(jnp.exp2(c[span - 1 : span] - c), hw)
        kdh = mm(keys_ref[b, :, :n], low) * left
        v = v_ref[b].astype(f32)
        step_wide = spread(step, hw)
        cols_ref[0, b] = gather_heads(v * kdh, hw)
        dlast_ref[b] = jnp.broadcast_to(
            jnp.sum(low.astype(f32) * h_ref[b].astype(f32), axis=0, keepdims=True), dlast_ref.shape[1:]
        )
        vw = (v * step_wide * left).astype(bf16)
        part = mm_nt(vw, low)

        @pl.when(i == 0)
        def _():
            dkacc[b] = part

        @pl.when(i != 0)
        def _():
            dkacc[b] += part

        @pl.when(i == groups - 1)
        def _():
            dk_ref[b] = dkacc[b]

        dv = dv_ref[b].astype(f32) + kdh * step_wide
        dcw, dcb = conv_back(
            dv, slope_ref[b].astype(f32), cin_ref[b].astype(f32), cw_ref[...], span, padded, cig_ref, b
        )
        if b == 0:
            dcw_ref[...] = dcw
            dcb_ref[...] = dcb
        else:
            dcw_ref[...] += dcw
            dcb_ref[...] += dcb


def back(later, carried, keys, v, dv, colpack, cin, cw, slope, bigs, splits, hw, span, collective_id):
    batch = v.shape[0]
    groups = colpack.shape[0]
    cb_w = HEADS * hw
    inner = groups * cb_w
    n = keys.shape[2] // 2
    ext = span + HALO
    taps = cw.shape[0]
    block = lambda rows: pl.BlockSpec((batch, rows, cb_w), lambda i: (0, 0, i))
    lanes = lambda rows: pl.BlockSpec((rows, cb_w), lambda i: (0, i))
    hbm = pl.BlockSpec(memory_space=pl.ANY)
    shapes = [(x.shape[0] // 32, x.shape[1]) for x in bigs]
    return pl.pallas_call(
        functools.partial(back_kernel, span, hw, groups, splits),
        grid=(groups,),
        in_specs=[
            block(n),
            block(n),
            pl.BlockSpec(keys.shape, lambda i: (0, 0, 0)),
            block(span),
            block(span),
            pl.BlockSpec((1,) + colpack.shape[1:], lambda i: (i, 0, 0, 0)),
            block(ext),
            lanes(taps),
            block(span),
        ]
        + [hbm] * len(bigs),
        out_specs=[
            block(ext),
            pl.BlockSpec((1, batch, span, HEADS), lambda i: (i, 0, 0, 0)),
            pl.BlockSpec((batch, span, n), lambda i: (0, 0, 0)),
            lanes(taps),
            lanes(1),
            block(8),
        ]
        + [pl.BlockSpec(s, lambda i: (0, 0)) for s in shapes],
        out_shape=[
            jax.ShapeDtypeStruct((batch, ext, inner), bf16),
            jax.ShapeDtypeStruct((groups, batch, span, HEADS), f32),
            jax.ShapeDtypeStruct((batch, span, n), f32),
            jax.ShapeDtypeStruct((taps, inner), f32),
            jax.ShapeDtypeStruct((1, inner), f32),
            jax.ShapeDtypeStruct((batch, 8, inner), f32),
        ]
        + [jax.ShapeDtypeStruct(s, f32) for s in shapes],
        scratch_shapes=[
            pltpu.VMEM((span + 32, cb_w), f32),
            pltpu.VMEM((batch, span, n), f32),
        ]
        + sum([Scatter.scratch(s[0], s[1], sp) for s, sp in zip(shapes, splits)], []),
        compiler_params=pltpu.CompilerParams(
            collective_id=collective_id if bigs else None,
            has_side_effects=bool(bigs),
            vmem_limit_bytes=58 * 1024 * 1024,
        ),
    )(later, carried, keys, v, dv, colpack, cin, cw, slope, *bigs)


def keys_back_kernel(span, dk_ref, dk2_ref, dq_ref, cin_ref, cw_ref, slope_ref, cig_ref, dcw_ref, dcb_ref, padded):
    batch = dk_ref.shape[0]
    padded[...] = jnp.zeros_like(padded)
    for b in range(batch):
        dv = jnp.concatenate([dk_ref[b] + dk2_ref[b], dq_ref[b]], axis=1)
        dcw, dcb = conv_back(
            dv, slope_ref[b].astype(f32), cin_ref[b].astype(f32), cw_ref[...], span, padded, cig_ref, b
        )
        if b == 0:
            dcw_ref[...] = dcw
            dcb_ref[...] = dcb
        else:
            dcw_ref[...] += dcw
            dcb_ref[...] += dcb


def keys_backward(dk, dk2, dq, cin, cw, slope, span):
    batch, ext, width = cin.shape
    return pl.pallas_call(
        functools.partial(keys_back_kernel, span),
        in_specs=[pl.BlockSpec(memory_space=pltpu.VMEM)] * 6,
        out_specs=[pl.BlockSpec(memory_space=pltpu.VMEM)] * 3,
        out_shape=[
            jax.ShapeDtypeStruct(cin.shape, bf16),
            jax.ShapeDtypeStruct(cw.shape, f32),
            jax.ShapeDtypeStruct((1, width), f32),
        ],
        scratch_shapes=[pltpu.VMEM((span + 32, width), f32)],
        compiler_params=params_of(40),
    )(dk, dk2, dq, cin, cw, slope)


def tail_kernel(span, splits, with_small, *refs):
    count = len(splits)
    (cig_ref, wc_ref, dgate_ref, wg_ref, keys_ref, wk_ref, low_ref, wd_ref) = refs[:8]
    resid_ref, mg_ref, gain_ref, parts_ref = refs[8:12]
    bigs = refs[12 : 12 + count]
    grad_ref, sums_ref = refs[12 + count : 14 + count]
    outs = refs[14 + count : 14 + 2 * count]
    rest = refs[14 + 2 * count :]
    acc, rim, rim_in, value, halo_send, halo_recv = rest[:6]
    i = pl.program_id(0)
    steps = pl.num_programs(0)
    half = steps // 2
    batch, _, width = resid_ref.shape
    ext = span + HALO
    chain = Chain(True, rim, rim_in, halo_send, halo_recv)
    place = Place() if count else None
    plan = small = None
    times = []
    if count:
        plan = Scatter(place, bigs[0], outs[0], *rest[6:13], splits[0])
        times = plan.steps()
        small = Small(place, value, sums_ref, *rest[13:17])

    @pl.when(i == 0)
    def _():
        greet_all(place, chain, (place.to_across,) if count else ())

    slots = TAIL_STEPS
    early = [(t, s) for t, s in times if t <= tail_start(slots - 1)]
    late = [s for t, s in times if t > tail_start(slots - 1)]
    at = {}
    for time, step in early:
        at.setdefault(min(k for k in range(slots) if tail_start(k) >= time), []).append(step)
    for slot, some in at.items():

        @pl.when(i == slot)
        def _(some=some):
            for step in some:
                step()

    flat = lambda ref: ref[...].reshape(batch * ext, ref.shape[2])

    @pl.when(i == 0)
    def _():
        acc[...] = mm_nt(flat(cig_ref), wc_ref[...])
        acc[...] += mm_nt(flat(keys_ref), wk_ref[...])
        acc[...] += mm_nt(flat(low_ref), wd_ref[...])

    @pl.when(jnp.logical_and(i > 0, i < half))
    def _():
        acc[...] += mm_nt(flat(cig_ref), wc_ref[...])

    @pl.when(i == half - 1)
    def _():
        for b in range(batch):
            rim[0, b] = acc[b * ext : b * ext + HALO].astype(bf16)

        @pl.when(chain.has_next)
        def _():
            chain.copy(0).start()

    @pl.when(i >= half)
    def _():
        for b in range(batch):
            rows = slice(b * ext + HALO, (b + 1) * ext)
            acc[rows] += mm_nt(dgate_ref[b], wg_ref[...])

    @pl.when(i == steps - 1)
    def _():
        @pl.when(chain.has_prev)
        def _():
            chain.copy(0).wait_recv()
            for b in range(batch):
                rows = slice((b + 1) * ext - HALO, (b + 1) * ext)
                acc[rows] += rim_in[0, b].astype(f32)

        total = jnp.zeros((1, width), f32)
        for b in range(batch):
            grad = acc[b * ext + HALO : (b + 1) * ext]
            x = resid_ref[b].astype(f32)
            rs = lax.rsqrt(jnp.mean(x * x, axis=-1, keepdims=True) + epsilon)
            nz = x * rs
            fg = grad * gain_ref[...]
            total = total + jnp.sum(grad * nz, axis=0, keepdims=True)
            mean = jnp.mean(fg * nz, axis=-1, keepdims=True)
            grad_ref[b] = (mg_ref[b].astype(f32) + rs * (fg - nz * mean)).astype(bf16)
        lead = width // 128
        value[lead:] = parts_ref[lead:]
        for r in range(lead):
            value[r : r + 1] = total[:, r * 128 : (r + 1) * 128]
        if small is None:
            sums_ref[...] = value[...]
        else:
            spots = [len(late) * k // 6 for k in range(6)]
            for j, step in enumerate(late):
                for k in range(6):
                    if spots[k] == j:
                        small.go(k)
                step()

        @pl.when(chain.has_next)
        def _():
            chain.copy(0).wait_send()


TAIL_STEPS = 12


def tail_start(k):
    return 2.2 * k


def tail(cig, w_conv, dgate, w_gate, cig_keys, step_low, w_dt, resid, mg, gain, parts, bigs, splits, span, collective_id):
    batch, ext, inner = cig.shape
    width = resid.shape[2]
    cb_w = inner // (TAIL_STEPS // 2)
    half = TAIL_STEPS // 2
    keys_w = cig_keys.shape[2]
    whole = lambda shape: pl.BlockSpec(shape, lambda i: (0,) * len(shape))
    first = lambda i: jnp.minimum(i, half - 1)
    then = lambda i: jnp.maximum(i - half, 0)
    hbm = pl.BlockSpec(memory_space=pl.ANY)
    shapes = [(x.shape[0] // 32, x.shape[1]) for x in bigs]
    return pl.pallas_call(
        functools.partial(tail_kernel, span, splits, bool(bigs)),
        grid=(TAIL_STEPS,),
        in_specs=[
            pl.BlockSpec((batch, ext, cb_w), lambda i: (0, 0, first(i))),
            pl.BlockSpec((width, cb_w), lambda i: (0, first(i))),
            pl.BlockSpec((batch, span, cb_w), lambda i: (0, 0, then(i))),
            pl.BlockSpec((width, cb_w), lambda i: (0, then(i))),
            whole(cig_keys.shape),
            pl.BlockSpec((width, keys_w), lambda i: (0, inner // keys_w)),
            whole(step_low.shape),
            whole(w_dt.shape),
            whole(resid.shape),
            whole(mg.shape),
            whole(gain.shape),
            whole(parts.shape),
        ]
        + [hbm] * len(bigs),
        out_specs=[whole(resid.shape), whole(parts.shape)] + [whole(s) for s in shapes],
        out_shape=[jax.ShapeDtypeStruct(resid.shape, bf16), jax.ShapeDtypeStruct(parts.shape, f32)]
        + [jax.ShapeDtypeStruct(s, f32) for s in shapes],
        scratch_shapes=[
            pltpu.VMEM((batch * ext, width), f32),
            pltpu.VMEM((1, batch, HALO, width), bf16),
            pltpu.VMEM((1, batch, HALO, width), bf16),
            pltpu.VMEM(parts.shape, f32),
            pltpu.SemaphoreType.DMA((1,)),
            pltpu.SemaphoreType.DMA((1,)),
        ]
        + sum([Scatter.scratch(s[0], s[1], sp) for s, sp in zip(shapes, splits)], [])
        + (Small.scratch(parts.shape) if bigs else []),
        compiler_params=pltpu.CompilerParams(
            collective_id=collective_id, has_side_effects=True, vmem_limit_bytes=60 * 1024 * 1024
        ),
    )(cig, w_conv, dgate, w_gate, cig_keys, w_conv, step_low, w_dt, resid, mg, gain, parts, *bigs)


def own_kernels():
    return lax.axis_size("dp") == 4 and lax.axis_size("seq") == 8


def gather_rows(shards, parts):
    return [
        lax.all_gather(s[:, p[0] : p[0] + p[1]], ("dp", "seq"), axis=0, tiled=True)
        for s, p in zip(shards, parts)
    ]


def scatter_rows(bigs, splits, small, collective_id):
    if own_kernels():
        return scatter(bigs, splits, small, collective_id)
    outs = [lax.psum_scatter(b, ("dp", "seq"), scatter_dimension=0, tiled=True).astype(f32) for b in bigs]
    return outs + ([] if small is None else [lax.psum(small, ("dp", "seq"))])


def half_of(width):
    return (width // 2 + 127) // 128 * 128


def ungrouped(cols):
    groups, batch, span, each = cols.shape
    return jnp.transpose(cols, (1, 2, 0, 3)).reshape(batch, span, groups * each)


def gate_start(k, blocks):
    return 1.0 * k if k < blocks else 1.0 * blocks + 1.6 * (k - blocks)


def back_start(k):
    return 2.9 * k


def on_device(
    resid_in, out_grad, lengths, norm_gain, in_proj, dt_proj, conv_weight, conv_bias, dt_bias, a_log,
    skip_scale, gate_gain, out_proj,
):
    batch, span, width = resid_in.shape
    inner = gate_gain.shape[0]
    heads = a_log.shape[0]
    hw = inner // heads
    n = (in_proj.shape[1] - 2 * inner) // 2
    cb_w = HEADS * hw
    positions = lax.axis_index("seq") * span + lax.iota(jnp.int32, span)
    mask = (positions[None, :] < lengths[:, None]).astype(f32)[..., None]

    conv_cols = in_proj.shape[1] - inner
    dt_pad = (-(conv_cols + heads)) % 128
    conv_all = conv_cols + heads + dt_pad
    dt_shard = jnp.pad(dt_proj, ((0, 0), (0, dt_pad)))
    shards, parts = (
        [in_proj, dt_shard, in_proj, out_proj],
        [(inner, conv_cols), (0, heads + dt_pad), (0, inner), (0, width)],
    )
    splits = [half_of(conv_cols), heads + dt_pad, half_of(inner), half_of(width)]
    later_splits = splits[2:]
    inside = own_kernels()
    weights = shards if inside else gather_rows(shards, parts)

    halo = shifted(resid_in[:, span - HALO :], "seq", 1)
    resid_wide = resid_in.astype(f32)
    rate = -jnp.exp(a_log)
    lane_pad = (0, (-heads) % 128)
    skip_wide = jnp.repeat(skip_scale, hw)[None]
    gain_wide = gate_gain[None]
    cw_keys, cw_vals = conv_weight[:, inner:], conv_weight[:, :inner]
    made = front(
        resid_in, halo, norm_gain[None], conv_weight, conv_bias[None], jnp.pad(dt_bias, lane_pad)[None],
        jnp.pad(rate, lane_pad)[None], skip_wide, gain_wide, weights, parts, splits if inside else [], hw, heads, n, 1,
    )
    x2, keys, slope_keys, cin_keys, colpack, rowpack, raw, step = made[:8]
    v, slope_vals, cin_vals, y, carried, gate, normed_out, rg = made[8:16]
    full_conv, full_dt, full_gate, full_out = made[16:] if inside else weights
    x_ext = x2.reshape(batch, span + HALO, width)
    mixer_out = jnp.dot(normed_out, full_out, preferred_element_type=f32)
    output = (mask * (resid_wide + mixer_out)).astype(bf16)

    mixer_grad = (mask * out_grad.astype(f32)).astype(bf16)
    mean = jnp.sum(mixer_grad.astype(f32) * mixer_out, axis=-1, keepdims=True) * (1.0 / inner)
    norms = jnp.concatenate([rg[..., :1], mean, jnp.zeros((batch, span, 6), f32)], axis=-1)
    grad_out = jnp.einsum("bsi,bsd->id", normed_out, mixer_grad, preferred_element_type=f32).astype(bf16)
    made = gate_backward(
        mixer_grad, full_out, y, gate, norms, gain_wide, v, keys, colpack, rowpack, carried, skip_wide,
        [grad_out] if inside else [], later_splits[1:] if inside else [], hw, span, 7,
    )
    dgate, dv, later, cols_one, dq, dk, dgain, dskip = made[:8]
    (sum_out,) = made[8:] if inside else scatter_rows([grad_out], later_splits[1:], None, 5)
    x_rows = x_ext[:, HALO:]
    grad_gate = jnp.einsum("bsd,bse->de", x_rows, dgate, preferred_element_type=f32).astype(bf16)
    made = back(
        later, carried, keys, v, dv, colpack, cin_vals, cw_vals, slope_vals,
        [grad_gate] if inside else [], later_splits[:1] if inside else [], hw, span, 2,
    )
    cig_vals, cols_two, dk2, dcw_vals, dcb_vals, dlast = made[:6]
    (sum_gate,) = made[6:] if inside else scatter_rows([grad_gate], later_splits[:1], None, 5)
    cig_keys, dcw_keys, dcb_keys = keys_backward(dk, dk2, dq, cin_keys, cw_keys, slope_keys, span)

    raw, step = raw[..., :heads], step[..., :heads]
    rise = ungrouped(cols_one[..., :HEADS])
    direct = ungrouped(cols_one[..., HEADS:])
    ahead = ungrouped(cols_two)
    moved = ahead * step
    tri = causal(span, False).astype(f32)
    block_decay = jnp.exp2(colpack[:, :, span - 1, :HEADS]).transpose(1, 0, 2).reshape(batch, heads)
    last = jnp.sum(moved, axis=1) + dlast[:, 0].reshape(batch, heads, hw).sum(-1) * block_decay
    dlog = rise - moved
    dlog = jnp.einsum("ts,bth->bsh", tri, dlog, precision=highest) + last[:, None, :]
    grad_a = jnp.sum(dlog * step, axis=(0, 1)) * rate
    step_grad = direct + ahead + dlog * rate
    dt_grad = step_grad * jax.nn.sigmoid(raw)
    grad_bias = jnp.sum(dt_grad, axis=(0, 1))
    step_low = jnp.pad(dt_grad.astype(bf16), ((0, 0), (HALO, 0), (0, dt_pad)))

    cig = jnp.concatenate([cig_vals, cig_keys, step_low], axis=-1)
    grad_conv = jnp.einsum("bsd,bse->de", x_ext, cig, preferred_element_type=f32).astype(bf16)
    pieces = (
        norm_gain,
        jnp.concatenate([dcw_vals, dcw_keys], axis=1),
        jnp.concatenate([dcb_vals, dcb_keys], axis=1)[0],
        dgain[0],
        grad_bias,
        grad_a,
        dskip[0].reshape(heads, hw).sum(-1),
    )
    flat = jnp.concatenate([p.reshape(-1) for p in pieces])
    packed = jnp.pad(flat, (0, (-flat.size) % 1024)).reshape(-1, 128)
    made = tail(
        cig_vals, full_conv, dgate, full_gate, cig_keys, step_low, full_dt, resid_in, mixer_grad,
        norm_gain[None], packed, [grad_conv] if inside else [], [half_of(conv_all)] if inside else [], span, 6,
    )
    input_grad, small = made[:2]
    if inside:
        sum_conv = made[2]
    else:
        sum_conv, small = scatter_rows([grad_conv], [half_of(conv_all)], small, 6)
    flat, sums, at = small.reshape(-1), [], 0
    for p in pieces:
        sums.append(flat[at : at + p.size].reshape(p.shape))
        at += p.size
    sum_norm, sum_cw, sum_cb, sum_gain, sum_bias, sum_a, sum_skip = sums
    return (
        output,
        input_grad,
        jnp.concatenate([sum_gate, sum_conv[:, :conv_cols]], axis=1),
        sum_conv[:, conv_cols : conv_cols + heads],
        sum_out,
        sum_norm,
        sum_cw,
        sum_cb,
        sum_bias,
        sum_a,
        sum_skip,
        sum_gain,
    )


def solution(mesh):
    rows = P("dp", "seq", None)
    shard = P(("dp", "seq"), None)
    return jax.shard_map(
        on_device,
        mesh=mesh,
        in_specs=(rows, rows, P("dp"), P(), shard, shard, P(), P(), P(), P(), P(), P(), shard),
        out_specs=(rows, rows, shard, shard, shard, P(), P(), P(), P(), P(), P(), P()),
        check_vma=False,
    )
```

```python
import functools

import jax
import jax.numpy as jnp
from jax import lax
from jax.experimental import pallas as pl
from jax.experimental.pallas import tpu as pltpu
from jax.sharding import PartitionSpec as P

epsilon = 1e-05
highest = lax.Precision.HIGHEST
HALO = 16
HEADS = 8
LOG2E = 1.4426950408889634
f32 = jnp.float32
bf16 = jnp.bfloat16
MESH = pl.DeviceIdType.MESH


def mm(a, b):
    return lax.dot_general(a, b, (((1,), (0,)), ((), ())), preferred_element_type=f32)


def mm_nt(a, b):
    return lax.dot_general(a, b, (((1,), (1,)), ((), ())), preferred_element_type=f32)


def mm_tn(a, b):
    return lax.dot_general(a, b, (((0,), (0,)), ((), ())), preferred_element_type=f32)


def shifted(block, axis, distance):
    devices = range(lax.axis_size(axis))
    route = [(i - distance, i) for i in devices if i - distance in devices]
    return lax.ppermute(block, axis, route)


def spread(cols, width):
    rows, heads = cols.shape
    low_half = lax.broadcasted_iota(jnp.int32, (rows, 2 * width), 1) < width
    pairs = [
        jnp.where(low_half, cols[:, i : i + 1], cols[:, i + 1 : i + 2]) for i in range(0, heads, 2)
    ]
    return jnp.concatenate(pairs, axis=1)


def gather_heads(x, width):
    rows, total = x.shape
    low_half = lax.broadcasted_iota(jnp.int32, (rows, 2 * width), 1) < width
    head_lane = lax.broadcasted_iota(jnp.int32, (rows, total // width), 1)
    out = jnp.zeros((rows, total // width), f32)
    for i in range(total // (2 * width)):
        pair = x[:, i * 2 * width : (i + 1) * 2 * width]
        one = jnp.sum(jnp.where(low_half, pair, 0.0), axis=1, keepdims=True)
        two = jnp.sum(jnp.where(low_half, 0.0, pair), axis=1, keepdims=True)
        out = jnp.where(head_lane == 2 * i, one, out)
        out = jnp.where(head_lane == 2 * i + 1, two, out)
    return out


def silu_parts(v):
    sg = 1.0 / (1.0 + jnp.exp(-v))
    return v * sg, sg


def silu_slope(v):
    act, sg = silu_parts(v)
    return act, sg * (1.0 + v * (1.0 - sg))


def conv_pre(a, cw, cb, span):
    first = HALO - (cw.shape[0] - 1)
    out = cb
    for k in range(cw.shape[0]):
        out = out + cw[k : k + 1] * a[first + k : first + k + span]
    return out


def params_of(limit_mb, dims=None):
    return pltpu.CompilerParams(vmem_limit_bytes=limit_mb * 1024 * 1024, dimension_semantics=dims)


def causal(span, transposed):
    one = lax.broadcasted_iota(jnp.int32, (span, span), 0)
    two = lax.broadcasted_iota(jnp.int32, (span, span), 1)
    return (one <= two) if transposed else (one >= two)


class Place:
    def __init__(self):
        self.dp = lax.axis_index("dp")
        self.seq = lax.axis_index("seq")
        y, x = self.dp // 2, self.dp % 2
        self.z, self.core = self.seq // 2, self.seq % 2
        self.dx = 2 * y + (1 - x)
        self.dy = 2 * (1 - y) + x
        self.dxy = 2 * (1 - y) + (1 - x)
        self.to_x = (self.dx, self.seq)
        self.to_y = (self.dy, self.seq)
        self.to_core = (self.dp, 2 * self.z + 1 - self.core)
        self.to_up = (self.dp, 2 * jnp.minimum(self.z + 1, 3) + self.core)
        self.to_down = (self.dp, 2 * jnp.maximum(self.z - 1, 0) + self.core)
        self.to_across = (self.dp, 2 * jnp.where(self.z < 2, self.z + 2, self.z - 2) + self.core)
        self.has_up = self.z < 3
        self.has_down = self.z > 0

    def near(self, k):
        z = self.z
        return (z, z + 1 - 2 * (z % 2), jnp.where(z < 2, 2, 1), jnp.where(z < 2, 3, 0))[k]

    def greet(self, others=()):
        barrier = pltpu.get_barrier_semaphore()
        for device in (self.to_x, self.to_y, self.to_core) + tuple(others):
            pl.semaphore_signal(barrier, inc=1, device_id=device, device_id_type=MESH)

        @pl.when(self.has_up)
        def _():
            pl.semaphore_signal(barrier, inc=1, device_id=self.to_up, device_id_type=MESH)

        @pl.when(self.has_down)
        def _():
            pl.semaphore_signal(barrier, inc=1, device_id=self.to_down, device_id_type=MESH)

        ends = self.has_up.astype(jnp.int32) + self.has_down.astype(jnp.int32)
        pl.semaphore_wait(barrier, 3 + len(others) + ends)


GATHER_KINDS = 11


def gather_steps(place, shard, full, split, own_sem, send, recv):
    width = full.shape[3]
    z, core = place.z, place.core
    every, left, right = pl.ds(0, width), pl.ds(0, split), pl.ds(split, width - split)
    two = split < width

    def view(d, zz, cc, cols):
        return full.at[d * 4 + zz, cc, :, cols]

    def copy(kind, slot, device, d, zz, cc, cols, src=None):
        dst = view(d, zz, cc, cols)
        return pltpu.make_async_remote_copy(
            src_ref=dst if src is None else src,
            dst_ref=dst,
            send_sem=send.at[kind, slot],
            recv_sem=recv.at[kind, slot],
            device_id=device,
            device_id_type=MESH,
        )

    def pieces(k):
        zk = place.near(k)
        src = shard if k == 0 else None
        dp = place.dp
        return dict(
            x=copy(2, k, place.to_x, dp, zk, core, every, src),
            y=copy(3, k, place.to_y, dp, zk, core, every, src),
            own=copy(6, k, place.to_core, dp, zk, core, every, src),
        )

    def along(k, up):
        zk = place.near(k)
        src = shard if k == 0 else None
        device = place.to_up if up else place.to_down
        dst = view(place.dp, zk, core, every)
        return pltpu.make_async_remote_copy(
            src_ref=dst if src is None else src,
            dst_ref=dst,
            send_sem=send.at[0 if up else 1, k],
            recv_sem=recv.at[0, zk],
            device_id=device,
            device_id_type=MESH,
        )

    def arrive(k):
        zk = place.near(k)
        if k > 0:
            along(k, True).wait_recv()

        @pl.when(jnp.logical_and(zk <= z, place.has_up))
        def _():
            along(k, True).start()

        @pl.when(jnp.logical_and(zk >= z, place.has_down))
        def _():
            along(k, False).start()

        pieces(k)["own"].start()

    def beyond(k):
        made = pieces(k)
        made["x"].start()
        made["y"].start()

    def cross(k):
        zk = place.near(k)
        return (
            copy(2, k, place.to_x, place.dx, zk, core, every),
            copy(3, k, place.to_y, place.dy, zk, core, every),
            copy(4, k, place.to_y, place.dx, zk, core, left),
            copy(5, k, place.to_x, place.dy, zk, core, right) if two else None,
            copy(7, k, place.to_core, place.dx, zk, core, every),
            copy(8, k, place.to_core, place.dy, zk, core, every),
        )

    def forward(k):
        from_x, from_y, left_on, right_on, core_x, core_y = cross(k)
        from_x.wait_recv()
        left_on.start()
        core_x.start()
        from_y.wait_recv()
        if two:
            right_on.start()
        core_y.start()

    def corner(k):
        zk = place.near(k)
        return (
            copy(4, k, place.to_y, place.dxy, zk, core, left),
            copy(5, k, place.to_x, place.dxy, zk, core, right) if two else None,
            copy(9, k, place.to_core, place.dxy, zk, core, left),
            copy(10, k, place.to_core, place.dxy, zk, core, right) if two else None,
        )

    def last(k):
        from_y, from_x, core_left, core_right = corner(k)
        from_y.wait_recv()
        core_left.start()
        if two:
            from_x.wait_recv()
            core_right.start()

    def mine():
        return pltpu.make_async_copy(shard, view(place.dp, z, core, every), own_sem)

    def along_z(k):
        if k == 0:
            mine().start()
        arrive(k)

    def finish():
        mine().wait()
        other = 1 - core
        for k in range(4):
            zk = place.near(k)
            for kind, d, cols in (
                (6, place.dp, every), (7, place.dx, every), (8, place.dy, every),
                (9, place.dxy, left), (10, place.dxy, right),
            ):
                if kind == 10 and not two:
                    continue
                copy(kind, k, place.to_core, d, zk, other, cols).wait_recv()
        for k in range(4):
            zk = place.near(k)

            @pl.when(jnp.logical_and(zk <= z, place.has_up))
            def _():
                along(k, True).wait_send()

            @pl.when(jnp.logical_and(zk >= z, place.has_down))
            def _():
                along(k, False).wait_send()

            made = pieces(k)
            made["x"].wait_send()
            made["y"].wait_send()
            made["own"].wait_send()
            for one in cross(k)[2:] + corner(k)[2:]:
                if one is not None:
                    one.wait_send()

    return along_z, beyond, forward, last, finish


def gather_groups(place, shard, full, split, own_sem, send, recv):
    width = full.shape[3]
    z, core = place.z, place.core
    every, left, right = pl.ds(0, width), pl.ds(0, split), pl.ds(split, width - split)

    def along(k, up):
        zk = place.near(k)
        dst = full.at[place.dp * 4 + zk, core]
        return pltpu.make_async_remote_copy(
            src_ref=shard if k == 0 else dst,
            dst_ref=dst,
            send_sem=send.at[0 if up else 1, k],
            recv_sem=recv.at[0, zk],
            device_id=place.to_up if up else place.to_down,
            device_id_type=MESH,
        )

    def group(kind, device, d, cc, cols):
        some = full.at[pl.ds(d * 4, 4), cc, :, cols]
        return pltpu.make_async_remote_copy(
            src_ref=some, dst_ref=some, send_sem=send.at[kind, 0], recv_sem=recv.at[kind, 0],
            device_id=device, device_id_type=MESH,
        )

    def mine():
        return pltpu.make_async_copy(shard, full.at[place.dp * 4 + z, core], own_sem)

    def moves(k):
        zk = place.near(k)
        return (
            (jnp.logical_and(zk <= z, place.has_up), along(k, True)),
            (jnp.logical_and(zk >= z, place.has_down), along(k, False)),
        )

    def along_z(k):
        if k == 0:
            mine().start()
        else:
            along(k, True).wait_recv()
        for flag, copy in moves(k):

            @pl.when(flag)
            def _(copy=copy):
                copy.start()

    p = place
    sides = lambda: (group(2, p.to_x, p.dp, core, every), group(3, p.to_y, p.dp, core, every))
    halves = lambda: (group(4, p.to_y, p.dx, core, left), group(5, p.to_x, p.dy, core, right))
    owners = (p.dp, p.dx, p.dy, p.dxy)
    cores = lambda cc: [group(6 + j, p.to_core, d, cc, every) for j, d in enumerate(owners)]

    def beyond():
        mine().wait()
        for copy in sides():
            copy.start()
        cores(core)[0].start()

    def forward():
        from_x, from_y = group(2, p.to_x, p.dx, core, every), group(3, p.to_y, p.dy, core, every)
        from_x.wait_recv()
        halves()[0].start()
        from_y.wait_recv()
        halves()[1].start()
        for copy in cores(core)[1:3]:
            copy.start()

    def last():
        group(4, p.to_y, p.dxy, core, left).wait_recv()
        group(5, p.to_x, p.dxy, core, right).wait_recv()
        cores(core)[3].start()

    def finish():
        for copy in cores(1 - core):
            copy.wait_recv()
        for k in range(4):
            for flag, copy in moves(k):

                @pl.when(flag)
                def _(copy=copy):
                    copy.wait_send()

        for copy in sides() + halves() + tuple(cores(core)):
            copy.wait_send()

    return along_z, beyond, forward, last, finish


def gather_scratch():
    return [
        pltpu.SemaphoreType.DMA,
        pltpu.SemaphoreType.DMA((GATHER_KINDS, 4)),
        pltpu.SemaphoreType.DMA((GATHER_KINDS, 4)),
    ]


def part_of(ref, part):
    return ref.at[:, pl.ds(part[0], part[1])]


class Scatter:
    def __init__(self, place, big, out, own, land_core, land_xy, land_z, local, send, recv, split):
        self.place, self.big, self.out = place, big, out
        self.own, self.land_core, self.land_xy, self.land_z = own, land_core, land_xy, land_z
        self.local, self.send, self.recv = local, send, recv
        self.rows, self.width = out.shape
        self.split = split
        self.left, self.right = slice(0, split), slice(split, self.width)

    def groups(self):
        p = self.place
        return (p.dxy, p.dx, p.dy, p.dp)

    def far(self, k):
        return self.place.near(3 - k)

    def source(self, d, zz, cc):
        start = pl.multiple_of((d * 8 + zz * 2 + cc) * self.rows, 16)
        return self.big.at[pl.ds(start, self.rows)]

    def remote(self, src, dst, kind, slot, device):
        return pltpu.make_async_remote_copy(
            src_ref=src, dst_ref=dst, send_sem=self.send.at[kind, slot], recv_sem=self.recv.at[kind, slot],
            device_id=device, device_id_type=MESH,
        )

    def to_other(self, i, k):
        p = self.place
        src = self.source(self.groups()[i], self.far(k), 1 - p.core)
        return self.remote(src, self.land_core.at[i, k], i, k, p.to_core)

    def load(self, i, k):
        p = self.place
        return pltpu.make_async_copy(
            self.source(self.groups()[i], self.far(k), p.core), self.own.at[i, k], self.local.at[i, k]
        )

    def start(self, k):
        for i in range(4):
            self.to_other(i, k).start()
            self.load(i, k).start()

    def join(self, i, k):
        self.load(i, k).wait()
        self.to_other(i, k).wait_recv()
        self.own[i, k] = self.own[i, k] + self.land_core[i, k]

    def side(self, kind, k):
        p = self.place
        left, right = pl.ds(0, self.split), pl.ds(self.split, self.width - self.split)
        group, cols, device = (
            (0, left, p.to_y),
            (0, right, p.to_x),
            (2, left, p.to_y),
            (1, right, p.to_x),
            (2, right, p.to_y),
            (1, left, p.to_x),
        )[kind]
        size = self.split if cols is left else self.width - self.split
        return self.remote(
            self.own.at[group, k, :, cols], self.land_xy.at[kind, k, :, pl.ds(0, size)], 4 + kind, k, device
        )

    def take(self, kind, group, cols, k):
        self.side(kind, k).wait_recv()
        size = cols.stop - cols.start
        self.own[group, k, :, cols] = self.own[group, k, :, cols] + self.land_xy[kind, k, :, 0:size]

    def corner(self, k):
        self.join(0, k)
        self.side(0, k).start()
        self.side(1, k).start()

    def sides(self, k):
        self.join(1, k)
        self.side(3, k).start()
        self.join(2, k)
        self.side(2, k).start()

    def turns(self, k):
        self.take(0, 1, self.left, k)
        self.side(5, k).start()
        self.take(1, 2, self.right, k)
        self.side(4, k).start()

    def along(self, k, up):
        p = self.place
        zk = self.far(k)
        return pltpu.make_async_remote_copy(
            src_ref=self.own.at[3, k],
            dst_ref=self.land_z.at[0 if up else 1, zk],
            send_sem=self.send.at[10, k],
            recv_sem=self.recv.at[10 if up else 11, zk],
            device_id=p.to_up if up else p.to_down,
            device_id_type=MESH,
        )

    def rising(self, k):
        return self.far(k) > self.place.z

    def behind(self, k):
        p = self.place
        rising = self.rising(k)
        return jnp.logical_or(
            jnp.logical_and(rising, p.has_down), jnp.logical_and(jnp.logical_not(rising), p.has_up)
        )

    def send_along(self, k):
        @pl.when(self.rising(k))
        def _():
            self.along(k, True).start()

        @pl.when(jnp.logical_not(self.rising(k)))
        def _():
            self.along(k, False).start()

    def mine(self, k):
        self.join(3, k)
        self.take(2, 3, self.left, k)
        self.take(3, 3, self.right, k)
        self.take(5, 3, self.left, k)
        self.take(4, 3, self.right, k)
        if k < 3:

            @pl.when(jnp.logical_not(self.behind(k)))
            def _():
                self.send_along(k)

    def line(self, k):
        zk = self.far(k)

        @pl.when(jnp.logical_and(self.behind(k), self.rising(k)))
        def _():
            self.along(k, True).wait_recv()
            self.own[3, k] = self.own[3, k] + self.land_z[0, zk]

        @pl.when(jnp.logical_and(self.behind(k), jnp.logical_not(self.rising(k))))
        def _():
            self.along(k, False).wait_recv()
            self.own[3, k] = self.own[3, k] + self.land_z[1, zk]

        @pl.when(self.behind(k))
        def _():
            self.send_along(k)

    def result(self):
        p = self.place
        self.out[...] = self.own[3, 3].astype(f32)

        @pl.when(p.has_down)
        def _():
            self.along(3, True).wait_recv()
            self.out[...] += self.land_z[0, p.z].astype(f32)

        @pl.when(p.has_up)
        def _():
            self.along(3, False).wait_recv()
            self.out[...] += self.land_z[1, p.z].astype(f32)

    def drain(self):
        for k in range(4):
            for i in range(4):
                self.to_other(i, k).wait_send()
            for kind in range(6):
                self.side(kind, k).wait_send()
            if k < 3:
                self.along(k, True).wait_send()

    def steps(self):
        start, corner, sides, turns, mine, line = (
            self.start, self.corner, self.sides, self.turns, self.mine, self.line
        )
        return [
            (0, lambda: start(0)),
            (2, lambda: start(1)),
            (3, lambda: corner(0)),
            (4, lambda: sides(0)),
            (6, lambda: start(2)),
            (8, lambda: turns(0)),
            (9, lambda: corner(1)),
            (10, lambda: sides(1)),
            (12, lambda: start(3)),
            (14, lambda: mine(0)),
            (17, lambda: turns(1)),
            (18, lambda: corner(2)),
            (19, lambda: sides(2)),
            (22, lambda: line(0)),
            (23, lambda: mine(1)),
            (26, lambda: turns(2)),
            (27, lambda: corner(3)),
            (28, lambda: sides(3)),
            (31, lambda: line(1)),
            (32, lambda: mine(2)),
            (35, lambda: turns(3)),
            (40, lambda: line(2)),
            (42, lambda: mine(3)),
            (47, self.result),
            (50, self.drain),
        ]

    @staticmethod
    def scratch(rows, width, split):
        half = max(split, width - split)
        return [
            pltpu.VMEM((4, 4, rows, width), bf16),
            pltpu.VMEM((4, 4, rows, width), bf16),
            pltpu.VMEM((6, 4, rows, half), bf16),
            pltpu.VMEM((2, 4, rows, width), bf16),
            pltpu.SemaphoreType.DMA((4, 4)),
            pltpu.SemaphoreType.DMA((11, 4)),
            pltpu.SemaphoreType.DMA((12, 4)),
        ]


class Small:
    def __init__(self, place, value, out, sent, landed, send, recv):
        p = place
        self.value, self.out, self.sent, self.landed, self.send, self.recv = value, out, sent, landed, send, recv
        pair = 2 * (p.z + 1 - 2 * (p.z % 2)) + p.core
        self.devices = (p.to_core, p.to_x, p.to_y, (p.dp, pair), p.to_across)

    def copy(self, i):
        return pltpu.make_async_remote_copy(
            src_ref=self.sent.at[i], dst_ref=self.landed.at[i], send_sem=self.send.at[i],
            recv_sem=self.recv.at[i], device_id=self.devices[i], device_id_type=MESH,
        )

    def go(self, i):
        if i == 0:
            self.sent[0] = self.value[...]
            self.copy(0).start()
            return
        self.copy(i - 1).wait_recv()
        total = self.sent[i - 1] + self.landed[i - 1]
        if i < 5:
            self.sent[i] = total
            self.copy(i).start()
        else:
            self.out[...] = total
            for k in range(5):
                self.copy(k).wait_send()

    @staticmethod
    def scratch(shape):
        return [
            pltpu.VMEM((5,) + shape, f32),
            pltpu.VMEM((5,) + shape, f32),
            pltpu.SemaphoreType.DMA((5,)),
            pltpu.SemaphoreType.DMA((5,)),
        ]


def scatter_kernel(splits, with_small, *refs):
    count = len(splits)
    ins = count + (1 if with_small else 0)
    bigs, outs = refs[:count], refs[ins : ins + count]
    scratch = refs[2 * ins :]
    place = Place()
    place.greet((place.to_across,) if with_small else ())
    plans = [
        Scatter(place, bigs[i], outs[i], *scratch[7 * i : 7 * i + 7], splits[i]) for i in range(count)
    ]
    small = None
    if with_small:
        small = Small(place, refs[count], refs[ins + count], *scratch[7 * count :])
    small_at = {0: 0, 5: 1, 9: 2, 13: 3, 17: 4, 21: 5}
    for i, steps in enumerate(zip(*[plan.steps() for plan in plans])):
        for _, step in steps:
            step()
        if small and i in small_at:
            small.go(small_at[i])


def scatter(bigs, splits, small, collective_id):
    count = len(bigs)
    spec = pl.BlockSpec(memory_space=pl.ANY)
    vmem = pl.BlockSpec(memory_space=pltpu.VMEM)
    shapes = [(b.shape[0] // 32, b.shape[1]) for b in bigs]
    extra = [] if small is None else [small]
    scratch = sum([Scatter.scratch(s[0], s[1], sp) for s, sp in zip(shapes, splits)], [])
    if small is not None:
        scratch = scratch + Small.scratch(small.shape)
    return pl.pallas_call(
        functools.partial(scatter_kernel, splits, small is not None),
        in_specs=[spec] * count + [vmem] * len(extra),
        out_specs=[vmem] * (count + len(extra)),
        out_shape=[jax.ShapeDtypeStruct(s, f32) for s in shapes]
        + [jax.ShapeDtypeStruct(e.shape, f32) for e in extra],
        scratch_shapes=scratch,
        compiler_params=pltpu.CompilerParams(
            collective_id=collective_id, has_side_effects=True, vmem_limit_bytes=60 * 1024 * 1024
        ),
    )(*bigs, *extra)


class Chain:
    def __init__(self, backward, sent, landed, send, recv):
        self.sent, self.landed, self.send, self.recv = sent, landed, send, recv
        me, count = lax.axis_index("seq"), lax.axis_size("seq")
        turn = -1 if backward else 1
        self.place = count - 1 - me if backward else me
        self.has_prev = self.place > 0
        self.has_next = self.place < count - 1
        self.next = (lax.axis_index("dp"), jnp.clip(me + turn, 0, count - 1))
        self.prev = (lax.axis_index("dp"), jnp.clip(me - turn, 0, count - 1))

    def copy(self, k):
        return pltpu.make_async_remote_copy(
            src_ref=self.sent.at[k], dst_ref=self.landed.at[k], send_sem=self.send.at[k],
            recv_sem=self.recv.at[k], device_id=self.next, device_id_type=MESH,
        )

    def pass_on(self, k, decay, local):
        @pl.when(self.has_prev)
        def _():
            self.copy(k).wait_recv()

        @pl.when(jnp.logical_not(self.has_prev))
        def _():
            self.landed[k] = jnp.zeros_like(self.landed[k])

        @pl.when(self.has_next)
        def _():
            self.sent[k] = (decay() * self.landed[k].astype(f32) + local()).astype(bf16)
            self.copy(k).start()

    def drain(self):
        @pl.when(self.has_next)
        def _():
            for k in range(self.sent.shape[0]):
                self.copy(k).wait_send()

    @staticmethod
    def scratch(count, n, size):
        return [
            pltpu.VMEM((count, n, size), bf16),
            pltpu.VMEM((count, n, size), bf16),
            pltpu.SemaphoreType.DMA((count,)),
            pltpu.SemaphoreType.DMA((count,)),
        ]


def greet_all(place, chain, others=()):
    barrier = pltpu.get_barrier_semaphore()
    flags = [chain.has_prev, chain.has_next]
    devices = [chain.prev, chain.next]
    total = chain.has_prev.astype(jnp.int32) + chain.has_next.astype(jnp.int32)
    if place is not None:
        flags += [place.has_up, place.has_down]
        devices += [place.to_up, place.to_down]
        total = total + place.has_up.astype(jnp.int32) + place.has_down.astype(jnp.int32) + 3 + len(others)
        for device in (place.to_x, place.to_y, place.to_core) + tuple(others):
            pl.semaphore_signal(barrier, inc=1, device_id=device, device_id_type=MESH)
    for flag, device in zip(flags, devices):

        @pl.when(flag)
        def _(device=device):
            pl.semaphore_signal(barrier, inc=1, device_id=device, device_id_type=MESH)

    pl.semaphore_wait(barrier, total)


def front_time(slot):
    if slot < 18:
        return 60 + 1.4 * slot
    if slot < 36:
        return 85 + 1.4 * (slot - 18)
    return 110 + 0.95 * (slot - 36)


GATE_STEPS = ((76, "f"), (90, "l"), (94, "end"))
OUT_STEPS = ((62, "z", 2), (70, "z", 3), (77, "b"), (114, "f"), (126, "l"))


def front_kernel(span, hw, heads, splits, parts, *refs):
    count = len(splits)
    (resid_ref, halo_ref, ngain_ref, cw_ref, cb_ref, bias_ref, rate_ref, skip_ref, gain_ref) = refs[:9]
    given = refs[9:13]
    x_ref, keys_ref, kslope_ref, kcin_ref, col_ref, row_ref, raw_ref, step_ref = refs[13:21]
    rows_ref, slope_ref, cin_ref, y_ref, carried_ref, gate_ref, no_ref, rg_ref = refs[21:29]
    fulls = refs[29 : 29 + count] if count else given
    rest = refs[29 + count :]
    values, local, scores, decays, gated, squares, wbuf, wkeys, wdt, wsem, ksem = rest[:11]
    chain = Chain(False, *rest[11:15])
    batch, _, width = resid_ref.shape
    ext = span + HALO
    groups = heads // HEADS
    cb_w = HEADS * hw
    inner = groups * cb_w
    n = keys_ref.shape[2] // 2
    i = pl.program_id(0)
    place = Place() if count else None
    plans = [
        (gather_steps if j < 2 else gather_groups)(
            place, part_of(given[j], parts[j]), fulls[j], splits[j], *rest[15 + 3 * j : 18 + 3 * j]
        )
        for j in range(count)
    ]
    low_half = lax.broadcasted_iota(jnp.int32, (span, 2 * hw), 1) < hw

    def weights(j, full):
        cols = pl.ds(pl.multiple_of(j * cb_w, cb_w), cb_w)
        return pltpu.make_async_copy(full.at[:, :, :, cols], wbuf.at[j % 2], wsem.at[j % 2])

    def key_weights():
        return (
            pltpu.make_async_copy(fulls[0].at[:, :, :, pl.ds(inner, 2 * n)], wkeys, ksem.at[0]),
            pltpu.make_async_copy(fulls[1], wdt, ksem.at[1]),
        )

    at = {}
    if count:
        todo = [(one[0], 2) + one[1:] for one in GATE_STEPS] + [(one[0], 3) + one[1:] for one in OUT_STEPS]
        for time, which, *what in sorted(todo):
            slot = min([j for j in range(54) if front_time(j) >= time] + [53])
            at.setdefault(slot, []).append((which, *what))

    def act(which, step, *k):
        along_z, beyond, forward, last, finish = plans[which]
        {"z": along_z, "b": beyond, "f": forward, "l": last, "end": finish}[step](*k)

    def hook(b):
        for slot in sorted(at):
            if slot % batch == b:

                @pl.when(i == 1 + slot // batch)
                def _(slot=slot):
                    for step in at[slot]:
                        act(*step)

    def input_norm():
        for b in range(batch):
            for src, lo, size in ((halo_ref, 0, HALO), (resid_ref, HALO, span)):
                x = src[b].astype(f32)
                rs = lax.rsqrt(jnp.mean(x * x, axis=-1, keepdims=True) + epsilon)
                x_ref[b * ext + lo : b * ext + lo + size] = (x * rs * ngain_ref[...]).astype(bf16)

    def key_part():
        cw, cb = cw_ref[:, inner:], cb_ref[:, inner:]
        acc = mm(x_ref[...], wkeys[...].reshape(width, 2 * n))
        raw_all = mm(x_ref[...], wdt[...].reshape(width, wdt.shape[3]))
        tri = causal(span, False).astype(f32)
        for b in range(batch):
            a = acc[b * ext : (b + 1) * ext]
            row, slope = silu_slope(conv_pre(a, cw, cb, span))
            keys_ref[b] = row.astype(bf16)
            kslope_ref[b] = slope.astype(bf16)
            kcin_ref[b] = a.astype(bf16)
            raw = raw_all[b * ext + HALO : (b + 1) * ext] + bias_ref[...]
            step = jnp.maximum(raw, 0.0) + jnp.log1p(jnp.exp(-jnp.abs(raw)))
            scaled = lax.dot_general(
                tri, step * rate_ref[...], (((1,), (0,)), ((), ())), precision=highest,
                preferred_element_type=f32,
            ) * LOG2E
            raw_ref[b] = raw
            step_ref[b] = step
            turned = jnp.transpose(scaled)
            for g in range(groups):
                some = slice(g * HEADS, (g + 1) * HEADS)
                col_ref[g, b] = jnp.concatenate([scaled[:, some], step[:, some]], axis=1)
                row_ref[g, b] = turned[some]

    @pl.when(i == 0)
    def _():
        greet_all(place, chain)
        def both(step, *k):
            act(0, step, *k)
            act(1, step, *k)

        if count:
            both("z", 0)
            both("b", 0)
        input_norm()
        if count:
            both("z", 1)
            both("b", 1)
            both("f", 0)
            both("z", 2)
            both("b", 2)
            act(2, "z", 0)
            both("f", 1)
            both("z", 3)
            both("b", 3)
            both("f", 2)
            act(2, "z", 1)
            both("l", 0)
            act(2, "z", 2)
            both("f", 3)
            act(3, "z", 0)
            both("l", 1)
            act(2, "z", 3)
            act(2, "b")
            both("l", 2)
            both("l", 3)
            act(3, "z", 1)
            both("end")
        for copy in key_weights():
            copy.start()
        weights(0, fulls[0]).start()
        for copy in key_weights():
            copy.wait()
        key_part()

    def values_part(g, b, acc):
        a = acc[b * ext : (b + 1) * ext]
        some = pl.ds(pl.multiple_of(g * cb_w, cb_w), cb_w)
        row, slope = silu_slope(conv_pre(a, cw_ref[:, some], cb_ref[:, some], span))
        row = row.astype(bf16)
        rows_ref[b] = row
        slope_ref[b] = slope.astype(bf16)
        values[g * batch + b] = row
        cin_ref[b] = a.astype(bf16)
        cols = col_ref[g, b]
        c, step = cols[:, :HEADS], cols[:, HEADS:]
        weight = jnp.exp2(c[span - 1 : span] - c) * step
        vw = (row.astype(f32) * spread(weight, hw)).astype(bf16)
        local[g * batch + b] = mm_tn(keys_ref[b, :, :n], vw)
        decays[g * batch + b] = spread(jnp.exp2(c[span - 1 : span]), hw)

    def rows_part(g, b):
        k_in, k_out = keys_ref[b, :, :n], keys_ref[b, :, n:]

        @pl.when(g == 0)
        def _():
            scores[b] = jnp.where(causal(span, False), mm_nt(k_out, k_in), 0.0)

        cols = col_ref[g, b]
        c, step = cols[:, :HEADS], cols[:, HEADS:]
        v = values[g * batch + b].astype(f32)
        vs = (v * spread(step, hw)).astype(bf16)
        s = scores[b]
        rows = row_ref[g, b]
        sums = []
        for p in range(HEADS // 2):
            pair = vs[:, p * 2 * hw : (p + 1) * 2 * hw]
            total = None
            for q in range(2):
                h = 2 * p + q
                gap = jnp.minimum(c[:, h : h + 1] - rows[h : h + 1, :], 0.0)
                u = (jnp.exp2(gap) * s).astype(bf16)
                keep = low_half if q == 0 else jnp.logical_not(low_half)
                term = mm(u, jnp.where(keep, pair, jnp.zeros_like(pair)))
                total = term if total is None else total + term
            sums.append(total)
        inside = jnp.concatenate(sums, axis=1)
        came = chain.landed[g * batch + b]
        carried_ref[b] = came
        skip = skip_ref[:, pl.ds(pl.multiple_of(g * cb_w, cb_w), cb_w)]
        y = inside + mm(k_out, came) * spread(jnp.exp2(c), hw) + skip * v
        y_ref[b] = y
        gated[g * batch + b] = y

    def gate_part(g, b, w):
        gate = mm(x_ref[b * ext + HALO : (b + 1) * ext], w)
        gate_ref[b] = gate.astype(bf16)
        act, _ = silu_parts(gate)
        gr = gated[g * batch + b] * act
        gated[g * batch + b] = gr
        total = sum([gr[:, j * 128 : (j + 1) * 128] * gr[:, j * 128 : (j + 1) * 128] for j in range(cb_w // 128)])
        squares[b] = jnp.where(g == 0, 0.0, squares[b]) + total

    @pl.when(jnp.logical_and(i > 0, i <= groups))
    def _():
        g = i - 1
        weights(g, fulls[0]).wait()

        @pl.when(g < groups - 1)
        def _():
            weights(g + 1, fulls[0]).start()

        acc = mm(x_ref[...], wbuf[g % 2].reshape(width, cb_w))
        for b in range(batch):
            hook(b)
            values_part(g, b, acc)

    @pl.when(jnp.logical_and(i > groups, i <= 2 * groups))
    def _():
        for b in range(batch):
            hook(b)
            rows_part(i - 1 - groups, b)

    @pl.when(i > 2 * groups)
    def _():
        g = i - 1 - 2 * groups

        @pl.when(g == 0)
        def _():
            weights(0, fulls[2]).start()

        weights(g, fulls[2]).wait()

        @pl.when(g < groups - 1)
        def _():
            weights(g + 1, fulls[2]).start()

        for b in range(batch):
            hook(b)
            gate_part(g, b, wbuf[g % 2].reshape(width, cb_w))

    def ready(j):
        for b in range(batch):
            k = j * batch + b
            chain.pass_on(k, lambda: decays[k], lambda: local[k])

    early = i - 1 - chain.place

    @pl.when(jnp.logical_and(jnp.logical_and(early >= 0, early < groups), i - 1 <= groups - 1 + early))
    def _():
        ready(early)

    late = i - groups

    @pl.when(jnp.logical_and(jnp.logical_and(late >= 0, late < groups), chain.place > groups - 1))
    def _():
        ready(late)

    @pl.when(i == 3 * groups)
    def _():
        for b in range(batch):
            total = jnp.sum(squares[b], axis=1, keepdims=True)
            rg = lax.rsqrt(total * (1.0 / inner) + epsilon)
            rg_ref[b] = jnp.broadcast_to(rg, rg_ref.shape[1:])
            for g in range(groups):
                part = slice(g * cb_w, (g + 1) * cb_w)
                no_ref[b, :, part] = (gated[g * batch + b] * rg * gain_ref[:, part]).astype(bf16)
        if count:
            act(3, "end")
        chain.drain()


def front(resid, halo, norm_gain, cw, cb, bias, rate, skip, gain, shards, parts, splits, hw, heads, n, collective_id):
    batch, span, width = resid.shape
    ext = span + HALO
    groups = heads // HEADS
    cb_w = HEADS * hw
    inner = groups * cb_w
    blocks = groups * batch
    lanes = bias.shape[1]
    hbm = pl.BlockSpec(memory_space=pl.ANY)
    count = len(splits)
    clip = lambda k: jnp.clip(k, 0, groups - 1)
    first = lambda i: clip(i - 1)
    then = lambda i: clip(i - 1 - groups)
    last = lambda i: clip(i - 1 - 2 * groups)
    once = lambda shape: pl.BlockSpec(shape, lambda i: (0,) * len(shape), pipeline_mode=pl.Buffered(1))
    block = lambda f, rows: pl.BlockSpec((batch, rows, cb_w), lambda i: (0, 0, f(i)))
    shaped = lambda shape, dtype: (once(shape), jax.ShapeDtypeStruct(shape, dtype))
    columns = lambda f, rows, dtype: (block(f, rows), jax.ShapeDtypeStruct((batch, rows, inner), dtype))
    outs = [
        shaped((batch * ext, width), bf16),
        shaped((batch, span, 2 * n), bf16),
        shaped((batch, span, 2 * n), bf16),
        shaped((batch, ext, 2 * n), bf16),
        shaped((groups, batch, span, 2 * HEADS), f32),
        shaped((groups, batch, HEADS, span), f32),
        shaped((batch, span, lanes), f32),
        shaped((batch, span, lanes), f32),
        columns(first, span, bf16),
        columns(first, span, bf16),
        columns(first, ext, bf16),
        columns(then, span, f32),
        columns(then, n, bf16),
        columns(last, span, bf16),
        shaped((batch, span, inner), bf16),
        shaped((batch, span, 8), f32),
    ]
    if count:
        outs += [
            (hbm, jax.ShapeDtypeStruct((16, 2, s.shape[0], p[1]), s.dtype)) for s, p in zip(shards, parts)
        ]
    else:
        shards = [s.reshape(16, 2, s.shape[0] // 32, s.shape[1]) for s in shards]
    small_ins = [resid, halo, norm_gain, cw, cb, bias, rate, skip, gain]
    return pl.pallas_call(
        functools.partial(front_kernel, span, hw, heads, splits, parts),
        grid=(1 + 3 * groups,),
        in_specs=[once(x.shape) for x in small_ins] + [hbm] * 4,
        out_specs=[o[0] for o in outs],
        out_shape=[o[1] for o in outs],
        scratch_shapes=[
            pltpu.VMEM((blocks, span, cb_w), bf16),
            pltpu.VMEM((blocks, n, cb_w), f32),
            pltpu.VMEM((batch, span, span), f32),
            pltpu.VMEM((blocks, 1, cb_w), f32),
            pltpu.VMEM((blocks, span, cb_w), f32),
            pltpu.VMEM((batch, span, 128), f32),
            pltpu.VMEM((2, 16, 2, width // 32, cb_w), bf16),
            pltpu.VMEM((16, 2, width // 32, 2 * n), bf16),
            pltpu.VMEM((16, 2, width // 32, lanes), bf16),
            pltpu.SemaphoreType.DMA((2,)),
            pltpu.SemaphoreType.DMA((2,)),
        ]
        + Chain.scratch(blocks, n, cb_w)
        + gather_scratch() * count,
        compiler_params=pltpu.CompilerParams(
            collective_id=collective_id, has_side_effects=True, vmem_limit_bytes=62 * 1024 * 1024
        ),
    )(*small_ins, *shards)


def scatter_beside(i, batch, slots, starts, splits, bigs, outs, scratch):
    if not splits:
        return lambda b: None
    place = Place()
    plans = [
        Scatter(place, bigs[j], outs[j], *scratch[7 * j : 7 * j + 7], splits[j]).steps()
        for j in range(len(splits))
    ]
    at = {}
    for steps in zip(*plans):
        for time, step in steps:
            slot = min([k for k in range(slots) if starts(k) >= time] + [slots - 1])
            at.setdefault(slot, []).append(step)

    def run(b):
        for slot, steps in at.items():
            if slot % batch == b:

                @pl.when(i == slot // batch)
                def _(steps=steps):
                    for step in steps:
                        step()

    return run


def gate_back_kernel(span, hw, groups, splits, *refs):
    count = len(splits)
    (mg_ref, w_ref, y_ref, gate_ref, norm_ref, gain_ref, v_ref, keys_ref, col_ref, row_ref) = refs[:10]
    h_ref, skip_ref = refs[10:12]
    bigs = refs[12 : 12 + count]
    (dgate_ref, dv_ref, later_ref, cols_ref, dq_ref, dk_ref, dgain_ref, dskip_ref) = refs[12 + count : 20 + count]
    outs = refs[20 + count : 20 + 2 * count]
    rest = refs[20 + 2 * count :]
    scores, dscores, dqacc, gbs, rises, local, decays = rest[:7]
    chain = Chain(True, *rest[7:11])
    batch = mg_ref.shape[0]
    blocks = groups * batch
    i = pl.program_id(0)
    g = i % groups
    n = keys_ref.shape[2] // 2
    skip = skip_ref[...]
    low_half = lax.broadcasted_iota(jnp.int32, (span, 2 * hw), 1) < hw

    @pl.when(i == 0)
    def _():
        greet_all(Place() if count else None, chain)

    hook = scatter_beside(i, batch, 2 * blocks, lambda k: gate_start(k, blocks), splits, bigs, outs, rest[11:])

    def gate_part(b):
        at = g * batch + b
        cols = col_ref[0, b]
        c = cols[:, :HEADS]
        no_grad = mm_nt(mg_ref[b], w_ref[...])
        gate = gate_ref[b].astype(f32)
        y = y_ref[b]
        rg = norm_ref[b][:, 0:1]
        mean = norm_ref[b][:, 1:2]
        act, sg = silu_parts(gate)
        gn = y * act * rg
        dgain = jnp.sum(no_grad * gn, axis=0, keepdims=True)
        dg = rg * (no_grad * gain_ref[...] - gn * mean)
        dgate_ref[b] = (dg * y * (sg * (1.0 + gate * (1.0 - sg)))).astype(bf16)
        gb = (dg * act).astype(bf16)
        gbs[at] = gb
        gf = gb.astype(f32)
        v = v_ref[b].astype(f32)
        dskip = jnp.sum(gf * v, axis=0, keepdims=True)
        rises[at] = gather_heads(gf * (y - skip * v), hw)
        ge = (gf * spread(jnp.exp2(c), hw)).astype(bf16)
        local[at] = mm_tn(keys_ref[b, :, n:], ge)
        decays[at] = spread(jnp.exp2(c[span - 1 : span]), hw)
        part = mm_nt(ge, h_ref[b])

        @pl.when(g == 0)
        def _():
            dqacc[b] = part

        @pl.when(g != 0)
        def _():
            dqacc[b] += part

        if b == 0:
            dgain_ref[...] = dgain
            dskip_ref[...] = dskip
        else:
            dgain_ref[...] += dgain
            dskip_ref[...] += dskip

    def block_part(b):
        at = g * batch + b
        cols = col_ref[0, b]
        c, step = cols[:, :HEADS], cols[:, HEADS:]
        k_in, k_out = keys_ref[b, :, :n], keys_ref[b, :, n:]

        @pl.when(g == 0)
        def _():
            scores[b] = jnp.where(causal(span, True), mm_nt(k_in, k_out), 0.0)
            dscores[b] = jnp.zeros_like(dscores[b])

        later_ref[b] = chain.landed[at]
        gb = gbs[at]
        gf = gb.astype(f32)
        v = v_ref[b].astype(f32)
        step_wide = spread(step, hw)
        vs = (v * step_wide).astype(bf16)
        rows = row_ref[0, b]
        s = scores[b]
        parts = []
        ds = dscores[b]
        for p in range(HEADS // 2):
            lanes = slice(p * 2 * hw, (p + 1) * 2 * hw)
            total = None
            for q in range(2):
                h = 2 * p + q
                gap = jnp.minimum(rows[h : h + 1, :] - c[:, h : h + 1], 0.0)
                decay = jnp.exp2(gap)
                u = (decay * s).astype(bf16)
                keep = low_half if q == 0 else jnp.logical_not(low_half)
                half = jnp.where(keep, gb[:, lanes], jnp.zeros_like(gb[:, lanes]))
                term = mm(u, half)
                total = term if total is None else total + term
                ds = ds + decay * mm_nt(vs[:, lanes], half)
            parts.append(total)
        dscores[b] = ds
        u_all = jnp.concatenate(parts, axis=1)
        dv_ref[b] = (u_all * step_wide + skip * gf).astype(bf16)
        fall = gather_heads(vs.astype(f32) * u_all, hw)
        direct = gather_heads(v * u_all, hw)
        cols_ref[0, b] = jnp.concatenate([rises[at] - fall, direct], axis=1)

        @pl.when(g == groups - 1)
        def _():
            low = jnp.where(causal(span, True), dscores[b], 0.0).astype(bf16)
            dq_ref[b] = dqacc[b] + mm_tn(low, k_in)
            dk_ref[b] = mm(low, k_out)

    lag = jnp.minimum(3 * chain.place, blocks - 1)
    for b in range(batch):
        hook(b)

        @pl.when(i < groups)
        def _():
            gate_part(b)

        @pl.when(i >= groups)
        def _():
            block_part(b)

        k = i * batch + b - lag

        @pl.when(jnp.logical_and(k >= 0, k < blocks))
        def _():
            chain.pass_on(k, lambda: decays[k], lambda: local[k])

    @pl.when(i == 2 * groups - 1)
    def _():
        chain.drain()


def gate_backward(
    mg, w_out, y, gate, norms, gain, v, keys, colpack, rowpack, carried, skip, bigs, splits, hw, span,
    collective_id,
):
    hbm = pl.BlockSpec(memory_space=pl.ANY)
    shapes = [(x.shape[0] // 32, x.shape[1]) for x in bigs]
    batch, _, width = mg.shape
    groups = colpack.shape[0]
    cb_w = HEADS * hw
    inner = groups * cb_w
    n = keys.shape[2] // 2
    blocks = groups * batch
    first = lambda i: jnp.minimum(i, groups - 1)
    then = lambda i: jnp.maximum(i - groups, 0)
    both = lambda i: i % groups
    block = lambda f, rows: pl.BlockSpec((batch, rows, cb_w), lambda i: (0, 0, f(i)))
    lanes = lambda f: pl.BlockSpec((1, cb_w), lambda i: (0, f(i)))
    whole = lambda shape: pl.BlockSpec(shape, lambda i: (0,) * len(shape))
    return pl.pallas_call(
        functools.partial(gate_back_kernel, span, hw, groups, splits),
        grid=(2 * groups,),
        in_specs=[
            whole(mg.shape),
            pl.BlockSpec((cb_w, width), lambda i: (first(i), 0)),
            block(first, span),
            block(first, span),
            whole(norms.shape),
            lanes(first),
            block(both, span),
            whole(keys.shape),
            pl.BlockSpec((1,) + colpack.shape[1:], lambda i: (both(i), 0, 0, 0)),
            pl.BlockSpec((1,) + rowpack.shape[1:], lambda i: (then(i), 0, 0, 0)),
            block(first, n),
            lanes(both),
        ]
        + [hbm] * len(bigs),
        out_specs=[
            block(first, span),
            block(then, span),
            block(then, n),
            pl.BlockSpec((1, batch, span, 2 * HEADS), lambda i: (then(i), 0, 0, 0)),
            whole((batch, span, n)),
            whole((batch, span, n)),
            lanes(first),
            lanes(first),
        ]
        + [whole(s) for s in shapes],
        out_shape=[
            jax.ShapeDtypeStruct((batch, span, inner), bf16),
            jax.ShapeDtypeStruct((batch, span, inner), bf16),
            jax.ShapeDtypeStruct((batch, n, inner), bf16),
            jax.ShapeDtypeStruct((groups, batch, span, 2 * HEADS), f32),
            jax.ShapeDtypeStruct((batch, span, n), f32),
            jax.ShapeDtypeStruct((batch, span, n), f32),
            jax.ShapeDtypeStruct((1, inner), f32),
            jax.ShapeDtypeStruct((1, inner), f32),
        ]
        + [jax.ShapeDtypeStruct(s, f32) for s in shapes],
        scratch_shapes=[
            pltpu.VMEM((batch, span, span), f32),
            pltpu.VMEM((batch, span, span), f32),
            pltpu.VMEM((batch, span, n), f32),
            pltpu.VMEM((blocks, span, cb_w), bf16),
            pltpu.VMEM((blocks, span, HEADS), f32),
            pltpu.VMEM((blocks, n, cb_w), f32),
            pltpu.VMEM((blocks, 1, cb_w), f32),
        ]
        + Chain.scratch(blocks, n, cb_w)
        + sum([Scatter.scratch(s[0], s[1], sp) for s, sp in zip(shapes, splits)], []),
        compiler_params=pltpu.CompilerParams(
            collective_id=collective_id, has_side_effects=True, vmem_limit_bytes=60 * 1024 * 1024
        ),
    )(mg, w_out, y, gate, norms, gain, v, keys, colpack, rowpack, carried, skip, *bigs)


def conv_back(dv, slope, a, cw, span, padded, out_ref, b):
    taps = cw.shape[0]
    ext = span + HALO
    pg = dv * slope
    padded[HALO : HALO + span] = pg
    total, dcw = None, []
    for k in range(taps):
        moved = padded[taps - 1 - k : taps - 1 - k + ext]
        term = cw[k : k + 1] * moved
        total = term if total is None else total + term
        dcw.append(jnp.sum(moved * a, axis=0, keepdims=True))
    out_ref[b] = total.astype(bf16)
    return jnp.concatenate(dcw, axis=0), jnp.sum(pg, axis=0, keepdims=True)


def back_kernel(span, hw, groups, splits, *refs):
    count = len(splits)
    (later_ref, h_ref, keys_ref, v_ref, dv_ref, col_ref, cin_ref, cw_ref, slope_ref) = refs[:9]
    bigs = refs[9 : 9 + count]
    cig_ref, cols_ref, dk_ref, dcw_ref, dcb_ref, dlast_ref = refs[9 + count : 15 + count]
    outs = refs[15 + count : 15 + 2 * count]
    rest = refs[15 + 2 * count :]
    padded, dkacc = rest[:2]
    i = pl.program_id(0)
    batch = dk_ref.shape[0]
    n = keys_ref.shape[2] // 2

    @pl.when(i == 0)
    def _():
        if count:
            Place().greet()
        padded[0:16] = jnp.zeros((16, padded.shape[1]), f32)
        padded[16 + span :] = jnp.zeros((padded.shape[0] - 16 - span, padded.shape[1]), f32)

    hook = scatter_beside(i, batch, groups * batch, back_start, splits, bigs, outs, rest[2:])
    for b in range(batch):
        hook(b)
        cols = col_ref[0, b]
        c, step = cols[:, :HEADS], cols[:, HEADS:]
        low = later_ref[b]
        left = spread(jnp.exp2(c[span - 1 : span] - c), hw)
        kdh = mm(keys_ref[b, :, :n], low) * left
        v = v_ref[b].astype(f32)
        step_wide = spread(step, hw)
        cols_ref[0, b] = gather_heads(v * kdh, hw)
        dlast_ref[b] = jnp.broadcast_to(
            jnp.sum(low.astype(f32) * h_ref[b].astype(f32), axis=0, keepdims=True), dlast_ref.shape[1:]
        )
        vw = (v * step_wide * left).astype(bf16)
        part = mm_nt(vw, low)

        @pl.when(i == 0)
        def _():
            dkacc[b] = part

        @pl.when(i != 0)
        def _():
            dkacc[b] += part

        @pl.when(i == groups - 1)
        def _():
            dk_ref[b] = dkacc[b]

        dv = dv_ref[b].astype(f32) + kdh * step_wide
        dcw, dcb = conv_back(
            dv, slope_ref[b].astype(f32), cin_ref[b].astype(f32), cw_ref[...], span, padded, cig_ref, b
        )
        if b == 0:
            dcw_ref[...] = dcw
            dcb_ref[...] = dcb
        else:
            dcw_ref[...] += dcw
            dcb_ref[...] += dcb


def back(later, carried, keys, v, dv, colpack, cin, cw, slope, bigs, splits, hw, span, collective_id):
    batch = v.shape[0]
    groups = colpack.shape[0]
    cb_w = HEADS * hw
    inner = groups * cb_w
    n = keys.shape[2] // 2
    ext = span + HALO
    taps = cw.shape[0]
    block = lambda rows: pl.BlockSpec((batch, rows, cb_w), lambda i: (0, 0, i))
    lanes = lambda rows: pl.BlockSpec((rows, cb_w), lambda i: (0, i))
    hbm = pl.BlockSpec(memory_space=pl.ANY)
    shapes = [(x.shape[0] // 32, x.shape[1]) for x in bigs]
    return pl.pallas_call(
        functools.partial(back_kernel, span, hw, groups, splits),
        grid=(groups,),
        in_specs=[
            block(n),
            block(n),
            pl.BlockSpec(keys.shape, lambda i: (0, 0, 0)),
            block(span),
            block(span),
            pl.BlockSpec((1,) + colpack.shape[1:], lambda i: (i, 0, 0, 0)),
            block(ext),
            lanes(taps),
            block(span),
        ]
        + [hbm] * len(bigs),
        out_specs=[
            block(ext),
            pl.BlockSpec((1, batch, span, HEADS), lambda i: (i, 0, 0, 0)),
            pl.BlockSpec((batch, span, n), lambda i: (0, 0, 0)),
            lanes(taps),
            lanes(1),
            block(8),
        ]
        + [pl.BlockSpec(s, lambda i: (0, 0)) for s in shapes],
        out_shape=[
            jax.ShapeDtypeStruct((batch, ext, inner), bf16),
            jax.ShapeDtypeStruct((groups, batch, span, HEADS), f32),
            jax.ShapeDtypeStruct((batch, span, n), f32),
            jax.ShapeDtypeStruct((taps, inner), f32),
            jax.ShapeDtypeStruct((1, inner), f32),
            jax.ShapeDtypeStruct((batch, 8, inner), f32),
        ]
        + [jax.ShapeDtypeStruct(s, f32) for s in shapes],
        scratch_shapes=[
            pltpu.VMEM((span + 32, cb_w), f32),
            pltpu.VMEM((batch, span, n), f32),
        ]
        + sum([Scatter.scratch(s[0], s[1], sp) for s, sp in zip(shapes, splits)], []),
        compiler_params=pltpu.CompilerParams(
            collective_id=collective_id if bigs else None,
            has_side_effects=bool(bigs),
            vmem_limit_bytes=58 * 1024 * 1024,
        ),
    )(later, carried, keys, v, dv, colpack, cin, cw, slope, *bigs)


def keys_back_kernel(span, dk_ref, dk2_ref, dq_ref, cin_ref, cw_ref, slope_ref, cig_ref, dcw_ref, dcb_ref, padded):
    batch = dk_ref.shape[0]
    padded[...] = jnp.zeros_like(padded)
    for b in range(batch):
        dv = jnp.concatenate([dk_ref[b] + dk2_ref[b], dq_ref[b]], axis=1)
        dcw, dcb = conv_back(
            dv, slope_ref[b].astype(f32), cin_ref[b].astype(f32), cw_ref[...], span, padded, cig_ref, b
        )
        if b == 0:
            dcw_ref[...] = dcw
            dcb_ref[...] = dcb
        else:
            dcw_ref[...] += dcw
            dcb_ref[...] += dcb


def keys_backward(dk, dk2, dq, cin, cw, slope, span):
    batch, ext, width = cin.shape
    return pl.pallas_call(
        functools.partial(keys_back_kernel, span),
        in_specs=[pl.BlockSpec(memory_space=pltpu.VMEM)] * 6,
        out_specs=[pl.BlockSpec(memory_space=pltpu.VMEM)] * 3,
        out_shape=[
            jax.ShapeDtypeStruct(cin.shape, bf16),
            jax.ShapeDtypeStruct(cw.shape, f32),
            jax.ShapeDtypeStruct((1, width), f32),
        ],
        scratch_shapes=[pltpu.VMEM((span + 32, width), f32)],
        compiler_params=params_of(40),
    )(dk, dk2, dq, cin, cw, slope)


def tail_kernel(span, splits, with_small, *refs):
    count = len(splits)
    (cig_ref, wc_ref, dgate_ref, wg_ref, keys_ref, wk_ref, low_ref, wd_ref) = refs[:8]
    resid_ref, mg_ref, gain_ref, parts_ref = refs[8:12]
    bigs = refs[12 : 12 + count]
    grad_ref, sums_ref = refs[12 + count : 14 + count]
    outs = refs[14 + count : 14 + 2 * count]
    rest = refs[14 + 2 * count :]
    acc, rim, rim_in, value, halo_send, halo_recv = rest[:6]
    i = pl.program_id(0)
    steps = pl.num_programs(0)
    half = steps // 2
    batch, _, width = resid_ref.shape
    ext = span + HALO
    chain = Chain(True, rim, rim_in, halo_send, halo_recv)
    place = Place() if count else None
    plan = small = None
    times = []
    if count:
        plan = Scatter(place, bigs[0], outs[0], *rest[6:13], splits[0])
        times = plan.steps()
        small = Small(place, value, sums_ref, *rest[13:17])

    @pl.when(i == 0)
    def _():
        greet_all(place, chain, (place.to_across,) if count else ())

    slots = TAIL_STEPS
    early = [(t, s) for t, s in times if t <= tail_start(slots - 1)]
    late = [s for t, s in times if t > tail_start(slots - 1)]
    at = {}
    for time, step in early:
        at.setdefault(min(k for k in range(slots) if tail_start(k) >= time), []).append(step)
    for slot, some in at.items():

        @pl.when(i == slot)
        def _(some=some):
            for step in some:
                step()

    flat = lambda ref: ref[...].reshape(batch * ext, ref.shape[2])

    @pl.when(i == 0)
    def _():
        acc[...] = mm_nt(flat(cig_ref), wc_ref[...])
        acc[...] += mm_nt(flat(keys_ref), wk_ref[...])
        acc[...] += mm_nt(flat(low_ref), wd_ref[...])

    @pl.when(jnp.logical_and(i > 0, i < half))
    def _():
        acc[...] += mm_nt(flat(cig_ref), wc_ref[...])

    @pl.when(i == half - 1)
    def _():
        for b in range(batch):
            rim[0, b] = acc[b * ext : b * ext + HALO].astype(bf16)

        @pl.when(chain.has_next)
        def _():
            chain.copy(0).start()

    @pl.when(i >= half)
    def _():
        for b in range(batch):
            rows = slice(b * ext + HALO, (b + 1) * ext)
            acc[rows] += mm_nt(dgate_ref[b], wg_ref[...])

    @pl.when(i == steps - 1)
    def _():
        @pl.when(chain.has_prev)
        def _():
            chain.copy(0).wait_recv()
            for b in range(batch):
                rows = slice((b + 1) * ext - HALO, (b + 1) * ext)
                acc[rows] += rim_in[0, b].astype(f32)

        total = jnp.zeros((1, width), f32)
        for b in range(batch):
            grad = acc[b * ext + HALO : (b + 1) * ext]
            x = resid_ref[b].astype(f32)
            rs = lax.rsqrt(jnp.mean(x * x, axis=-1, keepdims=True) + epsilon)
            nz = x * rs
            fg = grad * gain_ref[...]
            total = total + jnp.sum(grad * nz, axis=0, keepdims=True)
            mean = jnp.mean(fg * nz, axis=-1, keepdims=True)
            grad_ref[b] = (mg_ref[b].astype(f32) + rs * (fg - nz * mean)).astype(bf16)
        lead = width // 128
        value[lead:] = parts_ref[lead:]
        for r in range(lead):
            value[r : r + 1] = total[:, r * 128 : (r + 1) * 128]
        if small is None:
            sums_ref[...] = value[...]
        else:
            spots = [len(late) * k // 6 for k in range(6)]
            for j, step in enumerate(late):
                for k in range(6):
                    if spots[k] == j:
                        small.go(k)
                step()

        @pl.when(chain.has_next)
        def _():
            chain.copy(0).wait_send()


TAIL_STEPS = 12


def tail_start(k):
    return 2.2 * k


def tail(cig, w_conv, dgate, w_gate, cig_keys, step_low, w_dt, resid, mg, gain, parts, bigs, splits, span, collective_id):
    batch, ext, inner = cig.shape
    width = resid.shape[2]
    cb_w = inner // (TAIL_STEPS // 2)
    half = TAIL_STEPS // 2
    keys_w = cig_keys.shape[2]
    whole = lambda shape: pl.BlockSpec(shape, lambda i: (0,) * len(shape))
    first = lambda i: jnp.minimum(i, half - 1)
    then = lambda i: jnp.maximum(i - half, 0)
    hbm = pl.BlockSpec(memory_space=pl.ANY)
    shapes = [(x.shape[0] // 32, x.shape[1]) for x in bigs]
    return pl.pallas_call(
        functools.partial(tail_kernel, span, splits, bool(bigs)),
        grid=(TAIL_STEPS,),
        in_specs=[
            pl.BlockSpec((batch, ext, cb_w), lambda i: (0, 0, first(i))),
            pl.BlockSpec((width, cb_w), lambda i: (0, first(i))),
            pl.BlockSpec((batch, span, cb_w), lambda i: (0, 0, then(i))),
            pl.BlockSpec((width, cb_w), lambda i: (0, then(i))),
            whole(cig_keys.shape),
            pl.BlockSpec((width, keys_w), lambda i: (0, inner // keys_w)),
            whole(step_low.shape),
            whole(w_dt.shape),
            whole(resid.shape),
            whole(mg.shape),
            whole(gain.shape),
            whole(parts.shape),
        ]
        + [hbm] * len(bigs),
        out_specs=[whole(resid.shape), whole(parts.shape)] + [whole(s) for s in shapes],
        out_shape=[jax.ShapeDtypeStruct(resid.shape, bf16), jax.ShapeDtypeStruct(parts.shape, f32)]
        + [jax.ShapeDtypeStruct(s, f32) for s in shapes],
        scratch_shapes=[
            pltpu.VMEM((batch * ext, width), f32),
            pltpu.VMEM((1, batch, HALO, width), bf16),
            pltpu.VMEM((1, batch, HALO, width), bf16),
            pltpu.VMEM(parts.shape, f32),
            pltpu.SemaphoreType.DMA((1,)),
            pltpu.SemaphoreType.DMA((1,)),
        ]
        + sum([Scatter.scratch(s[0], s[1], sp) for s, sp in zip(shapes, splits)], [])
        + (Small.scratch(parts.shape) if bigs else []),
        compiler_params=pltpu.CompilerParams(
            collective_id=collective_id, has_side_effects=True, vmem_limit_bytes=60 * 1024 * 1024
        ),
    )(cig, w_conv, dgate, w_gate, cig_keys, w_conv, step_low, w_dt, resid, mg, gain, parts, *bigs)


def own_kernels():
    return lax.axis_size("dp") == 4 and lax.axis_size("seq") == 8


def gather_rows(shards, parts):
    return [
        lax.all_gather(s[:, p[0] : p[0] + p[1]], ("dp", "seq"), axis=0, tiled=True)
        for s, p in zip(shards, parts)
    ]


def scatter_rows(bigs, splits, small, collective_id):
    if own_kernels():
        return scatter(bigs, splits, small, collective_id)
    outs = [lax.psum_scatter(b, ("dp", "seq"), scatter_dimension=0, tiled=True).astype(f32) for b in bigs]
    return outs + ([] if small is None else [lax.psum(small, ("dp", "seq"))])


def half_of(width):
    return (width // 2 + 127) // 128 * 128


def ungrouped(cols):
    groups, batch, span, each = cols.shape
    return jnp.transpose(cols, (1, 2, 0, 3)).reshape(batch, span, groups * each)


def gate_start(k, blocks):
    return 1.0 * k if k < blocks else 1.0 * blocks + 1.6 * (k - blocks)


def back_start(k):
    return 2.9 * k


def on_device(
    resid_in, out_grad, lengths, norm_gain, in_proj, dt_proj, conv_weight, conv_bias, dt_bias, a_log,
    skip_scale, gate_gain, out_proj,
):
    batch, span, width = resid_in.shape
    inner = gate_gain.shape[0]
    heads = a_log.shape[0]
    hw = inner // heads
    n = (in_proj.shape[1] - 2 * inner) // 2
    cb_w = HEADS * hw
    positions = lax.axis_index("seq") * span + lax.iota(jnp.int32, span)
    mask = (positions[None, :] < lengths[:, None]).astype(f32)[..., None]

    conv_cols = in_proj.shape[1] - inner
    dt_pad = (-(conv_cols + heads)) % 128
    conv_all = conv_cols + heads + dt_pad
    dt_shard = jnp.pad(dt_proj, ((0, 0), (0, dt_pad)))
    shards, parts = (
        [in_proj, dt_shard, in_proj, out_proj],
        [(inner, conv_cols), (0, heads + dt_pad), (0, inner), (0, width)],
    )
    splits = [half_of(conv_cols), heads + dt_pad, half_of(inner), half_of(width)]
    later_splits = splits[2:]
    inside = own_kernels()
    weights = shards if inside else gather_rows(shards, parts)

    halo = shifted(resid_in[:, span - HALO :], "seq", 1)
    resid_wide = resid_in.astype(f32)
    rate = -jnp.exp(a_log)
    lane_pad = (0, (-heads) % 128)
    skip_wide = jnp.repeat(skip_scale, hw)[None]
    gain_wide = gate_gain[None]
    cw_keys, cw_vals = conv_weight[:, inner:], conv_weight[:, :inner]
    made = front(
        resid_in, halo, norm_gain[None], conv_weight, conv_bias[None], jnp.pad(dt_bias, lane_pad)[None],
        jnp.pad(rate, lane_pad)[None], skip_wide, gain_wide, weights, parts, splits if inside else [], hw, heads, n, 1,
    )
    x2, keys, slope_keys, cin_keys, colpack, rowpack, raw, step = made[:8]
    v, slope_vals, cin_vals, y, carried, gate, normed_out, rg = made[8:16]
    full_conv, full_dt, full_gate, full_out = [w.reshape(-1, w.shape[-1]) for w in (made[16:] if inside else weights)]
    x_ext = x2.reshape(batch, span + HALO, width)
    mixer_out = jnp.dot(normed_out, full_out, preferred_element_type=f32)
    output = (mask * (resid_wide + mixer_out)).astype(bf16)

    mixer_grad = (mask * out_grad.astype(f32)).astype(bf16)
    mean = jnp.sum(mixer_grad.astype(f32) * mixer_out, axis=-1, keepdims=True) * (1.0 / inner)
    norms = jnp.concatenate([rg[..., :1], mean, jnp.zeros((batch, span, 6), f32)], axis=-1)
    grad_out = jnp.einsum("bsi,bsd->id", normed_out, mixer_grad, preferred_element_type=f32).astype(bf16)
    made = gate_backward(
        mixer_grad, full_out, y, gate, norms, gain_wide, v, keys, colpack, rowpack, carried, skip_wide,
        [grad_out] if inside else [], later_splits[1:] if inside else [], hw, span, 7,
    )
    dgate, dv, later, cols_one, dq, dk, dgain, dskip = made[:8]
    (sum_out,) = made[8:] if inside else scatter_rows([grad_out], later_splits[1:], None, 5)
    x_rows = x_ext[:, HALO:]
    grad_gate = jnp.einsum("bsd,bse->de", x_rows, dgate, preferred_element_type=f32).astype(bf16)
    made = back(
        later, carried, keys, v, dv, colpack, cin_vals, cw_vals, slope_vals,
        [grad_gate] if inside else [], later_splits[:1] if inside else [], hw, span, 2,
    )
    cig_vals, cols_two, dk2, dcw_vals, dcb_vals, dlast = made[:6]
    (sum_gate,) = made[6:] if inside else scatter_rows([grad_gate], later_splits[:1], None, 5)
    cig_keys, dcw_keys, dcb_keys = keys_backward(dk, dk2, dq, cin_keys, cw_keys, slope_keys, span)

    raw, step = raw[..., :heads], step[..., :heads]
    rise = ungrouped(cols_one[..., :HEADS])
    direct = ungrouped(cols_one[..., HEADS:])
    ahead = ungrouped(cols_two)
    moved = ahead * step
    tri = causal(span, False).astype(f32)
    block_decay = jnp.exp2(colpack[:, :, span - 1, :HEADS]).transpose(1, 0, 2).reshape(batch, heads)
    last = jnp.sum(moved, axis=1) + dlast[:, 0].reshape(batch, heads, hw).sum(-1) * block_decay
    dlog = rise - moved
    dlog = jnp.einsum("ts,bth->bsh", tri, dlog, precision=highest) + last[:, None, :]
    grad_a = jnp.sum(dlog * step, axis=(0, 1)) * rate
    step_grad = direct + ahead + dlog * rate
    dt_grad = step_grad * jax.nn.sigmoid(raw)
    grad_bias = jnp.sum(dt_grad, axis=(0, 1))
    step_low = jnp.pad(dt_grad.astype(bf16), ((0, 0), (HALO, 0), (0, dt_pad)))

    cig = jnp.concatenate([cig_vals, cig_keys, step_low], axis=-1)
    grad_conv = jnp.einsum("bsd,bse->de", x_ext, cig, preferred_element_type=f32).astype(bf16)
    pieces = (
        norm_gain,
        jnp.concatenate([dcw_vals, dcw_keys], axis=1),
        jnp.concatenate([dcb_vals, dcb_keys], axis=1)[0],
        dgain[0],
        grad_bias,
        grad_a,
        dskip[0].reshape(heads, hw).sum(-1),
    )
    flat = jnp.concatenate([p.reshape(-1) for p in pieces])
    packed = jnp.pad(flat, (0, (-flat.size) % 1024)).reshape(-1, 128)
    made = tail(
        cig_vals, full_conv, dgate, full_gate, cig_keys, step_low, full_dt, resid_in, mixer_grad,
        norm_gain[None], packed, [grad_conv] if inside else [], [half_of(conv_all)] if inside else [], span, 6,
    )
    input_grad, small = made[:2]
    if inside:
        sum_conv = made[2]
    else:
        sum_conv, small = scatter_rows([grad_conv], [half_of(conv_all)], small, 6)
    flat, sums, at = small.reshape(-1), [], 0
    for p in pieces:
        sums.append(flat[at : at + p.size].reshape(p.shape))
        at += p.size
    sum_norm, sum_cw, sum_cb, sum_gain, sum_bias, sum_a, sum_skip = sums
    return (
        output,
        input_grad,
        jnp.concatenate([sum_gate, sum_conv[:, :conv_cols]], axis=1),
        sum_conv[:, conv_cols : conv_cols + heads],
        sum_out,
        sum_norm,
        sum_cw,
        sum_cb,
        sum_bias,
        sum_a,
        sum_skip,
        sum_gain,
    )


def solution(mesh):
    rows = P("dp", "seq", None)
    shard = P(("dp", "seq"), None)
    return jax.shard_map(
        on_device,
        mesh=mesh,
        in_specs=(rows, rows, P("dp"), P(), shard, shard, P(), P(), P(), P(), P(), P(), shard),
        out_specs=(rows, rows, shard, shard, shard, P(), P(), P(), P(), P(), P(), P()),
        check_vma=False,
    )
```

```python
import functools

import jax
import jax.numpy as jnp
from jax import lax
from jax.experimental import pallas as pl
from jax.experimental.pallas import tpu as pltpu
from jax.sharding import PartitionSpec as P

epsilon = 1e-05
highest = lax.Precision.HIGHEST
HALO = 16
HEADS = 8
LOG2E = 1.4426950408889634
f32 = jnp.float32
bf16 = jnp.bfloat16
MESH = pl.DeviceIdType.MESH


def mm(a, b):
    return lax.dot_general(a, b, (((1,), (0,)), ((), ())), preferred_element_type=f32)


def mm_nt(a, b):
    return lax.dot_general(a, b, (((1,), (1,)), ((), ())), preferred_element_type=f32)


def mm_tn(a, b):
    return lax.dot_general(a, b, (((0,), (0,)), ((), ())), preferred_element_type=f32)


def spread(cols, width):
    rows, heads = cols.shape
    low_half = lax.broadcasted_iota(jnp.int32, (rows, 2 * width), 1) < width
    pairs = [
        jnp.where(low_half, cols[:, i : i + 1], cols[:, i + 1 : i + 2]) for i in range(0, heads, 2)
    ]
    return jnp.concatenate(pairs, axis=1)


def gather_heads(x, width):
    rows, total = x.shape
    low_half = lax.broadcasted_iota(jnp.int32, (rows, 2 * width), 1) < width
    head_lane = lax.broadcasted_iota(jnp.int32, (rows, total // width), 1)
    out = jnp.zeros((rows, total // width), f32)
    for i in range(total // (2 * width)):
        pair = x[:, i * 2 * width : (i + 1) * 2 * width]
        one = jnp.sum(jnp.where(low_half, pair, 0.0), axis=1, keepdims=True)
        two = jnp.sum(jnp.where(low_half, 0.0, pair), axis=1, keepdims=True)
        out = jnp.where(head_lane == 2 * i, one, out)
        out = jnp.where(head_lane == 2 * i + 1, two, out)
    return out


def silu_parts(v):
    sg = 1.0 / (1.0 + jnp.exp(-v))
    return v * sg, sg


def silu_slope(v):
    act, sg = silu_parts(v)
    return act, sg * (1.0 + v * (1.0 - sg))


def conv_pre(a, cw, cb, span):
    first = HALO - (cw.shape[0] - 1)
    out = cb
    for k in range(cw.shape[0]):
        out = out + cw[k : k + 1] * a[first + k : first + k + span]
    return out


def params_of(limit_mb, dims=None):
    return pltpu.CompilerParams(vmem_limit_bytes=limit_mb * 1024 * 1024, dimension_semantics=dims)


def causal(span, transposed):
    one = lax.broadcasted_iota(jnp.int32, (span, span), 0)
    two = lax.broadcasted_iota(jnp.int32, (span, span), 1)
    return (one <= two) if transposed else (one >= two)


class Place:
    def __init__(self):
        self.dp = lax.axis_index("dp")
        self.seq = lax.axis_index("seq")
        y, x = self.dp // 2, self.dp % 2
        self.z, self.core = self.seq // 2, self.seq % 2
        self.dx = 2 * y + (1 - x)
        self.dy = 2 * (1 - y) + x
        self.dxy = 2 * (1 - y) + (1 - x)
        self.to_x = (self.dx, self.seq)
        self.to_y = (self.dy, self.seq)
        self.to_core = (self.dp, 2 * self.z + 1 - self.core)
        self.to_up = (self.dp, 2 * jnp.minimum(self.z + 1, 3) + self.core)
        self.to_down = (self.dp, 2 * jnp.maximum(self.z - 1, 0) + self.core)
        self.to_across = (self.dp, 2 * jnp.where(self.z < 2, self.z + 2, self.z - 2) + self.core)
        self.has_up = self.z < 3
        self.has_down = self.z > 0

    def near(self, k):
        z = self.z
        return (z, z + 1 - 2 * (z % 2), jnp.where(z < 2, 2, 1), jnp.where(z < 2, 3, 0))[k]

    def greet(self, others=()):
        barrier = pltpu.get_barrier_semaphore()
        for device in (self.to_x, self.to_y, self.to_core) + tuple(others):
            pl.semaphore_signal(barrier, inc=1, device_id=device, device_id_type=MESH)

        @pl.when(self.has_up)
        def _():
            pl.semaphore_signal(barrier, inc=1, device_id=self.to_up, device_id_type=MESH)

        @pl.when(self.has_down)
        def _():
            pl.semaphore_signal(barrier, inc=1, device_id=self.to_down, device_id_type=MESH)

        ends = self.has_up.astype(jnp.int32) + self.has_down.astype(jnp.int32)
        pl.semaphore_wait(barrier, 3 + len(others) + ends)


GATHER_KINDS = 11


def gather_steps(place, shard, full, split, own_sem, send, recv):
    width = full.shape[3]
    z, core = place.z, place.core
    every, left, right = pl.ds(0, width), pl.ds(0, split), pl.ds(split, width - split)
    two = split < width

    def view(d, zz, cc, cols):
        return full.at[d * 4 + zz, cc, :, cols]

    def copy(kind, slot, device, d, zz, cc, cols, src=None):
        dst = view(d, zz, cc, cols)
        return pltpu.make_async_remote_copy(
            src_ref=dst if src is None else src,
            dst_ref=dst,
            send_sem=send.at[kind, slot],
            recv_sem=recv.at[kind, slot],
            device_id=device,
            device_id_type=MESH,
        )

    def pieces(k):
        zk = place.near(k)
        src = shard if k == 0 else None
        dp = place.dp
        return dict(
            x=copy(2, k, place.to_x, dp, zk, core, every, src),
            y=copy(3, k, place.to_y, dp, zk, core, every, src),
            own=copy(6, k, place.to_core, dp, zk, core, every, src),
        )

    def along(k, up):
        zk = place.near(k)
        src = shard if k == 0 else None
        device = place.to_up if up else place.to_down
        dst = view(place.dp, zk, core, every)
        return pltpu.make_async_remote_copy(
            src_ref=dst if src is None else src,
            dst_ref=dst,
            send_sem=send.at[0 if up else 1, k],
            recv_sem=recv.at[0, zk],
            device_id=device,
            device_id_type=MESH,
        )

    def arrive(k):
        zk = place.near(k)
        if k > 0:
            along(k, True).wait_recv()

        @pl.when(jnp.logical_and(zk <= z, place.has_up))
        def _():
            along(k, True).start()

        @pl.when(jnp.logical_and(zk >= z, place.has_down))
        def _():
            along(k, False).start()

        pieces(k)["own"].start()

    def beyond(k):
        made = pieces(k)
        made["x"].start()
        made["y"].start()

    def cross(k):
        zk = place.near(k)
        return (
            copy(2, k, place.to_x, place.dx, zk, core, every),
            copy(3, k, place.to_y, place.dy, zk, core, every),
            copy(4, k, place.to_y, place.dx, zk, core, left),
            copy(5, k, place.to_x, place.dy, zk, core, right) if two else None,
            copy(7, k, place.to_core, place.dx, zk, core, every),
            copy(8, k, place.to_core, place.dy, zk, core, every),
        )

    def forward(k):
        from_x, from_y, left_on, right_on, core_x, core_y = cross(k)
        from_x.wait_recv()
        left_on.start()
        core_x.start()
        from_y.wait_recv()
        if two:
            right_on.start()
        core_y.start()

    def corner(k):
        zk = place.near(k)
        return (
            copy(4, k, place.to_y, place.dxy, zk, core, left),
            copy(5, k, place.to_x, place.dxy, zk, core, right) if two else None,
            copy(9, k, place.to_core, place.dxy, zk, core, left),
            copy(10, k, place.to_core, place.dxy, zk, core, right) if two else None,
        )

    def last(k):
        from_y, from_x, core_left, core_right = corner(k)
        from_y.wait_recv()
        core_left.start()
        if two:
            from_x.wait_recv()
            core_right.start()

    def mine():
        return pltpu.make_async_copy(shard, view(place.dp, z, core, every), own_sem)

    def along_z(k):
        if k == 0:
            mine().start()
        arrive(k)

    def finish():
        mine().wait()
        other = 1 - core
        for k in range(4):
            zk = place.near(k)
            for kind, d, cols in (
                (6, place.dp, every), (7, place.dx, every), (8, place.dy, every),
                (9, place.dxy, left), (10, place.dxy, right),
            ):
                if kind == 10 and not two:
                    continue
                copy(kind, k, place.to_core, d, zk, other, cols).wait_recv()
        for k in range(4):
            zk = place.near(k)

            @pl.when(jnp.logical_and(zk <= z, place.has_up))
            def _():
                along(k, True).wait_send()

            @pl.when(jnp.logical_and(zk >= z, place.has_down))
            def _():
                along(k, False).wait_send()

            made = pieces(k)
            made["x"].wait_send()
            made["y"].wait_send()
            made["own"].wait_send()
            for one in cross(k)[2:] + corner(k)[2:]:
                if one is not None:
                    one.wait_send()

    return along_z, beyond, forward, last, finish


def gather_groups(place, shard, full, split, own_sem, send, recv):
    width = full.shape[3]
    z, core = place.z, place.core
    every, left, right = pl.ds(0, width), pl.ds(0, split), pl.ds(split, width - split)

    def along(k, up):
        zk = place.near(k)
        dst = full.at[place.dp * 4 + zk, core]
        return pltpu.make_async_remote_copy(
            src_ref=shard if k == 0 else dst,
            dst_ref=dst,
            send_sem=send.at[0 if up else 1, k],
            recv_sem=recv.at[0, zk],
            device_id=place.to_up if up else place.to_down,
            device_id_type=MESH,
        )

    def group(kind, device, d, cc, cols):
        some = full.at[pl.ds(d * 4, 4), cc, :, cols]
        return pltpu.make_async_remote_copy(
            src_ref=some, dst_ref=some, send_sem=send.at[kind, 0], recv_sem=recv.at[kind, 0],
            device_id=device, device_id_type=MESH,
        )

    def mine():
        return pltpu.make_async_copy(shard, full.at[place.dp * 4 + z, core], own_sem)

    def moves(k):
        zk = place.near(k)
        return (
            (jnp.logical_and(zk <= z, place.has_up), along(k, True)),
            (jnp.logical_and(zk >= z, place.has_down), along(k, False)),
        )

    def along_z(k):
        if k == 0:
            mine().start()
        else:
            along(k, True).wait_recv()
        for flag, copy in moves(k):

            @pl.when(flag)
            def _(copy=copy):
                copy.start()

    p = place
    sides = lambda: (group(2, p.to_x, p.dp, core, every), group(3, p.to_y, p.dp, core, every))
    halves = lambda: (group(4, p.to_y, p.dx, core, left), group(5, p.to_x, p.dy, core, right))
    owners = (p.dp, p.dx, p.dy, p.dxy)
    cores = lambda cc: [group(6 + j, p.to_core, d, cc, every) for j, d in enumerate(owners)]

    def beyond():
        mine().wait()
        for copy in sides():
            copy.start()
        cores(core)[0].start()

    def forward():
        from_x, from_y = group(2, p.to_x, p.dx, core, every), group(3, p.to_y, p.dy, core, every)
        from_x.wait_recv()
        halves()[0].start()
        from_y.wait_recv()
        halves()[1].start()
        for copy in cores(core)[1:3]:
            copy.start()

    def last():
        group(4, p.to_y, p.dxy, core, left).wait_recv()
        group(5, p.to_x, p.dxy, core, right).wait_recv()
        cores(core)[3].start()

    def finish():
        for copy in cores(1 - core):
            copy.wait_recv()
        for k in range(4):
            for flag, copy in moves(k):

                @pl.when(flag)
                def _(copy=copy):
                    copy.wait_send()

        for copy in sides() + halves() + tuple(cores(core)):
            copy.wait_send()

    return along_z, beyond, forward, last, finish


def gather_scratch():
    return [
        pltpu.SemaphoreType.DMA,
        pltpu.SemaphoreType.DMA((GATHER_KINDS, 4)),
        pltpu.SemaphoreType.DMA((GATHER_KINDS, 4)),
    ]


def part_of(ref, part):
    return ref.at[:, pl.ds(part[0], part[1])]


class Scatter:
    def __init__(self, place, big, out, own, land_core, land_xy, land_z, local, send, recv, split):
        self.place, self.big, self.out = place, big, out
        self.own, self.land_core, self.land_xy, self.land_z = own, land_core, land_xy, land_z
        self.local, self.send, self.recv = local, send, recv
        self.rows, self.width = out.shape
        self.split = split
        self.left, self.right = slice(0, split), slice(split, self.width)

    def groups(self):
        p = self.place
        return (p.dxy, p.dx, p.dy, p.dp)

    def far(self, k):
        return self.place.near(3 - k)

    def source(self, d, zz, cc):
        start = pl.multiple_of((d * 8 + zz * 2 + cc) * self.rows, 16)
        return self.big.at[pl.ds(start, self.rows)]

    def remote(self, src, dst, kind, slot, device):
        return pltpu.make_async_remote_copy(
            src_ref=src, dst_ref=dst, send_sem=self.send.at[kind, slot], recv_sem=self.recv.at[kind, slot],
            device_id=device, device_id_type=MESH,
        )

    def to_other(self, i, k):
        p = self.place
        src = self.source(self.groups()[i], self.far(k), 1 - p.core)
        return self.remote(src, self.land_core.at[i, k], i, k, p.to_core)

    def load(self, i, k):
        p = self.place
        return pltpu.make_async_copy(
            self.source(self.groups()[i], self.far(k), p.core), self.own.at[i, k], self.local.at[i, k]
        )

    def start(self, k):
        for i in range(4):
            self.to_other(i, k).start()
            self.load(i, k).start()

    def join(self, i, k):
        self.load(i, k).wait()
        self.to_other(i, k).wait_recv()
        self.own[i, k] = self.own[i, k] + self.land_core[i, k]

    def side(self, kind, k):
        p = self.place
        left, right = pl.ds(0, self.split), pl.ds(self.split, self.width - self.split)
        group, cols, device = (
            (0, left, p.to_y),
            (0, right, p.to_x),
            (2, left, p.to_y),
            (1, right, p.to_x),
            (2, right, p.to_y),
            (1, left, p.to_x),
        )[kind]
        size = self.split if cols is left else self.width - self.split
        return self.remote(
            self.own.at[group, k, :, cols], self.land_xy.at[kind, k, :, pl.ds(0, size)], 4 + kind, k, device
        )

    def take(self, kind, group, cols, k):
        self.side(kind, k).wait_recv()
        size = cols.stop - cols.start
        self.own[group, k, :, cols] = self.own[group, k, :, cols] + self.land_xy[kind, k, :, 0:size]

    def corner(self, k):
        self.join(0, k)
        self.side(0, k).start()
        self.side(1, k).start()

    def sides(self, k):
        self.join(1, k)
        self.side(3, k).start()
        self.join(2, k)
        self.side(2, k).start()

    def turns(self, k):
        self.take(0, 1, self.left, k)
        self.side(5, k).start()
        self.take(1, 2, self.right, k)
        self.side(4, k).start()

    def along(self, k, up):
        p = self.place
        zk = self.far(k)
        return pltpu.make_async_remote_copy(
            src_ref=self.own.at[3, k],
            dst_ref=self.land_z.at[0 if up else 1, zk],
            send_sem=self.send.at[10, k],
            recv_sem=self.recv.at[10 if up else 11, zk],
            device_id=p.to_up if up else p.to_down,
            device_id_type=MESH,
        )

    def rising(self, k):
        return self.far(k) > self.place.z

    def behind(self, k):
        p = self.place
        rising = self.rising(k)
        return jnp.logical_or(
            jnp.logical_and(rising, p.has_down), jnp.logical_and(jnp.logical_not(rising), p.has_up)
        )

    def send_along(self, k):
        @pl.when(self.rising(k))
        def _():
            self.along(k, True).start()

        @pl.when(jnp.logical_not(self.rising(k)))
        def _():
            self.along(k, False).start()

    def mine(self, k):
        self.join(3, k)
        self.take(2, 3, self.left, k)
        self.take(3, 3, self.right, k)
        self.take(5, 3, self.left, k)
        self.take(4, 3, self.right, k)
        if k < 3:

            @pl.when(jnp.logical_not(self.behind(k)))
            def _():
                self.send_along(k)

    def line(self, k):
        zk = self.far(k)

        @pl.when(jnp.logical_and(self.behind(k), self.rising(k)))
        def _():
            self.along(k, True).wait_recv()
            self.own[3, k] = self.own[3, k] + self.land_z[0, zk]

        @pl.when(jnp.logical_and(self.behind(k), jnp.logical_not(self.rising(k))))
        def _():
            self.along(k, False).wait_recv()
            self.own[3, k] = self.own[3, k] + self.land_z[1, zk]

        @pl.when(self.behind(k))
        def _():
            self.send_along(k)

    def result(self):
        p = self.place
        self.out[...] = self.own[3, 3].astype(f32)

        @pl.when(p.has_down)
        def _():
            self.along(3, True).wait_recv()
            self.out[...] += self.land_z[0, p.z].astype(f32)

        @pl.when(p.has_up)
        def _():
            self.along(3, False).wait_recv()
            self.out[...] += self.land_z[1, p.z].astype(f32)

    def drain(self):
        for k in range(4):
            for i in range(4):
                self.to_other(i, k).wait_send()
            for kind in range(6):
                self.side(kind, k).wait_send()
            if k < 3:
                self.along(k, True).wait_send()

    def steps(self):
        start, corner, sides, turns, mine, line = (
            self.start, self.corner, self.sides, self.turns, self.mine, self.line
        )
        return [
            (0, lambda: start(0)),
            (2, lambda: start(1)),
            (3, lambda: corner(0)),
            (4, lambda: sides(0)),
            (6, lambda: start(2)),
            (8, lambda: turns(0)),
            (9, lambda: corner(1)),
            (10, lambda: sides(1)),
            (12, lambda: start(3)),
            (14, lambda: mine(0)),
            (17, lambda: turns(1)),
            (18, lambda: corner(2)),
            (19, lambda: sides(2)),
            (22, lambda: line(0)),
            (23, lambda: mine(1)),
            (26, lambda: turns(2)),
            (27, lambda: corner(3)),
            (28, lambda: sides(3)),
            (31, lambda: line(1)),
            (32, lambda: mine(2)),
            (35, lambda: turns(3)),
            (40, lambda: line(2)),
            (42, lambda: mine(3)),
            (47, self.result),
            (50, self.drain),
        ]

    @staticmethod
    def scratch(rows, width, split):
        half = max(split, width - split)
        return [
            pltpu.VMEM((4, 4, rows, width), bf16),
            pltpu.VMEM((4, 4, rows, width), bf16),
            pltpu.VMEM((6, 4, rows, half), bf16),
            pltpu.VMEM((2, 4, rows, width), bf16),
            pltpu.SemaphoreType.DMA((4, 4)),
            pltpu.SemaphoreType.DMA((11, 4)),
            pltpu.SemaphoreType.DMA((12, 4)),
        ]


class Small:
    def __init__(self, place, value, out, sent, landed, send, recv):
        p = place
        self.value, self.out, self.sent, self.landed, self.send, self.recv = value, out, sent, landed, send, recv
        pair = 2 * (p.z + 1 - 2 * (p.z % 2)) + p.core
        self.devices = (p.to_core, p.to_x, p.to_y, (p.dp, pair), p.to_across)

    def copy(self, i):
        return pltpu.make_async_remote_copy(
            src_ref=self.sent.at[i], dst_ref=self.landed.at[i], send_sem=self.send.at[i],
            recv_sem=self.recv.at[i], device_id=self.devices[i], device_id_type=MESH,
        )

    def go(self, i):
        if i == 0:
            self.sent[0] = self.value[...]
            self.copy(0).start()
            return
        self.copy(i - 1).wait_recv()
        total = self.sent[i - 1] + self.landed[i - 1]
        if i < 5:
            self.sent[i] = total
            self.copy(i).start()
        else:
            self.out[...] = total
            for k in range(5):
                self.copy(k).wait_send()

    @staticmethod
    def scratch(shape):
        return [
            pltpu.VMEM((5,) + shape, f32),
            pltpu.VMEM((5,) + shape, f32),
            pltpu.SemaphoreType.DMA((5,)),
            pltpu.SemaphoreType.DMA((5,)),
        ]


def scatter_kernel(splits, with_small, *refs):
    count = len(splits)
    ins = count + (1 if with_small else 0)
    bigs, outs = refs[:count], refs[ins : ins + count]
    scratch = refs[2 * ins :]
    place = Place()
    place.greet((place.to_across,) if with_small else ())
    plans = [
        Scatter(place, bigs[i], outs[i], *scratch[7 * i : 7 * i + 7], splits[i]) for i in range(count)
    ]
    small = None
    if with_small:
        small = Small(place, refs[count], refs[ins + count], *scratch[7 * count :])
    small_at = {0: 0, 5: 1, 9: 2, 13: 3, 17: 4, 21: 5}
    for i, steps in enumerate(zip(*[plan.steps() for plan in plans])):
        for _, step in steps:
            step()
        if small and i in small_at:
            small.go(small_at[i])


def scatter(bigs, splits, small, collective_id):
    count = len(bigs)
    spec = pl.BlockSpec(memory_space=pl.ANY)
    vmem = pl.BlockSpec(memory_space=pltpu.VMEM)
    shapes = [(b.shape[0] // 32, b.shape[1]) for b in bigs]
    extra = [] if small is None else [small]
    scratch = sum([Scatter.scratch(s[0], s[1], sp) for s, sp in zip(shapes, splits)], [])
    if small is not None:
        scratch = scratch + Small.scratch(small.shape)
    return pl.pallas_call(
        functools.partial(scatter_kernel, splits, small is not None),
        in_specs=[spec] * count + [vmem] * len(extra),
        out_specs=[vmem] * (count + len(extra)),
        out_shape=[jax.ShapeDtypeStruct(s, f32) for s in shapes]
        + [jax.ShapeDtypeStruct(e.shape, f32) for e in extra],
        scratch_shapes=scratch,
        compiler_params=pltpu.CompilerParams(
            collective_id=collective_id, has_side_effects=True, vmem_limit_bytes=60 * 1024 * 1024
        ),
    )(*bigs, *extra)


class Chain:
    def __init__(self, backward, sent, landed, send, recv):
        self.sent, self.landed, self.send, self.recv = sent, landed, send, recv
        me, count = lax.axis_index("seq"), lax.axis_size("seq")
        turn = -1 if backward else 1
        self.place = count - 1 - me if backward else me
        self.has_prev = self.place > 0
        self.has_next = self.place < count - 1
        self.next = (lax.axis_index("dp"), jnp.clip(me + turn, 0, count - 1))
        self.prev = (lax.axis_index("dp"), jnp.clip(me - turn, 0, count - 1))

    def copy(self, k):
        return pltpu.make_async_remote_copy(
            src_ref=self.sent.at[k], dst_ref=self.landed.at[k], send_sem=self.send.at[k],
            recv_sem=self.recv.at[k], device_id=self.next, device_id_type=MESH,
        )

    def pass_on(self, k, decay, local):
        @pl.when(self.has_prev)
        def _():
            self.copy(k).wait_recv()

        @pl.when(jnp.logical_not(self.has_prev))
        def _():
            self.landed[k] = jnp.zeros_like(self.landed[k])

        @pl.when(self.has_next)
        def _():
            self.sent[k] = (decay() * self.landed[k].astype(f32) + local()).astype(bf16)
            self.copy(k).start()

    def drain(self):
        @pl.when(self.has_next)
        def _():
            for k in range(self.sent.shape[0]):
                self.copy(k).wait_send()

    @staticmethod
    def scratch(count, n, size):
        return [
            pltpu.VMEM((count, n, size), bf16),
            pltpu.VMEM((count, n, size), bf16),
            pltpu.SemaphoreType.DMA((count,)),
            pltpu.SemaphoreType.DMA((count,)),
        ]


def greet_all(place, chain, others=()):
    barrier = pltpu.get_barrier_semaphore()
    flags = [chain.has_prev, chain.has_next]
    devices = [chain.prev, chain.next]
    total = chain.has_prev.astype(jnp.int32) + chain.has_next.astype(jnp.int32)
    if place is not None:
        flags += [place.has_up, place.has_down]
        devices += [place.to_up, place.to_down]
        total = total + place.has_up.astype(jnp.int32) + place.has_down.astype(jnp.int32) + 3 + len(others)
        for device in (place.to_x, place.to_y, place.to_core) + tuple(others):
            pl.semaphore_signal(barrier, inc=1, device_id=device, device_id_type=MESH)
    for flag, device in zip(flags, devices):

        @pl.when(flag)
        def _(device=device):
            pl.semaphore_signal(barrier, inc=1, device_id=device, device_id_type=MESH)

    pl.semaphore_wait(barrier, total)


def front_time(slot):
    if slot < 18:
        return 60 + 1.4 * slot
    if slot < 36:
        return 85 + 1.4 * (slot - 18)
    return 110 + 0.95 * (slot - 36)


GATE_STEPS = ((76, "f"), (90, "l"), (94, "end"))
OUT_STEPS = ((62, "z", 2), (70, "z", 3), (77, "b"), (114, "f"), (126, "l"))


def front_kernel(span, hw, heads, splits, parts, *refs):
    count = len(splits)
    (resid_ref, ngain_ref, cw_ref, cb_ref, bias_ref, rate_ref, skip_ref, gain_ref) = refs[:8]
    given = refs[8:12]
    x_ref, keys_ref, kslope_ref, kcin_ref, col_ref, row_ref, raw_ref, step_ref = refs[12:20]
    rows_ref, slope_ref, cin_ref, y_ref, carried_ref, gate_ref, no_ref, rg_ref = refs[20:28]
    fulls = refs[28 : 28 + count] if count else given
    halo_ref, halo_send, halo_recv = refs[28 + count : 31 + count]
    rest = refs[31 + count :]
    values, local, scores, decays, gated, squares, wbuf, wkeys, wdt, wsem, ksem = rest[:11]
    chain = Chain(False, *rest[11:15])
    batch, _, width = resid_ref.shape
    ext = span + HALO
    groups = heads // HEADS
    cb_w = HEADS * hw
    inner = groups * cb_w
    n = keys_ref.shape[2] // 2
    i = pl.program_id(0)
    place = Place() if count else None
    plans = [
        (gather_steps if j < 2 else gather_groups)(
            place, part_of(given[j], parts[j]), fulls[j], splits[j], *rest[15 + 3 * j : 18 + 3 * j]
        )
        for j in range(count)
    ]
    low_half = lax.broadcasted_iota(jnp.int32, (span, 2 * hw), 1) < hw

    def weights(j, full):
        cols = pl.ds(pl.multiple_of(j * cb_w, cb_w), cb_w)
        return pltpu.make_async_copy(full.at[:, :, :, cols], wbuf.at[j % 2], wsem.at[j % 2])

    def key_weights():
        return (
            pltpu.make_async_copy(fulls[0].at[:, :, :, pl.ds(inner, 2 * n)], wkeys, ksem.at[0]),
            pltpu.make_async_copy(fulls[1], wdt, ksem.at[1]),
        )

    at = {}
    if count:
        todo = [(one[0], 2) + one[1:] for one in GATE_STEPS] + [(one[0], 3) + one[1:] for one in OUT_STEPS]
        for time, which, *what in sorted(todo):
            slot = min([j for j in range(54) if front_time(j) >= time] + [53])
            at.setdefault(slot, []).append((which, *what))

    def act(which, step, *k):
        along_z, beyond, forward, last, finish = plans[which]
        {"z": along_z, "b": beyond, "f": forward, "l": last, "end": finish}[step](*k)

    def hook(b):
        for slot in sorted(at):
            if slot % batch == b:

                @pl.when(i == 1 + slot // batch)
                def _(slot=slot):
                    for step in at[slot]:
                        act(*step)

    def borrowed():
        return pltpu.make_async_remote_copy(
            src_ref=resid_ref.at[:, pl.ds(span - HALO, HALO)], dst_ref=halo_ref, send_sem=halo_send,
            recv_sem=halo_recv, device_id=chain.next, device_id_type=MESH,
        )

    def lend():
        @pl.when(chain.has_next)
        def _():
            borrowed().start()

    def normed(x):
        x = x.astype(f32)
        rs = lax.rsqrt(jnp.mean(x * x, axis=-1, keepdims=True) + epsilon)
        return (x * rs * ngain_ref[...]).astype(bf16)

    def input_norm():
        for b in range(batch):
            x_ref[b * ext + HALO : (b + 1) * ext] = normed(resid_ref[b])

        @pl.when(chain.has_prev)
        def _():
            borrowed().wait_recv()

        @pl.when(jnp.logical_not(chain.has_prev))
        def _():
            halo_ref[...] = jnp.zeros_like(halo_ref)

        for b in range(batch):
            x_ref[b * ext : b * ext + HALO] = normed(halo_ref[b])

        @pl.when(chain.has_next)
        def _():
            borrowed().wait_send()

    def key_part():
        cw, cb = cw_ref[:, inner:], cb_ref[:, inner:]
        acc = mm(x_ref[...], wkeys[...].reshape(width, 2 * n))
        raw_all = mm(x_ref[...], wdt[...].reshape(width, wdt.shape[3]))
        tri = causal(span, False).astype(f32)
        for b in range(batch):
            a = acc[b * ext : (b + 1) * ext]
            row, slope = silu_slope(conv_pre(a, cw, cb, span))
            keys_ref[b] = row.astype(bf16)
            kslope_ref[b] = slope.astype(bf16)
            kcin_ref[b] = a.astype(bf16)
            raw = raw_all[b * ext + HALO : (b + 1) * ext] + bias_ref[...]
            step = jnp.maximum(raw, 0.0) + jnp.log1p(jnp.exp(-jnp.abs(raw)))
            scaled = lax.dot_general(
                tri, step * rate_ref[...], (((1,), (0,)), ((), ())), precision=highest,
                preferred_element_type=f32,
            ) * LOG2E
            raw_ref[b] = raw
            step_ref[b] = step
            turned = jnp.transpose(scaled)
            for g in range(groups):
                some = slice(g * HEADS, (g + 1) * HEADS)
                col_ref[g, b] = jnp.concatenate([scaled[:, some], step[:, some]], axis=1)
                row_ref[g, b] = turned[some]

    @pl.when(i == 0)
    def _():
        greet_all(place, chain)
        lend()

        def both(step, *k):
            act(0, step, *k)
            act(1, step, *k)

        if count:
            both("z", 0)
            both("b", 0)
        input_norm()
        if count:
            both("z", 1)
            both("b", 1)
            both("f", 0)
            both("z", 2)
            both("b", 2)
            act(2, "z", 0)
            both("f", 1)
            both("z", 3)
            both("b", 3)
            both("f", 2)
            act(2, "z", 1)
            both("l", 0)
            act(2, "z", 2)
            both("f", 3)
            act(3, "z", 0)
            both("l", 1)
            act(2, "z", 3)
            act(2, "b")
            both("l", 2)
            both("l", 3)
            act(3, "z", 1)
            both("end")
        for copy in key_weights():
            copy.start()
        weights(0, fulls[0]).start()
        for copy in key_weights():
            copy.wait()
        key_part()

    def values_part(g, b, acc):
        a = acc[b * ext : (b + 1) * ext]
        some = pl.ds(pl.multiple_of(g * cb_w, cb_w), cb_w)
        row, slope = silu_slope(conv_pre(a, cw_ref[:, some], cb_ref[:, some], span))
        row = row.astype(bf16)
        rows_ref[b] = row
        slope_ref[b] = slope.astype(bf16)
        values[g * batch + b] = row
        cin_ref[b] = a.astype(bf16)
        cols = col_ref[g, b]
        c, step = cols[:, :HEADS], cols[:, HEADS:]
        weight = jnp.exp2(c[span - 1 : span] - c) * step
        vw = (row.astype(f32) * spread(weight, hw)).astype(bf16)
        local[g * batch + b] = mm_tn(keys_ref[b, :, :n], vw)
        decays[g * batch + b] = spread(jnp.exp2(c[span - 1 : span]), hw)

    def rows_part(g, b):
        k_in, k_out = keys_ref[b, :, :n], keys_ref[b, :, n:]

        @pl.when(g == 0)
        def _():
            scores[b] = jnp.where(causal(span, False), mm_nt(k_out, k_in), 0.0)

        cols = col_ref[g, b]
        c, step = cols[:, :HEADS], cols[:, HEADS:]
        v = values[g * batch + b].astype(f32)
        vs = (v * spread(step, hw)).astype(bf16)
        s = scores[b]
        rows = row_ref[g, b]
        sums = []
        for p in range(HEADS // 2):
            pair = vs[:, p * 2 * hw : (p + 1) * 2 * hw]
            total = None
            for q in range(2):
                h = 2 * p + q
                gap = jnp.minimum(c[:, h : h + 1] - rows[h : h + 1, :], 0.0)
                u = (jnp.exp2(gap) * s).astype(bf16)
                keep = low_half if q == 0 else jnp.logical_not(low_half)
                term = mm(u, jnp.where(keep, pair, jnp.zeros_like(pair)))
                total = term if total is None else total + term
            sums.append(total)
        inside = jnp.concatenate(sums, axis=1)
        came = chain.landed[g * batch + b]
        carried_ref[b] = came
        skip = skip_ref[:, pl.ds(pl.multiple_of(g * cb_w, cb_w), cb_w)]
        y = inside + mm(k_out, came) * spread(jnp.exp2(c), hw) + skip * v
        y_ref[b] = y
        gated[g * batch + b] = y

    def gate_part(g, b, w):
        gate = mm(x_ref[b * ext + HALO : (b + 1) * ext], w)
        gate_ref[b] = gate.astype(bf16)
        act, _ = silu_parts(gate)
        gr = gated[g * batch + b] * act
        gated[g * batch + b] = gr
        total = sum([gr[:, j * 128 : (j + 1) * 128] * gr[:, j * 128 : (j + 1) * 128] for j in range(cb_w // 128)])
        squares[b] = jnp.where(g == 0, 0.0, squares[b]) + total

    @pl.when(jnp.logical_and(i > 0, i <= groups))
    def _():
        g = i - 1
        weights(g, fulls[0]).wait()

        @pl.when(g < groups - 1)
        def _():
            weights(g + 1, fulls[0]).start()

        acc = mm(x_ref[...], wbuf[g % 2].reshape(width, cb_w))
        for b in range(batch):
            hook(b)
            values_part(g, b, acc)

    @pl.when(jnp.logical_and(i > groups, i <= 2 * groups))
    def _():
        for b in range(batch):
            hook(b)
            rows_part(i - 1 - groups, b)

    @pl.when(i > 2 * groups)
    def _():
        g = i - 1 - 2 * groups

        @pl.when(g == 0)
        def _():
            weights(0, fulls[2]).start()

        weights(g, fulls[2]).wait()

        @pl.when(g < groups - 1)
        def _():
            weights(g + 1, fulls[2]).start()

        for b in range(batch):
            hook(b)
            gate_part(g, b, wbuf[g % 2].reshape(width, cb_w))

    def ready(j):
        for b in range(batch):
            k = j * batch + b
            chain.pass_on(k, lambda: decays[k], lambda: local[k])

    early = i - 1 - chain.place

    @pl.when(jnp.logical_and(jnp.logical_and(early >= 0, early < groups), i - 1 <= groups - 1 + early))
    def _():
        ready(early)

    late = i - groups

    @pl.when(jnp.logical_and(jnp.logical_and(late >= 0, late < groups), chain.place > groups - 1))
    def _():
        ready(late)

    @pl.when(i == 3 * groups)
    def _():
        for b in range(batch):
            total = jnp.sum(squares[b], axis=1, keepdims=True)
            rg = lax.rsqrt(total * (1.0 / inner) + epsilon)
            rg_ref[b] = jnp.broadcast_to(rg, rg_ref.shape[1:])
            for g in range(groups):
                part = slice(g * cb_w, (g + 1) * cb_w)
                no_ref[b, :, part] = (gated[g * batch + b] * rg * gain_ref[:, part]).astype(bf16)
        if count:
            act(3, "end")
        chain.drain()


def front(resid, norm_gain, cw, cb, bias, rate, skip, gain, shards, parts, splits, hw, heads, n, collective_id):
    batch, span, width = resid.shape
    ext = span + HALO
    groups = heads // HEADS
    cb_w = HEADS * hw
    inner = groups * cb_w
    blocks = groups * batch
    lanes = bias.shape[1]
    hbm = pl.BlockSpec(memory_space=pl.ANY)
    count = len(splits)
    clip = lambda k: jnp.clip(k, 0, groups - 1)
    first = lambda i: clip(i - 1)
    then = lambda i: clip(i - 1 - groups)
    last = lambda i: clip(i - 1 - 2 * groups)
    once = lambda shape: pl.BlockSpec(shape, lambda i: (0,) * len(shape), pipeline_mode=pl.Buffered(1))
    block = lambda f, rows: pl.BlockSpec((batch, rows, cb_w), lambda i: (0, 0, f(i)))
    shaped = lambda shape, dtype: (once(shape), jax.ShapeDtypeStruct(shape, dtype))
    columns = lambda f, rows, dtype: (block(f, rows), jax.ShapeDtypeStruct((batch, rows, inner), dtype))
    outs = [
        shaped((batch * ext, width), bf16),
        shaped((batch, span, 2 * n), bf16),
        shaped((batch, span, 2 * n), bf16),
        shaped((batch, ext, 2 * n), bf16),
        shaped((groups, batch, span, 2 * HEADS), f32),
        shaped((groups, batch, HEADS, span), f32),
        shaped((batch, span, lanes), f32),
        shaped((batch, span, lanes), f32),
        columns(first, span, bf16),
        columns(first, span, bf16),
        columns(first, ext, bf16),
        columns(then, span, f32),
        columns(then, n, bf16),
        columns(last, span, bf16),
        shaped((batch, span, inner), bf16),
        shaped((batch, span, 8), f32),
    ]
    if count:
        outs += [
            (hbm, jax.ShapeDtypeStruct((16, 2, s.shape[0], p[1]), s.dtype)) for s, p in zip(shards, parts)
        ]
    else:
        shards = [s.reshape(16, 2, s.shape[0] // 32, s.shape[1]) for s in shards]
    small_ins = [resid, norm_gain, cw, cb, bias, rate, skip, gain]
    return pl.pallas_call(
        functools.partial(front_kernel, span, hw, heads, splits, parts),
        grid=(1 + 3 * groups,),
        in_specs=[once(x.shape) for x in small_ins] + [hbm] * 4,
        out_specs=[o[0] for o in outs],
        out_shape=[o[1] for o in outs],
        scratch_shapes=[
            pltpu.VMEM((batch, HALO, width), bf16),
            pltpu.SemaphoreType.DMA,
            pltpu.SemaphoreType.DMA,
            pltpu.VMEM((blocks, span, cb_w), bf16),
            pltpu.VMEM((blocks, n, cb_w), f32),
            pltpu.VMEM((batch, span, span), f32),
            pltpu.VMEM((blocks, 1, cb_w), f32),
            pltpu.VMEM((blocks, span, cb_w), f32),
            pltpu.VMEM((batch, span, 128), f32),
            pltpu.VMEM((2, 16, 2, width // 32, cb_w), bf16),
            pltpu.VMEM((16, 2, width // 32, 2 * n), bf16),
            pltpu.VMEM((16, 2, width // 32, lanes), bf16),
            pltpu.SemaphoreType.DMA((2,)),
            pltpu.SemaphoreType.DMA((2,)),
        ]
        + Chain.scratch(blocks, n, cb_w)
        + gather_scratch() * count,
        compiler_params=pltpu.CompilerParams(
            collective_id=collective_id, has_side_effects=True, vmem_limit_bytes=62 * 1024 * 1024
        ),
    )(*small_ins, *shards)


def scatter_beside(i, batch, slots, starts, splits, bigs, outs, scratch):
    if not splits:
        return lambda b: None
    place = Place()
    plans = [
        Scatter(place, bigs[j], outs[j], *scratch[7 * j : 7 * j + 7], splits[j]).steps()
        for j in range(len(splits))
    ]
    at = {}
    for steps in zip(*plans):
        for time, step in steps:
            slot = min([k for k in range(slots) if starts(k) >= time] + [slots - 1])
            at.setdefault(slot, []).append(step)

    def run(b):
        for slot, steps in at.items():
            if slot % batch == b:

                @pl.when(i == slot // batch)
                def _(steps=steps):
                    for step in steps:
                        step()

    return run


def gate_back_kernel(span, hw, groups, splits, *refs):
    count = len(splits)
    (mg_ref, w_ref, y_ref, gate_ref, norm_ref, gain_ref, v_ref, keys_ref, col_ref, row_ref) = refs[:10]
    h_ref, skip_ref = refs[10:12]
    bigs = refs[12 : 12 + count]
    (dgate_ref, dv_ref, later_ref, cols_ref, dq_ref, dk_ref, dgain_ref, dskip_ref) = refs[12 + count : 20 + count]
    outs = refs[20 + count : 20 + 2 * count]
    rest = refs[20 + 2 * count :]
    scores, dscores, dqacc, gbs, rises, local, decays = rest[:7]
    chain = Chain(True, *rest[7:11])
    batch = mg_ref.shape[0]
    blocks = groups * batch
    i = pl.program_id(0)
    g = i % groups
    n = keys_ref.shape[2] // 2
    skip = skip_ref[...]
    low_half = lax.broadcasted_iota(jnp.int32, (span, 2 * hw), 1) < hw

    @pl.when(i == 0)
    def _():
        greet_all(Place() if count else None, chain)

    hook = scatter_beside(i, batch, 2 * blocks, lambda k: gate_start(k, blocks), splits, bigs, outs, rest[11:])

    def gate_part(b):
        at = g * batch + b
        cols = col_ref[0, b]
        c = cols[:, :HEADS]
        no_grad = mm_nt(mg_ref[b], w_ref[...])
        gate = gate_ref[b].astype(f32)
        y = y_ref[b]
        rg = norm_ref[b][:, 0:1]
        mean = norm_ref[b][:, 1:2]
        act, sg = silu_parts(gate)
        gn = y * act * rg
        dgain = jnp.sum(no_grad * gn, axis=0, keepdims=True)
        dg = rg * (no_grad * gain_ref[...] - gn * mean)
        dgate_ref[b] = (dg * y * (sg * (1.0 + gate * (1.0 - sg)))).astype(bf16)
        gb = (dg * act).astype(bf16)
        gbs[at] = gb
        gf = gb.astype(f32)
        v = v_ref[b].astype(f32)
        dskip = jnp.sum(gf * v, axis=0, keepdims=True)
        rises[at] = gather_heads(gf * (y - skip * v), hw)
        ge = (gf * spread(jnp.exp2(c), hw)).astype(bf16)
        local[at] = mm_tn(keys_ref[b, :, n:], ge)
        decays[at] = spread(jnp.exp2(c[span - 1 : span]), hw)
        part = mm_nt(ge, h_ref[b])

        @pl.when(g == 0)
        def _():
            dqacc[b] = part

        @pl.when(g != 0)
        def _():
            dqacc[b] += part

        if b == 0:
            dgain_ref[...] = dgain
            dskip_ref[...] = dskip
        else:
            dgain_ref[...] += dgain
            dskip_ref[...] += dskip

    def block_part(b):
        at = g * batch + b
        cols = col_ref[0, b]
        c, step = cols[:, :HEADS], cols[:, HEADS:]
        k_in, k_out = keys_ref[b, :, :n], keys_ref[b, :, n:]

        @pl.when(g == 0)
        def _():
            scores[b] = jnp.where(causal(span, True), mm_nt(k_in, k_out), 0.0)
            dscores[b] = jnp.zeros_like(dscores[b])

        later_ref[b] = chain.landed[at]
        gb = gbs[at]
        gf = gb.astype(f32)
        v = v_ref[b].astype(f32)
        step_wide = spread(step, hw)
        vs = (v * step_wide).astype(bf16)
        rows = row_ref[0, b]
        s = scores[b]
        parts = []
        ds = dscores[b]
        for p in range(HEADS // 2):
            lanes = slice(p * 2 * hw, (p + 1) * 2 * hw)
            total = None
            for q in range(2):
                h = 2 * p + q
                gap = jnp.minimum(rows[h : h + 1, :] - c[:, h : h + 1], 0.0)
                decay = jnp.exp2(gap)
                u = (decay * s).astype(bf16)
                keep = low_half if q == 0 else jnp.logical_not(low_half)
                half = jnp.where(keep, gb[:, lanes], jnp.zeros_like(gb[:, lanes]))
                term = mm(u, half)
                total = term if total is None else total + term
                ds = ds + decay * mm_nt(vs[:, lanes], half)
            parts.append(total)
        dscores[b] = ds
        u_all = jnp.concatenate(parts, axis=1)
        dv_ref[b] = (u_all * step_wide + skip * gf).astype(bf16)
        fall = gather_heads(vs.astype(f32) * u_all, hw)
        direct = gather_heads(v * u_all, hw)
        cols_ref[0, b] = jnp.concatenate([rises[at] - fall, direct], axis=1)

        @pl.when(g == groups - 1)
        def _():
            low = jnp.where(causal(span, True), dscores[b], 0.0).astype(bf16)
            dq_ref[b] = dqacc[b] + mm_tn(low, k_in)
            dk_ref[b] = mm(low, k_out)

    lag = jnp.minimum(5 * chain.place // 2, blocks - 1)
    for b in range(batch):
        hook(b)

        @pl.when(i < groups)
        def _():
            gate_part(b)

        @pl.when(i >= groups)
        def _():
            block_part(b)

        k = i * batch + b - lag

        @pl.when(jnp.logical_and(k >= 0, k < blocks))
        def _():
            chain.pass_on(k, lambda: decays[k], lambda: local[k])

    @pl.when(i == 2 * groups - 1)
    def _():
        chain.drain()


def gate_backward(
    mg, w_out, y, gate, norms, gain, v, keys, colpack, rowpack, carried, skip, bigs, splits, hw, span,
    collective_id,
):
    hbm = pl.BlockSpec(memory_space=pl.ANY)
    shapes = [(x.shape[0] // 32, x.shape[1]) for x in bigs]
    batch, _, width = mg.shape
    groups = colpack.shape[0]
    cb_w = HEADS * hw
    inner = groups * cb_w
    n = keys.shape[2] // 2
    blocks = groups * batch
    first = lambda i: jnp.minimum(i, groups - 1)
    then = lambda i: jnp.maximum(i - groups, 0)
    both = lambda i: i % groups
    block = lambda f, rows: pl.BlockSpec((batch, rows, cb_w), lambda i: (0, 0, f(i)))
    lanes = lambda f: pl.BlockSpec((1, cb_w), lambda i: (0, f(i)))
    whole = lambda shape: pl.BlockSpec(shape, lambda i: (0,) * len(shape))
    return pl.pallas_call(
        functools.partial(gate_back_kernel, span, hw, groups, splits),
        grid=(2 * groups,),
        in_specs=[
            whole(mg.shape),
            pl.BlockSpec((cb_w, width), lambda i: (first(i), 0)),
            block(first, span),
            block(first, span),
            whole(norms.shape),
            lanes(first),
            block(both, span),
            whole(keys.shape),
            pl.BlockSpec((1,) + colpack.shape[1:], lambda i: (both(i), 0, 0, 0)),
            pl.BlockSpec((1,) + rowpack.shape[1:], lambda i: (then(i), 0, 0, 0)),
            block(first, n),
            lanes(both),
        ]
        + [hbm] * len(bigs),
        out_specs=[
            block(first, span),
            block(then, span),
            block(then, n),
            pl.BlockSpec((1, batch, span, 2 * HEADS), lambda i: (then(i), 0, 0, 0)),
            whole((batch, span, n)),
            whole((batch, span, n)),
            lanes(first),
            lanes(first),
        ]
        + [whole(s) for s in shapes],
        out_shape=[
            jax.ShapeDtypeStruct((batch, span, inner), bf16),
            jax.ShapeDtypeStruct((batch, span, inner), bf16),
            jax.ShapeDtypeStruct((batch, n, inner), bf16),
            jax.ShapeDtypeStruct((groups, batch, span, 2 * HEADS), f32),
            jax.ShapeDtypeStruct((batch, span, n), f32),
            jax.ShapeDtypeStruct((batch, span, n), f32),
            jax.ShapeDtypeStruct((1, inner), f32),
            jax.ShapeDtypeStruct((1, inner), f32),
        ]
        + [jax.ShapeDtypeStruct(s, f32) for s in shapes],
        scratch_shapes=[
            pltpu.VMEM((batch, span, span), f32),
            pltpu.VMEM((batch, span, span), f32),
            pltpu.VMEM((batch, span, n), f32),
            pltpu.VMEM((blocks, span, cb_w), bf16),
            pltpu.VMEM((blocks, span, HEADS), f32),
            pltpu.VMEM((blocks, n, cb_w), f32),
            pltpu.VMEM((blocks, 1, cb_w), f32),
        ]
        + Chain.scratch(blocks, n, cb_w)
        + sum([Scatter.scratch(s[0], s[1], sp) for s, sp in zip(shapes, splits)], []),
        compiler_params=pltpu.CompilerParams(
            collective_id=collective_id, has_side_effects=True, vmem_limit_bytes=60 * 1024 * 1024
        ),
    )(mg, w_out, y, gate, norms, gain, v, keys, colpack, rowpack, carried, skip, *bigs)


def conv_back(dv, slope, a, cw, span, padded, out_ref, b):
    taps = cw.shape[0]
    ext = span + HALO
    pg = dv * slope
    padded[HALO : HALO + span] = pg
    total, dcw = None, []
    for k in range(taps):
        moved = padded[taps - 1 - k : taps - 1 - k + ext]
        term = cw[k : k + 1] * moved
        total = term if total is None else total + term
        dcw.append(jnp.sum(moved * a, axis=0, keepdims=True))
    out_ref[b] = total.astype(bf16)
    return jnp.concatenate(dcw, axis=0), jnp.sum(pg, axis=0, keepdims=True)


def back_kernel(span, hw, groups, splits, *refs):
    count = len(splits)
    (later_ref, h_ref, keys_ref, v_ref, dv_ref, col_ref, cin_ref, cw_ref, slope_ref) = refs[:9]
    bigs = refs[9 : 9 + count]
    cig_ref, cols_ref, dk_ref, dcw_ref, dcb_ref, dlast_ref = refs[9 + count : 15 + count]
    outs = refs[15 + count : 15 + 2 * count]
    rest = refs[15 + 2 * count :]
    padded, dkacc = rest[:2]
    i = pl.program_id(0)
    batch = dk_ref.shape[0]
    n = keys_ref.shape[2] // 2

    @pl.when(i == 0)
    def _():
        if count:
            Place().greet()
        padded[0:16] = jnp.zeros((16, padded.shape[1]), f32)
        padded[16 + span :] = jnp.zeros((padded.shape[0] - 16 - span, padded.shape[1]), f32)

    hook = scatter_beside(i, batch, groups * batch, back_start, splits, bigs, outs, rest[2:])
    for b in range(batch):
        hook(b)
        cols = col_ref[0, b]
        c, step = cols[:, :HEADS], cols[:, HEADS:]
        low = later_ref[b]
        left = spread(jnp.exp2(c[span - 1 : span] - c), hw)
        kdh = mm(keys_ref[b, :, :n], low) * left
        v = v_ref[b].astype(f32)
        step_wide = spread(step, hw)
        cols_ref[0, b] = gather_heads(v * kdh, hw)
        dlast_ref[b] = jnp.broadcast_to(
            jnp.sum(low.astype(f32) * h_ref[b].astype(f32), axis=0, keepdims=True), dlast_ref.shape[1:]
        )
        vw = (v * step_wide * left).astype(bf16)
        part = mm_nt(vw, low)

        @pl.when(i == 0)
        def _():
            dkacc[b] = part

        @pl.when(i != 0)
        def _():
            dkacc[b] += part

        @pl.when(i == groups - 1)
        def _():
            dk_ref[b] = dkacc[b]

        dv = dv_ref[b].astype(f32) + kdh * step_wide
        dcw, dcb = conv_back(
            dv, slope_ref[b].astype(f32), cin_ref[b].astype(f32), cw_ref[...], span, padded, cig_ref, b
        )
        if b == 0:
            dcw_ref[...] = dcw
            dcb_ref[...] = dcb
        else:
            dcw_ref[...] += dcw
            dcb_ref[...] += dcb


def back(later, carried, keys, v, dv, colpack, cin, cw, slope, bigs, splits, hw, span, collective_id):
    batch = v.shape[0]
    groups = colpack.shape[0]
    cb_w = HEADS * hw
    inner = groups * cb_w
    n = keys.shape[2] // 2
    ext = span + HALO
    taps = cw.shape[0]
    block = lambda rows: pl.BlockSpec((batch, rows, cb_w), lambda i: (0, 0, i))
    lanes = lambda rows: pl.BlockSpec((rows, cb_w), lambda i: (0, i))
    hbm = pl.BlockSpec(memory_space=pl.ANY)
    shapes = [(x.shape[0] // 32, x.shape[1]) for x in bigs]
    return pl.pallas_call(
        functools.partial(back_kernel, span, hw, groups, splits),
        grid=(groups,),
        in_specs=[
            block(n),
            block(n),
            pl.BlockSpec(keys.shape, lambda i: (0, 0, 0)),
            block(span),
            block(span),
            pl.BlockSpec((1,) + colpack.shape[1:], lambda i: (i, 0, 0, 0)),
            block(ext),
            lanes(taps),
            block(span),
        ]
        + [hbm] * len(bigs),
        out_specs=[
            block(ext),
            pl.BlockSpec((1, batch, span, HEADS), lambda i: (i, 0, 0, 0)),
            pl.BlockSpec((batch, span, n), lambda i: (0, 0, 0)),
            lanes(taps),
            lanes(1),
            block(8),
        ]
        + [pl.BlockSpec(s, lambda i: (0, 0)) for s in shapes],
        out_shape=[
            jax.ShapeDtypeStruct((batch, ext, inner), bf16),
            jax.ShapeDtypeStruct((groups, batch, span, HEADS), f32),
            jax.ShapeDtypeStruct((batch, span, n), f32),
            jax.ShapeDtypeStruct((taps, inner), f32),
            jax.ShapeDtypeStruct((1, inner), f32),
            jax.ShapeDtypeStruct((batch, 8, inner), f32),
        ]
        + [jax.ShapeDtypeStruct(s, f32) for s in shapes],
        scratch_shapes=[
            pltpu.VMEM((span + 32, cb_w), f32),
            pltpu.VMEM((batch, span, n), f32),
        ]
        + sum([Scatter.scratch(s[0], s[1], sp) for s, sp in zip(shapes, splits)], []),
        compiler_params=pltpu.CompilerParams(
            collective_id=collective_id if bigs else None,
            has_side_effects=bool(bigs),
            vmem_limit_bytes=58 * 1024 * 1024,
        ),
    )(later, carried, keys, v, dv, colpack, cin, cw, slope, *bigs)


def keys_back_kernel(span, dk_ref, dk2_ref, dq_ref, cin_ref, cw_ref, slope_ref, cig_ref, dcw_ref, dcb_ref, padded):
    batch = dk_ref.shape[0]
    padded[...] = jnp.zeros_like(padded)
    for b in range(batch):
        dv = jnp.concatenate([dk_ref[b] + dk2_ref[b], dq_ref[b]], axis=1)
        dcw, dcb = conv_back(
            dv, slope_ref[b].astype(f32), cin_ref[b].astype(f32), cw_ref[...], span, padded, cig_ref, b
        )
        if b == 0:
            dcw_ref[...] = dcw
            dcb_ref[...] = dcb
        else:
            dcw_ref[...] += dcw
            dcb_ref[...] += dcb


def keys_backward(dk, dk2, dq, cin, cw, slope, span):
    batch, ext, width = cin.shape
    return pl.pallas_call(
        functools.partial(keys_back_kernel, span),
        in_specs=[pl.BlockSpec(memory_space=pltpu.VMEM)] * 6,
        out_specs=[pl.BlockSpec(memory_space=pltpu.VMEM)] * 3,
        out_shape=[
            jax.ShapeDtypeStruct(cin.shape, bf16),
            jax.ShapeDtypeStruct(cw.shape, f32),
            jax.ShapeDtypeStruct((1, width), f32),
        ],
        scratch_shapes=[pltpu.VMEM((span + 32, width), f32)],
        compiler_params=params_of(40),
    )(dk, dk2, dq, cin, cw, slope)


def tail_kernel(span, splits, with_small, *refs):
    count = len(splits)
    (cig_ref, wc_ref, dgate_ref, wg_ref, keys_ref, wk_ref, low_ref, wd_ref) = refs[:8]
    resid_ref, mg_ref, gain_ref, parts_ref = refs[8:12]
    bigs = refs[12 : 12 + count]
    grad_ref, sums_ref = refs[12 + count : 14 + count]
    outs = refs[14 + count : 14 + 2 * count]
    rest = refs[14 + 2 * count :]
    acc, rim, rim_in, value, halo_send, halo_recv = rest[:6]
    i = pl.program_id(0)
    steps = pl.num_programs(0)
    half = steps // 2
    batch, _, width = resid_ref.shape
    ext = span + HALO
    chain = Chain(True, rim, rim_in, halo_send, halo_recv)
    place = Place() if count else None
    plan = small = None
    times = []
    if count:
        plan = Scatter(place, bigs[0], outs[0], *rest[6:13], splits[0])
        times = plan.steps()
        small = Small(place, value, sums_ref, *rest[13:17])

    @pl.when(i == 0)
    def _():
        greet_all(place, chain, (place.to_across,) if count else ())

    slots = TAIL_STEPS
    early = [(t, s) for t, s in times if t <= tail_start(slots - 1)]
    late = [s for t, s in times if t > tail_start(slots - 1)]
    at = {}
    for time, step in early:
        at.setdefault(min(k for k in range(slots) if tail_start(k) >= time), []).append(step)
    for slot, some in at.items():

        @pl.when(i == slot)
        def _(some=some):
            for step in some:
                step()

    flat = lambda ref: ref[...].reshape(batch * ext, ref.shape[2])

    @pl.when(i == 0)
    def _():
        acc[...] = mm_nt(flat(cig_ref), wc_ref[...])
        acc[...] += mm_nt(flat(keys_ref), wk_ref[...])
        acc[...] += mm_nt(flat(low_ref), wd_ref[...])

    @pl.when(jnp.logical_and(i > 0, i < half))
    def _():
        acc[...] += mm_nt(flat(cig_ref), wc_ref[...])

    @pl.when(i == half - 1)
    def _():
        for b in range(batch):
            rim[0, b] = acc[b * ext : b * ext + HALO].astype(bf16)

        @pl.when(chain.has_next)
        def _():
            chain.copy(0).start()

    @pl.when(i >= half)
    def _():
        for b in range(batch):
            rows = slice(b * ext + HALO, (b + 1) * ext)
            acc[rows] += mm_nt(dgate_ref[b], wg_ref[...])

    @pl.when(i == steps - 1)
    def _():
        @pl.when(chain.has_prev)
        def _():
            chain.copy(0).wait_recv()
            for b in range(batch):
                rows = slice((b + 1) * ext - HALO, (b + 1) * ext)
                acc[rows] += rim_in[0, b].astype(f32)

        for step in late[:2]:
            step()
        total = jnp.zeros((1, width), f32)
        for b in range(batch):
            for step in late[2 + b : 3 + b]:
                step()
            grad = acc[b * ext + HALO : (b + 1) * ext]
            x = resid_ref[b].astype(f32)
            rs = lax.rsqrt(jnp.mean(x * x, axis=-1, keepdims=True) + epsilon)
            nz = x * rs
            fg = grad * gain_ref[...]
            total = total + jnp.sum(grad * nz, axis=0, keepdims=True)
            mean = jnp.mean(fg * nz, axis=-1, keepdims=True)
            grad_ref[b] = (mg_ref[b].astype(f32) + rs * (fg - nz * mean)).astype(bf16)
        lead = width // 128
        value[lead:] = parts_ref[lead:]
        for r in range(lead):
            value[r : r + 1] = total[:, r * 128 : (r + 1) * 128]
        if small is None:
            sums_ref[...] = value[...]
        else:
            after = late[2 + batch :]
            spots = [len(after) * k // 6 for k in range(6)]
            for j, step in enumerate(after):
                for k in range(6):
                    if spots[k] == j:
                        small.go(k)
                step()

        @pl.when(chain.has_next)
        def _():
            chain.copy(0).wait_send()


TAIL_STEPS = 12


def tail_start(k):
    return 2.2 * k


def tail(cig, w_conv, dgate, w_gate, cig_keys, step_low, w_dt, resid, mg, gain, parts, bigs, splits, span, collective_id):
    batch, ext, inner = cig.shape
    width = resid.shape[2]
    cb_w = inner // (TAIL_STEPS // 2)
    half = TAIL_STEPS // 2
    keys_w = cig_keys.shape[2]
    whole = lambda shape: pl.BlockSpec(shape, lambda i: (0,) * len(shape))
    first = lambda i: jnp.minimum(i, half - 1)
    then = lambda i: jnp.maximum(i - half, 0)
    hbm = pl.BlockSpec(memory_space=pl.ANY)
    shapes = [(x.shape[0] // 32, x.shape[1]) for x in bigs]
    return pl.pallas_call(
        functools.partial(tail_kernel, span, splits, bool(bigs)),
        grid=(TAIL_STEPS,),
        in_specs=[
            pl.BlockSpec((batch, ext, cb_w), lambda i: (0, 0, first(i))),
            pl.BlockSpec((width, cb_w), lambda i: (0, first(i))),
            pl.BlockSpec((batch, span, cb_w), lambda i: (0, 0, then(i))),
            pl.BlockSpec((width, cb_w), lambda i: (0, then(i))),
            whole(cig_keys.shape),
            pl.BlockSpec((width, keys_w), lambda i: (0, inner // keys_w)),
            whole(step_low.shape),
            whole(w_dt.shape),
            whole(resid.shape),
            whole(mg.shape),
            whole(gain.shape),
            whole(parts.shape),
        ]
        + [hbm] * len(bigs),
        out_specs=[whole(resid.shape), whole(parts.shape)] + [whole(s) for s in shapes],
        out_shape=[jax.ShapeDtypeStruct(resid.shape, bf16), jax.ShapeDtypeStruct(parts.shape, f32)]
        + [jax.ShapeDtypeStruct(s, f32) for s in shapes],
        scratch_shapes=[
            pltpu.VMEM((batch * ext, width), f32),
            pltpu.VMEM((1, batch, HALO, width), bf16),
            pltpu.VMEM((1, batch, HALO, width), bf16),
            pltpu.VMEM(parts.shape, f32),
            pltpu.SemaphoreType.DMA((1,)),
            pltpu.SemaphoreType.DMA((1,)),
        ]
        + sum([Scatter.scratch(s[0], s[1], sp) for s, sp in zip(shapes, splits)], [])
        + (Small.scratch(parts.shape) if bigs else []),
        compiler_params=pltpu.CompilerParams(
            collective_id=collective_id, has_side_effects=True, vmem_limit_bytes=60 * 1024 * 1024
        ),
    )(cig, w_conv, dgate, w_gate, cig_keys, w_conv, step_low, w_dt, resid, mg, gain, parts, *bigs)


def own_kernels():
    return lax.axis_size("dp") == 4 and lax.axis_size("seq") == 8


def gather_rows(shards, parts):
    return [
        lax.all_gather(s[:, p[0] : p[0] + p[1]], ("dp", "seq"), axis=0, tiled=True)
        for s, p in zip(shards, parts)
    ]


def scatter_rows(bigs, splits, small, collective_id):
    if own_kernels():
        return scatter(bigs, splits, small, collective_id)
    outs = [lax.psum_scatter(b, ("dp", "seq"), scatter_dimension=0, tiled=True).astype(f32) for b in bigs]
    return outs + ([] if small is None else [lax.psum(small, ("dp", "seq"))])


def half_of(width):
    return (width // 2 + 127) // 128 * 128


def ungrouped(cols):
    groups, batch, span, each = cols.shape
    return jnp.transpose(cols, (1, 2, 0, 3)).reshape(batch, span, groups * each)


def gate_start(k, blocks):
    return 1.0 * k if k < blocks else 1.0 * blocks + 1.6 * (k - blocks)


def back_start(k):
    return 2.9 * k


def on_device(
    resid_in, out_grad, lengths, norm_gain, in_proj, dt_proj, conv_weight, conv_bias, dt_bias, a_log,
    skip_scale, gate_gain, out_proj,
):
    batch, span, width = resid_in.shape
    inner = gate_gain.shape[0]
    heads = a_log.shape[0]
    hw = inner // heads
    n = (in_proj.shape[1] - 2 * inner) // 2
    cb_w = HEADS * hw
    positions = lax.axis_index("seq") * span + lax.iota(jnp.int32, span)
    mask = (positions[None, :] < lengths[:, None]).astype(f32)[..., None]

    conv_cols = in_proj.shape[1] - inner
    dt_pad = (-(conv_cols + heads)) % 128
    conv_all = conv_cols + heads + dt_pad
    dt_shard = jnp.pad(dt_proj, ((0, 0), (0, dt_pad)))
    shards, parts = (
        [in_proj, dt_shard, in_proj, out_proj],
        [(inner, conv_cols), (0, heads + dt_pad), (0, inner), (0, width)],
    )
    splits = [half_of(conv_cols), heads + dt_pad, half_of(inner), half_of(width)]
    later_splits = splits[2:]
    inside = own_kernels()
    weights = shards if inside else gather_rows(shards, parts)

    resid_wide = resid_in.astype(f32)
    rate = -jnp.exp(a_log)
    lane_pad = (0, (-heads) % 128)
    skip_wide = jnp.repeat(skip_scale, hw)[None]
    gain_wide = gate_gain[None]
    cw_keys, cw_vals = conv_weight[:, inner:], conv_weight[:, :inner]
    made = front(
        resid_in, norm_gain[None], conv_weight, conv_bias[None], jnp.pad(dt_bias, lane_pad)[None],
        jnp.pad(rate, lane_pad)[None], skip_wide, gain_wide, weights, parts, splits if inside else [], hw, heads, n, 1,
    )
    x2, keys, slope_keys, cin_keys, colpack, rowpack, raw, step = made[:8]
    v, slope_vals, cin_vals, y, carried, gate, normed_out, rg = made[8:16]
    full_conv, full_dt, full_gate, full_out = [w.reshape(-1, w.shape[-1]) for w in (made[16:] if inside else weights)]
    x_ext = x2.reshape(batch, span + HALO, width)
    mixer_out = jnp.dot(normed_out, full_out, preferred_element_type=f32)
    output = (mask * (resid_wide + mixer_out)).astype(bf16)

    mixer_grad = (mask * out_grad.astype(f32)).astype(bf16)
    mean = jnp.sum(mixer_grad.astype(f32) * mixer_out, axis=-1, keepdims=True) * (1.0 / inner)
    norms = jnp.concatenate([rg[..., :1], mean, jnp.zeros((batch, span, 6), f32)], axis=-1)
    grad_out = jnp.einsum("bsi,bsd->id", normed_out, mixer_grad, preferred_element_type=f32).astype(bf16)
    made = gate_backward(
        mixer_grad, full_out, y, gate, norms, gain_wide, v, keys, colpack, rowpack, carried, skip_wide,
        [grad_out] if inside else [], later_splits[1:] if inside else [], hw, span, 7,
    )
    dgate, dv, later, cols_one, dq, dk, dgain, dskip = made[:8]
    (sum_out,) = made[8:] if inside else scatter_rows([grad_out], later_splits[1:], None, 5)
    x_rows = x_ext[:, HALO:]
    grad_gate = jnp.einsum("bsd,bse->de", x_rows, dgate, preferred_element_type=f32).astype(bf16)
    made = back(
        later, carried, keys, v, dv, colpack, cin_vals, cw_vals, slope_vals,
        [grad_gate] if inside else [], later_splits[:1] if inside else [], hw, span, 2,
    )
    cig_vals, cols_two, dk2, dcw_vals, dcb_vals, dlast = made[:6]
    (sum_gate,) = made[6:] if inside else scatter_rows([grad_gate], later_splits[:1], None, 5)
    cig_keys, dcw_keys, dcb_keys = keys_backward(dk, dk2, dq, cin_keys, cw_keys, slope_keys, span)

    raw, step = raw[..., :heads], step[..., :heads]
    rise = ungrouped(cols_one[..., :HEADS])
    direct = ungrouped(cols_one[..., HEADS:])
    ahead = ungrouped(cols_two)
    moved = ahead * step
    tri = causal(span, False).astype(f32)
    block_decay = jnp.exp2(colpack[:, :, span - 1, :HEADS]).transpose(1, 0, 2).reshape(batch, heads)
    last = jnp.sum(moved, axis=1) + dlast[:, 0].reshape(batch, heads, hw).sum(-1) * block_decay
    dlog = rise - moved
    dlog = jnp.einsum("ts,bth->bsh", tri, dlog, precision=highest) + last[:, None, :]
    grad_a = jnp.sum(dlog * step, axis=(0, 1)) * rate
    step_grad = direct + ahead + dlog * rate
    dt_grad = step_grad * jax.nn.sigmoid(raw)
    grad_bias = jnp.sum(dt_grad, axis=(0, 1))
    step_low = jnp.pad(dt_grad.astype(bf16), ((0, 0), (HALO, 0), (0, dt_pad)))

    cig = jnp.concatenate([cig_vals, cig_keys, step_low], axis=-1)
    grad_conv = jnp.einsum("bsd,bse->de", x_ext, cig, preferred_element_type=f32).astype(bf16)
    pieces = (
        norm_gain,
        jnp.concatenate([dcw_vals, dcw_keys], axis=1),
        jnp.concatenate([dcb_vals, dcb_keys], axis=1)[0],
        dgain[0],
        grad_bias,
        grad_a,
        dskip[0].reshape(heads, hw).sum(-1),
    )
    flat = jnp.concatenate([p.reshape(-1) for p in pieces])
    packed = jnp.pad(flat, (0, (-flat.size) % 1024)).reshape(-1, 128)
    made = tail(
        cig_vals, full_conv, dgate, full_gate, cig_keys, step_low, full_dt, resid_in, mixer_grad,
        norm_gain[None], packed, [grad_conv] if inside else [], [half_of(conv_all)] if inside else [], span, 6,
    )
    input_grad, small = made[:2]
    if inside:
        sum_conv = made[2]
    else:
        sum_conv, small = scatter_rows([grad_conv], [half_of(conv_all)], small, 6)
    flat, sums, at = small.reshape(-1), [], 0
    for p in pieces:
        sums.append(flat[at : at + p.size].reshape(p.shape))
        at += p.size
    sum_norm, sum_cw, sum_cb, sum_gain, sum_bias, sum_a, sum_skip = sums
    return (
        output,
        input_grad,
        jnp.concatenate([sum_gate, sum_conv[:, :conv_cols]], axis=1),
        sum_conv[:, conv_cols : conv_cols + heads],
        sum_out,
        sum_norm,
        sum_cw,
        sum_cb,
        sum_bias,
        sum_a,
        sum_skip,
        sum_gain,
    )


def solution(mesh):
    rows = P("dp", "seq", None)
    shard = P(("dp", "seq"), None)
    return jax.shard_map(
        on_device,
        mesh=mesh,
        in_specs=(rows, rows, P("dp"), P(), shard, shard, P(), P(), P(), P(), P(), P(), shard),
        out_specs=(rows, rows, shard, shard, shard, P(), P(), P(), P(), P(), P(), P()),
        check_vma=False,
    )
```

```python
import functools

import jax
import jax.numpy as jnp
from jax import lax
from jax.experimental import pallas as pl
from jax.experimental.pallas import tpu as pltpu
from jax.sharding import PartitionSpec as P

epsilon = 1e-05
highest = lax.Precision.HIGHEST
HALO = 16
HEADS = 8
LOG2E = 1.4426950408889634
f32 = jnp.float32
bf16 = jnp.bfloat16
MESH = pl.DeviceIdType.MESH


def mm(a, b):
    return lax.dot_general(a, b, (((1,), (0,)), ((), ())), preferred_element_type=f32)


def mm_nt(a, b):
    return lax.dot_general(a, b, (((1,), (1,)), ((), ())), preferred_element_type=f32)


def mm_tn(a, b):
    return lax.dot_general(a, b, (((0,), (0,)), ((), ())), preferred_element_type=f32)


def spread(cols, width):
    rows, heads = cols.shape
    low_half = lax.broadcasted_iota(jnp.int32, (rows, 2 * width), 1) < width
    pairs = [
        jnp.where(low_half, cols[:, i : i + 1], cols[:, i + 1 : i + 2]) for i in range(0, heads, 2)
    ]
    return jnp.concatenate(pairs, axis=1)


def gather_heads(x, width):
    rows, total = x.shape
    low_half = lax.broadcasted_iota(jnp.int32, (rows, 2 * width), 1) < width
    head_lane = lax.broadcasted_iota(jnp.int32, (rows, total // width), 1)
    out = jnp.zeros((rows, total // width), f32)
    for i in range(total // (2 * width)):
        pair = x[:, i * 2 * width : (i + 1) * 2 * width]
        one = jnp.sum(jnp.where(low_half, pair, 0.0), axis=1, keepdims=True)
        two = jnp.sum(jnp.where(low_half, 0.0, pair), axis=1, keepdims=True)
        out = jnp.where(head_lane == 2 * i, one, out)
        out = jnp.where(head_lane == 2 * i + 1, two, out)
    return out


def silu_parts(v):
    sg = 1.0 / (1.0 + jnp.exp(-v))
    return v * sg, sg


def silu_slope(v):
    act, sg = silu_parts(v)
    return act, sg * (1.0 + v * (1.0 - sg))


def conv_pre(a, cw, cb, span):
    first = HALO - (cw.shape[0] - 1)
    out = cb
    for k in range(cw.shape[0]):
        out = out + cw[k : k + 1] * a[first + k : first + k + span]
    return out


def params_of(limit_mb, dims=None):
    return pltpu.CompilerParams(vmem_limit_bytes=limit_mb * 1024 * 1024, dimension_semantics=dims)


def causal(span, transposed):
    one = lax.broadcasted_iota(jnp.int32, (span, span), 0)
    two = lax.broadcasted_iota(jnp.int32, (span, span), 1)
    return (one <= two) if transposed else (one >= two)


class Place:
    def __init__(self):
        self.dp = lax.axis_index("dp")
        self.seq = lax.axis_index("seq")
        y, x = self.dp // 2, self.dp % 2
        self.z, self.core = self.seq // 2, self.seq % 2
        self.dx = 2 * y + (1 - x)
        self.dy = 2 * (1 - y) + x
        self.dxy = 2 * (1 - y) + (1 - x)
        self.to_x = (self.dx, self.seq)
        self.to_y = (self.dy, self.seq)
        self.to_core = (self.dp, 2 * self.z + 1 - self.core)
        self.to_up = (self.dp, 2 * jnp.minimum(self.z + 1, 3) + self.core)
        self.to_down = (self.dp, 2 * jnp.maximum(self.z - 1, 0) + self.core)
        self.to_across = (self.dp, 2 * jnp.where(self.z < 2, self.z + 2, self.z - 2) + self.core)
        self.has_up = self.z < 3
        self.has_down = self.z > 0

    def near(self, k):
        z = self.z
        return (z, z + 1 - 2 * (z % 2), jnp.where(z < 2, 2, 1), jnp.where(z < 2, 3, 0))[k]

    def greet(self, others=()):
        barrier = pltpu.get_barrier_semaphore()
        for device in (self.to_x, self.to_y, self.to_core) + tuple(others):
            pl.semaphore_signal(barrier, inc=1, device_id=device, device_id_type=MESH)

        @pl.when(self.has_up)
        def _():
            pl.semaphore_signal(barrier, inc=1, device_id=self.to_up, device_id_type=MESH)

        @pl.when(self.has_down)
        def _():
            pl.semaphore_signal(barrier, inc=1, device_id=self.to_down, device_id_type=MESH)

        ends = self.has_up.astype(jnp.int32) + self.has_down.astype(jnp.int32)
        pl.semaphore_wait(barrier, 3 + len(others) + ends)


GATHER_KINDS = 11


def gather_steps(place, shard, full, split, own_sem, send, recv):
    width = full.shape[3]
    z, core = place.z, place.core
    every, left, right = pl.ds(0, width), pl.ds(0, split), pl.ds(split, width - split)
    two = split < width

    def view(d, zz, cc, cols):
        return full.at[d * 4 + zz, cc, :, cols]

    def copy(kind, slot, device, d, zz, cc, cols, src=None):
        dst = view(d, zz, cc, cols)
        return pltpu.make_async_remote_copy(
            src_ref=dst if src is None else src,
            dst_ref=dst,
            send_sem=send.at[kind, slot],
            recv_sem=recv.at[kind, slot],
            device_id=device,
            device_id_type=MESH,
        )

    def pieces(k):
        zk = place.near(k)
        src = shard if k == 0 else None
        dp = place.dp
        return dict(
            x=copy(2, k, place.to_x, dp, zk, core, every, src),
            y=copy(3, k, place.to_y, dp, zk, core, every, src),
            own=copy(6, k, place.to_core, dp, zk, core, every, src),
        )

    def along(k, up):
        zk = place.near(k)
        src = shard if k == 0 else None
        device = place.to_up if up else place.to_down
        dst = view(place.dp, zk, core, every)
        return pltpu.make_async_remote_copy(
            src_ref=dst if src is None else src,
            dst_ref=dst,
            send_sem=send.at[0 if up else 1, k],
            recv_sem=recv.at[0, zk],
            device_id=device,
            device_id_type=MESH,
        )

    def arrive(k):
        zk = place.near(k)
        if k > 0:
            along(k, True).wait_recv()

        @pl.when(jnp.logical_and(zk <= z, place.has_up))
        def _():
            along(k, True).start()

        @pl.when(jnp.logical_and(zk >= z, place.has_down))
        def _():
            along(k, False).start()

        pieces(k)["own"].start()

    def beyond(k):
        made = pieces(k)
        made["x"].start()
        made["y"].start()

    def cross(k):
        zk = place.near(k)
        return (
            copy(2, k, place.to_x, place.dx, zk, core, every),
            copy(3, k, place.to_y, place.dy, zk, core, every),
            copy(4, k, place.to_y, place.dx, zk, core, left),
            copy(5, k, place.to_x, place.dy, zk, core, right) if two else None,
            copy(7, k, place.to_core, place.dx, zk, core, every),
            copy(8, k, place.to_core, place.dy, zk, core, every),
        )

    def forward(k):
        from_x, from_y, left_on, right_on, core_x, core_y = cross(k)
        from_x.wait_recv()
        left_on.start()
        core_x.start()
        from_y.wait_recv()
        if two:
            right_on.start()
        core_y.start()

    def corner(k):
        zk = place.near(k)
        return (
            copy(4, k, place.to_y, place.dxy, zk, core, left),
            copy(5, k, place.to_x, place.dxy, zk, core, right) if two else None,
            copy(9, k, place.to_core, place.dxy, zk, core, left),
            copy(10, k, place.to_core, place.dxy, zk, core, right) if two else None,
        )

    def last(k):
        from_y, from_x, core_left, core_right = corner(k)
        from_y.wait_recv()
        core_left.start()
        if two:
            from_x.wait_recv()
            core_right.start()

    def mine():
        return pltpu.make_async_copy(shard, view(place.dp, z, core, every), own_sem)

    def along_z(k):
        if k == 0:
            mine().start()
        arrive(k)

    def finish():
        mine().wait()
        other = 1 - core
        for k in range(4):
            zk = place.near(k)
            for kind, d, cols in (
                (6, place.dp, every), (7, place.dx, every), (8, place.dy, every),
                (9, place.dxy, left), (10, place.dxy, right),
            ):
                if kind == 10 and not two:
                    continue
                copy(kind, k, place.to_core, d, zk, other, cols).wait_recv()
        for k in range(4):
            zk = place.near(k)

            @pl.when(jnp.logical_and(zk <= z, place.has_up))
            def _():
                along(k, True).wait_send()

            @pl.when(jnp.logical_and(zk >= z, place.has_down))
            def _():
                along(k, False).wait_send()

            made = pieces(k)
            made["x"].wait_send()
            made["y"].wait_send()
            made["own"].wait_send()
            for one in cross(k)[2:] + corner(k)[2:]:
                if one is not None:
                    one.wait_send()

    return along_z, beyond, forward, last, finish


def gather_groups(place, shard, full, split, own_sem, send, recv):
    width = full.shape[3]
    z, core = place.z, place.core
    every, left, right = pl.ds(0, width), pl.ds(0, split), pl.ds(split, width - split)

    def along(k, up):
        zk = place.near(k)
        dst = full.at[place.dp * 4 + zk, core]
        return pltpu.make_async_remote_copy(
            src_ref=shard if k == 0 else dst,
            dst_ref=dst,
            send_sem=send.at[0 if up else 1, k],
            recv_sem=recv.at[0, zk],
            device_id=place.to_up if up else place.to_down,
            device_id_type=MESH,
        )

    def group(kind, device, d, cc, cols):
        some = full.at[pl.ds(d * 4, 4), cc, :, cols]
        return pltpu.make_async_remote_copy(
            src_ref=some, dst_ref=some, send_sem=send.at[kind, 0], recv_sem=recv.at[kind, 0],
            device_id=device, device_id_type=MESH,
        )

    def mine():
        return pltpu.make_async_copy(shard, full.at[place.dp * 4 + z, core], own_sem)

    def moves(k):
        zk = place.near(k)
        return (
            (jnp.logical_and(zk <= z, place.has_up), along(k, True)),
            (jnp.logical_and(zk >= z, place.has_down), along(k, False)),
        )

    def along_z(k):
        if k == 0:
            mine().start()
        else:
            along(k, True).wait_recv()
        for flag, copy in moves(k):

            @pl.when(flag)
            def _(copy=copy):
                copy.start()

    p = place
    sides = lambda: (group(2, p.to_x, p.dp, core, every), group(3, p.to_y, p.dp, core, every))
    halves = lambda: (group(4, p.to_y, p.dx, core, left), group(5, p.to_x, p.dy, core, right))
    owners = (p.dp, p.dx, p.dy, p.dxy)
    cores = lambda cc: [group(6 + j, p.to_core, d, cc, every) for j, d in enumerate(owners)]

    def beyond():
        mine().wait()
        for copy in sides():
            copy.start()
        cores(core)[0].start()

    def forward():
        from_x, from_y = group(2, p.to_x, p.dx, core, every), group(3, p.to_y, p.dy, core, every)
        from_x.wait_recv()
        halves()[0].start()
        from_y.wait_recv()
        halves()[1].start()
        for copy in cores(core)[1:3]:
            copy.start()

    def last():
        group(4, p.to_y, p.dxy, core, left).wait_recv()
        group(5, p.to_x, p.dxy, core, right).wait_recv()
        cores(core)[3].start()

    def finish():
        for copy in cores(1 - core):
            copy.wait_recv()
        for k in range(4):
            for flag, copy in moves(k):

                @pl.when(flag)
                def _(copy=copy):
                    copy.wait_send()

        for copy in sides() + halves() + tuple(cores(core)):
            copy.wait_send()

    return along_z, beyond, forward, last, finish


def gather_scratch():
    return [
        pltpu.SemaphoreType.DMA,
        pltpu.SemaphoreType.DMA((GATHER_KINDS, 4)),
        pltpu.SemaphoreType.DMA((GATHER_KINDS, 4)),
    ]


def part_of(ref, part):
    return ref.at[:, pl.ds(part[0], part[1])]


class Scatter:
    def __init__(self, place, big, out, own, land_core, land_xy, land_z, local, send, recv, split):
        self.place, self.big, self.out = place, big, out
        self.own, self.land_core, self.land_xy, self.land_z = own, land_core, land_xy, land_z
        self.local, self.send, self.recv = local, send, recv
        self.rows, self.width = out.shape
        self.split = split
        self.left, self.right = slice(0, split), slice(split, self.width)

    def groups(self):
        p = self.place
        return (p.dxy, p.dx, p.dy, p.dp)

    def far(self, k):
        return self.place.near(3 - k)

    def source(self, d, zz, cc):
        start = pl.multiple_of((d * 8 + zz * 2 + cc) * self.rows, 16)
        return self.big.at[pl.ds(start, self.rows)]

    def remote(self, src, dst, kind, slot, device):
        return pltpu.make_async_remote_copy(
            src_ref=src, dst_ref=dst, send_sem=self.send.at[kind, slot], recv_sem=self.recv.at[kind, slot],
            device_id=device, device_id_type=MESH,
        )

    def to_other(self, i, k):
        p = self.place
        src = self.source(self.groups()[i], self.far(k), 1 - p.core)
        return self.remote(src, self.land_core.at[i, k], i, k, p.to_core)

    def load(self, i, k):
        p = self.place
        return pltpu.make_async_copy(
            self.source(self.groups()[i], self.far(k), p.core), self.own.at[i, k], self.local.at[i, k]
        )

    def start(self, k):
        for i in range(4):
            self.to_other(i, k).start()
            self.load(i, k).start()

    def join(self, i, k):
        self.load(i, k).wait()
        self.to_other(i, k).wait_recv()
        self.own[i, k] = self.own[i, k] + self.land_core[i, k]

    def side(self, kind, k):
        p = self.place
        left, right = pl.ds(0, self.split), pl.ds(self.split, self.width - self.split)
        group, cols, device = (
            (0, left, p.to_y),
            (0, right, p.to_x),
            (2, left, p.to_y),
            (1, right, p.to_x),
            (2, right, p.to_y),
            (1, left, p.to_x),
        )[kind]
        size = self.split if cols is left else self.width - self.split
        return self.remote(
            self.own.at[group, k, :, cols], self.land_xy.at[kind, k, :, pl.ds(0, size)], 4 + kind, k, device
        )

    def take(self, kind, group, cols, k):
        self.side(kind, k).wait_recv()
        size = cols.stop - cols.start
        self.own[group, k, :, cols] = self.own[group, k, :, cols] + self.land_xy[kind, k, :, 0:size]

    def corner(self, k):
        self.join(0, k)
        self.side(0, k).start()
        self.side(1, k).start()

    def sides(self, k):
        self.join(1, k)
        self.side(3, k).start()
        self.join(2, k)
        self.side(2, k).start()

    def turns(self, k):
        self.take(0, 1, self.left, k)
        self.side(5, k).start()
        self.take(1, 2, self.right, k)
        self.side(4, k).start()

    def along(self, k, up):
        p = self.place
        zk = self.far(k)
        return pltpu.make_async_remote_copy(
            src_ref=self.own.at[3, k],
            dst_ref=self.land_z.at[0 if up else 1, zk],
            send_sem=self.send.at[10, k],
            recv_sem=self.recv.at[10 if up else 11, zk],
            device_id=p.to_up if up else p.to_down,
            device_id_type=MESH,
        )

    def rising(self, k):
        return self.far(k) > self.place.z

    def behind(self, k):
        p = self.place
        rising = self.rising(k)
        return jnp.logical_or(
            jnp.logical_and(rising, p.has_down), jnp.logical_and(jnp.logical_not(rising), p.has_up)
        )

    def send_along(self, k):
        @pl.when(self.rising(k))
        def _():
            self.along(k, True).start()

        @pl.when(jnp.logical_not(self.rising(k)))
        def _():
            self.along(k, False).start()

    def mine(self, k):
        self.join(3, k)
        self.take(2, 3, self.left, k)
        self.take(3, 3, self.right, k)
        self.take(5, 3, self.left, k)
        self.take(4, 3, self.right, k)
        if k < 3:

            @pl.when(jnp.logical_not(self.behind(k)))
            def _():
                self.send_along(k)

    def line(self, k):
        zk = self.far(k)

        @pl.when(jnp.logical_and(self.behind(k), self.rising(k)))
        def _():
            self.along(k, True).wait_recv()
            self.own[3, k] = self.own[3, k] + self.land_z[0, zk]

        @pl.when(jnp.logical_and(self.behind(k), jnp.logical_not(self.rising(k))))
        def _():
            self.along(k, False).wait_recv()
            self.own[3, k] = self.own[3, k] + self.land_z[1, zk]

        @pl.when(self.behind(k))
        def _():
            self.send_along(k)

    def result(self):
        p = self.place
        self.out[...] = self.own[3, 3].astype(f32)

        @pl.when(p.has_down)
        def _():
            self.along(3, True).wait_recv()
            self.out[...] += self.land_z[0, p.z].astype(f32)

        @pl.when(p.has_up)
        def _():
            self.along(3, False).wait_recv()
            self.out[...] += self.land_z[1, p.z].astype(f32)

    def drain(self):
        for k in range(4):
            for i in range(4):
                self.to_other(i, k).wait_send()
            for kind in range(6):
                self.side(kind, k).wait_send()
            if k < 3:
                self.along(k, True).wait_send()

    def steps(self):
        start, corner, sides, turns, mine, line = (
            self.start, self.corner, self.sides, self.turns, self.mine, self.line
        )
        return [
            (0, lambda: start(0)),
            (2, lambda: start(1)),
            (3, lambda: corner(0)),
            (4, lambda: sides(0)),
            (6, lambda: start(2)),
            (8, lambda: turns(0)),
            (9, lambda: corner(1)),
            (10, lambda: sides(1)),
            (12, lambda: start(3)),
            (14, lambda: mine(0)),
            (17, lambda: turns(1)),
            (18, lambda: corner(2)),
            (19, lambda: sides(2)),
            (22, lambda: line(0)),
            (23, lambda: mine(1)),
            (26, lambda: turns(2)),
            (27, lambda: corner(3)),
            (28, lambda: sides(3)),
            (31, lambda: line(1)),
            (32, lambda: mine(2)),
            (35, lambda: turns(3)),
            (40, lambda: line(2)),
            (42, lambda: mine(3)),
            (47, self.result),
            (50, self.drain),
        ]

    @staticmethod
    def scratch(rows, width, split):
        half = max(split, width - split)
        return [
            pltpu.VMEM((4, 4, rows, width), bf16),
            pltpu.VMEM((4, 4, rows, width), bf16),
            pltpu.VMEM((6, 4, rows, half), bf16),
            pltpu.VMEM((2, 4, rows, width), bf16),
            pltpu.SemaphoreType.DMA((4, 4)),
            pltpu.SemaphoreType.DMA((11, 4)),
            pltpu.SemaphoreType.DMA((12, 4)),
        ]


class Small:
    def __init__(self, place, value, out, sent, landed, send, recv):
        p = place
        self.value, self.out, self.sent, self.landed, self.send, self.recv = value, out, sent, landed, send, recv
        pair = 2 * (p.z + 1 - 2 * (p.z % 2)) + p.core
        self.devices = (p.to_core, p.to_x, p.to_y, (p.dp, pair), p.to_across)

    def copy(self, i):
        return pltpu.make_async_remote_copy(
            src_ref=self.sent.at[i], dst_ref=self.landed.at[i], send_sem=self.send.at[i],
            recv_sem=self.recv.at[i], device_id=self.devices[i], device_id_type=MESH,
        )

    def go(self, i):
        if i == 0:
            self.sent[0] = self.value[...]
            self.copy(0).start()
            return
        self.copy(i - 1).wait_recv()
        total = self.sent[i - 1] + self.landed[i - 1]
        if i < 5:
            self.sent[i] = total
            self.copy(i).start()
        else:
            self.out[...] = total
            for k in range(5):
                self.copy(k).wait_send()

    @staticmethod
    def scratch(shape):
        return [
            pltpu.VMEM((5,) + shape, f32),
            pltpu.VMEM((5,) + shape, f32),
            pltpu.SemaphoreType.DMA((5,)),
            pltpu.SemaphoreType.DMA((5,)),
        ]


def scatter_kernel(splits, with_small, *refs):
    count = len(splits)
    ins = count + (1 if with_small else 0)
    bigs, outs = refs[:count], refs[ins : ins + count]
    scratch = refs[2 * ins :]
    place = Place()
    place.greet((place.to_across,) if with_small else ())
    plans = [
        Scatter(place, bigs[i], outs[i], *scratch[7 * i : 7 * i + 7], splits[i]) for i in range(count)
    ]
    small = None
    if with_small:
        small = Small(place, refs[count], refs[ins + count], *scratch[7 * count :])
    small_at = {0: 0, 5: 1, 9: 2, 13: 3, 17: 4, 21: 5}
    for i, steps in enumerate(zip(*[plan.steps() for plan in plans])):
        for _, step in steps:
            step()
        if small and i in small_at:
            small.go(small_at[i])


def scatter(bigs, splits, small, collective_id):
    count = len(bigs)
    spec = pl.BlockSpec(memory_space=pl.ANY)
    vmem = pl.BlockSpec(memory_space=pltpu.VMEM)
    shapes = [(b.shape[0] // 32, b.shape[1]) for b in bigs]
    extra = [] if small is None else [small]
    scratch = sum([Scatter.scratch(s[0], s[1], sp) for s, sp in zip(shapes, splits)], [])
    if small is not None:
        scratch = scratch + Small.scratch(small.shape)
    return pl.pallas_call(
        functools.partial(scatter_kernel, splits, small is not None),
        in_specs=[spec] * count + [vmem] * len(extra),
        out_specs=[vmem] * (count + len(extra)),
        out_shape=[jax.ShapeDtypeStruct(s, f32) for s in shapes]
        + [jax.ShapeDtypeStruct(e.shape, f32) for e in extra],
        scratch_shapes=scratch,
        compiler_params=pltpu.CompilerParams(
            collective_id=collective_id, has_side_effects=True, vmem_limit_bytes=60 * 1024 * 1024
        ),
    )(*bigs, *extra)


class Chain:
    def __init__(self, backward, sent, landed, send, recv):
        self.sent, self.landed, self.send, self.recv = sent, landed, send, recv
        me, count = lax.axis_index("seq"), lax.axis_size("seq")
        turn = -1 if backward else 1
        self.place = count - 1 - me if backward else me
        self.has_prev = self.place > 0
        self.has_next = self.place < count - 1
        self.next = (lax.axis_index("dp"), jnp.clip(me + turn, 0, count - 1))
        self.prev = (lax.axis_index("dp"), jnp.clip(me - turn, 0, count - 1))

    def copy(self, k):
        return pltpu.make_async_remote_copy(
            src_ref=self.sent.at[k], dst_ref=self.landed.at[k], send_sem=self.send.at[k],
            recv_sem=self.recv.at[k], device_id=self.next, device_id_type=MESH,
        )

    def pass_on(self, k, decay, local):
        @pl.when(self.has_prev)
        def _():
            self.copy(k).wait_recv()

        @pl.when(jnp.logical_not(self.has_prev))
        def _():
            self.landed[k] = jnp.zeros_like(self.landed[k])

        @pl.when(self.has_next)
        def _():
            self.sent[k] = (decay() * self.landed[k].astype(f32) + local()).astype(bf16)
            self.copy(k).start()

    def drain(self):
        @pl.when(self.has_next)
        def _():
            for k in range(self.sent.shape[0]):
                self.copy(k).wait_send()

    @staticmethod
    def scratch(count, n, size):
        return [
            pltpu.VMEM((count, n, size), bf16),
            pltpu.VMEM((count, n, size), bf16),
            pltpu.SemaphoreType.DMA((count,)),
            pltpu.SemaphoreType.DMA((count,)),
        ]


def greet_all(place, chain, others=()):
    barrier = pltpu.get_barrier_semaphore()
    flags = [chain.has_prev, chain.has_next]
    devices = [chain.prev, chain.next]
    total = chain.has_prev.astype(jnp.int32) + chain.has_next.astype(jnp.int32)
    if place is not None:
        flags += [place.has_up, place.has_down]
        devices += [place.to_up, place.to_down]
        total = total + place.has_up.astype(jnp.int32) + place.has_down.astype(jnp.int32) + 3 + len(others)
        for device in (place.to_x, place.to_y, place.to_core) + tuple(others):
            pl.semaphore_signal(barrier, inc=1, device_id=device, device_id_type=MESH)
    for flag, device in zip(flags, devices):

        @pl.when(flag)
        def _(device=device):
            pl.semaphore_signal(barrier, inc=1, device_id=device, device_id_type=MESH)

    pl.semaphore_wait(barrier, total)


def front_time(slot):
    if slot < 18:
        return 60 + 1.4 * slot
    if slot < 36:
        return 85 + 1.4 * (slot - 18)
    return 110 + 0.95 * (slot - 36)


GATE_STEPS = ((76, "f"), (90, "l"), (94, "end"))
OUT_STEPS = ((62, "z", 2), (70, "z", 3), (77, "b"), (114, "f"), (126, "l"))


def front_kernel(span, hw, heads, splits, parts, *refs):
    count = len(splits)
    (resid_ref, ngain_ref, cw_ref, cb_ref, bias_ref, rate_ref, skip_ref, gain_ref) = refs[:8]
    given = refs[8:12]
    x_ref, keys_ref, kslope_ref, kcin_ref, col_ref, row_ref, raw_ref, step_ref = refs[12:20]
    rows_ref, slope_ref, cin_ref, y_ref, carried_ref, gate_ref, no_ref, rg_ref = refs[20:28]
    fulls = refs[28 : 28 + count] if count else given
    halo_ref, halo_send, halo_recv, dt_rows = refs[28 + count : 32 + count]
    rest = refs[32 + count :]
    sources = [part_of(given[j], parts[j]) if j != 1 else dt_rows for j in range(count)]
    values, local, scores, decays, gated, squares, wbuf, wkeys, wdt, wsem, ksem = rest[:11]
    chain = Chain(False, *rest[11:15])
    batch, _, width = resid_ref.shape
    ext = span + HALO
    groups = heads // HEADS
    cb_w = HEADS * hw
    inner = groups * cb_w
    n = keys_ref.shape[2] // 2
    i = pl.program_id(0)
    place = Place() if count else None
    plans = [
        (gather_steps if j < 2 else gather_groups)(
            place, sources[j], fulls[j], splits[j], *rest[15 + 3 * j : 18 + 3 * j]
        )
        for j in range(count)
    ]
    low_half = lax.broadcasted_iota(jnp.int32, (span, 2 * hw), 1) < hw

    def weights(j, full):
        cols = pl.ds(pl.multiple_of(j * cb_w, cb_w), cb_w)
        return pltpu.make_async_copy(full.at[:, :, :, cols], wbuf.at[j % 2], wsem.at[j % 2])

    def key_weights():
        return (
            pltpu.make_async_copy(fulls[0].at[:, :, :, pl.ds(inner, 2 * n)], wkeys, ksem.at[0]),
            pltpu.make_async_copy(fulls[1], wdt, ksem.at[1]),
        )

    at = {}
    if count:
        todo = [(one[0], 2) + one[1:] for one in GATE_STEPS] + [(one[0], 3) + one[1:] for one in OUT_STEPS]
        for time, which, *what in sorted(todo):
            slot = min([j for j in range(54) if front_time(j) >= time] + [53])
            at.setdefault(slot, []).append((which, *what))

    def act(which, step, *k):
        along_z, beyond, forward, last, finish = plans[which]
        {"z": along_z, "b": beyond, "f": forward, "l": last, "end": finish}[step](*k)

    def hook(b):
        for slot in sorted(at):
            if slot % batch == b:

                @pl.when(i == 1 + slot // batch)
                def _(slot=slot):
                    for step in at[slot]:
                        act(*step)

    def borrowed():
        return pltpu.make_async_remote_copy(
            src_ref=resid_ref.at[:, pl.ds(span - HALO, HALO)], dst_ref=halo_ref, send_sem=halo_send,
            recv_sem=halo_recv, device_id=chain.next, device_id_type=MESH,
        )

    def lend():
        @pl.when(chain.has_next)
        def _():
            borrowed().start()

    def normed(x):
        x = x.astype(f32)
        rs = lax.rsqrt(jnp.mean(x * x, axis=-1, keepdims=True) + epsilon)
        return (x * rs * ngain_ref[...]).astype(bf16)

    def input_norm():
        for b in range(batch):
            x_ref[b * ext + HALO : (b + 1) * ext] = normed(resid_ref[b])

        @pl.when(chain.has_prev)
        def _():
            borrowed().wait_recv()

        @pl.when(jnp.logical_not(chain.has_prev))
        def _():
            halo_ref[...] = jnp.zeros_like(halo_ref)

        for b in range(batch):
            x_ref[b * ext : b * ext + HALO] = normed(halo_ref[b])

        @pl.when(chain.has_next)
        def _():
            borrowed().wait_send()

    def key_part():
        cw, cb = cw_ref[:, inner:], cb_ref[:, inner:]
        acc = mm(x_ref[...], wkeys[...].reshape(width, 2 * n))
        raw_all = mm(x_ref[...], wdt[...].reshape(width, wdt.shape[3]))
        tri = causal(span, False).astype(f32)
        for b in range(batch):
            a = acc[b * ext : (b + 1) * ext]
            row, slope = silu_slope(conv_pre(a, cw, cb, span))
            keys_ref[b] = row.astype(bf16)
            kslope_ref[b] = slope.astype(bf16)
            kcin_ref[b] = a.astype(bf16)
            raw = raw_all[b * ext + HALO : (b + 1) * ext] + bias_ref[...]
            step = jnp.maximum(raw, 0.0) + jnp.log1p(jnp.exp(-jnp.abs(raw)))
            scaled = lax.dot_general(
                tri, step * rate_ref[...], (((1,), (0,)), ((), ())), precision=highest,
                preferred_element_type=f32,
            ) * LOG2E
            raw_ref[b] = raw
            step_ref[b] = step
            turned = jnp.transpose(scaled)
            for g in range(groups):
                some = slice(g * HEADS, (g + 1) * HEADS)
                col_ref[g, b] = jnp.concatenate([scaled[:, some], step[:, some]], axis=1)
                row_ref[g, b] = turned[some]

    @pl.when(i == 0)
    def _():
        greet_all(place, chain)
        lend()

        def both(step, *k):
            act(0, step, *k)
            act(1, step, *k)

        if count:
            gap = jnp.zeros((dt_rows.shape[0], dt_rows.shape[1] - heads), bf16)
            dt_rows[...] = jnp.concatenate([given[1][...], gap], axis=1)
            both("z", 0)
            both("b", 0)
        input_norm()
        if count:
            both("z", 1)
            both("b", 1)
            both("f", 0)
            both("z", 2)
            both("b", 2)
            act(2, "z", 0)
            both("f", 1)
            both("z", 3)
            both("b", 3)
            both("f", 2)
            act(2, "z", 1)
            both("l", 0)
            act(2, "z", 2)
            both("f", 3)
            act(3, "z", 0)
            both("l", 1)
            act(2, "z", 3)
            act(2, "b")
            both("l", 2)
            both("l", 3)
            act(3, "z", 1)
            both("end")
        for copy in key_weights():
            copy.start()
        weights(0, fulls[0]).start()
        for copy in key_weights():
            copy.wait()
        key_part()

    def values_part(g, b, acc):
        a = acc[b * ext : (b + 1) * ext]
        some = pl.ds(pl.multiple_of(g * cb_w, cb_w), cb_w)
        row, slope = silu_slope(conv_pre(a, cw_ref[:, some], cb_ref[:, some], span))
        row = row.astype(bf16)
        rows_ref[b] = row
        slope_ref[b] = slope.astype(bf16)
        values[g * batch + b] = row
        cin_ref[b] = a.astype(bf16)
        cols = col_ref[g, b]
        c, step = cols[:, :HEADS], cols[:, HEADS:]
        weight = jnp.exp2(c[span - 1 : span] - c) * step
        vw = (row.astype(f32) * spread(weight, hw)).astype(bf16)
        local[g * batch + b] = mm_tn(keys_ref[b, :, :n], vw)
        decays[g * batch + b] = spread(jnp.exp2(c[span - 1 : span]), hw)

    def rows_part(g, b):
        k_in, k_out = keys_ref[b, :, :n], keys_ref[b, :, n:]

        @pl.when(g == 0)
        def _():
            scores[b] = jnp.where(causal(span, False), mm_nt(k_out, k_in), 0.0)

        cols = col_ref[g, b]
        c, step = cols[:, :HEADS], cols[:, HEADS:]
        v = values[g * batch + b].astype(f32)
        vs = (v * spread(step, hw)).astype(bf16)
        s = scores[b]
        rows = row_ref[g, b]
        sums = []
        for p in range(HEADS // 2):
            pair = vs[:, p * 2 * hw : (p + 1) * 2 * hw]
            total = None
            for q in range(2):
                h = 2 * p + q
                gap = jnp.minimum(c[:, h : h + 1] - rows[h : h + 1, :], 0.0)
                u = (jnp.exp2(gap) * s).astype(bf16)
                keep = low_half if q == 0 else jnp.logical_not(low_half)
                term = mm(u, jnp.where(keep, pair, jnp.zeros_like(pair)))
                total = term if total is None else total + term
            sums.append(total)
        inside = jnp.concatenate(sums, axis=1)
        came = chain.landed[g * batch + b]
        carried_ref[b] = came
        skip = skip_ref[:, pl.ds(pl.multiple_of(g * cb_w, cb_w), cb_w)]
        y = inside + mm(k_out, came) * spread(jnp.exp2(c), hw) + skip * v
        y_ref[b] = y
        gated[g * batch + b] = y

    def gate_part(g, b, w):
        gate = mm(x_ref[b * ext + HALO : (b + 1) * ext], w)
        gate_ref[b] = gate.astype(bf16)
        act, _ = silu_parts(gate)
        gr = gated[g * batch + b] * act
        gated[g * batch + b] = gr
        total = sum([gr[:, j * 128 : (j + 1) * 128] * gr[:, j * 128 : (j + 1) * 128] for j in range(cb_w // 128)])
        squares[b] = jnp.where(g == 0, 0.0, squares[b]) + total

    @pl.when(jnp.logical_and(i > 0, i <= groups))
    def _():
        g = i - 1
        weights(g, fulls[0]).wait()

        @pl.when(g < groups - 1)
        def _():
            weights(g + 1, fulls[0]).start()

        acc = mm(x_ref[...], wbuf[g % 2].reshape(width, cb_w))
        for b in range(batch):
            hook(b)
            values_part(g, b, acc)

    @pl.when(jnp.logical_and(i > groups, i <= 2 * groups))
    def _():
        for b in range(batch):
            hook(b)
            rows_part(i - 1 - groups, b)

    @pl.when(i > 2 * groups)
    def _():
        g = i - 1 - 2 * groups

        @pl.when(g == 0)
        def _():
            weights(0, fulls[2]).start()

        weights(g, fulls[2]).wait()

        @pl.when(g < groups - 1)
        def _():
            weights(g + 1, fulls[2]).start()

        for b in range(batch):
            hook(b)
            gate_part(g, b, wbuf[g % 2].reshape(width, cb_w))

    def ready(j):
        for b in range(batch):
            k = j * batch + b
            chain.pass_on(k, lambda: decays[k], lambda: local[k])

    early = i - 1 - chain.place

    @pl.when(jnp.logical_and(jnp.logical_and(early >= 0, early < groups), i - 1 <= groups - 1 + early))
    def _():
        ready(early)

    late = i - groups

    @pl.when(jnp.logical_and(jnp.logical_and(late >= 0, late < groups), chain.place > groups - 1))
    def _():
        ready(late)

    @pl.when(i == 3 * groups)
    def _():
        for b in range(batch):
            total = jnp.sum(squares[b], axis=1, keepdims=True)
            rg = lax.rsqrt(total * (1.0 / inner) + epsilon)
            rg_ref[b] = jnp.broadcast_to(rg, rg_ref.shape[1:])
            for g in range(groups):
                part = slice(g * cb_w, (g + 1) * cb_w)
                no_ref[b, :, part] = (gated[g * batch + b] * rg * gain_ref[:, part]).astype(bf16)
        if count:
            act(3, "end")
        chain.drain()


def front(resid, norm_gain, cw, cb, bias, rate, skip, gain, shards, parts, splits, hw, heads, n, collective_id):
    batch, span, width = resid.shape
    ext = span + HALO
    groups = heads // HEADS
    cb_w = HEADS * hw
    inner = groups * cb_w
    blocks = groups * batch
    lanes = bias.shape[1]
    hbm = pl.BlockSpec(memory_space=pl.ANY)
    count = len(splits)
    clip = lambda k: jnp.clip(k, 0, groups - 1)
    first = lambda i: clip(i - 1)
    then = lambda i: clip(i - 1 - groups)
    last = lambda i: clip(i - 1 - 2 * groups)
    once = lambda shape: pl.BlockSpec(shape, lambda i: (0,) * len(shape), pipeline_mode=pl.Buffered(1))
    block = lambda f, rows: pl.BlockSpec((batch, rows, cb_w), lambda i: (0, 0, f(i)))
    shaped = lambda shape, dtype: (once(shape), jax.ShapeDtypeStruct(shape, dtype))
    columns = lambda f, rows, dtype: (block(f, rows), jax.ShapeDtypeStruct((batch, rows, inner), dtype))
    outs = [
        shaped((batch * ext, width), bf16),
        shaped((batch, span, 2 * n), bf16),
        shaped((batch, span, 2 * n), bf16),
        shaped((batch, ext, 2 * n), bf16),
        shaped((groups, batch, span, 2 * HEADS), f32),
        shaped((groups, batch, HEADS, span), f32),
        shaped((batch, span, lanes), f32),
        shaped((batch, span, lanes), f32),
        columns(first, span, bf16),
        columns(first, span, bf16),
        columns(first, ext, bf16),
        columns(then, span, f32),
        columns(then, n, bf16),
        columns(last, span, bf16),
        shaped((batch, span, inner), bf16),
        shaped((batch, span, 8), f32),
    ]
    if count:
        outs += [
            (hbm, jax.ShapeDtypeStruct((16, 2, s.shape[0], p[1]), s.dtype)) for s, p in zip(shards, parts)
        ]
    else:
        shards = [s.reshape(16, 2, s.shape[0] // 32, s.shape[1]) for s in shards]
    given_specs = [hbm, once(shards[1].shape) if count else hbm, hbm, hbm]
    small_ins = [resid, norm_gain, cw, cb, bias, rate, skip, gain]
    return pl.pallas_call(
        functools.partial(front_kernel, span, hw, heads, splits, parts),
        grid=(1 + 3 * groups,),
        in_specs=[once(x.shape) for x in small_ins] + given_specs,
        out_specs=[o[0] for o in outs],
        out_shape=[o[1] for o in outs],
        scratch_shapes=[
            pltpu.VMEM((batch, HALO, width), bf16),
            pltpu.SemaphoreType.DMA,
            pltpu.SemaphoreType.DMA,
            pltpu.VMEM((width // 32, lanes), bf16),
            pltpu.VMEM((blocks, span, cb_w), bf16),
            pltpu.VMEM((blocks, n, cb_w), f32),
            pltpu.VMEM((batch, span, span), f32),
            pltpu.VMEM((blocks, 1, cb_w), f32),
            pltpu.VMEM((blocks, span, cb_w), f32),
            pltpu.VMEM((batch, span, 128), f32),
            pltpu.VMEM((2, 16, 2, width // 32, cb_w), bf16),
            pltpu.VMEM((16, 2, width // 32, 2 * n), bf16),
            pltpu.VMEM((16, 2, width // 32, lanes), bf16),
            pltpu.SemaphoreType.DMA((2,)),
            pltpu.SemaphoreType.DMA((2,)),
        ]
        + Chain.scratch(blocks, n, cb_w)
        + gather_scratch() * count,
        compiler_params=pltpu.CompilerParams(
            collective_id=collective_id, has_side_effects=True, vmem_limit_bytes=62 * 1024 * 1024
        ),
    )(*small_ins, *shards)


def scatter_beside(i, batch, slots, starts, splits, bigs, outs, scratch):
    if not splits:
        return lambda b: None
    place = Place()
    plans = [
        Scatter(place, bigs[j], outs[j], *scratch[7 * j : 7 * j + 7], splits[j]).steps()
        for j in range(len(splits))
    ]
    at = {}
    for steps in zip(*plans):
        for time, step in steps:
            slot = min([k for k in range(slots) if starts(k) >= time] + [slots - 1])
            at.setdefault(slot, []).append(step)

    def run(b):
        for slot, steps in at.items():
            if slot % batch == b:

                @pl.when(i == slot // batch)
                def _(steps=steps):
                    for step in steps:
                        step()

    return run


def gate_back_kernel(span, hw, groups, splits, *refs):
    count = len(splits)
    (mg_ref, w_ref, y_ref, gate_ref, norm_ref, gain_ref, v_ref, keys_ref, col_ref, row_ref) = refs[:10]
    h_ref, skip_ref = refs[10:12]
    bigs = refs[12 : 12 + count]
    (dgate_ref, dv_ref, later_ref, cols_ref, dq_ref, dk_ref, dgain_ref, dskip_ref) = refs[12 + count : 20 + count]
    outs = refs[20 + count : 20 + 2 * count]
    rest = refs[20 + 2 * count :]
    scores, dscores, dqacc, gbs, rises, local, decays = rest[:7]
    chain = Chain(True, *rest[7:11])
    batch = mg_ref.shape[0]
    blocks = groups * batch
    i = pl.program_id(0)
    g = i % groups
    n = keys_ref.shape[2] // 2
    skip = skip_ref[...]
    low_half = lax.broadcasted_iota(jnp.int32, (span, 2 * hw), 1) < hw

    @pl.when(i == 0)
    def _():
        greet_all(Place() if count else None, chain)

    hook = scatter_beside(i, batch, 2 * blocks, lambda k: gate_start(k, blocks), splits, bigs, outs, rest[11:])

    def gate_part(b):
        at = g * batch + b
        cols = col_ref[0, b]
        c = cols[:, :HEADS]
        no_grad = mm_nt(mg_ref[b], w_ref[...])
        gate = gate_ref[b].astype(f32)
        y = y_ref[b]
        rg = norm_ref[b][:, 0:1]
        mean = norm_ref[b][:, 1:2]
        act, sg = silu_parts(gate)
        gn = y * act * rg
        dgain = jnp.sum(no_grad * gn, axis=0, keepdims=True)
        dg = rg * (no_grad * gain_ref[...] - gn * mean)
        dgate_ref[b] = (dg * y * (sg * (1.0 + gate * (1.0 - sg)))).astype(bf16)
        gb = (dg * act).astype(bf16)
        gbs[at] = gb
        gf = gb.astype(f32)
        v = v_ref[b].astype(f32)
        dskip = jnp.sum(gf * v, axis=0, keepdims=True)
        rises[at] = gather_heads(gf * (y - skip * v), hw)
        ge = (gf * spread(jnp.exp2(c), hw)).astype(bf16)
        local[at] = mm_tn(keys_ref[b, :, n:], ge)
        decays[at] = spread(jnp.exp2(c[span - 1 : span]), hw)
        part = mm_nt(ge, h_ref[b])

        @pl.when(g == 0)
        def _():
            dqacc[b] = part

        @pl.when(g != 0)
        def _():
            dqacc[b] += part

        if b == 0:
            dgain_ref[...] = dgain
            dskip_ref[...] = dskip
        else:
            dgain_ref[...] += dgain
            dskip_ref[...] += dskip

    def block_part(b):
        at = g * batch + b
        cols = col_ref[0, b]
        c, step = cols[:, :HEADS], cols[:, HEADS:]
        k_in, k_out = keys_ref[b, :, :n], keys_ref[b, :, n:]

        @pl.when(g == 0)
        def _():
            scores[b] = jnp.where(causal(span, True), mm_nt(k_in, k_out), 0.0)
            dscores[b] = jnp.zeros_like(dscores[b])

        later_ref[b] = chain.landed[at]
        gb = gbs[at]
        gf = gb.astype(f32)
        v = v_ref[b].astype(f32)
        step_wide = spread(step, hw)
        vs = (v * step_wide).astype(bf16)
        rows = row_ref[0, b]
        s = scores[b]
        parts = []
        ds = dscores[b]
        for p in range(HEADS // 2):
            lanes = slice(p * 2 * hw, (p + 1) * 2 * hw)
            total = None
            for q in range(2):
                h = 2 * p + q
                gap = jnp.minimum(rows[h : h + 1, :] - c[:, h : h + 1], 0.0)
                decay = jnp.exp2(gap)
                u = (decay * s).astype(bf16)
                keep = low_half if q == 0 else jnp.logical_not(low_half)
                half = jnp.where(keep, gb[:, lanes], jnp.zeros_like(gb[:, lanes]))
                term = mm(u, half)
                total = term if total is None else total + term
                ds = ds + decay * mm_nt(vs[:, lanes], half)
            parts.append(total)
        dscores[b] = ds
        u_all = jnp.concatenate(parts, axis=1)
        dv_ref[b] = (u_all * step_wide + skip * gf).astype(bf16)
        fall = gather_heads(vs.astype(f32) * u_all, hw)
        direct = gather_heads(v * u_all, hw)
        cols_ref[0, b] = jnp.concatenate([rises[at] - fall, direct], axis=1)

        @pl.when(g == groups - 1)
        def _():
            low = jnp.where(causal(span, True), dscores[b], 0.0).astype(bf16)
            dq_ref[b] = dqacc[b] + mm_tn(low, k_in)
            dk_ref[b] = mm(low, k_out)

    lag = jnp.minimum(5 * chain.place // 2, blocks - 1)
    for b in range(batch):
        hook(b)

        @pl.when(i < groups)
        def _():
            gate_part(b)

        @pl.when(i >= groups)
        def _():
            block_part(b)

        k = i * batch + b - lag

        @pl.when(jnp.logical_and(k >= 0, k < blocks))
        def _():
            chain.pass_on(k, lambda: decays[k], lambda: local[k])

    @pl.when(i == 2 * groups - 1)
    def _():
        chain.drain()


def gate_backward(
    mg, w_out, y, gate, norms, gain, v, keys, colpack, rowpack, carried, skip, bigs, splits, hw, span,
    collective_id,
):
    hbm = pl.BlockSpec(memory_space=pl.ANY)
    shapes = [(x.shape[0] // 32, x.shape[1]) for x in bigs]
    batch, _, width = mg.shape
    groups = colpack.shape[0]
    cb_w = HEADS * hw
    inner = groups * cb_w
    n = keys.shape[2] // 2
    blocks = groups * batch
    first = lambda i: jnp.minimum(i, groups - 1)
    then = lambda i: jnp.maximum(i - groups, 0)
    both = lambda i: i % groups
    block = lambda f, rows: pl.BlockSpec((batch, rows, cb_w), lambda i: (0, 0, f(i)))
    lanes = lambda f: pl.BlockSpec((1, cb_w), lambda i: (0, f(i)))
    whole = lambda shape: pl.BlockSpec(shape, lambda i: (0,) * len(shape))
    return pl.pallas_call(
        functools.partial(gate_back_kernel, span, hw, groups, splits),
        grid=(2 * groups,),
        in_specs=[
            whole(mg.shape),
            pl.BlockSpec((cb_w, width), lambda i: (first(i), 0)),
            block(first, span),
            block(first, span),
            whole(norms.shape),
            lanes(first),
            block(both, span),
            whole(keys.shape),
            pl.BlockSpec((1,) + colpack.shape[1:], lambda i: (both(i), 0, 0, 0)),
            pl.BlockSpec((1,) + rowpack.shape[1:], lambda i: (then(i), 0, 0, 0)),
            block(first, n),
            lanes(both),
        ]
        + [hbm] * len(bigs),
        out_specs=[
            block(first, span),
            block(then, span),
            block(then, n),
            pl.BlockSpec((1, batch, span, 2 * HEADS), lambda i: (then(i), 0, 0, 0)),
            whole((batch, span, n)),
            whole((batch, span, n)),
            lanes(first),
            lanes(first),
        ]
        + [whole(s) for s in shapes],
        out_shape=[
            jax.ShapeDtypeStruct((batch, span, inner), bf16),
            jax.ShapeDtypeStruct((batch, span, inner), bf16),
            jax.ShapeDtypeStruct((batch, n, inner), bf16),
            jax.ShapeDtypeStruct((groups, batch, span, 2 * HEADS), f32),
            jax.ShapeDtypeStruct((batch, span, n), f32),
            jax.ShapeDtypeStruct((batch, span, n), f32),
            jax.ShapeDtypeStruct((1, inner), f32),
            jax.ShapeDtypeStruct((1, inner), f32),
        ]
        + [jax.ShapeDtypeStruct(s, f32) for s in shapes],
        scratch_shapes=[
            pltpu.VMEM((batch, span, span), f32),
            pltpu.VMEM((batch, span, span), f32),
            pltpu.VMEM((batch, span, n), f32),
            pltpu.VMEM((blocks, span, cb_w), bf16),
            pltpu.VMEM((blocks, span, HEADS), f32),
            pltpu.VMEM((blocks, n, cb_w), f32),
            pltpu.VMEM((blocks, 1, cb_w), f32),
        ]
        + Chain.scratch(blocks, n, cb_w)
        + sum([Scatter.scratch(s[0], s[1], sp) for s, sp in zip(shapes, splits)], []),
        compiler_params=pltpu.CompilerParams(
            collective_id=collective_id, has_side_effects=True, vmem_limit_bytes=60 * 1024 * 1024
        ),
    )(mg, w_out, y, gate, norms, gain, v, keys, colpack, rowpack, carried, skip, *bigs)


def conv_back(dv, slope, a, cw, span, padded, out_ref, b):
    taps = cw.shape[0]
    ext = span + HALO
    pg = dv * slope
    padded[HALO : HALO + span] = pg
    total, dcw = None, []
    for k in range(taps):
        moved = padded[taps - 1 - k : taps - 1 - k + ext]
        term = cw[k : k + 1] * moved
        total = term if total is None else total + term
        dcw.append(jnp.sum(moved * a, axis=0, keepdims=True))
    out_ref[b] = total.astype(bf16)
    return jnp.concatenate(dcw, axis=0), jnp.sum(pg, axis=0, keepdims=True)


def back_kernel(span, hw, groups, splits, *refs):
    count = len(splits)
    (later_ref, h_ref, keys_ref, v_ref, dv_ref, col_ref, cin_ref, cw_ref, slope_ref) = refs[:9]
    bigs = refs[9 : 9 + count]
    cig_ref, cols_ref, dk_ref, dcw_ref, dcb_ref, dlast_ref = refs[9 + count : 15 + count]
    outs = refs[15 + count : 15 + 2 * count]
    rest = refs[15 + 2 * count :]
    padded, dkacc = rest[:2]
    i = pl.program_id(0)
    batch = dk_ref.shape[0]
    n = keys_ref.shape[2] // 2

    @pl.when(i == 0)
    def _():
        if count:
            Place().greet()
        padded[0:16] = jnp.zeros((16, padded.shape[1]), f32)
        padded[16 + span :] = jnp.zeros((padded.shape[0] - 16 - span, padded.shape[1]), f32)

    hook = scatter_beside(i, batch, groups * batch, back_start, splits, bigs, outs, rest[2:])
    for b in range(batch):
        hook(b)
        cols = col_ref[0, b]
        c, step = cols[:, :HEADS], cols[:, HEADS:]
        low = later_ref[b]
        left = spread(jnp.exp2(c[span - 1 : span] - c), hw)
        kdh = mm(keys_ref[b, :, :n], low) * left
        v = v_ref[b].astype(f32)
        step_wide = spread(step, hw)
        cols_ref[0, b] = gather_heads(v * kdh, hw)
        dlast_ref[b] = jnp.broadcast_to(
            jnp.sum(low.astype(f32) * h_ref[b].astype(f32), axis=0, keepdims=True), dlast_ref.shape[1:]
        )
        vw = (v * step_wide * left).astype(bf16)
        part = mm_nt(vw, low)

        @pl.when(i == 0)
        def _():
            dkacc[b] = part

        @pl.when(i != 0)
        def _():
            dkacc[b] += part

        @pl.when(i == groups - 1)
        def _():
            dk_ref[b] = dkacc[b]

        dv = dv_ref[b].astype(f32) + kdh * step_wide
        dcw, dcb = conv_back(
            dv, slope_ref[b].astype(f32), cin_ref[b].astype(f32), cw_ref[...], span, padded, cig_ref, b
        )
        if b == 0:
            dcw_ref[...] = dcw
            dcb_ref[...] = dcb
        else:
            dcw_ref[...] += dcw
            dcb_ref[...] += dcb


def back(later, carried, keys, v, dv, colpack, cin, cw, slope, bigs, splits, hw, span, collective_id):
    batch = v.shape[0]
    groups = colpack.shape[0]
    cb_w = HEADS * hw
    inner = groups * cb_w
    n = keys.shape[2] // 2
    ext = span + HALO
    taps = cw.shape[0]
    block = lambda rows: pl.BlockSpec((batch, rows, cb_w), lambda i: (0, 0, i))
    lanes = lambda rows: pl.BlockSpec((rows, cb_w), lambda i: (0, i))
    hbm = pl.BlockSpec(memory_space=pl.ANY)
    shapes = [(x.shape[0] // 32, x.shape[1]) for x in bigs]
    return pl.pallas_call(
        functools.partial(back_kernel, span, hw, groups, splits),
        grid=(groups,),
        in_specs=[
            block(n),
            block(n),
            pl.BlockSpec(keys.shape, lambda i: (0, 0, 0)),
            block(span),
            block(span),
            pl.BlockSpec((1,) + colpack.shape[1:], lambda i: (i, 0, 0, 0)),
            block(ext),
            lanes(taps),
            block(span),
        ]
        + [hbm] * len(bigs),
        out_specs=[
            block(ext),
            pl.BlockSpec((1, batch, span, HEADS), lambda i: (i, 0, 0, 0)),
            pl.BlockSpec((batch, span, n), lambda i: (0, 0, 0)),
            lanes(taps),
            lanes(1),
            block(8),
        ]
        + [pl.BlockSpec(s, lambda i: (0, 0)) for s in shapes],
        out_shape=[
            jax.ShapeDtypeStruct((batch, ext, inner), bf16),
            jax.ShapeDtypeStruct((groups, batch, span, HEADS), f32),
            jax.ShapeDtypeStruct((batch, span, n), f32),
            jax.ShapeDtypeStruct((taps, inner), f32),
            jax.ShapeDtypeStruct((1, inner), f32),
            jax.ShapeDtypeStruct((batch, 8, inner), f32),
        ]
        + [jax.ShapeDtypeStruct(s, f32) for s in shapes],
        scratch_shapes=[
            pltpu.VMEM((span + 32, cb_w), f32),
            pltpu.VMEM((batch, span, n), f32),
        ]
        + sum([Scatter.scratch(s[0], s[1], sp) for s, sp in zip(shapes, splits)], []),
        compiler_params=pltpu.CompilerParams(
            collective_id=collective_id if bigs else None,
            has_side_effects=bool(bigs),
            vmem_limit_bytes=58 * 1024 * 1024,
        ),
    )(later, carried, keys, v, dv, colpack, cin, cw, slope, *bigs)


def keys_back_kernel(span, dk_ref, dk2_ref, dq_ref, cin_ref, cw_ref, slope_ref, cig_ref, dcw_ref, dcb_ref, padded):
    batch = dk_ref.shape[0]
    padded[...] = jnp.zeros_like(padded)
    for b in range(batch):
        dv = jnp.concatenate([dk_ref[b] + dk2_ref[b], dq_ref[b]], axis=1)
        dcw, dcb = conv_back(
            dv, slope_ref[b].astype(f32), cin_ref[b].astype(f32), cw_ref[...], span, padded, cig_ref, b
        )
        if b == 0:
            dcw_ref[...] = dcw
            dcb_ref[...] = dcb
        else:
            dcw_ref[...] += dcw
            dcb_ref[...] += dcb


def keys_backward(dk, dk2, dq, cin, cw, slope, span):
    batch, ext, width = cin.shape
    return pl.pallas_call(
        functools.partial(keys_back_kernel, span),
        in_specs=[pl.BlockSpec(memory_space=pltpu.VMEM)] * 6,
        out_specs=[pl.BlockSpec(memory_space=pltpu.VMEM)] * 3,
        out_shape=[
            jax.ShapeDtypeStruct(cin.shape, bf16),
            jax.ShapeDtypeStruct(cw.shape, f32),
            jax.ShapeDtypeStruct((1, width), f32),
        ],
        scratch_shapes=[pltpu.VMEM((span + 32, width), f32)],
        compiler_params=params_of(40),
    )(dk, dk2, dq, cin, cw, slope)


def tail_kernel(span, splits, with_small, *refs):
    count = len(splits)
    (cig_ref, wc_ref, dgate_ref, wg_ref, keys_ref, wk_ref, low_ref, wd_ref) = refs[:8]
    resid_ref, mg_ref, gain_ref, parts_ref = refs[8:12]
    bigs = refs[12 : 12 + count]
    grad_ref, sums_ref = refs[12 + count : 14 + count]
    outs = refs[14 + count : 14 + 2 * count]
    rest = refs[14 + 2 * count :]
    acc, rim, rim_in, value, halo_send, halo_recv = rest[:6]
    i = pl.program_id(0)
    steps = pl.num_programs(0)
    half = steps // 2
    batch, _, width = resid_ref.shape
    ext = span + HALO
    chain = Chain(True, rim, rim_in, halo_send, halo_recv)
    place = Place() if count else None
    plan = small = None
    times = []
    if count:
        plan = Scatter(place, bigs[0], outs[0], *rest[6:13], splits[0])
        times = plan.steps()
        small = Small(place, value, sums_ref, *rest[13:17])

    @pl.when(i == 0)
    def _():
        greet_all(place, chain, (place.to_across,) if count else ())

    slots = TAIL_STEPS
    early = [(t, s) for t, s in times if t <= tail_start(slots - 1)]
    late = [s for t, s in times if t > tail_start(slots - 1)]
    at = {}
    for time, step in early:
        at.setdefault(min(k for k in range(slots) if tail_start(k) >= time), []).append(step)
    for slot, some in at.items():

        @pl.when(i == slot)
        def _(some=some):
            for step in some:
                step()

    flat = lambda ref: ref[...].reshape(batch * ext, ref.shape[2])

    @pl.when(i == 0)
    def _():
        acc[...] = mm_nt(flat(cig_ref), wc_ref[...])
        acc[...] += mm_nt(flat(keys_ref), wk_ref[...])
        acc[...] += mm_nt(flat(low_ref), wd_ref[...])

    @pl.when(jnp.logical_and(i > 0, i < half))
    def _():
        acc[...] += mm_nt(flat(cig_ref), wc_ref[...])

    @pl.when(i == half - 1)
    def _():
        for b in range(batch):
            rim[0, b] = acc[b * ext : b * ext + HALO].astype(bf16)

        @pl.when(chain.has_next)
        def _():
            chain.copy(0).start()

    @pl.when(i >= half)
    def _():
        for b in range(batch):
            rows = slice(b * ext + HALO, (b + 1) * ext)
            acc[rows] += mm_nt(dgate_ref[b], wg_ref[...])

    @pl.when(i == steps - 1)
    def _():
        @pl.when(chain.has_prev)
        def _():
            chain.copy(0).wait_recv()
            for b in range(batch):
                rows = slice((b + 1) * ext - HALO, (b + 1) * ext)
                acc[rows] += rim_in[0, b].astype(f32)

        for step in late[:2]:
            step()
        total = jnp.zeros((1, width), f32)
        for b in range(batch):
            for step in late[2 + b : 3 + b]:
                step()
            grad = acc[b * ext + HALO : (b + 1) * ext]
            x = resid_ref[b].astype(f32)
            rs = lax.rsqrt(jnp.mean(x * x, axis=-1, keepdims=True) + epsilon)
            nz = x * rs
            fg = grad * gain_ref[...]
            total = total + jnp.sum(grad * nz, axis=0, keepdims=True)
            mean = jnp.mean(fg * nz, axis=-1, keepdims=True)
            grad_ref[b] = (mg_ref[b].astype(f32) + rs * (fg - nz * mean)).astype(bf16)
        lead = width // 128
        value[lead:] = parts_ref[lead:]
        for r in range(lead):
            value[r : r + 1] = total[:, r * 128 : (r + 1) * 128]
        if small is None:
            sums_ref[...] = value[...]
        else:
            after = late[2 + batch :]
            spots = [len(after) * k // 6 for k in range(6)]
            for j, step in enumerate(after):
                for k in range(6):
                    if spots[k] == j:
                        small.go(k)
                step()

        @pl.when(chain.has_next)
        def _():
            chain.copy(0).wait_send()


TAIL_STEPS = 12


def tail_start(k):
    return 2.2 * k


def tail(cig, w_conv, dgate, w_gate, cig_keys, step_low, w_dt, resid, mg, gain, parts, bigs, splits, span, collective_id):
    batch, ext, inner = cig.shape
    width = resid.shape[2]
    cb_w = inner // (TAIL_STEPS // 2)
    half = TAIL_STEPS // 2
    keys_w = cig_keys.shape[2]
    whole = lambda shape: pl.BlockSpec(shape, lambda i: (0,) * len(shape))
    first = lambda i: jnp.minimum(i, half - 1)
    then = lambda i: jnp.maximum(i - half, 0)
    hbm = pl.BlockSpec(memory_space=pl.ANY)
    shapes = [(x.shape[0] // 32, x.shape[1]) for x in bigs]
    return pl.pallas_call(
        functools.partial(tail_kernel, span, splits, bool(bigs)),
        grid=(TAIL_STEPS,),
        in_specs=[
            pl.BlockSpec((batch, ext, cb_w), lambda i: (0, 0, first(i))),
            pl.BlockSpec((width, cb_w), lambda i: (0, first(i))),
            pl.BlockSpec((batch, span, cb_w), lambda i: (0, 0, then(i))),
            pl.BlockSpec((width, cb_w), lambda i: (0, then(i))),
            whole(cig_keys.shape),
            pl.BlockSpec((width, keys_w), lambda i: (0, inner // keys_w)),
            whole(step_low.shape),
            whole(w_dt.shape),
            whole(resid.shape),
            whole(mg.shape),
            whole(gain.shape),
            whole(parts.shape),
        ]
        + [hbm] * len(bigs),
        out_specs=[whole(resid.shape), whole(parts.shape)] + [whole(s) for s in shapes],
        out_shape=[jax.ShapeDtypeStruct(resid.shape, bf16), jax.ShapeDtypeStruct(parts.shape, f32)]
        + [jax.ShapeDtypeStruct(s, f32) for s in shapes],
        scratch_shapes=[
            pltpu.VMEM((batch * ext, width), f32),
            pltpu.VMEM((1, batch, HALO, width), bf16),
            pltpu.VMEM((1, batch, HALO, width), bf16),
            pltpu.VMEM(parts.shape, f32),
            pltpu.SemaphoreType.DMA((1,)),
            pltpu.SemaphoreType.DMA((1,)),
        ]
        + sum([Scatter.scratch(s[0], s[1], sp) for s, sp in zip(shapes, splits)], [])
        + (Small.scratch(parts.shape) if bigs else []),
        compiler_params=pltpu.CompilerParams(
            collective_id=collective_id, has_side_effects=True, vmem_limit_bytes=60 * 1024 * 1024
        ),
    )(cig, w_conv, dgate, w_gate, cig_keys, w_conv, step_low, w_dt, resid, mg, gain, parts, *bigs)


def own_kernels():
    return lax.axis_size("dp") == 4 and lax.axis_size("seq") == 8


def gather_rows(shards, parts):
    return [
        lax.all_gather(s[:, p[0] : p[0] + p[1]], ("dp", "seq"), axis=0, tiled=True)
        for s, p in zip(shards, parts)
    ]


def scatter_rows(bigs, splits, small, collective_id):
    if own_kernels():
        return scatter(bigs, splits, small, collective_id)
    outs = [lax.psum_scatter(b, ("dp", "seq"), scatter_dimension=0, tiled=True).astype(f32) for b in bigs]
    return outs + ([] if small is None else [lax.psum(small, ("dp", "seq"))])


def half_of(width):
    return (width // 2 + 127) // 128 * 128


def ungrouped(cols):
    groups, batch, span, each = cols.shape
    return jnp.transpose(cols, (1, 2, 0, 3)).reshape(batch, span, groups * each)


def gate_start(k, blocks):
    return 1.0 * k if k < blocks else 1.0 * blocks + 1.6 * (k - blocks)


def back_start(k):
    return 2.9 * k


def on_device(
    resid_in, out_grad, lengths, norm_gain, in_proj, dt_proj, conv_weight, conv_bias, dt_bias, a_log,
    skip_scale, gate_gain, out_proj,
):
    batch, span, width = resid_in.shape
    inner = gate_gain.shape[0]
    heads = a_log.shape[0]
    hw = inner // heads
    n = (in_proj.shape[1] - 2 * inner) // 2
    cb_w = HEADS * hw
    positions = lax.axis_index("seq") * span + lax.iota(jnp.int32, span)
    mask = (positions[None, :] < lengths[:, None]).astype(f32)[..., None]

    conv_cols = in_proj.shape[1] - inner
    dt_pad = (-(conv_cols + heads)) % 128
    conv_all = conv_cols + heads + dt_pad
    dt_shard = jnp.pad(dt_proj, ((0, 0), (0, dt_pad)))
    shards, parts = (
        [in_proj, dt_proj if own_kernels() else dt_shard, in_proj, out_proj],
        [(inner, conv_cols), (0, heads + dt_pad), (0, inner), (0, width)],
    )
    splits = [half_of(conv_cols), heads + dt_pad, half_of(inner), half_of(width)]
    later_splits = splits[2:]
    inside = own_kernels()
    weights = shards if inside else gather_rows(shards, parts)

    resid_wide = resid_in.astype(f32)
    rate = -jnp.exp(a_log)
    lane_pad = (0, (-heads) % 128)
    skip_wide = jnp.repeat(skip_scale, hw)[None]
    gain_wide = gate_gain[None]
    cw_keys, cw_vals = conv_weight[:, inner:], conv_weight[:, :inner]
    made = front(
        resid_in, norm_gain[None], conv_weight, conv_bias[None], jnp.pad(dt_bias, lane_pad)[None],
        jnp.pad(rate, lane_pad)[None], skip_wide, gain_wide, weights, parts, splits if inside else [], hw, heads, n, 1,
    )
    x2, keys, slope_keys, cin_keys, colpack, rowpack, raw, step = made[:8]
    v, slope_vals, cin_vals, y, carried, gate, normed_out, rg = made[8:16]
    full_conv, full_dt, full_gate, full_out = [w.reshape(-1, w.shape[-1]) for w in (made[16:] if inside else weights)]
    x_ext = x2.reshape(batch, span + HALO, width)
    mixer_out = jnp.dot(normed_out, full_out, preferred_element_type=f32)
    output = (mask * (resid_wide + mixer_out)).astype(bf16)

    mixer_grad = (mask * out_grad.astype(f32)).astype(bf16)
    mean = jnp.sum(mixer_grad.astype(f32) * mixer_out, axis=-1, keepdims=True) * (1.0 / inner)
    norms = jnp.concatenate([rg[..., :1], mean, jnp.zeros((batch, span, 6), f32)], axis=-1)
    grad_out = jnp.einsum("bsi,bsd->id", normed_out, mixer_grad, preferred_element_type=f32).astype(bf16)
    made = gate_backward(
        mixer_grad, full_out, y, gate, norms, gain_wide, v, keys, colpack, rowpack, carried, skip_wide,
        [grad_out] if inside else [], later_splits[1:] if inside else [], hw, span, 7,
    )
    dgate, dv, later, cols_one, dq, dk, dgain, dskip = made[:8]
    (sum_out,) = made[8:] if inside else scatter_rows([grad_out], later_splits[1:], None, 5)
    x_rows = x_ext[:, HALO:]
    grad_gate = jnp.einsum("bsd,bse->de", x_rows, dgate, preferred_element_type=f32).astype(bf16)
    made = back(
        later, carried, keys, v, dv, colpack, cin_vals, cw_vals, slope_vals,
        [grad_gate] if inside else [], later_splits[:1] if inside else [], hw, span, 2,
    )
    cig_vals, cols_two, dk2, dcw_vals, dcb_vals, dlast = made[:6]
    (sum_gate,) = made[6:] if inside else scatter_rows([grad_gate], later_splits[:1], None, 5)
    cig_keys, dcw_keys, dcb_keys = keys_backward(dk, dk2, dq, cin_keys, cw_keys, slope_keys, span)

    raw, step = raw[..., :heads], step[..., :heads]
    rise = ungrouped(cols_one[..., :HEADS])
    direct = ungrouped(cols_one[..., HEADS:])
    ahead = ungrouped(cols_two)
    moved = ahead * step
    tri = causal(span, False).astype(f32)
    block_decay = jnp.exp2(colpack[:, :, span - 1, :HEADS]).transpose(1, 0, 2).reshape(batch, heads)
    last = jnp.sum(moved, axis=1) + dlast[:, 0].reshape(batch, heads, hw).sum(-1) * block_decay
    dlog = rise - moved
    dlog = jnp.einsum("ts,bth->bsh", tri, dlog, precision=highest) + last[:, None, :]
    grad_a = jnp.sum(dlog * step, axis=(0, 1)) * rate
    step_grad = direct + ahead + dlog * rate
    dt_grad = step_grad * jax.nn.sigmoid(raw)
    grad_bias = jnp.sum(dt_grad, axis=(0, 1))
    step_low = jnp.pad(dt_grad.astype(bf16), ((0, 0), (HALO, 0), (0, dt_pad)))

    cig = jnp.concatenate([cig_vals, cig_keys, step_low], axis=-1)
    grad_conv = jnp.einsum("bsd,bse->de", x_ext, cig, preferred_element_type=f32).astype(bf16)
    pieces = (
        norm_gain,
        jnp.concatenate([dcw_vals, dcw_keys], axis=1),
        jnp.concatenate([dcb_vals, dcb_keys], axis=1)[0],
        dgain[0],
        grad_bias,
        grad_a,
        dskip[0].reshape(heads, hw).sum(-1),
    )
    flat = jnp.concatenate([p.reshape(-1) for p in pieces])
    packed = jnp.pad(flat, (0, (-flat.size) % 1024)).reshape(-1, 128)
    made = tail(
        cig_vals, full_conv, dgate, full_gate, cig_keys, step_low, full_dt, resid_in, mixer_grad,
        norm_gain[None], packed, [grad_conv] if inside else [], [half_of(conv_all)] if inside else [], span, 6,
    )
    input_grad, small = made[:2]
    if inside:
        sum_conv = made[2]
    else:
        sum_conv, small = scatter_rows([grad_conv], [half_of(conv_all)], small, 6)
    flat, sums, at = small.reshape(-1), [], 0
    for p in pieces:
        sums.append(flat[at : at + p.size].reshape(p.shape))
        at += p.size
    sum_norm, sum_cw, sum_cb, sum_gain, sum_bias, sum_a, sum_skip = sums
    return (
        output,
        input_grad,
        jnp.concatenate([sum_gate, sum_conv[:, :conv_cols]], axis=1),
        sum_conv[:, conv_cols : conv_cols + heads],
        sum_out,
        sum_norm,
        sum_cw,
        sum_cb,
        sum_bias,
        sum_a,
        sum_skip,
        sum_gain,
    )


def solution(mesh):
    rows = P("dp", "seq", None)
    shard = P(("dp", "seq"), None)
    return jax.shard_map(
        on_device,
        mesh=mesh,
        in_specs=(rows, rows, P("dp"), P(), shard, shard, P(), P(), P(), P(), P(), P(), shard),
        out_specs=(rows, rows, shard, shard, shard, P(), P(), P(), P(), P(), P(), P()),
        check_vma=False,
    )
```
